32 devices in a mesh: section: 2 (over y), dp: 16 (over z, x, core).
Axes of the slice: x: 2, y: 2, z: 4, core: 2. Of those that a mesh axis runs over, the one named last changes fastest.
Arguments:
- tokens: int32 [32, 128], P('dp'), may hold values from 0 to 31
- lengths: int32 [32, 4], P('dp'), may hold values from 1 to 112, 128 in all within a row
- counted: int32 [32, 128], P('dp'), may hold values from 0 to 1
- partners: int32 [128], P('dp'), may hold values from 0 to 127, as said below
- qkv_weight: float32 [2, 1024, 3072], P('section', 'dp'), may hold values from -0.1875 to 0.1875
- out_weight: float32 [2, 1024, 1024], P('section', 'dp'), may hold values from -0.75 to 0.75
- up_weight: float32 [2, 1024, 4096], P('section', 'dp'), may hold values from -0.1875 to 0.1875
- down_weight: float32 [2, 4096, 1024], P('section', 'dp'), may hold values from -0.09375 to 0.09375
- vectors: float32 [2, 7168], P('section', 'dp')
- tables: float32 [66, 1024], P(None, ('section', 'dp'))
- head_bias: float32 [32], replicated, may hold values from -3 to 3
- qkv_moment: float32 [2, 1024, 3072], P('section', 'dp'), may hold values from -2.3841858e-06 to 2.3841858e-06
- out_moment: float32 [2, 1024, 1024], P('section', 'dp'), may hold values from -2.3841858e-06 to 2.3841858e-06
- up_moment: float32 [2, 1024, 4096], P('section', 'dp'), may hold values from -2.3841858e-06 to 2.3841858e-06
- down_moment: float32 [2, 4096, 1024], P('section', 'dp'), may hold values from -2.3841858e-06 to 2.3841858e-06
- vector_moment: float32 [2, 7168], P('section', 'dp'), may hold values from -9.536743e-06 to 9.536743e-06
- table_moment: float32 [66, 1024], P(None, ('section', 'dp')), may hold values from -9.536743e-06 to 9.536743e-06
- bias_moment: float32 [32], replicated, may hold values from -9.536743e-06 to 9.536743e-06
- qkv_square: float32 [2, 1024, 3072], P('section', 'dp'), may hold values from 9.536743e-13 to 3.3378602e-12
- out_square: float32 [2, 1024, 1024], P('section', 'dp'), may hold values from 9.536743e-13 to 3.3378602e-12
- up_square: float32 [2, 1024, 4096], P('section', 'dp'), may hold values from 9.536743e-13 to 3.3378602e-12
- down_square: float32 [2, 4096, 1024], P('section', 'dp'), may hold values from 9.536743e-13 to 3.3378602e-12
- vector_square: float32 [2, 7168], P('section', 'dp'), may hold values from 1.5258789e-11 to 5.3405762e-11
- table_square: float32 [66, 1024], P(None, ('section', 'dp')), may hold values from 1.5258789e-11 to 5.3405762e-11
- bias_square: float32 [32], replicated, may hold values from 1.5258789e-11 to 5.3405762e-11
Outputs:
- grad_norm: float32 [], replicated
- loss_parts: float32 [3], replicated
- moment_qkv: float32 [2, 1024, 3072], P('section', 'dp')
- square_qkv: float32 [2, 1024, 3072], P('section', 'dp')
- weight_qkv: float32 [2, 1024, 3072], P('section', 'dp')
- moment_out: float32 [2, 1024, 1024], P('section', 'dp')
- square_out: float32 [2, 1024, 1024], P('section', 'dp')
- weight_out: float32 [2, 1024, 1024], P('section', 'dp')
- moment_up: float32 [2, 1024, 4096], P('section', 'dp')
- square_up: float32 [2, 1024, 4096], P('section', 'dp')
- weight_up: float32 [2, 1024, 4096], P('section', 'dp')
- moment_down: float32 [2, 4096, 1024], P('section', 'dp')
- square_down: float32 [2, 4096, 1024], P('section', 'dp')
- weight_down: float32 [2, 4096, 1024], P('section', 'dp')
- moment_vector: float32 [2, 7168], P('section', 'dp')
- square_vector: float32 [2, 7168], P('section', 'dp')
- weight_vector: float32 [2, 7168], P('section', 'dp')
- moment_table: float32 [66, 1024], P(None, ('section', 'dp'))
- square_table: float32 [66, 1024], P(None, ('section', 'dp'))
- weight_table: float32 [66, 1024], P(None, ('section', 'dp'))
- moment_bias: float32 [32], replicated
- square_bias: float32 [32], replicated
- weight_bias: float32 [32], replicated
The draws below stay inside these ranges and needn't reach their ends.
Inputs may be any that keep to these rules, and one draw needn't show every extreme that they name: Each row holds the lengths of the 4 sequences of one pack and sums to 128. Sequences come in pairs: partners[partners[i]] = i and partners[i] != i.
All inputs are finite; a program needn't handle non-finite values.
Results may differ from the reference program's by a relative error of at most 0.015.
The reference program's roundings to bfloat16 on the way count: a program that leaves them out, or rounds other values in their place, can miss the bound.
Values may be sent and summed in bfloat16 or wider, within the bound.
No kernel may reach another device: no remote copies, remote signals or barrier semaphores. Data moves between devices by JAX's collectives and lax.ppermute only.
A program may use at most 256 MiB of HBM per device.

```python
import math
import jax
import jax.numpy as jnp
import numpy as np
from jax import lax

HEAD = 64
D = 1024
FF = 4096
V = 32
ROT = 32
SLOT = 128
SPP = 4
STEP = 10
LAYERS = 2
PACKS = 32
NSEQ = 128


def draw_counted(key, part):
    key = jax.random.fold_in(key, 11)
    rolls = jax.random.randint(key, (PACKS, SLOT), 0, 100)
    level = 30 + 60 * jnp.arange(PACKS, dtype=jnp.int32) // PACKS
    return (rolls < level[:, None]).astype(jnp.int32)


def draw_partners(key, part):
    key = jax.random.fold_in(key, 12)
    order = jax.random.permutation(key, NSEQ).astype(jnp.int32)
    pairs = order.reshape(NSEQ // 2, 2)
    partner = jnp.zeros((NSEQ,), jnp.int32)
    partner = partner.at[pairs[:, 0]].set(pairs[:, 1]).at[pairs[:, 1]].set(pairs[:, 0])
    return partner.astype(jnp.int32)


def draw_vectors(key, part):
    key = jax.random.fold_in(key, 13)
    first_key, second_key = jax.random.split(key)
    ramp = jnp.arange(D, dtype=jnp.float32) / D
    noise = jax.random.uniform(first_key, (LAYERS, D), jnp.float32, 0.8, 1.2)
    gain = (0.5 + ramp)[None, :] * noise
    rest = 0.3 * jax.random.normal(second_key, (LAYERS, 2 * D + FF), jnp.float32)
    return jnp.concatenate([gain, rest], 1).astype(jnp.float32)


def draw_tables(key, part):
    key = jax.random.fold_in(key, 14)
    keys = jax.random.split(key, 4)
    ramp = jnp.arange(D, dtype=jnp.float32) / D
    noise = jax.random.uniform(keys[2], (1, D), jnp.float32, 0.8, 1.2)
    embed = jax.random.normal(keys[0], (V, D), jnp.float32)
    head = 2.0 * D ** (-0.5) * jax.random.normal(keys[1], (V, D), jnp.float32)
    gain = (0.5 + ramp)[None, :] * noise
    bias = 0.3 * jax.random.normal(keys[3], (1, D), jnp.float32)
    return jnp.concatenate([embed, head, gain, bias], 0).astype(jnp.float32)


def place_ends(drawn, rng, low, top_value):
    longest = drawn.shape.index(max(drawn.shape))
    spots = []
    for shift in (0, 1):
        where = [jax.random.randint(jax.random.fold_in(rng, axis), (), 0, length) for axis, length in enumerate(drawn.shape)]
        where[longest] = (where[longest] + shift) % drawn.shape[longest]
        spots.append(tuple(where))
    return drawn.at[spots[0]].set(low).at[spots[1]].set(top_value)


def steps_of(own_key, dims, cuts, low, high):
    level = 1.0
    for dim, shards_of in cuts:
        draws = jax.random.uniform(jax.random.fold_in(jax.random.fold_in(own_key, 6), dim), (shards_of,), jnp.float32, low / len(cuts), high / len(cuts))
        level = level * jnp.repeat(jnp.exp(draws), dims[dim] // shards_of).reshape((-1,) + (1,) * (len(dims) - 1 - dim))
    return level


def split_up(amount, total, reach, lean):
    weights = [(1 << 20) // math.isqrt(rank ** lean) + 1 for rank in range(2, amount + 1)]
    surplus, holding = total - reach - (amount - 1), [1] * (amount - 1)
    while surplus > 0:
        candidates = [i for i in range(amount - 1) if holding[i] < reach]
        pool, left = sum([weights[i] for i in candidates]), surplus
        for i in candidates:
            extra = min(reach - holding[i], max(1, left * weights[i] // pool), surplus)
            holding[i] = holding[i] + extra
            surplus = surplus - extra
    return np.array([reach] + holding)


def ragged_sizes(key, count, total, bound, lean):
    if count == 2:
        one = jax.random.randint(key, (), max(1, total - bound), min(bound, total - 1) + 1)
        return jnp.stack([one, total - one])
    sizes = jnp.asarray(split_up(count, total, bound, lean), jnp.int32)
    pairs = (count - 1) // 2
    source_of, receiver = sizes[1:1 + 2 * pairs:2], sizes[2:2 + 2 * pairs:2]
    slack = jnp.minimum(source_of - 1, bound - receiver)
    moved = jax.random.randint(jax.random.fold_in(key, 1), (pairs,), 0, 1 << 20) % (slack + 1)
    sizes = sizes.at[1:1 + 2 * pairs:2].set(source_of - moved).at[2:2 + 2 * pairs:2].set(receiver + moved)
    return sizes[jax.random.permutation(jax.random.fold_in(key, 2), count)]


def scatter_about(rng, shape, scale, most, cuts=(), kind=jnp.bfloat16):
    array = jax.random.normal(rng, shape, jnp.float32) * scale
    if len(cuts) > 0:
        array = steps_of(rng, shape, cuts, -0.22, 0.18) * array
    return jnp.clip(array, min=-most, max=most).astype(kind)


def setup_inputs(seed: int = 0) -> dict:
    seeds = jax.random.split(jax.random.key(seed), 26)
    return {
        "tokens": place_ends(jax.random.randint(seeds[0], (PACKS, SLOT), 0, V), jax.random.fold_in(seeds[0], 1), 0, V - 1).astype(jnp.int32),
        "lengths": jax.vmap(lambda own: ragged_sizes(own, SPP, SLOT, SLOT - max(SPP, SLOT // 8), 2))(jax.random.split(seeds[1], PACKS)).reshape((PACKS, SPP)).astype(jnp.int32),
        "counted": draw_counted(jax.random.fold_in(seeds[25], 71), 0),
        "partners": draw_partners(jax.random.fold_in(seeds[25], 71), 0),
        "qkv_weight": scatter_about(seeds[4], (LAYERS, D, 3 * D), D ** -0.5, 0.1875, ((0, 2), (1, 16)), jnp.float32),
        "out_weight": scatter_about(seeds[5], (LAYERS, D, D), (D * 2 * SPP // SLOT) ** -0.5, 0.75, ((0, 2), (1, 16)), jnp.float32),
        "up_weight": scatter_about(seeds[6], (LAYERS, D, FF), D ** -0.5, 0.1875, ((0, 2), (1, 16)), jnp.float32),
        "down_weight": scatter_about(seeds[7], (LAYERS, FF, D), FF ** -0.5, 0.09375, ((0, 2), (1, 16)), jnp.float32),
        "vectors": draw_vectors(jax.random.fold_in(seeds[25], 71), 0),
        "tables": draw_tables(jax.random.fold_in(seeds[25], 71), 0),
        "head_bias": scatter_about(seeds[10], (V,), 0.5, 3.0, (), jnp.float32),
        "qkv_moment": scatter_about(seeds[11], (LAYERS, D, 3 * D), (0.0022 * (LAYERS * (4 * D * D + 2 * D * FF)) ** -0.5), 2.384185791015625e-06, ((0, 2), (1, 16)), jnp.float32),
        "out_moment": scatter_about(seeds[12], (LAYERS, D, D), (0.0022 * (LAYERS * (4 * D * D + 2 * D * FF)) ** -0.5), 2.384185791015625e-06, ((0, 2), (1, 16)), jnp.float32),
        "up_moment": scatter_about(seeds[13], (LAYERS, D, FF), (0.0022 * (LAYERS * (4 * D * D + 2 * D * FF)) ** -0.5), 2.384185791015625e-06, ((0, 2), (1, 16)), jnp.float32),
        "down_moment": scatter_about(seeds[14], (LAYERS, FF, D), (0.0022 * (LAYERS * (4 * D * D + 2 * D * FF)) ** -0.5), 2.384185791015625e-06, ((0, 2), (1, 16)), jnp.float32),
        "vector_moment": scatter_about(seeds[15], (LAYERS, 3 * D + FF), (0.0088 * (LAYERS * (4 * D * D + 2 * D * FF)) ** -0.5), 9.5367431640625e-06, ((0, 2), (1, 16)), jnp.float32),
        "table_moment": scatter_about(seeds[16], (2 * V + 2, D), (0.0088 * (LAYERS * (4 * D * D + 2 * D * FF)) ** -0.5), 9.5367431640625e-06, ((1, 32),), jnp.float32),
        "bias_moment": scatter_about(seeds[17], (V,), (0.0088 * (LAYERS * (4 * D * D + 2 * D * FF)) ** -0.5), 9.5367431640625e-06, (), jnp.float32),
        "qkv_square": jnp.clip(jnp.exp(math.log(3.337860153204697e-12) - 1.252763 * jax.random.uniform(seeds[18], (LAYERS, D, 3 * D), jnp.float32) ** steps_of(seeds[18], (LAYERS, D, 3 * D), ((0, 2), (1, 16)), -0.2, 0.2)), 9.536743139984538e-13, 3.337860153204697e-12),
        "out_square": jnp.clip(jnp.exp(math.log(3.337860153204697e-12) - 1.252763 * jax.random.uniform(seeds[19], (LAYERS, D, D), jnp.float32) ** steps_of(seeds[19], (LAYERS, D, D), ((0, 2), (1, 16)), -0.2, 0.2)), 9.536743139984538e-13, 3.337860153204697e-12),
        "up_square": jnp.clip(jnp.exp(math.log(3.337860153204697e-12) - 1.252763 * jax.random.uniform(seeds[20], (LAYERS, D, FF), jnp.float32) ** steps_of(seeds[20], (LAYERS, D, FF), ((0, 2), (1, 16)), -0.2, 0.2)), 9.536743139984538e-13, 3.337860153204697e-12),
        "down_square": jnp.clip(jnp.exp(math.log(3.337860153204697e-12) - 1.252763 * jax.random.uniform(seeds[21], (LAYERS, FF, D), jnp.float32) ** steps_of(seeds[21], (LAYERS, FF, D), ((0, 2), (1, 16)), -0.2, 0.2)), 9.536743139984538e-13, 3.337860153204697e-12),
        "vector_square": jnp.clip(jnp.exp(math.log(5.340576245127515e-11) - 1.252763 * jax.random.uniform(seeds[22], (LAYERS, 3 * D + FF), jnp.float32) ** steps_of(seeds[22], (LAYERS, 3 * D + FF), ((0, 2), (1, 16)), -0.2, 0.2)), 1.525878902397526e-11, 5.340576245127515e-11),
        "table_square": jnp.clip(jnp.exp(math.log(5.340576245127515e-11) - 1.252763 * jax.random.uniform(seeds[23], (2 * V + 2, D), jnp.float32) ** steps_of(seeds[23], (2 * V + 2, D), ((1, 32),), -0.2, 0.2)), 1.525878902397526e-11, 5.340576245127515e-11),
        "bias_square": jnp.clip(jnp.exp(jax.random.uniform(seeds[24], (V,), jnp.float32, math.log(1.525878902397526e-11), math.log(5.340576245127515e-11))), 1.525878902397526e-11, 5.340576245127515e-11),
    }


@jax.custom_vjp
def low(v):
    return lax.optimization_barrier(v.astype(jnp.bfloat16)).astype(jnp.float32)

@jax.custom_vjp
def low_back(v):
    return v

def low_keep(v):
    return (low(v), None)

def low_pass(kept, grad):
    return (grad,)

def back_keep(v):
    return (v, None)

def back_low(kept, grad):
    return (low(grad),)
low.defvjp(low_keep, low_pass)
low_back.defvjp(back_keep, back_low)
EPS_NORM = 1e-05
PENALTY = 2.0
CLIP_AT = 0.02
RATE_MAT = 0.02
RATE_OUT = 0.1
RATE_VEC = 0.2
BETA_ONE = 0.9
BETA_TWO = 0.95
EPS_ADAM = 1e-08
DECAY = 0.1

def matmul(left, right):
    return jnp.dot(left, right, precision=lax.Precision.HIGHEST, preferred_element_type=jnp.float32)

def layer_norm(x, gain, bias):
    mean = lax.optimization_barrier(jnp.mean(x, -1, keepdims=True))
    centred = x - mean
    variance = lax.optimization_barrier(jnp.mean(centred * centred, -1, keepdims=True))
    return centred * lax.rsqrt(variance + EPS_NORM) * gain + bias

def pack_layout(lengths_row, tokens_row, counted_row):
    slots = tokens_row.shape[0]
    ends = jnp.cumsum(lengths_row).astype(jnp.int32)
    starts = ends - lengths_row
    index = jnp.arange(slots, dtype=jnp.int32)
    segment = lax.optimization_barrier(jnp.sum((index[:, None] >= ends[None, :]).astype(jnp.int32), 1))
    member = segment[:, None] == jnp.arange(lengths_row.shape[0], dtype=jnp.int32)[None, :]
    position = index - lax.optimization_barrier(jnp.sum(jnp.where(member, starts[None, :], 0), 1))
    target = jnp.concatenate([tokens_row[1:], jnp.zeros((1,), jnp.int32)])
    same = jnp.concatenate([segment[1:] == segment[:-1], jnp.zeros((1,), bool)])
    weight = (same & (counted_row == 1)).astype(jnp.float32)
    return (segment, member, position, target, weight)

def rope_tables(position):
    half = ROT // 2
    freq = 10000.0 ** (-2.0 * jnp.arange(half, dtype=jnp.float32) / ROT)
    angle = position.astype(jnp.float32)[:, None] * freq[None, :]
    return (jnp.cos(angle)[:, None, :], jnp.sin(angle)[:, None, :])

def rotate(values, cosine, sine):
    half = ROT // 2
    first = values[..., :half]
    second = values[..., half:ROT]
    return jnp.concatenate([first * cosine - second * sine, second * cosine + first * sine, values[..., ROT:]], -1)

def block(x, qkv, wout, wup, wdown, vec, cosine, sine, mask):
    rows, width = x.shape
    heads = width // HEAD
    scale = 1.0 / math.sqrt(HEAD)
    gain, bias = (vec[:width], vec[width:2 * width])
    bias_down, bias_up = (vec[2 * width:3 * width], vec[3 * width:])
    h_low = low(layer_norm(x, gain, bias))
    proj = low_back(matmul(h_low, qkv))
    query = low(rotate(proj[:, :width].reshape(rows, heads, HEAD), cosine, sine))
    keys = low(rotate(proj[:, width:2 * width].reshape(rows, heads, HEAD), cosine, sine))
    values = low(proj[:, 2 * width:].reshape(rows, heads, HEAD))
    scores = low_back(jnp.einsum('shd,thd->hst', query, keys, precision=lax.Precision.HIGHEST) * scale)
    scores = jnp.where(mask[None], scores, -1e+30)
    probs = low(jax.nn.softmax(scores, -1))
    attended = jnp.einsum('hst,thd->shd', probs, values, precision=lax.Precision.HIGHEST).reshape(rows, width)
    attended = low_back(low(attended))
    active = low(jax.nn.gelu(low_back(matmul(h_low, wup) + bias_up), approximate=True))
    return x + low_back(matmul(attended, wout) + matmul(active, wdown) + bias_down)

def pack_forward(params, token_row, position, segment, target, weight, member):
    qkv, wout, wup, wdown, vec, tab, out_bias = params
    cosine, sine = rope_tables(position)
    index = jnp.arange(token_row.shape[0], dtype=jnp.int32)
    mask = (segment[:, None] == segment[None, :]) & (index[None, :] <= index[:, None])
    x = jnp.take(tab[:V], token_row, axis=0)
    for layer in range(LAYERS):
        x = block(x, qkv[layer], wout[layer], wup[layer], wdown[layer], vec[layer], cosine, sine, mask)
        if layer < LAYERS - 1:
            x = low_back(low(x))
    final = low(layer_norm(x, tab[2 * V], tab[2 * V + 1]))
    logits = low_back(matmul(final, tab[V:2 * V].T) + out_bias)
    logp = jax.nn.log_softmax(logits, -1)
    picked = jnp.take_along_axis(logp, target[:, None], 1)[:, 0] * weight
    return (-jnp.sum(picked), lax.optimization_barrier(jnp.sum(member.astype(jnp.float32) * picked[:, None], 0)))

def group_loss(params, batch):
    token_row, position, segment, target, weight, member = batch
    return jax.vmap(pack_forward, in_axes=(None, 0, 0, 0, 0, 0, 0))(params, token_row, position, segment, target, weight, member)

def adam(weight, first, second, grad, rate, decay):
    first_new = BETA_ONE * first + (1.0 - BETA_ONE) * grad
    second_new = BETA_TWO * second + (1.0 - BETA_TWO) * grad * grad
    update = first_new / (1.0 - BETA_ONE ** STEP) / (jnp.sqrt(second_new / (1.0 - BETA_TWO ** STEP)) + EPS_ADAM)
    return (first_new, second_new, weight - rate * (update + decay * weight))

def reference(tokens, lengths, counted, partners, qkv_weight, out_weight, up_weight, down_weight, vectors, tables, head_bias, qkv_moment, out_moment, up_moment, down_moment, vector_moment, table_moment, bias_moment, qkv_square, out_square, up_square, down_square, vector_square, table_square, bias_square):
    masters = (qkv_weight, out_weight, up_weight, down_weight, vectors, tables, head_bias)
    moments = (qkv_moment, out_moment, up_moment, down_moment, vector_moment, table_moment, bias_moment)
    squares_in = (qkv_square, out_square, up_square, down_square, vector_square, table_square, bias_square)
    segment, member, position, target, weight = jax.vmap(pack_layout)(lengths, tokens, counted)
    count = jnp.sum(weight)
    per_seq = lax.optimization_barrier(jnp.sum(member.astype(jnp.float32) * weight[..., None], 1)).reshape(NSEQ)
    group = math.gcd(PACKS, 16)
    batch = tuple((a.reshape((PACKS // group, group) + a.shape[1:]) for a in (tokens, position, segment, target, weight, member)))
    saved = jax.checkpoint(group_loss)

    def total_loss(params):
        lowered = tuple((low(p) for p in params))
        ce_parts, lik_sums = lax.map(lambda piece: saved(lowered, piece), batch)
        likelihood = lik_sums.reshape(NSEQ) / jnp.maximum(per_seq, 1.0)
        differ = likelihood - likelihood[partners]
        penalty = 0.5 * jnp.sum(differ * differ)
        ce_sum = jnp.sum(ce_parts)
        return (ce_sum / count + PENALTY * penalty / NSEQ, (ce_sum, penalty))
    value_now, backward, extras = jax.vjp(total_loss, masters, has_aux=True)
    grads = backward(jnp.ones_like(value_now))[0]
    grad_norm = jnp.sqrt(sum((jnp.sum(g * g) for g in grads)))
    factor = jnp.minimum(1.0, CLIP_AT / grad_norm)
    rates = (RATE_MAT, RATE_OUT, RATE_MAT, RATE_MAT, RATE_VEC, RATE_VEC, RATE_VEC)
    decays = (DECAY, DECAY, DECAY, DECAY, 0.0, 0.0, 0.0)
    results = []
    for number in range(7):
        results.extend(adam(masters[number], moments[number], squares_in[number], grads[number] * factor, rates[number], decays[number]))
    loss_parts = jnp.stack([extras[0], count, extras[1]])
    return (grad_norm, loss_parts, results[0], results[1], results[2], results[3], results[4], results[5], results[6], results[7], results[8], results[9], results[10], results[11], results[12], results[13], results[14], results[15], results[16], results[17], results[18], results[19], results[20])
```

```python
import math

import jax
import jax.numpy as jnp
from jax import lax
from jax.sharding import Mesh
from jax.sharding import PartitionSpec as P

HEAD = 64
ROT = 32
STEP = 10

EPS_NORM = 1e-05
PENALTY = 2.0
CLIP_AT = 0.02
RATE_MAT = 0.02
RATE_OUT = 0.1
RATE_VEC = 0.2
BETA_ONE = 0.9
BETA_TWO = 0.95
EPS_ADAM = 1e-08
DECAY = 0.1
GELU_C = 0.7978845608028654

ALL = ("y", "h", "k", "x", "c")
PLANE = ("h", "k", "x", "c")
LOW = jnp.bfloat16
F32 = jnp.float32
EXACT = lax.Precision.HIGHEST


def mm(left, right):
    return jnp.dot(left, right, preferred_element_type=F32)


def mm_t(left, right):
    return lax.dot_general(left, right, (((1,), (1,)), ((), ())), preferred_element_type=F32)


def t_mm(left, right):
    return lax.dot_general(left, right, (((0,), (0,)), ((), ())), preferred_element_type=F32)


def mm_exact(left, right, dims):
    return lax.dot_general(
        left.astype(F32), right.astype(F32), (dims, ((), ())), precision=EXACT
    )


def pick(array, index):
    return lax.dynamic_index_in_dim(array, index, 0, keepdims=False)


def spread(value, axes):
    many = lax.axis_size(axes)
    return lax.all_to_all(jnp.broadcast_to(value[None], (many,) + value.shape), axes, 0, 0, tiled=True)


def trade(pieces, axes):
    return lax.all_to_all(pieces, axes, 0, 0, tiled=True)


def shift(value, axis, by):
    many = lax.axis_size(axis)
    return lax.ppermute(value, axis, [(i, (i + by) % many) for i in range(many)])


def ordered(own, other, bit, axis):
    return jnp.stack(
        [jnp.where(bit == 0, own, other), jnp.where(bit == 0, other, own)], axis
    )


def layer_norm(x, gain, bias):
    mean = jnp.mean(x, -1, keepdims=True)
    centred = x - mean
    inverse = lax.rsqrt(jnp.mean(centred * centred, -1, keepdims=True) + EPS_NORM)
    normed = centred * inverse
    return (normed * gain + bias, normed, inverse)


def norm_back(grad, normed, inverse, gain):
    scaled = grad * gain
    return inverse * (
        scaled
        - jnp.mean(scaled, -1, keepdims=True)
        - normed * jnp.mean(scaled * normed, -1, keepdims=True)
    )


def gelu_pair(value):
    inner = jnp.tanh(GELU_C * (value + 0.044715 * value * value * value))
    result = 0.5 * value * (1.0 + inner)
    slope = 0.5 * (1.0 + inner) + 0.5 * value * (1.0 - inner * inner) * GELU_C * (
        1.0 + 3.0 * 0.044715 * value * value
    )
    return (result, slope)


def one_hot(row, vocab, dtype):
    return (row[:, None] == jnp.arange(vocab, dtype=jnp.int32)[None, :]).astype(dtype)


def pack_layout(lengths_row, slots):
    ends = jnp.cumsum(lengths_row)
    starts = ends - lengths_row
    index = jnp.arange(slots, dtype=jnp.int32)
    segment = jnp.sum((index[:, None] >= ends[None, :]).astype(jnp.int32), 1)
    member = segment[:, None] == jnp.arange(lengths_row.shape[0], dtype=jnp.int32)[None, :]
    position = index - jnp.sum(jnp.where(member, starts[None, :], 0), 1)
    return (segment, position)


def rope_tables(position):
    half = ROT // 2
    freq = 10000.0 ** (-2.0 * jnp.arange(half, dtype=F32) / ROT)
    angle = position.astype(F32)[..., None] * freq
    return (jnp.cos(angle)[..., None, :], jnp.sin(angle)[..., None, :])


def rotate(values, cosine, sine, sign):
    half = ROT // 2
    first = values[..., :half]
    second = values[..., half:ROT]
    return jnp.concatenate(
        [
            first * cosine - sign * second * sine,
            second * cosine + sign * first * sine,
            values[..., ROT:],
        ],
        -1,
    )


def attend(query, keys, values, mask):
    scores = jnp.einsum("pshd,pthd->phst", query, keys, preferred_element_type=F32)
    scores = jnp.where(mask[:, None], scores * (1.0 / math.sqrt(HEAD)), -1e30)
    expo = jnp.exp(scores - jnp.max(scores, -1, keepdims=True))
    probs = expo / jnp.sum(expo, -1, keepdims=True)
    out = jnp.einsum("phst,pthd->pshd", probs.astype(LOW), values, preferred_element_type=F32)
    return (out.astype(LOW), probs)


def attend_back(d_out, probs, query, keys, values):
    scale = 1.0 / math.sqrt(HEAD)
    d_values = jnp.einsum("phst,pshd->pthd", probs.astype(LOW), d_out, preferred_element_type=F32)
    d_probs = jnp.einsum("pshd,pthd->phst", d_out, values, preferred_element_type=F32)
    d_scores = (probs * (d_probs - jnp.sum(probs * d_probs, -1, keepdims=True))).astype(LOW)
    d_query = jnp.einsum("phst,pthd->pshd", d_scores, keys, preferred_element_type=F32) * scale
    d_keys = jnp.einsum("phst,pshd->pthd", d_scores, query, preferred_element_type=F32) * scale
    return (d_query, d_keys, d_values)


def adam(weight, first, second, grad, rate, decay):
    first_new = BETA_ONE * first + (1.0 - BETA_ONE) * grad
    second_new = BETA_TWO * second + (1.0 - BETA_TWO) * grad * grad
    update = (
        first_new
        / (1.0 - BETA_ONE**STEP)
        / (jnp.sqrt(second_new / (1.0 - BETA_TWO**STEP)) + EPS_ADAM)
    )
    return (first_new, second_new, weight - rate * (update + decay * weight))


class Group:
    def __init__(self, sections, spans):
        self.sections = sections
        self.spans = spans
        self.offsets = [(dk, dy) for dk in range(2) for dy in range(sections)]

    def route(self, dk, dy, sign):
        s = self.sections
        return [
            (a * 2 + b, ((a + sign * dy) % s) * 2 + (b + sign * dk) % 2)
            for a in range(s)
            for b in range(2)
        ]

    def gather(self, value):
        pieces = []
        for dk, dy in self.offsets:
            piece = value
            if (dk, dy) != (0, 0):
                piece = lax.ppermute(value, ("y", "k"), self.route(dk, dy, 1))
            pieces.append(piece)
        mine = jnp.stack(pieces)
        return jnp.stack([mine, shift(mine, "c", 1)])

    def scatter(self, parts):
        mine = parts[0] + shift(parts[1].astype(LOW), "c", 1).astype(F32)
        total = mine[0]
        for number, (dk, dy) in enumerate(self.offsets):
            if (dk, dy) == (0, 0):
                continue
            piece = lax.ppermute(mine[number].astype(LOW), ("y", "k"), self.route(dk, dy, -1))
            total = total + piece.astype(F32)
        return total


def across_gather(piece, x):
    spans = lax.axis_size("h")
    h = lax.axis_index("h")
    if spans == 2:
        both = ordered(piece, shift(piece, "h", 1), h, 0)
    else:
        stacked = jnp.stack([piece] + [shift(piece, "h", s) for s in range(1, spans)])
        both = jnp.take(stacked, (h - jnp.arange(spans)) % spans, axis=0)
    return ordered(both, shift(both, "x", 1), x, 1)


def across_scatter(parts, x):
    spans = lax.axis_size("h")
    h = lax.axis_index("h")
    flipped = jnp.swapaxes(parts, 0, 1)
    away = shift(pick(flipped, 1 - x).astype(LOW), "x", 1).astype(F32)
    mine = pick(flipped, x) + away
    total = pick(mine, h)
    for s in range(1, spans):
        total = total + shift(pick(mine, (h + s) % spans).astype(LOW), "h", s).astype(F32)
    return total


def body(
    tokens,
    lengths,
    counted,
    partners,
    qkv_weight,
    out_weight,
    up_weight,
    down_weight,
    vectors,
    tables,
    head_bias,
    qkv_moment,
    out_moment,
    up_moment,
    down_moment,
    vector_moment,
    table_moment,
    bias_moment,
    qkv_square,
    out_square,
    up_square,
    down_square,
    vector_square,
    table_square,
    bias_square,
):
    sections = lax.axis_size("y")
    spans = lax.axis_size("h")
    plane = lax.axis_size(PLANE)
    everyone = sections * plane
    y, h, k, x, c = (lax.axis_index(a) for a in ALL)
    me = lax.axis_index(PLANE)
    group = Group(sections, spans)
    micro, slots = tokens.shape
    per_pack = lengths.shape[1]
    width = qkv_weight.shape[2] // 3
    hidden = up_weight.shape[2]
    vocab = head_bias.shape[0]
    own_in = qkv_weight.shape[1]
    own_out = out_weight.shape[1]
    own_ff = down_weight.shape[1]
    shares = 4 * sections
    heads = width // HEAD
    shard_heads = heads // shares
    shard_width = width // shares
    shard_ff = hidden // shares
    rows = micro * slots // sections
    block_rows = micro * slots
    group_rows = 4 * block_rows
    group_packs = 4 * micro
    own_packs = max(1, rows // slots)
    own_pack_rows = min(rows, slots)

    low_qkv = qkv_weight[0].astype(LOW)
    low_out = out_weight[0].astype(LOW)
    low_up = up_weight[0].astype(LOW)
    low_down = down_weight[0].astype(LOW)

    table_part = tables.shape[1]
    vector_part = vectors.shape[1]
    small = jnp.concatenate(
        [
            tables.astype(LOW).reshape(-1),
            vectors[0].astype(LOW),
            lengths.astype(LOW).reshape(-1),
        ]
    )
    small_all = spread(small, ALL)
    cut_one = tables.size
    cut_two = cut_one + vector_part
    table_low = (
        small_all[:, :cut_one]
        .reshape(everyone, tables.shape[0], table_part)
        .transpose(1, 0, 2)
        .reshape(tables.shape[0], width)
    )
    vec_low = small_all[:, cut_one:cut_two].reshape(sections, plane * vector_part)
    vec_all = vec_low.astype(F32)
    lengths_all = small_all[:, cut_two:].astype(jnp.int32)
    embed = table_low[:vocab].astype(F32)
    head_low = table_low[vocab : 2 * vocab]
    final_gain = table_low[2 * vocab].astype(F32)
    final_bias = table_low[2 * vocab + 1].astype(F32)
    out_bias = head_bias.astype(LOW).astype(F32)

    segment, position = jax.vmap(lambda row: pack_layout(row, slots))(lengths)
    target = jnp.concatenate([tokens[:, 1:], jnp.zeros((micro, 1), jnp.int32)], 1)
    same = jnp.concatenate([segment[:, 1:] == segment[:, :-1], jnp.zeros((micro, 1), bool)], 1)
    weight = (same & (counted == 1)).astype(F32)
    sequence = segment + per_pack * jnp.arange(micro, dtype=jnp.int32)[:, None]

    def own(array):
        return lax.dynamic_slice_in_dim(array.reshape((block_rows,) + array.shape[2:]), y * rows, rows, 0)

    own_target = own(target)
    own_weight = own(weight)
    own_sequence = own(sequence)
    first_pack = (y * rows) // slots

    def packs_of(array):
        return lax.dynamic_slice_in_dim(array, first_pack, own_packs, 0)

    pack_tokens = packs_of(tokens)
    pack_segment = packs_of(segment)
    pack_position = packs_of(position)
    own_tokens = own(tokens).reshape(own_packs, own_pack_rows)
    own_segment = own(segment).reshape(own_packs, own_pack_rows)
    own_position = own(position).reshape(own_packs, own_pack_rows)
    pack_index = jnp.broadcast_to(jnp.arange(slots, dtype=jnp.int32), (own_packs, slots))
    own_index = (
        jnp.broadcast_to(jnp.arange(own_pack_rows, dtype=jnp.int32), (own_packs, own_pack_rows))
        + (y * rows) % slots
    )
    own_mask = (own_segment[:, :, None] == pack_segment[:, None, :]) & (
        pack_index[:, None, :] <= own_index[:, :, None]
    )

    lengths_plane = lengths_all.reshape(sections, spans, 2, 2, 2, micro * per_pack)[0]
    lengths_group = pick(lengths_plane, h)[:, :, :, :]
    lengths_group = lax.dynamic_index_in_dim(lengths_group, x, 1, keepdims=False)

    def in_group(values, fill):
        return values

    parts = []
    for dc in range(2):
        for dk in range(2):
            block_lengths = pick(pick(lengths_group, (k - dk) % 2), (c - dc) % 2)
            parts.append(block_lengths.reshape(micro, per_pack))
    group_lengths = jnp.concatenate(parts, 0)
    group_segment, group_position = jax.vmap(lambda row: pack_layout(row, slots))(group_lengths)
    turn = (y - jnp.arange(sections)) % sections

    def by_offset(array):
        cut = array.reshape((4, sections, rows) + array.shape[2:])
        return jnp.take(cut, turn, axis=1).reshape((4 * sections * rows,) + array.shape[2:])

    if rows % slots == 0:
        group_segment = by_offset(group_segment).reshape(group_packs, slots)
        group_position = by_offset(group_position).reshape(group_packs, slots)
    group_index = jnp.arange(slots, dtype=jnp.int32)
    group_mask = (group_segment[:, :, None] == group_segment[:, None, :]) & (
        group_index[None, :] <= group_index[:, None]
    )
    group_cos, group_sin = rope_tables(group_position)

    def to_group(value):
        got = group.gather(value).reshape((4, sections, rows) + value.shape[1:])
        if rows % slots:
            got = jnp.take(got, turn, axis=1)
        return got.reshape((group_rows,) + value.shape[1:])

    def from_group(value):
        cut = value.reshape((4, sections, rows) + value.shape[1:])
        if rows % slots:
            cut = jnp.take(cut, turn, axis=1)
        return group.scatter(cut.reshape((2, 2 * sections, rows) + value.shape[1:]))

    part_ff = own_ff // sections

    def columns_by_shard(qkv_rows, up_rows):
        cut_qkv = qkv_rows.reshape(own_in, 3, 2, 2, sections, shard_width)
        cut_up = up_rows.reshape(own_in, spans, 2, 2, 2, sections, part_ff)
        pieces = []
        for cc in range(2):
            for kk in range(2):
                for yy in range(sections):
                    pieces.append(
                        jnp.concatenate(
                            [cut_qkv[:, j, cc, kk, yy] for j in range(3)]
                            + [
                                cut_up[:, hh, kk, xx, cc, yy]
                                for hh in range(spans)
                                for xx in range(2)
                            ],
                            1,
                        )
                    )
        return jnp.stack(pieces).reshape((2, 2, sections) + pieces[0].shape)

    def columns_back(shards):
        cut = shards[..., : 3 * shard_width].reshape(2, 2, sections, own_in, 3, shard_width)
        qkv_rows = cut.transpose(3, 4, 0, 1, 2, 5).reshape(own_in, 3 * width)
        cut = shards[..., 3 * shard_width :].reshape(
            2, 2, sections, own_in, spans, 2, part_ff
        )
        up_rows = cut.transpose(3, 4, 1, 5, 0, 2, 6).reshape(own_in, hidden)
        return (qkv_rows, up_rows)

    small_out = width // everyone

    def out_routes(layer):
        routes = [[] for _ in range(sections)]
        for yy in range(sections):
            for hh in range(spans):
                for kk in range(2):
                    for xx in range(2):
                        for cc in range(2):
                            share = (cc * 2 + kk) * sections + yy
                            number = share * (2 * spans) + hh * 2 + xx
                            device = yy * plane + ((hh * 2 + kk) * 2 + xx) * 2 + cc
                            owner = layer * plane + number // sections
                            routes[number % sections].append((owner, device))
        return routes

    share_index = (c * 2 + k) * sections + y
    out_part = (share_index * (2 * spans) + h * 2 + x) % sections

    by_shard = columns_by_shard(low_qkv, low_up)
    shard_weights = []
    for layer in range(1, sections):
        cut_down = low_down.reshape(sections, part_ff, width)
        down_piece = cut_down[layer]
        for yy in range(sections):
            if yy != layer:
                got = lax.ppermute(cut_down[yy], "y", [(layer, yy)])
                down_piece = jnp.where(y == yy, got, down_piece)
        cut_out = low_out.reshape(sections, small_out, width)
        out_piece = jnp.zeros((small_out, width), LOW)
        for p, route in enumerate(out_routes(layer)):
            got = lax.ppermute(cut_out[p], ALL, route)
            out_piece = jnp.where(out_part == p, got, out_piece)
        tail = across_gather(jnp.concatenate([down_piece, out_piece], 0), x)
        w_down = tail[:, :, :part_ff].reshape(shard_ff, width)
        w_out = tail[:, :, part_ff:].reshape(shard_width, width)
        mine = by_shard[:, :, layer]
        for yy in range(sections):
            if yy != layer:
                got = lax.ppermute(by_shard[:, :, yy], "y", [(layer, yy)])
                mine = jnp.where(y == yy, got, mine)
        keep = pick(mine, c)
        give = shift(pick(mine, 1 - c), "c", 1)
        over_c = ordered(keep, give, c, 1)
        keep = pick(over_c, k)
        give = shift(pick(over_c, 1 - k), "k", 1)
        over_k = ordered(keep, give, k, 0)
        whole = across_gather(over_k, x)
        w_in = whole.transpose(0, 2, 1, 3, 4, 5).reshape(width, -1)
        shard_weights.append((w_in, w_out, w_down))

    first_out = low_out
    for yy in range(1, sections):
        got = lax.ppermute(low_out, "y", [(0, yy)])
        first_out = jnp.where(y == yy, got, first_out)
    pieces = jnp.stack([first_out] + [shift(first_out, "h", s) for s in range(1, spans)])
    pieces = jnp.take(pieces, (h - jnp.arange(spans)) % spans, axis=0)
    pieces = ordered(pieces, shift(pieces, "k", 1), k, 1)
    pieces = ordered(pieces, shift(pieces, "x", 1), x, 2)
    pieces = ordered(pieces, shift(pieces, "c", 1), c, 3)
    first_out = pieces.reshape(width, width)

    gain0, bias0 = vec_all[0, :width], vec_all[0, width : 2 * width]
    bias_down0, bias_up0 = vec_all[0, 2 * width : 3 * width], vec_all[0, 3 * width :]
    h0_full, normed0, inverse0 = layer_norm(embed, gain0, bias0)
    h0 = h0_full.astype(LOW)
    columns = jnp.concatenate(
        [
            low_qkv.reshape(own_in, plane, -1).transpose(1, 0, 2),
            low_up.reshape(own_in, plane, -1).transpose(1, 0, 2),
        ],
        2,
    )
    columns = trade(columns, PLANE).reshape(width, -1)
    both = mm(h0, columns)
    qkv_cols = 3 * width // plane
    proj_own = both[:, :qkv_cols]
    u_own = both[:, qkv_cols:] + lax.dynamic_slice_in_dim(bias_up0, me * own_ff, own_ff, 0)
    a0, slope0 = gelu_pair(u_own)
    a0 = a0.astype(LOW)
    ffn_part = jnp.where(y == 0, mm(a0, low_down), 0.0)
    ffn_cols = trade(ffn_part.reshape(vocab, everyone, -1).transpose(1, 0, 2), ALL)
    ffn_cols = jnp.sum(ffn_cols, 0)
    ffn_table = spread(ffn_cols, ALL).transpose(1, 0, 2).reshape(vocab, width)
    for yy in range(1, sections):
        got = lax.ppermute(proj_own, "y", [(0, yy)])
        proj_own = jnp.where(y == yy, got, proj_own)
    proj_table = spread(proj_own, PLANE).transpose(1, 0, 2).reshape(vocab, 3 * width)

    hot_pack = one_hot(pack_tokens.reshape(-1), vocab, LOW)
    hot_own = one_hot(own_tokens.reshape(-1), vocab, LOW)

    def exact_rows(hot, table):
        high = table.astype(LOW)
        rest = table - high.astype(F32)
        middle = rest.astype(LOW)
        lowest = (rest - middle.astype(F32)).astype(LOW)
        return mm(jnp.concatenate([hot, hot, hot], 1), jnp.concatenate([high, middle, lowest], 0))

    own_cos, own_sin = rope_tables(own_position)
    pack_cos, pack_sin = rope_tables(pack_position)
    q_own = exact_rows(hot_own, proj_table[:, :width])
    k_pack = exact_rows(hot_pack, proj_table[:, width : 2 * width])
    v_pack = mm(hot_pack, proj_table[:, 2 * width :].astype(LOW))
    query0 = rotate(q_own.reshape(own_packs, own_pack_rows, heads, HEAD), own_cos, own_sin, 1.0)
    query0 = query0.astype(LOW)
    keys0 = rotate(k_pack.reshape(own_packs, slots, heads, HEAD), pack_cos, pack_sin, 1.0)
    keys0 = keys0.astype(LOW)
    values0 = v_pack.reshape(own_packs, slots, heads, HEAD).astype(LOW)
    att0, probs0 = attend(query0, keys0, values0, own_mask)
    att0 = att0.reshape(rows, width)
    stay = embed + ffn_table + bias_down0
    xs = exact_rows(hot_own, stay) + mm(att0, first_out)

    kept = []
    for layer in range(1, sections):
        xs = xs.astype(LOW).astype(F32)
        w_in, w_out, w_down = shard_weights[layer - 1]
        vec = vec_all[layer]
        gain, bias, bias_down = (vec[j * width : (j + 1) * width] for j in range(3))
        cut = vec[3 * width :].reshape(spans, 2, 2, 2, sections, part_ff)
        cut = lax.dynamic_index_in_dim(cut, k, 1, keepdims=False)
        cut = lax.dynamic_index_in_dim(cut, c, 2, keepdims=False)
        bias_up = lax.dynamic_index_in_dim(cut, y, 2, keepdims=False).reshape(shard_ff)
        normed_in, normed, inverse = layer_norm(xs, gain, bias)
        hs = to_group(normed_in.astype(LOW))
        proj = mm(hs, w_in[:, : 3 * shard_width])
        q, ky, v = (
            proj[:, j * shard_width : (j + 1) * shard_width].reshape(
                group_packs, slots, shard_heads, HEAD
            )
            for j in range(3)
        )
        q = rotate(q, group_cos, group_sin, 1.0).astype(LOW)
        ky = rotate(ky, group_cos, group_sin, 1.0).astype(LOW)
        v = v.astype(LOW)
        att, probs = attend(q, ky, v, group_mask)
        att = att.reshape(group_rows, shard_width)
        act, slope = gelu_pair(mm(hs, w_in[:, 3 * shard_width :]) + bias_up)
        act = act.astype(LOW)
        branch = from_group(mm(att, w_out) + mm(act, w_down))
        kept.append((normed, inverse, gain, hs, q, ky, v, probs, att, act, slope))
        xs = xs + branch + bias_down

    normed_in, normed_f, inverse_f = layer_norm(xs, final_gain, final_bias)
    final_low = normed_in.astype(LOW)
    logits = mm_t(final_low, head_low) + out_bias
    top = jnp.max(logits, -1, keepdims=True)
    logp = logits - (top + jnp.log(jnp.sum(jnp.exp(logits - top), -1, keepdims=True)))
    target_hot = one_hot(own_target, vocab, F32)
    picked = jnp.sum(target_hot * logp, 1) * own_weight
    local_seqs = micro * per_pack
    seq_hot = one_hot(own_sequence, local_seqs, F32)
    lik_sum = jnp.sum(seq_hot * picked[:, None], 0)
    seq_count = jnp.sum(one_hot(sequence.reshape(-1), local_seqs, F32) * weight.reshape(-1)[:, None], 0)
    sums = spread(jnp.concatenate([lik_sum, seq_count]), ALL).reshape(sections, plane, 2, local_seqs)
    lik_sums = jnp.sum(sums[:, :, 0], 0).reshape(-1)
    counts = sums[0, :, 1].reshape(-1)
    loss_total = -jnp.sum(lik_sums)
    count_total = jnp.sum(counts)
    lik_all = lik_sums / jnp.maximum(counts, 1.0)
    lik_own = lax.dynamic_slice_in_dim(lik_all, me * local_seqs, local_seqs, 0)
    differ = lik_own - jnp.take(lik_all, partners)
    penalty_local = jnp.where(y == 0, 0.5 * jnp.sum(differ * differ), 0.0)
    seq_term = PENALTY * 2.0 * differ / lik_all.shape[0] / jnp.maximum(seq_count, 1.0)
    coeff = own_weight * (-1.0 / count_total + jnp.sum(seq_hot * seq_term[None, :], 1))
    d_logits = (coeff[:, None] * (target_hot - jnp.exp(logp))).astype(LOW)
    head_grad = t_mm(d_logits, final_low)
    bias_local = jnp.sum(d_logits.astype(F32), 0)
    d_final = mm(d_logits, head_low)
    dy = norm_back(d_final, normed_f, inverse_f, final_gain)
    table_local = jnp.concatenate(
        [head_grad, jnp.sum(d_final * normed_f, 0)[None], jnp.sum(d_final, 0)[None]], 0
    )

    shard_grads = []
    vector_locals = []
    for layer in range(sections - 1, 0, -1):
        w_in, w_out, w_down = shard_weights[layer - 1]
        normed, inverse, gain, hs, q, ky, v, probs, att, act, slope = kept[layer - 1]
        own_low = dy.astype(LOW)
        d_rows = to_group(own_low)
        out_grad = t_mm(att, d_rows)
        down_grad = t_mm(act, d_rows)
        d_att = mm_t(d_rows, w_out).astype(LOW).reshape(group_packs, slots, shard_heads, HEAD)
        d_pre = (mm_t(d_rows, w_down) * slope).astype(LOW)
        dq, dk, dv = attend_back(d_att, probs, q, ky, v)
        d_proj = jnp.concatenate(
            [
                rotate(dq, group_cos, group_sin, -1.0).reshape(group_rows, shard_width),
                rotate(dk, group_cos, group_sin, -1.0).reshape(group_rows, shard_width),
                dv.reshape(group_rows, shard_width),
            ],
            1,
        ).astype(LOW)
        d_in = jnp.concatenate([d_proj, d_pre], 1)
        in_grad = t_mm(hs, d_in)
        d_norm = from_group(mm_t(d_in, w_in))
        bias_up_grad = jnp.sum(d_pre.astype(F32), 0).reshape(spans, 2, part_ff)
        place = (
            (jnp.arange(2) == k)[None, :, None, None, None, None]
            & (jnp.arange(2) == c)[None, None, None, :, None, None]
            & (jnp.arange(sections) == y)[None, None, None, None, :, None]
        )
        bias_up_grad = jnp.where(place, bias_up_grad[:, None, :, None, None, :], 0.0)
        vector_locals.append(
            jnp.concatenate(
                [
                    jnp.sum(d_norm * normed, 0),
                    jnp.sum(d_norm, 0),
                    jnp.sum(own_low.astype(F32), 0),
                    bias_up_grad.reshape(-1),
                ]
            )
        )
        dy = (dy + norm_back(d_norm, normed, inverse, gain)).astype(LOW).astype(F32)
        tail = jnp.concatenate(
            [
                down_grad.reshape(spans, 2, part_ff, width),
                out_grad.reshape(spans, 2, small_out, width),
            ],
            2,
        )
        tail = across_scatter(tail, x).astype(LOW)
        down_piece, out_piece = tail[:part_ff], tail[part_ff:]
        down_rows = jnp.stack(
            [
                down_piece if yy == layer else lax.ppermute(down_piece, "y", [(yy, layer)])
                for yy in range(sections)
            ]
        ).reshape(own_ff, width)
        out_rows = jnp.stack(
            [
                lax.ppermute(out_piece, ALL, [(b, a) for a, b in route])
                for route in out_routes(layer)
            ]
        ).reshape(own_out, width)
        inner = in_grad.reshape(spans, 2, 2, 2, own_in, -1).transpose(0, 2, 1, 3, 4, 5)
        inner = across_scatter(inner, x).astype(LOW)
        keep = pick(inner, k)
        give = shift(pick(inner, 1 - k), "k", 1)
        over_k = ordered(keep, give, k, 1)
        keep = pick(over_k, c)
        give = shift(pick(over_k, 1 - c), "c", 1)
        over_c = ordered(keep, give, c, 0)
        shards = jnp.stack(
            [
                over_c if yy == layer else lax.ppermute(over_c, "y", [(yy, layer)])
                for yy in range(sections)
            ],
            2,
        )
        qkv_rows, up_rows = columns_back(shards)
        shard_grads.append((qkv_rows, out_rows, up_rows, down_rows))
    shard_grads = shard_grads[::-1]
    vector_locals = vector_locals[::-1]

    own_low = dy.astype(LOW)
    dyb_token = t_mm(hot_own, own_low)
    d_att = mm_t(own_low, first_out).astype(LOW).reshape(own_packs, own_pack_rows, heads, HEAD)
    dq, dk, dv = attend_back(d_att, probs0, query0, keys0, values0)
    dq = rotate(dq, own_cos, own_sin, -1.0).reshape(-1, width).astype(LOW)
    dk = rotate(dk, pack_cos, pack_sin, -1.0).reshape(-1, width).astype(LOW)
    dv = dv.reshape(-1, width).astype(LOW)
    token_part = jnp.concatenate(
        [dyb_token, t_mm(hot_own, dq), t_mm(hot_pack, dk), t_mm(hot_pack, dv)], 1
    )
    token_cols = trade(token_part.reshape(vocab, everyone, -1).transpose(1, 0, 2), ALL)
    token_sums = spread(jnp.sum(token_cols, 0), ALL).transpose(1, 0, 2).reshape(vocab, -1)
    dyb_sum, dproj_sum = token_sums[:, :width], token_sums[:, width:]
    first_out_grad = t_mm(att0, own_low)
    down_first = mm_exact(a0, dyb_sum, ((0,), (0,)))
    du_own = mm_exact(dyb_sum, low_down, ((1,), (1,))) * slope0
    du_sum = spread(du_own, PLANE).transpose(1, 0, 2).reshape(vocab, hidden)
    h0_own = lax.dynamic_slice_in_dim(h0, me * own_in, own_in, 1)
    qkv_first = mm_exact(h0_own, dproj_sum, ((0,), (0,)))
    up_first = mm_exact(h0_own, du_sum, ((0,), (0,)))
    dh_own = mm_exact(dproj_sum, low_qkv, ((1,), (1,))) + mm_exact(du_sum, low_up, ((1,), (1,)))
    for yy in range(1, sections):
        got = lax.ppermute(dh_own, "y", [(0, yy)])
        dh_own = jnp.where(y == yy, got, dh_own)
    dh = spread(dh_own, PLANE).transpose(1, 0, 2).reshape(vocab, width)
    embed_grad = dyb_sum + norm_back(dh, normed0, inverse0, gain0)
    vector_first = jnp.concatenate(
        [jnp.sum(dh * normed0, 0), jnp.sum(dh, 0), jnp.sum(dyb_sum, 0), jnp.sum(du_sum, 0)]
    )
    part = first_out_grad.reshape(spans, 2, 2, 2, own_out, width)
    part = jnp.moveaxis(part, 3, 0)
    part = pick(part, c) + shift(pick(part, 1 - c).astype(LOW), "c", 1).astype(F32)
    part = jnp.moveaxis(part, 2, 0)
    part = pick(part, x) + shift(pick(part, 1 - x).astype(LOW), "x", 1).astype(F32)
    part = jnp.moveaxis(part, 1, 0)
    part = pick(part, k) + shift(pick(part, 1 - k).astype(LOW), "k", 1).astype(F32)
    total = pick(part, h)
    for s in range(1, spans):
        total = total + shift(pick(part, (h + s) % spans).astype(LOW), "h", s).astype(F32)
    out_first = total
    for yy in range(1, sections):
        out_first = out_first + lax.ppermute(total.astype(LOW), "y", [(yy, 0)]).astype(F32)

    first = (qkv_first, out_first, up_first, down_first)
    grads = []
    for number in range(4):
        grad = first[number]
        for layer in range(1, sections):
            grad = jnp.where(y == layer, shard_grads[layer - 1][number].astype(F32), grad)
        grads.append(grad[None])
    vector_cut = jnp.stack([jnp.zeros_like(vector_locals[0])] + vector_locals)
    vector_cut = vector_cut.reshape(everyone, vector_part)
    table_cut = table_local.reshape(-1, everyone, table_part).transpose(1, 0, 2)
    mixed = jnp.concatenate([vector_cut, table_cut.reshape(everyone, -1)], 1)
    mixed = jnp.sum(trade(mixed, ALL), 0)
    vector_own = lax.dynamic_slice_in_dim(vector_first, me * vector_part, vector_part, 0)
    vector_grad = jnp.where(y == 0, vector_own, mixed[:vector_part])
    number = y * plane + me
    embed_own = lax.dynamic_slice_in_dim(embed_grad, number * table_part, table_part, 1)
    table_grad = jnp.concatenate([embed_own, mixed[vector_part:].reshape(-1, table_part)], 0)

    squares = sum((jnp.sum(g * g) for g in grads)) + jnp.sum(vector_grad * vector_grad)
    squares = squares + jnp.sum(table_grad * table_grad)
    last = jnp.concatenate([squares[None], penalty_local[None], bias_local])
    last = jnp.sum(spread(last, ALL), 0)
    penalty = last[1]
    bias_grad = last[2:]
    grad_norm = jnp.sqrt(last[0] + jnp.sum(bias_grad * bias_grad))
    factor = jnp.minimum(1.0, CLIP_AT / grad_norm)
    grads = grads + [vector_grad[None], table_grad, bias_grad]
    masters = (qkv_weight, out_weight, up_weight, down_weight, vectors, tables, head_bias)
    moments = (
        qkv_moment,
        out_moment,
        up_moment,
        down_moment,
        vector_moment,
        table_moment,
        bias_moment,
    )
    squares_in = (
        qkv_square,
        out_square,
        up_square,
        down_square,
        vector_square,
        table_square,
        bias_square,
    )
    rates = (RATE_MAT, RATE_OUT, RATE_MAT, RATE_MAT, RATE_VEC, RATE_VEC, RATE_VEC)
    decays = (DECAY, DECAY, DECAY, DECAY, 0.0, 0.0, 0.0)
    results = []
    for number in range(7):
        results.extend(
            adam(
                masters[number],
                moments[number],
                squares_in[number],
                grads[number] * factor,
                rates[number],
                decays[number],
            )
        )
    loss_parts = jnp.stack([loss_total, count_total, penalty])
    return (grad_norm, loss_parts, *results)


def solution(mesh):
    sections, plane = mesh.shape["section"], mesh.shape["dp"]
    fine = Mesh(mesh.devices.reshape(sections, plane // 8, 2, 2, 2), ALL)
    matrix = P("y", PLANE, None)
    vector = P("y", PLANE)
    table = P(None, ALL)
    states = (matrix, matrix, matrix, matrix, vector, table, P())
    results = []
    for spec in states:
        results.extend([spec] * 3)
    return jax.shard_map(
        body,
        mesh=fine,
        in_specs=(P(PLANE, None), P(PLANE, None), P(PLANE, None), P(PLANE))
        + states
        + states
        + states,
        out_specs=(P(), P(), *results),
        check_vma=False,
    )
```

```python
import math

import jax
import jax.numpy as jnp
import numpy as np
from jax import lax
from jax.experimental import pallas as pl
from jax.experimental.pallas import tpu as pltpu
from jax.sharding import Mesh
from jax.sharding import PartitionSpec as P

HEAD = 64
ROT = 32
STEP = 10

EPS_NORM = 1e-05
PENALTY = 2.0
CLIP_AT = 0.02
RATE_MAT = 0.02
RATE_OUT = 0.1
RATE_VEC = 0.2
BETA_ONE = 0.9
BETA_TWO = 0.95
EPS_ADAM = 1e-08
DECAY = 0.1
GELU_C = 0.7978845608028654

ALL = ("y", "h", "k", "x", "c")
PLANE = ("h", "k", "x", "c")
LOW = jnp.bfloat16
F32 = jnp.float32
EXACT = lax.Precision.HIGHEST


def mm(left, right):
    return jnp.dot(left, right, preferred_element_type=F32)


def mm_t(left, right):
    return lax.dot_general(left, right, (((1,), (1,)), ((), ())), preferred_element_type=F32)


def t_mm(left, right):
    return lax.dot_general(left, right, (((0,), (0,)), ((), ())), preferred_element_type=F32)


def mm_exact(left, right, dims):
    return lax.dot_general(
        left.astype(F32), right.astype(F32), (dims, ((), ())), precision=EXACT
    )


def pick(array, index):
    return lax.dynamic_index_in_dim(array, index, 0, keepdims=False)


def spread(value, axes):
    many = lax.axis_size(axes)
    return lax.all_to_all(jnp.broadcast_to(value[None], (many,) + value.shape), axes, 0, 0, tiled=True)


def trade(pieces, axes):
    return lax.all_to_all(pieces, axes, 0, 0, tiled=True)


def shift(value, axis, by):
    many = lax.axis_size(axis)
    return lax.ppermute(value, axis, [(i, (i + by) % many) for i in range(many)])


def after(value, *earlier):
    return lax.optimization_barrier((value,) + earlier)[0]


def together(*values):
    return lax.optimization_barrier(values)


def ordered(own, other, bit, axis):
    return jnp.stack(
        [jnp.where(bit == 0, own, other), jnp.where(bit == 0, other, own)], axis
    )


def layer_norm(x, gain, bias):
    mean = jnp.mean(x, -1, keepdims=True)
    centred = x - mean
    inverse = lax.rsqrt(jnp.mean(centred * centred, -1, keepdims=True) + EPS_NORM)
    normed = centred * inverse
    return (normed * gain + bias, normed, inverse)


def norm_back(grad, normed, inverse, gain):
    scaled = grad * gain
    return inverse * (
        scaled
        - jnp.mean(scaled, -1, keepdims=True)
        - normed * jnp.mean(scaled * normed, -1, keepdims=True)
    )


def gelu_pair(value):
    inner = jnp.tanh(GELU_C * (value + 0.044715 * value * value * value))
    result = 0.5 * value * (1.0 + inner)
    slope = 0.5 * (1.0 + inner) + 0.5 * value * (1.0 - inner * inner) * GELU_C * (
        1.0 + 3.0 * 0.044715 * value * value
    )
    return (result, slope)


def one_hot(row, vocab, dtype):
    return (row[:, None] == jnp.arange(vocab, dtype=jnp.int32)[None, :]).astype(dtype)


def pack_layout(lengths_row, slots):
    ends = jnp.cumsum(lengths_row)
    starts = ends - lengths_row
    index = jnp.arange(slots, dtype=jnp.int32)
    segment = jnp.sum((index[:, None] >= ends[None, :]).astype(jnp.int32), 1)
    member = segment[:, None] == jnp.arange(lengths_row.shape[0], dtype=jnp.int32)[None, :]
    position = index - jnp.sum(jnp.where(member, starts[None, :], 0), 1)
    return (segment, position)


LANES = 128
VMEM_LIMIT = 44 * 1024 * 1024
SCALE = 1.0 / math.sqrt(HEAD)


def rope_rows(position):
    half = ROT // 2
    freq = 10000.0 ** (-2.0 * jnp.arange(half, dtype=F32) / ROT)
    angle = position.astype(F32)[:, None] * freq
    cosine, sine = (jnp.cos(angle), jnp.sin(angle))
    none, one = (jnp.zeros_like(sine), jnp.ones_like(sine))
    many = LANES // HEAD
    rest = HEAD // half - 2
    return jnp.stack(
        [
            jnp.concatenate(([cosine, cosine] + [one] * rest) * many, 1),
            jnp.concatenate(([-sine, none] + [none] * rest) * many, 1),
            jnp.concatenate(([none, sine] + [none] * rest) * many, 1),
        ]
    )


def turn_by(value, rope, sign):
    above = pltpu.roll(value, LANES - ROT // 2, 1)
    below = pltpu.roll(value, ROT // 2, 1)
    return value * rope[0] + sign * (above * rope[1] + below * rope[2])


def head_lanes(shape):
    lane = lax.broadcasted_iota(jnp.int32, shape, 1)
    return [(lane // HEAD) == number for number in range(LANES // HEAD)]


def soft(query, keys, bias):
    scores = mm_t(query, keys) * SCALE + bias
    expo = jnp.exp(scores - jnp.max(scores, -1, keepdims=True))
    return expo / jnp.sum(expo, -1, keepdims=True)


def attend_pair(query, keys, values, bias):
    out = jnp.zeros(query.shape, F32)
    nothing = jnp.zeros((), LOW)
    for mine_q, mine_k in zip(head_lanes(query.shape), head_lanes(keys.shape)):
        probs = soft(jnp.where(mine_q, query, nothing), keys, bias).astype(LOW)
        out = out + mm(probs, jnp.where(mine_k, values, nothing))
    return out.astype(LOW)


def attend_pair_back(d_out, query, keys, values, bias):
    d_query = jnp.zeros(query.shape, F32)
    d_keys = jnp.zeros(keys.shape, F32)
    d_values = jnp.zeros(keys.shape, F32)
    nothing = jnp.zeros((), LOW)
    for mine_q, mine_k in zip(head_lanes(query.shape), head_lanes(keys.shape)):
        query_h = jnp.where(mine_q, query, nothing)
        d_out_h = jnp.where(mine_q, d_out, nothing)
        probs = soft(query_h, keys, bias)
        d_values = d_values + t_mm(probs.astype(LOW), d_out_h)
        d_probs = mm_t(d_out_h, values)
        d_scores = probs * (d_probs - jnp.sum(probs * d_probs, -1, keepdims=True))
        d_scores = d_scores.astype(LOW)
        d_query = d_query + mm(d_scores, jnp.where(mine_k, keys, nothing))
        d_keys = d_keys + t_mm(d_scores, query_h)
    return (d_query * SCALE, d_keys * SCALE, d_values)


def whole_spec(shape):
    return pl.BlockSpec(shape, lambda *_: (0,) * len(shape))


def params():
    return pltpu.CompilerParams(vmem_limit_bytes=VMEM_LIMIT)


def upper_forward(hs, w_in, w_out, w_down, bias_up, rope, bias, slots):
    total, width = hs.shape
    lanes, units = (w_out.shape[0], w_down.shape[0])
    step = total // 2

    def kernel(h_ref, win_ref, wout_ref, wdown_ref, bup_ref, rope_ref, bias_ref, keep_ref, send_ref, qkv_ref, att_ref, act_ref, slope_ref):
        h = h_ref[...]
        proj = mm(h, win_ref[:, : 3 * lanes])
        for g in range(lanes // LANES):
            spans = [slice(j * lanes + g * LANES, j * lanes + (g + 1) * LANES) for j in range(3)]
            qkv_ref[:, spans[0]] = turn_by(proj[:, spans[0]], rope_ref, 1.0).astype(LOW)
            qkv_ref[:, spans[1]] = turn_by(proj[:, spans[1]], rope_ref, 1.0).astype(LOW)
            qkv_ref[:, spans[2]] = proj[:, spans[2]].astype(LOW)
            for pack in range(step // slots):
                here = slice(pack * slots, (pack + 1) * slots)
                q, k, v = (qkv_ref[here, spans[j]] for j in range(3))
                att_ref[here, g * LANES : (g + 1) * LANES] = attend_pair(q, k, v, bias_ref[here, :])
        act, slope = gelu_pair(mm(h, win_ref[:, 3 * lanes :]) + bup_ref[...])
        act = act.astype(LOW)
        act_ref[...] = act
        slope_ref[...] = slope
        out = mm(att_ref[...], wout_ref[...]) + mm(act, wdown_ref[...])

        @pl.when(pl.program_id(0) == 0)
        def _():
            send_ref[...] = out.astype(LOW)

        @pl.when(pl.program_id(0) == 1)
        def _():
            keep_ref[...] = out

    def by_rows(columns):
        return pl.BlockSpec((step, columns), lambda s: (1 - s, 0))

    return pl.pallas_call(
        kernel,
        grid=(2,),
        in_specs=[
            by_rows(width),
            whole_spec(w_in.shape),
            whole_spec(w_out.shape),
            whole_spec(w_down.shape),
            whole_spec((1, units)),
            pl.BlockSpec((3, step, LANES), lambda s: (0, 1 - s, 0)),
            by_rows(slots),
        ],
        out_specs=[
            whole_spec((step, width)),
            whole_spec((step, width)),
            by_rows(3 * lanes),
            by_rows(lanes),
            by_rows(units),
            by_rows(units),
        ],
        out_shape=[
            jax.ShapeDtypeStruct((step, width), F32),
            jax.ShapeDtypeStruct((step, width), LOW),
            jax.ShapeDtypeStruct((total, 3 * lanes), LOW),
            jax.ShapeDtypeStruct((total, lanes), LOW),
            jax.ShapeDtypeStruct((total, units), LOW),
            jax.ShapeDtypeStruct((total, units), F32),
        ],
        compiler_params=params(),
        name="upper_forward",
    )(hs, w_in, w_out, w_down, bias_up[None], rope, bias)


def upper_backward(d_rows, qkv, slope, w_in, w_out, w_down, rope, bias, slots):
    total, width = d_rows.shape
    lanes, units = (w_out.shape[0], w_down.shape[0])
    step = total // 2

    def kernel(d_ref, qkv_ref, slope_ref, win_ref, wout_ref, wdown_ref, rope_ref, bias_ref, keep_ref, send_ref, din_ref, sum_ref):
        d_out = d_ref[...]
        d_att = mm_t(d_out, wout_ref[...]).astype(LOW)
        d_pre = (mm_t(d_out, wdown_ref[...]) * slope_ref[...]).astype(LOW)
        din_ref[:, 3 * lanes :] = d_pre
        sums = jnp.sum(d_pre.astype(F32), 0, keepdims=True)
        for g in range(lanes // LANES):
            spans = [slice(j * lanes + g * LANES, j * lanes + (g + 1) * LANES) for j in range(3)]
            for pack in range(step // slots):
                here = slice(pack * slots, (pack + 1) * slots)
                q, k, v = (qkv_ref[here, spans[j]] for j in range(3))
                dq, dk, dv = attend_pair_back(
                    d_att[here, g * LANES : (g + 1) * LANES], q, k, v, bias_ref[here, :]
                )
                turned = [rope_ref[j, here, :] for j in range(3)]
                din_ref[here, spans[0]] = turn_by(dq, turned, -1.0).astype(LOW)
                din_ref[here, spans[1]] = turn_by(dk, turned, -1.0).astype(LOW)
                din_ref[here, spans[2]] = dv.astype(LOW)
        d_norm = mm_t(din_ref[...], win_ref[...])

        @pl.when(pl.program_id(0) == 0)
        def _():
            send_ref[...] = d_norm.astype(LOW)
            sum_ref[...] = sums

        @pl.when(pl.program_id(0) == 1)
        def _():
            keep_ref[...] = d_norm
            sum_ref[...] += sums

    def by_rows(columns):
        return pl.BlockSpec((step, columns), lambda s: (1 - s, 0))

    return pl.pallas_call(
        kernel,
        grid=(2,),
        in_specs=[
            by_rows(width),
            by_rows(3 * lanes),
            by_rows(units),
            whole_spec(w_in.shape),
            whole_spec(w_out.shape),
            whole_spec(w_down.shape),
            pl.BlockSpec((3, step, LANES), lambda s: (0, 1 - s, 0)),
            by_rows(slots),
        ],
        out_specs=[
            whole_spec((step, width)),
            whole_spec((step, width)),
            by_rows(3 * lanes + units),
            whole_spec((1, units)),
        ],
        out_shape=[
            jax.ShapeDtypeStruct((step, width), F32),
            jax.ShapeDtypeStruct((step, width), LOW),
            jax.ShapeDtypeStruct((total, 3 * lanes + units), LOW),
            jax.ShapeDtypeStruct((1, units), F32),
        ],
        compiler_params=params(),
        name="upper_backward",
    )(d_rows, qkv, slope, w_in, w_out, w_down, rope, bias)


def exact_rows(hot, table):
    high = table.astype(LOW)
    rest = table - high.astype(F32)
    middle = rest.astype(LOW)
    lowest = (rest - middle.astype(F32)).astype(LOW)
    return mm(hot, high) + (mm(hot, middle) + mm(hot, lowest))


def first_forward(table, hot_own, hot_pack, rope_own, rope_pack, bias, packs):
    vocab = table.shape[0]
    width = table.shape[1] // 3
    pairs = width // LANES
    own_rows = hot_own.shape[0] // packs
    pack_rows = hot_pack.shape[0] // packs

    def kernel(tq_ref, tk_ref, tv_ref, hot_ref, hotp_ref, ro_ref, rp_ref, bias_ref, q_ref, k_ref, v_ref, att_ref):
        hot = hot_ref[...]
        hotp = hotp_ref[...]
        q = turn_by(exact_rows(hot, tq_ref[...]), ro_ref, 1.0).astype(LOW)
        k = turn_by(exact_rows(hotp, tk_ref[...]), rp_ref, 1.0).astype(LOW)
        v = mm(hotp, tv_ref[...].astype(LOW)).astype(LOW)
        q_ref[...] = q
        k_ref[...] = k
        v_ref[...] = v
        att_ref[...] = attend_pair(q, k, v, bias_ref[...])

    def table_spec(which):
        return pl.BlockSpec((vocab, LANES), lambda p, j: (0, which * pairs + j))

    def rows_spec(many, columns):
        return pl.BlockSpec((many, columns), lambda p, j: (p, 0))

    def rope_spec(many):
        return pl.BlockSpec((3, many, LANES), lambda p, j: (0, p, 0))

    def pair_spec(many):
        return pl.BlockSpec((many, LANES), lambda p, j: (p, j))

    owned, packed = (hot_own.shape[0], hot_pack.shape[0])
    return pl.pallas_call(
        kernel,
        grid=(packs, pairs),
        in_specs=[
            table_spec(0),
            table_spec(1),
            table_spec(2),
            rows_spec(own_rows, vocab),
            rows_spec(pack_rows, vocab),
            rope_spec(own_rows),
            rope_spec(pack_rows),
            rows_spec(own_rows, pack_rows),
        ],
        out_specs=[
            pair_spec(own_rows),
            pair_spec(pack_rows),
            pair_spec(pack_rows),
            pair_spec(own_rows),
        ],
        out_shape=[
            jax.ShapeDtypeStruct((owned, width), LOW),
            jax.ShapeDtypeStruct((packed, width), LOW),
            jax.ShapeDtypeStruct((packed, width), LOW),
            jax.ShapeDtypeStruct((owned, width), LOW),
        ],
        compiler_params=params(),
        name="first_forward",
    )(table, table, table, hot_own, hot_pack, rope_own, rope_pack, bias)


def cost(microseconds):
    return pl.CostEstimate(flops=max(1, int(microseconds * 1e9 * 1.0)), bytes_accessed=0, transcendentals=0)


def simple(kernel, name, outs, *args, smem=(), us=1.0, scratch=()):
    specs = [
        pl.BlockSpec(memory_space=pltpu.SMEM) if i in smem else whole_spec(arg.shape)
        for i, arg in enumerate(args)
    ]
    return pl.pallas_call(
        kernel,
        grid=(1,),
        in_specs=specs,
        out_specs=[whole_spec(shape) for shape, _ in outs],
        out_shape=[jax.ShapeDtypeStruct(shape, kind) for shape, kind in outs],
        scratch_shapes=list(scratch),
        compiler_params=params(),
        cost_estimate=cost(us),
        name=name,
    )(*args)


def first_finish(att, first_out, hot, stay, gain, bias):
    rows, width = att.shape

    def kernel(att_ref, out_ref, hot_ref, stay_ref, gain_ref, bias_ref, x_ref, h_ref):
        x = mm(att_ref[...], out_ref[...]) + exact_rows(hot_ref[...], stay_ref[...])
        x = x.astype(LOW)
        x_ref[...] = x
        h_ref[...] = layer_norm(x.astype(F32), gain_ref[...], bias_ref[...])[0].astype(LOW)

    outs = [((rows, width), LOW), ((rows, width), LOW)]
    return simple(kernel, "first_finish", outs, att, first_out, hot, stay, gain[None], bias[None])


def loss_forward(base, pieces, bias_down, gain, bias, head_low, out_bias, target_hot, seq_weight):
    rows, width = base.shape
    vocab = head_low.shape[0]
    seqs = seq_weight.shape[1]

    def kernel(x_ref, *refs):
        piece_refs = refs[: len(pieces)]
        down_ref, gain_ref, bias_ref, head_ref, hbias_ref, hot_ref, seq_ref = refs[len(pieces) : -5]
        norm_ref, inv_ref, final_ref, logp_ref, lik_ref = refs[-5:]
        x = x_ref[...].astype(F32)
        for ref in piece_refs:
            x = x + ref[...].astype(F32)
        out, normed, inverse = layer_norm(x + down_ref[...], gain_ref[...], bias_ref[...])
        norm_ref[...] = normed
        inv_ref[...] = inverse
        final = out.astype(LOW)
        final_ref[...] = final
        logits = mm_t(final, head_ref[...]) + hbias_ref[...]
        top = jnp.max(logits, -1, keepdims=True)
        logp = logits - (top + jnp.log(jnp.sum(jnp.exp(logits - top), -1, keepdims=True)))
        logp_ref[...] = logp
        picked = jnp.sum(hot_ref[...] * logp, 1, keepdims=True)
        lik_ref[...] = jnp.sum(seq_ref[...] * picked, 0, keepdims=True)

    outs = [
        ((rows, width), F32),
        ((rows, 1), F32),
        ((rows, width), LOW),
        ((rows, vocab), F32),
        ((1, seqs), F32),
    ]
    return simple(
        kernel,
        "loss_forward",
        outs,
        base,
        *pieces,
        bias_down[None],
        gain[None],
        bias[None],
        head_low,
        out_bias[None],
        target_hot,
        seq_weight,
    )


def loss_backward(sums, partners, place, normed, inverse, final_low, logp, head_low, gain, target_hot, seq_weight, plane):
    rows, width = normed.shape
    vocab = head_low.shape[0]
    seqs = seq_weight.shape[1]
    devices = sums.shape[0]
    total_seqs = plane * seqs

    def kernel(sums_ref, partner_ref, place_ref, norm_ref, inv_ref, final_ref, logp_ref, head_ref, gain_ref, hot_ref, seq_ref, dy_ref, low_ref, table_ref, bias_ref, down_ref, scalar_ref):
        got = sums_ref[...]
        row = lax.broadcasted_iota(jnp.int32, got.shape, 0)
        column = lax.broadcasted_iota(jnp.int32, got.shape, 1)
        owner = lax.rem(row, plane)
        is_sum = column < seqs
        is_count = (column >= seqs) & (row < plane)
        loss = -jnp.sum(jnp.where(is_sum, got, 0.0))
        count = jnp.sum(jnp.where(is_count, got, 0.0))

        def likelihood(device, number):
            here = owner == device
            amount = jnp.sum(jnp.where(here & is_count & (column == seqs + number), got, 0.0))
            amount = jnp.maximum(amount, 1.0)
            total = jnp.sum(jnp.where(here & (column == number), got, 0.0))
            return (total / amount, amount)

        coeff = jnp.zeros((rows, 1), F32)
        penalty = 0.0
        for number in range(seqs):
            mine, amount = likelihood(place_ref[0], number)
            partner = partner_ref[number]
            other, _ = likelihood(partner // seqs, lax.rem(partner, seqs))
            differ = mine - other
            penalty = penalty + 0.5 * differ * differ
            term = -1.0 / count + PENALTY * 2.0 * differ / total_seqs / amount
            coeff = coeff + seq_ref[:, number : number + 1] * term
        d_logits = (coeff * (hot_ref[...] - jnp.exp(logp_ref[...]))).astype(LOW)
        d_final = mm(d_logits, head_ref[...])
        normed = norm_ref[...]
        dy = norm_back(d_final, normed, inv_ref[...], gain_ref[...])
        dy_ref[...] = dy
        low = dy.astype(LOW)
        low_ref[...] = low
        table_ref[:vocab, :] = t_mm(d_logits, final_ref[...])
        table_ref[vocab : vocab + 1, :] = jnp.sum(d_final * normed, 0, keepdims=True)
        table_ref[vocab + 1 : vocab + 2, :] = jnp.sum(d_final, 0, keepdims=True)
        bias_ref[...] = jnp.sum(d_logits.astype(F32), 0, keepdims=True)
        down_ref[...] = jnp.sum(low.astype(F32), 0, keepdims=True)
        lane = lax.broadcasted_iota(jnp.int32, (1, LANES), 1)
        scalar_ref[...] = jnp.where(lane == 0, loss, jnp.where(lane == 1, count, penalty))

    outs = [
        ((rows, width), F32),
        ((rows, width), LOW),
        ((vocab + 2, width), F32),
        ((1, vocab), F32),
        ((1, width), F32),
        ((1, LANES), F32),
    ]
    return simple(
        kernel,
        "loss_backward",
        outs,
        sums,
        partners,
        place,
        normed,
        inverse,
        final_low,
        logp,
        head_low,
        gain[None],
        target_hot,
        seq_weight,
        smem=(1, 2),
    )


def input_backward(pieces, x_low, dy, gain, hot):
    rows, width = dy.shape
    vocab = hot.shape[1]

    def kernel(*refs):
        piece_refs = refs[: len(pieces)]
        x_ref, dy_ref, gain_ref, hot_ref, low_ref, vec_ref, token_ref = refs[len(pieces) :]
        d_norm = piece_refs[0][...]
        for ref in piece_refs[1:]:
            d_norm = d_norm + ref[...].astype(F32)
        gain_row = gain_ref[...]
        _, normed, inverse = layer_norm(x_ref[...].astype(F32), gain_row, 0.0)
        low = (dy_ref[...] + norm_back(d_norm, normed, inverse, gain_row)).astype(LOW)
        low_ref[...] = low
        vec_ref[0:1, :] = jnp.sum(d_norm * normed, 0, keepdims=True)
        vec_ref[1:2, :] = jnp.sum(d_norm, 0, keepdims=True)
        vec_ref[2:3, :] = jnp.sum(low.astype(F32), 0, keepdims=True)
        token_ref[...] = t_mm(hot_ref[...], low)

    outs = [((rows, width), LOW), ((3, width), F32), ((vocab, width), F32)]
    return simple(kernel, "input_backward", outs, *pieces, x_low, dy, gain[None], hot)


def first_backward(d_rows, query, keys, values, att, hot_own, hot_pack, rope_own, rope_pack, bias, first_out, packs):
    width = first_out.shape[0]
    vocab = hot_own.shape[1]
    pairs = width // LANES
    own_rows = hot_own.shape[0] // packs
    pack_rows = hot_pack.shape[0] // packs

    def kernel(d_ref, q_ref, k_ref, v_ref, att_ref, hot_ref, hotp_ref, ro_ref, rp_ref, bias_ref, out_ref, tq_ref, tk_ref, tv_ref, grad_ref):
        d_out = d_ref[...]
        d_att = mm_t(d_out, out_ref[...]).astype(LOW)
        dq, dk, dv = attend_pair_back(d_att, q_ref[...], k_ref[...], v_ref[...], bias_ref[...])
        dq = turn_by(dq, ro_ref, -1.0).astype(LOW)
        dk = turn_by(dk, rp_ref, -1.0).astype(LOW)
        hot = hot_ref[...]
        hotp = hotp_ref[...]
        parts = (t_mm(hot, dq), t_mm(hotp, dk), t_mm(hotp, dv.astype(LOW)), t_mm(att_ref[...], d_out))
        refs = (tq_ref, tk_ref, tv_ref, grad_ref)

        @pl.when(pl.program_id(1) == 0)
        def _():
            for ref, part in zip(refs, parts):
                ref[...] = part

        @pl.when(pl.program_id(1) > 0)
        def _():
            for ref, part in zip(refs, parts):
                ref[...] += part

    def rows_spec(many, columns):
        return pl.BlockSpec((many, columns), lambda j, p: (p, 0))

    def rope_spec(many):
        return pl.BlockSpec((3, many, LANES), lambda j, p: (0, p, 0))

    def pair_spec(many):
        return pl.BlockSpec((many, LANES), lambda j, p: (p, j))

    token_spec = pl.BlockSpec((vocab, LANES), lambda j, p: (0, j))
    return pl.pallas_call(
        kernel,
        grid=(pairs, packs),
        in_specs=[
            rows_spec(own_rows, width),
            pair_spec(own_rows),
            pair_spec(pack_rows),
            pair_spec(pack_rows),
            pair_spec(own_rows),
            rows_spec(own_rows, vocab),
            rows_spec(pack_rows, vocab),
            rope_spec(own_rows),
            rope_spec(pack_rows),
            rows_spec(own_rows, pack_rows),
            pl.BlockSpec((LANES, width), lambda j, p: (j, 0)),
        ],
        out_specs=[
            token_spec,
            token_spec,
            token_spec,
            pl.BlockSpec((LANES, width), lambda j, p: (j, 0)),
        ],
        out_shape=[
            jax.ShapeDtypeStruct((vocab, width), F32),
            jax.ShapeDtypeStruct((vocab, width), F32),
            jax.ShapeDtypeStruct((vocab, width), F32),
            jax.ShapeDtypeStruct((width, width), F32),
        ],
        compiler_params=params(),
        cost_estimate=cost(10.5),
        name="first_backward",
    )(d_rows, query, keys, values, att, hot_own, hot_pack, rope_own, rope_pack, bias, first_out)


def adam(weight, first, second, grad, rate, decay):
    first_new = BETA_ONE * first + (1.0 - BETA_ONE) * grad
    second_new = BETA_TWO * second + (1.0 - BETA_TWO) * grad * grad
    update = (
        first_new
        / (1.0 - BETA_ONE**STEP)
        / (jnp.sqrt(second_new / (1.0 - BETA_TWO**STEP)) + EPS_ADAM)
    )
    return (first_new, second_new, weight - rate * (update + decay * weight))


class Group:
    def __init__(self, sections, spans):
        self.sections = sections
        self.spans = spans
        self.offsets = [(dk, dy) for dk in range(2) for dy in range(sections)]

    def route(self, dk, dy, sign):
        s = self.sections
        return [
            (a * 2 + b, ((a + sign * dy) % s) * 2 + (b + sign * dk) % 2)
            for a in range(s)
            for b in range(2)
        ]

    def gather(self, value):
        pieces = []
        for dk, dy in self.offsets:
            piece = value
            if (dk, dy) != (0, 0):
                piece = lax.ppermute(value, ("y", "k"), self.route(dk, dy, 1))
            pieces.append(piece)
        mine = jnp.stack(pieces)
        return jnp.stack([mine, shift(mine, "c", 1)])

    def scatter(self, keep, send):
        mine = keep + shift(send, "c", 1).astype(F32)
        pieces = [mine[0]]
        for number, (dk, dy) in enumerate(self.offsets):
            if (dk, dy) != (0, 0):
                pieces.append(
                    lax.ppermute(mine[number].astype(LOW), ("y", "k"), self.route(dk, dy, -1))
                )
        return pieces


def across_gather(piece, x, first, second, last):
    spans = lax.axis_size("h")
    h = lax.axis_index("h")
    piece = after(piece, first)
    if spans == 2:
        both = ordered(piece, after(shift(piece, "h", 1), second), h, 0)
    else:
        stacked = jnp.stack([piece] + [shift(piece, "h", s) for s in range(1, spans)])
        both = jnp.take(stacked, (h - jnp.arange(spans)) % spans, axis=0)
    return ordered(both, after(shift(both, "x", 1), last), x, 1)


def across_scatter(parts, x, first, second, last):
    spans = lax.axis_size("h")
    h = lax.axis_index("h")
    flipped = jnp.swapaxes(parts, 0, 1)
    away = shift(after(pick(flipped, 1 - x).astype(LOW), first), "x", 1)
    mine = pick(flipped, x) + after(away, second).astype(F32)
    total = pick(mine, h)
    for s in range(1, spans):
        away = shift(pick(mine, (h + s) % spans).astype(LOW), "h", s)
        total = total + after(away, last).astype(F32)
    return total


def scalars_of(*values):
    return jnp.stack([jnp.asarray(v, jnp.int32) for v in values])


def flip(value, axes, bits):
    mask = 0
    for bit in bits:
        mask = 2 * mask + bit
    many = 2 ** len(bits)
    return lax.ppermute(value, axes, [(i, i ^ mask) for i in range(many)])


NEAR = [(0, 1), (1, 0), (1, 1)]
def fast_loss_forward(base, pieces, vec, low_tables, out_bias, target_hot, seq_weight, seq_count):
    rows, width = base.shape
    vocab = target_hot.shape[1]

    def kernel(x_ref, p0, p1, p2, p3, vec_ref, low_ref, hbias_ref, hot_ref, seq_ref, count_ref, norm_ref, inv_ref, final_ref, logp_ref, sums_ref):
        x = x_ref[...].astype(F32) + p0[...]
        x = x + p1[...].astype(F32) + p2[...].astype(F32) + p3[...].astype(F32)
        gain = low_ref[2 * vocab : 2 * vocab + 1, :].astype(F32)
        bias = low_ref[2 * vocab + 1 : 2 * vocab + 2, :].astype(F32)
        out, normed, inverse = layer_norm(x + vec_ref[1:2, 2 * width : 3 * width], gain, bias)
        norm_ref[...] = normed
        inv_ref[...] = inverse
        final = out.astype(LOW)
        final_ref[...] = final
        logits = mm_t(final, low_ref[vocab : 2 * vocab, :]) + hbias_ref[...].astype(LOW).astype(F32)
        top = jnp.max(logits, -1, keepdims=True)
        logp = logits - (top + jnp.log(jnp.sum(jnp.exp(logits - top), -1, keepdims=True)))
        logp_ref[...] = logp
        picked = jnp.sum(hot_ref[...] * logp, 1, keepdims=True)
        row = jnp.sum(seq_ref[...] * picked, 0, keepdims=True)
        counts = count_ref[...]
        line = lax.broadcasted_iota(jnp.int32, counts.shape, 0)
        lane = lax.broadcasted_iota(jnp.int32, counts.shape, 1)
        seqs = counts.shape[0]
        row = row + jnp.sum(jnp.where(lane == line + seqs, counts, 0.0), 0, keepdims=True)
        sums_ref[...] = row

    outs = [
        ((rows, width), F32),
        ((rows, 1), F32),
        ((rows, width), LOW),
        ((rows, vocab), F32),
        ((1, LANES), F32),
    ]
    return simple(
        kernel,
        "loss_forward",
        outs,
        base,
        *pieces,
        vec,
        low_tables,
        out_bias[None],
        target_hot,
        seq_weight,
        seq_count,
    )


def fast_loss_backward(sums, partners, place, normed, inverse, final_low, logp, low_tables, target_hot, seq_weight, plane, seqs):
    rows, width = normed.shape
    vocab = target_hot.shape[1]
    total_seqs = plane * seqs

    def kernel(sums_ref, partner_ref, place_ref, norm_ref, inv_ref, final_ref, logp_ref, low_ref, hot_ref, seq_ref, dy_ref, low_out_ref, table_ref, bias_ref, down_ref, scalar_ref):
        got = sums_ref[...]
        row = lax.broadcasted_iota(jnp.int32, got.shape, 0)
        column = lax.broadcasted_iota(jnp.int32, got.shape, 1)
        owner = lax.rem(row, plane)
        is_sum = column < seqs
        is_count = (column >= seqs) & (column < 2 * seqs) & (row < plane)
        loss = -jnp.sum(jnp.where(is_sum, got, 0.0))
        count = jnp.sum(jnp.where(is_count, got, 0.0))

        def likelihood(device, number):
            here = owner == device
            amount = jnp.sum(jnp.where(here & is_count & (column == seqs + number), got, 0.0))
            amount = jnp.maximum(amount, 1.0)
            total = jnp.sum(jnp.where(here & (column == number), got, 0.0))
            return (total / amount, amount)

        coeff = jnp.zeros((rows, 1), F32)
        penalty = 0.0
        for number in range(seqs):
            mine, amount = likelihood(place_ref[5], number)
            partner = partner_ref[number]
            other, _ = likelihood(partner // seqs, lax.rem(partner, seqs))
            differ = mine - other
            penalty = penalty + 0.5 * differ * differ
            term = -1.0 / count + PENALTY * 2.0 * differ / total_seqs / amount
            coeff = coeff + seq_ref[:, number : number + 1] * term
        d_logits = (coeff * (hot_ref[...] - jnp.exp(logp_ref[...]))).astype(LOW)
        d_final = mm(d_logits, low_ref[vocab : 2 * vocab, :])
        normed = norm_ref[...]
        gain = low_ref[2 * vocab : 2 * vocab + 1, :].astype(F32)
        dy = norm_back(d_final, normed, inv_ref[...], gain)
        dy_ref[...] = dy
        low = dy.astype(LOW)
        low_out_ref[...] = low
        line = lax.broadcasted_iota(jnp.int32, (8, width), 0)
        ends = jnp.where(
            line == 0,
            jnp.sum(d_final * normed, 0, keepdims=True),
            jnp.where(line == 1, jnp.sum(d_final, 0, keepdims=True), 0.0),
        )
        grads = jnp.concatenate(
            [
                t_mm(d_logits, final_ref[...]),
                ends,
                jnp.zeros((LANES - vocab - 8, width), F32),
            ],
            0,
        )
        table_ref[...] = grads.T
        bias_ref[...] = jnp.sum(d_logits.astype(F32), 0, keepdims=True)
        down_ref[...] = jnp.sum(low.astype(F32), 0, keepdims=True)
        lane = lax.broadcasted_iota(jnp.int32, (1, LANES), 1)
        scalar_ref[...] = jnp.where(lane == 0, loss, jnp.where(lane == 1, count, penalty))

    outs = [
        ((rows, width), F32),
        ((rows, width), LOW),
        ((width, LANES), F32),
        ((1, vocab), F32),
        ((1, width), F32),
        ((1, LANES), F32),
    ]
    return simple(
        kernel,
        "loss_backward",
        outs,
        sums,
        partners,
        place,
        normed,
        inverse,
        final_low,
        logp,
        low_tables,
        target_hot,
        seq_weight,
        smem=(1, 2),
    )


def rope_constant(slots):
    half = ROT // 2
    freq = np.float32(10000.0) ** (np.float32(-2.0) * np.arange(half, dtype=np.float32) / ROT)
    angle = np.arange(slots, dtype=np.float32)[:, None] * freq.astype(np.float32)
    cosine = np.cos(angle.astype(np.float64)).astype(np.float32)
    sine = np.sin(angle.astype(np.float64)).astype(np.float32)
    none, one = (np.zeros_like(sine), np.ones_like(sine))
    many = LANES // HEAD
    rest = HEAD // half - 2
    return np.stack(
        [
            np.concatenate(([cosine, cosine] + [one] * rest) * many, 1),
            np.concatenate(([-sine, none] + [none] * rest) * many, 1),
            np.concatenate(([none, sine] + [none] * rest) * many, 1),
        ]
    )


FLIPS = [(0, 0), (0, 1), (1, 0), (1, 1)]


def cut_weights(qkv, up, down, out, place):
    own_in, own_ff, width = (qkv.shape[0], down.shape[0], out.shape[1])
    part = own_ff // 2
    some = out.shape[0] // 2

    def kernel(qkv_ref, up_ref, down_ref, out_ref, place_ref, shard_ref, keep_ref, send_ref, one_ref, two_ref):
        y = place_ref[0]
        for yy in range(2):
            for kk in range(2):
                for cc in range(2):
                    number = (yy * 2 + kk) * 2 + cc
                    start = ((cc * 2 + kk) * 2 + yy) * LANES
                    for j in range(3):
                        shard_ref[number, :, j * LANES : (j + 1) * LANES] = qkv_ref[
                            :, j * width + start : j * width + start + LANES
                        ].astype(LOW)
                    for j in range(4):
                        start = (j // 2 * 8 + kk * 4 + j % 2 * 2 + cc) * own_ff + yy * part
                        shard_ref[number, :, (3 + j) * LANES : (4 + j) * LANES] = up_ref[
                            :, start : start + part
                        ].astype(LOW)
        keep_ref[...] = down_ref[pl.ds(pl.multiple_of(y * part, part), part), :].astype(LOW)
        send_ref[...] = down_ref[pl.ds(pl.multiple_of((1 - y) * part, part), part), :].astype(LOW)
        one_ref[...] = out_ref[pl.ds(pl.multiple_of(y * some, some), some), :].astype(LOW)
        two_ref[...] = out_ref[pl.ds(pl.multiple_of((1 - y) * some, some), some), :].astype(LOW)

    outs = [((8, own_in, 7 * LANES), LOW)] + [((part, width), LOW)] * 2 + [((some, width), LOW)] * 2
    return simple(kernel, "cut_weights", outs, qkv, up, down, out, place, smem=(4,))


def slot_tables(meta, counted, place, rope_of_position):
    slots = counted.shape[1]
    packs = meta.shape[0]
    per_pack = 4
    seqs = 2 * per_pack

    def kernel(len_ref, tok_ref, count_ref, place_ref, table_ref, bias_ref, rope_ref, hot_ref, target_ref, seqw_ref, seqc_ref):
        y = place_ref[0]
        row = lax.broadcasted_iota(jnp.int32, (slots, slots), 0)
        column = lax.broadcasted_iota(jnp.int32, (slots, slots), 1)

        def segments(pack, index):
            ends = []
            total = 0
            for j in range(per_pack):
                total = total + len_ref[pack, slots + j]
                ends.append(total)
            number = jnp.zeros(index.shape, jnp.int32)
            for j in range(per_pack):
                number = number + (index >= ends[j]).astype(jnp.int32)
            return number, ends

        for block in range(packs // 2):
            for dy in range(2):
                pack = block * 2 + lax.rem(y + dy, 2)
                here = pl.ds((block * 2 + dy) * slots, slots)
                by_row, ends = segments(pack, row)
                by_column, _ = segments(pack, column)
                seen = (by_row == by_column) & (column <= row)
                bias_ref[here, :] = jnp.where(seen, 0.0, -1e30)
                for part in range(3):
                    turned = table_ref[part]
                    for j in range(1, per_pack):
                        moved = pltpu.roll(table_ref[part], ends[j - 1], 0)
                        turned = jnp.where(by_row >= j, moved, turned)
                    rope_ref[part, here, :] = turned
                token = jnp.where(
                    y == dy, tok_ref[block * 2 : block * 2 + 1, :slots], tok_ref[block * 2 + 1 : block * 2 + 2, :slots]
                )
                hot = jnp.where(row == token, 1.0, 0.0)
                hot_ref[here, :] = hot.T[:, : hot_ref.shape[1]].astype(LOW)
        index = lax.broadcasted_iota(jnp.int32, (1, slots), 1)
        counts = jnp.zeros((seqs, slots), F32)
        seq_line = lax.broadcasted_iota(jnp.int32, (seqs, slots), 0)
        for pack in range(2):
            number, _ = segments(pack, index)
            following = pltpu.roll(number.astype(F32), slots - 1, 1)
            same = (following == number.astype(F32)) & (index < slots - 1)
            weight = jnp.where(same & (count_ref[pack : pack + 1, :] == 1), 1.0, 0.0)
            by_seq = jnp.where(seq_line == number + pack * per_pack, weight, 0.0)
            counts = counts + by_seq

            @pl.when(pack == y)
            def _():
                target = pltpu.roll(tok_ref[pack : pack + 1, :slots].astype(F32), slots - 1, 1)
                hot = jnp.where(row.astype(F32) == target, 1.0, 0.0)
                target_ref[...] = hot.T[:, : target_ref.shape[1]]
                padded = jnp.concatenate([by_seq, jnp.zeros((slots - seqs, slots), F32)], 0)
                seqw_ref[...] = padded.T

        seqc_ref[...] = jnp.broadcast_to(jnp.sum(counts, 1, keepdims=True), (seqs, LANES))

    outs = [
        ((packs * slots, slots), F32),
        ((3, packs * slots, LANES), F32),
        ((packs * slots, 32), LOW),
        ((slots, 32), F32),
        ((slots, LANES), F32),
        ((seqs, LANES), F32),
    ]
    return simple(
        kernel, "slot_tables", outs, meta, meta, counted, place, rope_of_position, smem=(0, 3), us=4.0
    )


def token_products(tables, weights, place):
    vocab = 32
    devices, _, lanes = tables.shape
    width = devices * vocab
    own_in, columns = weights.shape[1:]
    total = devices // 2 * 448

    def kernel(tab_ref, w_ref, place_ref, low_ref, vec_ref, h_ref, norm_ref, inv_ref, part_ref):
        h, x = place_ref[1], place_ref[3]
        flat = tab_ref[:, :vocab, :].astype(F32).reshape(width, lanes).T
        low_ref[...] = flat.astype(LOW)
        first_half = lax.broadcasted_iota(jnp.int32, (1, LANES), 1) < LANES // 2
        for pair in range(devices // 2):
            line, at = pair // (devices // 4), pair % (devices // 4) * 7 * LANES
            even = tab_ref[2 * pair, vocab : vocab + 4, :].astype(F32)
            odd = pltpu.roll(tab_ref[2 * pair + 1, vocab : vocab + 4, :].astype(F32), LANES // 2, 1)
            for q in range(7):
                if q < 3:
                    value = even[q : q + 1]
                elif q == 3:
                    value = jnp.where(first_half, even[3:4], odd[0:1])
                else:
                    value = jnp.where(first_half, odd[q - 4 : q - 3], odd[q - 3 : q - 2])
                vec_ref[line : line + 1, at + q * LANES : at + (q + 1) * LANES] = value
        out, normed, inverse = layer_norm(
            flat[:vocab], vec_ref[0:1, :width], vec_ref[0:1, width : 2 * width]
        )
        norm_ref[...] = normed
        inv_ref[...] = inverse
        h_ref[...] = out.astype(LOW)
        rows = 2 * own_in
        sums = jnp.zeros((vocab, columns), F32)
        for kk in range(2):
            start = pl.multiple_of(((h * 2 + kk) * 2 + x) * rows, LANES)
            block = w_ref[2 * kk : 2 * kk + 2].reshape(rows, columns)
            sums = sums + mm(h_ref[:, pl.ds(start, rows)], block)
        part_ref[...] = sums

    outs = [
        ((lanes, width), LOW),
        ((2, total), F32),
        ((vocab, width), LOW),
        ((vocab, width), F32),
        ((vocab, 1), F32),
        ((vocab, columns), F32),
    ]
    return simple(kernel, "token_products", outs, tables, weights, place, smem=(2,))


def shard_rows(weights, down_keep, down_far, out_one, out_two, place):
    part, width = down_keep.shape
    some = out_one.shape[0]
    own_in, columns = weights.shape[1:]

    def kernel(w_ref, keep_ref, far_ref, one_ref, two_ref, place_ref, upper_ref, first_ref):
        y, x = place_ref[0], place_ref[3]
        upper_ref[: 4 * own_in, :columns] = w_ref[4:].reshape(4 * own_in, columns)
        keep, far = keep_ref[...], far_ref[...]
        upper_ref[4 * own_in :, :] = jnp.where(y == 0, far, keep)
        first_ref[:part, :] = jnp.where(y == 0, keep, far)
        one, two = one_ref[...], two_ref[...]
        first_ref[part:, :] = jnp.where(x == 0, one, two)
        out = jnp.where(x == 0, two, one)
        for j in range(width // LANES):
            upper_ref[j * some : (j + 1) * some, columns:] = out[:, j * LANES : (j + 1) * LANES]

    outs = [((4 * own_in + part, width), LOW), ((part + some, width), LOW)]
    return simple(
        kernel, "shard_rows", outs, weights, down_keep, down_far, out_one, out_two, place, smem=(5,)
    )


def across(value):
    far = flip(value, ("h",), (1,))
    return [value, flip(value, ("x",), (1,)), far, flip(far, ("x",), (1,))]


def group_pieces(value):
    near = [value] + [flip(value, ("y", "k"), (dy, dk)) for dk, dy in NEAR]
    return near + [flip(piece, ("c",), (1,)) for piece in near]


def group_sums(keep, send):
    got = flip(send, ("c",), (1,))
    rows, width = (keep.shape[0] // 4, keep.shape[1])

    def kernel(keep_ref, got_ref, *refs):
        for j, ref in enumerate(refs):
            here = slice(j * rows, (j + 1) * rows)
            ref[...] = (keep_ref[here, :] + got_ref[here, :].astype(F32)).astype(ref.dtype)

    outs = [((rows, width), F32)] + [((rows, width), LOW)] * 3
    mine = simple(kernel, "group_sums", outs, keep, got)
    return [mine[0]] + [flip(piece, ("y", "k"), (dy, dk)) for piece, (dk, dy) in zip(mine[1:], NEAR)]


def block_of(place_ref, number):
    dh, dx = FLIPS[number]
    return (place_ref[1] + dh) % 2 * 2 + (place_ref[3] + dx) % 2


def first_group_forward(parts, tails, vec, place, hot, rope, bias):
    vocab, columns = parts[0].shape
    total, slots = bias.shape
    tail_rows, width = tails[0].shape
    part = LANES
    some = tail_rows - part
    units = 4 * part
    step = total // 2

    def kernel(*refs):
        part_refs, tail_refs = refs[:4], refs[4:8]
        vec_ref, place_ref, hot_ref, rope_ref, bias_ref = refs[8:13]
        keep_ref, send_ref, qkv_ref, att_ref, act_ref, slope_ref, wout_ref, wdown_ref = refs[13:21]
        table_ref, ffn_ref = refs[21:]
        first = pl.program_id(0) == 0

        @pl.when(first)
        def _():
            for number, ref in enumerate(tail_refs):
                block = block_of(place_ref, number)
                wdown_ref[pl.ds(pl.multiple_of(block * part, part), part), :] = ref[:part, :]
                wout_ref[pl.ds(pl.multiple_of(block * some, some), some), :] = ref[part:, :]
            sums = part_refs[0][...] + part_refs[1][...] + part_refs[2][...] + part_refs[3][...]
            table_ref[...] = sums[:, : 3 * LANES]
            y, k, c = place_ref[0], place_ref[2], place_ref[4]
            bias_up = jnp.concatenate(
                [
                    vec_ref[0:1, pl.ds(unit_start(width, j, y, k, c, part), part)]
                    for j in range(4)
                ],
                1,
            )
            act, slope = gelu_pair(sums[:, 3 * LANES :] + bias_up)
            act = act.astype(LOW)
            act_ref[...] = act
            slope_ref[...] = slope
            ffn_ref[...] = mm(act, wdown_ref[...])

        for pack in range(step // slots):
            here = slice(pack * slots, (pack + 1) * slots)
            hot_here = hot_ref[here, :]
            rope_here = [rope_ref[j, here, :] for j in range(3)]
            q = turn_by(exact_rows(hot_here, table_ref[:, :LANES]), rope_here, 1.0).astype(LOW)
            k = turn_by(
                exact_rows(hot_here, table_ref[:, LANES : 2 * LANES]), rope_here, 1.0
            ).astype(LOW)
            v = mm(hot_here, table_ref[:, 2 * LANES :].astype(LOW)).astype(LOW)
            qkv_ref[here, :LANES] = q
            qkv_ref[here, LANES : 2 * LANES] = k
            qkv_ref[here, 2 * LANES :] = v
            att_ref[here, :] = attend_pair(q, k, v, bias_ref[here, :])
        out = mm(att_ref[...], wout_ref[...]) + exact_rows(hot_ref[...], ffn_ref[...])

        @pl.when(first)
        def _():
            send_ref[...] = out.astype(LOW)

        @pl.when(jnp.logical_not(first))
        def _():
            keep_ref[...] = out

    def by_rows(columns):
        return pl.BlockSpec((step, columns), lambda s: (1 - s, 0))

    args = (*parts, *tails, vec)
    return pl.pallas_call(
        kernel,
        grid=(2,),
        in_specs=[whole_spec(arg.shape) for arg in args]
        + [
            pl.BlockSpec(memory_space=pltpu.SMEM),
            by_rows(vocab),
            pl.BlockSpec((3, step, LANES), lambda s: (0, 1 - s, 0)),
            by_rows(slots),
        ],
        out_specs=[
            whole_spec((step, width)),
            whole_spec((step, width)),
            by_rows(3 * LANES),
            by_rows(LANES),
            whole_spec((vocab, units)),
            whole_spec((vocab, units)),
            whole_spec((4 * some, width)),
            whole_spec((units, width)),
        ],
        out_shape=[
            jax.ShapeDtypeStruct((step, width), F32),
            jax.ShapeDtypeStruct((step, width), LOW),
            jax.ShapeDtypeStruct((total, 3 * LANES), LOW),
            jax.ShapeDtypeStruct((total, LANES), LOW),
            jax.ShapeDtypeStruct((vocab, units), LOW),
            jax.ShapeDtypeStruct((vocab, units), F32),
            jax.ShapeDtypeStruct((4 * some, width), LOW),
            jax.ShapeDtypeStruct((units, width), LOW),
        ],
        scratch_shapes=[pltpu.VMEM((vocab, 3 * LANES), F32), pltpu.VMEM((vocab, width), F32)],
        compiler_params=params(),
        cost_estimate=cost(9),
        name="first_group_forward",
    )(*args, place, hot, rope, bias)


def unit_start(width, j, y, k, c, part):
    unit = (j // 2 * 8 + k * 4 + j % 2 * 2 + c) * 2 * part + y * part
    return pl.multiple_of(3 * width + unit, LANES)


def first_finish_rows(pieces, hot, low_tables, vec):
    rows, width = pieces[0].shape
    vocab = hot.shape[1]

    def kernel(p0, p1, p2, p3, hot_ref, low_ref, vec_ref, x_ref, h_ref):
        stay = low_ref[:vocab, :].astype(F32) + vec_ref[0:1, 2 * width : 3 * width]
        x = exact_rows(hot_ref[:rows, :], stay) + p0[...]
        x = x + p1[...].astype(F32) + p2[...].astype(F32) + p3[...].astype(F32)
        x = x.astype(LOW)
        x_ref[...] = x
        h_ref[...] = layer_norm(
            x.astype(F32), vec_ref[1:2, :width], vec_ref[1:2, width : 2 * width]
        )[0].astype(LOW)

    outs = [((rows, width), LOW), ((rows, width), LOW)]
    return simple(kernel, "first_finish", outs, *pieces, hot, low_tables, vec)


def group_forward(pieces, shards, vec, place, rope, bias):
    slots, width = pieces[0].shape
    total = slots * len(pieces)
    step = total // 2
    part = LANES
    units, columns = 4 * part, 7 * LANES
    in_rows = shards[0].shape[0] - part
    some = in_rows // 8

    def kernel(*refs):
        piece_refs, shard_refs = refs[:8], refs[8:12]
        vec_ref, place_ref, rope_ref, bias_ref = refs[12:16]
        keep_ref, send_ref, h_ref, qkv_ref, att_ref, act_ref, slope_ref = refs[16:23]
        win_ref, wout_ref, wdown_ref = refs[23:]
        half = 1 - pl.program_id(0)

        @pl.when(half == 1)
        def _():
            for number, ref in enumerate(shard_refs):
                block = block_of(place_ref, number)
                rows = in_rows // 2
                for kk in range(2):
                    start = (block // 2 * 4 + kk * 2 + block % 2) * rows
                    win_ref[pl.ds(pl.multiple_of(start, rows), rows), :] = ref[
                        kk * rows : (kk + 1) * rows, :columns
                    ]
                here = pl.ds(pl.multiple_of(block * some, some), some)
                for j in range(width // LANES):
                    wout_ref[here, j * LANES : (j + 1) * LANES] = ref[
                        j * some : (j + 1) * some, columns:
                    ]
                wdown_ref[pl.ds(pl.multiple_of(block * part, part), part), :] = ref[in_rows:, :]

        for s in range(2):

            @pl.when(half == s)
            def _():
                for j in range(4):
                    h_ref[j * slots : (j + 1) * slots, :] = piece_refs[4 * s + j][...]

        h = h_ref[...]
        proj = mm(h, win_ref[:, : 3 * LANES])
        spans = [slice(j * LANES, (j + 1) * LANES) for j in range(3)]
        qkv_ref[:, spans[0]] = turn_by(proj[:, spans[0]], rope_ref, 1.0).astype(LOW)
        qkv_ref[:, spans[1]] = turn_by(proj[:, spans[1]], rope_ref, 1.0).astype(LOW)
        qkv_ref[:, spans[2]] = proj[:, spans[2]].astype(LOW)
        for pack in range(step // slots):
            here = slice(pack * slots, (pack + 1) * slots)
            q, k, v = (qkv_ref[here, spans[j]] for j in range(3))
            att_ref[here, :] = attend_pair(q, k, v, bias_ref[here, :])
        y, k, c = place_ref[0], place_ref[2], place_ref[4]
        bias_up = jnp.concatenate(
            [vec_ref[1:2, pl.ds(unit_start(width, j, y, k, c, part), part)] for j in range(4)], 1
        )
        act, slope = gelu_pair(mm(h, win_ref[:, 3 * LANES :]) + bias_up)
        act = act.astype(LOW)
        act_ref[...] = act
        slope_ref[...] = slope
        out = mm(att_ref[...], wout_ref[...]) + mm(act, wdown_ref[...])

        @pl.when(half == 1)
        def _():
            send_ref[...] = out.astype(LOW)

        @pl.when(half == 0)
        def _():
            keep_ref[...] = out

    def by_rows(columns):
        return pl.BlockSpec((step, columns), lambda s: (1 - s, 0))

    args = (*pieces, *shards, vec)
    shapes = [
        ((step, width), F32),
        ((step, width), LOW),
        ((total, width), LOW),
        ((total, 3 * LANES), LOW),
        ((total, LANES), LOW),
        ((total, units), LOW),
        ((total, units), F32),
        ((width, columns), LOW),
        ((LANES, width), LOW),
        ((units, width), LOW),
    ]
    return pl.pallas_call(
        kernel,
        grid=(2,),
        in_specs=[whole_spec(arg.shape) for arg in args]
        + [
            pl.BlockSpec(memory_space=pltpu.SMEM),
            pl.BlockSpec((3, step, LANES), lambda s: (0, 1 - s, 0)),
            by_rows(slots),
        ],
        out_specs=[
            whole_spec(shape) if number < 2 or number > 6 else by_rows(shape[1])
            for number, (shape, _) in enumerate(shapes)
        ],
        out_shape=[jax.ShapeDtypeStruct(shape, kind) for shape, kind in shapes],
        compiler_params=params(),
        cost_estimate=cost(12.5),
        name="group_forward",
    )(*args, place, rope, bias)


def group_backward(pieces, qkv, slope, w_in, w_out, w_down, rope, bias):
    slots, width = pieces[0].shape
    total = slots * len(pieces)
    units = w_down.shape[0]
    step = total // 2

    def kernel(*refs):
        piece_refs = refs[:8]
        win_ref, wout_ref, wdown_ref, qkv_ref, slope_ref, rope_ref, bias_ref = refs[8:15]
        keep_ref, send_ref, d_ref, din_ref, sum_ref = refs[15:]
        half = 1 - pl.program_id(0)
        for s in range(2):

            @pl.when(half == s)
            def _():
                for j in range(4):
                    d_ref[j * slots : (j + 1) * slots, :] = piece_refs[4 * s + j][...]

        d_out = d_ref[...]
        d_att = mm_t(d_out, wout_ref[...]).astype(LOW)
        d_pre = (mm_t(d_out, wdown_ref[...]) * slope_ref[...]).astype(LOW)
        din_ref[:, 3 * LANES :] = d_pre
        sums = jnp.sum(d_pre.astype(F32), 0, keepdims=True)
        spans = [slice(j * LANES, (j + 1) * LANES) for j in range(3)]
        for pack in range(step // slots):
            here = slice(pack * slots, (pack + 1) * slots)
            q, k, v = (qkv_ref[here, spans[j]] for j in range(3))
            dq, dk, dv = attend_pair_back(d_att[here, :], q, k, v, bias_ref[here, :])
            turned = [rope_ref[j, here, :] for j in range(3)]
            din_ref[here, spans[0]] = turn_by(dq, turned, -1.0).astype(LOW)
            din_ref[here, spans[1]] = turn_by(dk, turned, -1.0).astype(LOW)
            din_ref[here, spans[2]] = dv.astype(LOW)
        d_norm = mm_t(din_ref[...], win_ref[...])

        @pl.when(half == 1)
        def _():
            send_ref[...] = d_norm.astype(LOW)
            sum_ref[...] = sums

        @pl.when(half == 0)
        def _():
            keep_ref[...] = d_norm
            sum_ref[...] += sums

    def by_rows(columns):
        return pl.BlockSpec((step, columns), lambda s: (1 - s, 0))

    args = (*pieces, w_in, w_out, w_down)
    return pl.pallas_call(
        kernel,
        grid=(2,),
        in_specs=[whole_spec(arg.shape) for arg in args]
        + [
            by_rows(3 * LANES),
            by_rows(units),
            pl.BlockSpec((3, step, LANES), lambda s: (0, 1 - s, 0)),
            by_rows(slots),
        ],
        out_specs=[
            whole_spec((step, width)),
            whole_spec((step, width)),
            by_rows(width),
            by_rows(3 * LANES + units),
            whole_spec((1, units)),
        ],
        out_shape=[
            jax.ShapeDtypeStruct((step, width), F32),
            jax.ShapeDtypeStruct((step, width), LOW),
            jax.ShapeDtypeStruct((total, width), LOW),
            jax.ShapeDtypeStruct((total, 3 * LANES + units), LOW),
            jax.ShapeDtypeStruct((1, units), F32),
        ],
        compiler_params=params(),
        cost_estimate=cost(13.4),
        name="group_backward",
    )(*args, qkv, slope, rope, bias)


def weight_gradients(hs, d_in, act, att, d_rows, place):
    width = hs.shape[1]
    columns = d_in.shape[1]
    block = LANES
    some = LANES // 4

    def kernel(h_ref, din_ref, act_ref, att_ref, d_ref, place_ref, keep_ref, send_ref, out_ref):
        x = place_ref[3]
        h = pl.program_id(0)

        @pl.when(h == 0)
        def _():
            out_ref[...] = t_mm(att_ref[...], d_ref[...])

        d_in = din_ref[...]
        d_rows = d_ref[...]
        for ref, xx in ((keep_ref, x), (send_ref, 1 - x)):
            for k in range(2):
                start = pl.multiple_of(((h * 2 + k) * 2 + xx) * block, LANES)
                grad = t_mm(h_ref[:, pl.ds(start, block)], d_in)
                ref[0, k * block : (k + 1) * block, :columns] = grad.astype(ref.dtype)
            start = pl.multiple_of((h * 2 + xx) * some, some)
            grad = out_ref[pl.ds(start, some), :].astype(ref.dtype)
            for j in range(width // LANES):
                ref[0, j * some : (j + 1) * some, columns:] = grad[:, j * LANES : (j + 1) * LANES]
            start = pl.multiple_of((h * 2 + xx) * block, LANES)
            grad = t_mm(act_ref[:, pl.ds(start, block)], d_rows)
            ref[0, 2 * block :, :] = grad.astype(ref.dtype)

    args = (hs, d_in, act, att, d_rows)
    shape = (2, 3 * block, width)
    return pl.pallas_call(
        kernel,
        grid=(2,),
        in_specs=[whole_spec(arg.shape) for arg in args]
        + [pl.BlockSpec(memory_space=pltpu.SMEM)],
        out_specs=[pl.BlockSpec((1,) + shape[1:], lambda h: (h, 0, 0))] * 2,
        out_shape=[jax.ShapeDtypeStruct(shape, F32), jax.ShapeDtypeStruct(shape, LOW)],
        scratch_shapes=[pltpu.VMEM((LANES, width), F32)],
        compiler_params=params(),
        cost_estimate=cost(6.2),
        name="weight_gradients",
    )(*args, place)


def add_and_split(keep, got, place):
    shape = keep.shape[1:]

    def kernel(keep_ref, got_ref, place_ref, mine_ref, send_ref):
        b = place_ref[1]
        mine_ref[...] = keep_ref[b] + got_ref[b].astype(F32)
        send_ref[...] = (keep_ref[1 - b] + got_ref[1 - b].astype(F32)).astype(LOW)

    return simple(
        kernel, "add_and_split", [(shape, F32), (shape, LOW)], keep, got, place, smem=(2,)
    )


def split_two(total):
    high = total.astype(LOW)
    return (high, (total - high.astype(F32)).astype(LOW))


def first_group_backward(pieces, qkv, att, slope, w_out, w_down, hot, rope, bias, place):
    slots, width = pieces[0].shape
    total = slots * len(pieces)
    vocab = hot.shape[1]
    units = w_down.shape[0]
    some = LANES // 4
    columns = 3 * LANES + units + width

    def kernel(*refs):
        piece_refs = refs[:8]
        qkv_ref, att_ref, slope_ref, wout_ref, wdown_ref, hot_ref, rope_ref, bias_ref, place_ref = refs[8:17]
        out_refs, sum_ref, grad_ref = refs[17:21], refs[21], refs[22]
        sum_ref[...] = jnp.zeros(sum_ref.shape, F32)
        grad_ref[...] = jnp.zeros(grad_ref.shape, F32)
        spans = [slice(j * LANES, (j + 1) * LANES) for j in range(3)]
        for pack, ref in enumerate(piece_refs):
            here = slice(pack * slots, (pack + 1) * slots)
            d_out = ref[...]
            hot_here = hot_ref[here, :]
            d_att = mm_t(d_out, wout_ref[...]).astype(LOW)
            q, k, v = (qkv_ref[here, spans[j]] for j in range(3))
            dq, dk, dv = attend_pair_back(d_att, q, k, v, bias_ref[here, :])
            turned = [rope_ref[j, here, :] for j in range(3)]
            sum_ref[:, spans[0]] += t_mm(hot_here, turn_by(dq, turned, -1.0).astype(LOW))
            sum_ref[:, spans[1]] += t_mm(hot_here, turn_by(dk, turned, -1.0).astype(LOW))
            sum_ref[:, spans[2]] += t_mm(hot_here, dv.astype(LOW))
            sum_ref[:, 3 * LANES + units :] += t_mm(hot_here, d_out)
            grad_ref[...] += t_mm(att_ref[here, :], d_out)
        high, rest = split_two(sum_ref[:, 3 * LANES + units :])
        down = wdown_ref[...]
        sum_ref[:, 3 * LANES : 3 * LANES + units] = (
            mm_t(high, down) + mm_t(rest, down)
        ) * slope_ref[...]
        for number, ref in enumerate(out_refs):
            ref[:, :columns] = sum_ref[...].astype(ref.dtype)
            start = pl.multiple_of(block_of(place_ref, number) * some, some)
            ref[:, columns:] = grad_ref[pl.ds(start, some), :].astype(ref.dtype)

    outs = [((vocab, columns + width), F32)] + [((vocab, columns + width), LOW)] * 3
    args = (*pieces, qkv, att, slope, w_out, w_down, hot, rope, bias, place)
    scratch = [pltpu.VMEM((vocab, columns), F32), pltpu.VMEM((LANES, width), F32)]
    return simple(kernel, "first_group_backward", outs, *args, smem=(16,), scratch=scratch, us=9.0)


def token_gradients(parts, h0, weights, act, place):
    vocab, width = h0.shape
    own_in, shard = weights.shape[1:]
    units = act.shape[1]
    part = units // 4

    def kernel(p0, p1, p2, p3, h_ref, w_ref, act_ref, place_ref, in_ref, down_ref, out_ref, dh_ref, rows_ref, act_out):
        total = p0[...] + p1[...].astype(F32) + p2[...].astype(F32) + p3[...].astype(F32)
        rows = total[:, shard : shard + width]
        rows_ref[...] = rows
        out_ref[...] = total[:, shard + width :].astype(LOW)
        high, rest = split_two(total[:, :shard])
        h, x = place_ref[1], place_ref[3]
        two = 2 * own_in
        dh_ref[2 * vocab :, :] = jnp.zeros((dh_ref.shape[0] - 2 * vocab, LANES), LOW)
        for kk in range(2):
            start = pl.multiple_of(((h * 2 + kk) * 2 + x) * two, LANES)
            mine = h_ref[:, pl.ds(start, two)]
            grad = t_mm(mine, high) + t_mm(mine, rest)
            in_ref[2 * kk : 2 * kk + 2] = grad.astype(LOW).reshape(2, own_in, shard)
            block = w_ref[2 * kk : 2 * kk + 2].reshape(two, shard)
            dh = mm_t(high, block) + mm_t(rest, block)
            dh_ref[kk * vocab : (kk + 1) * vocab, :] = dh.astype(LOW)
        act_out[...] = total[:, 3 * LANES : shard]
        start = pl.multiple_of((h * 2 + x) * part, LANES)
        bias = jnp.sum(act_out[:, pl.ds(start, part)], 0, keepdims=True)
        dh_ref[2 * vocab : 2 * vocab + 1, :] = bias.astype(LOW)
        mine = act_ref[:, pl.ds(start, part)]
        high, rest = split_two(rows)
        down_ref[...] = (t_mm(mine, high) + t_mm(mine, rest)).astype(LOW)

    outs = [
        ((4, own_in, shard), LOW),
        ((part, width), LOW),
        ((vocab, width), LOW),
        ((2 * vocab + 16, LANES), LOW),
        ((vocab, width), F32),
    ]
    scratch = [pltpu.VMEM((vocab, units), F32)]
    args = (*parts, h0, weights, act, place)
    return simple(kernel, "token_gradients", outs, *args, smem=(7,), scratch=scratch)


def owner_pieces(keep, got, first_in, first_down, first_out, place):
    width = keep.shape[1]
    own_in, columns = first_in.shape[1:]
    part = first_down.shape[0]
    some = first_out.shape[0]

    def kernel(keep_ref, got_ref, in_ref, down_ref, out_ref, place_ref, shard_ref, mine_ref, send_ref, one_ref, two_ref, sum_ref):
        y, x = place_ref[0], place_ref[3]
        sum_ref[...] = (keep_ref[...] + got_ref[...].astype(F32)).astype(LOW)
        shard_ref[:4] = in_ref[...]
        for j in range(4):
            shard_ref[4 + j] = sum_ref[j * own_in : (j + 1) * own_in, :columns]
        upper = sum_ref[4 * own_in :, :]
        first = down_ref[...]
        mine_ref[...] = jnp.where(y == 0, first, upper)
        send_ref[...] = jnp.where(y == 0, upper, first)
        for j in range(width // LANES):
            here = slice(j * LANES, (j + 1) * LANES)
            upper = sum_ref[j * some : (j + 1) * some, columns:]
            first = out_ref[:, here]
            one_ref[:, here] = jnp.where(x == 0, first, upper)
            two_ref[:, here] = jnp.where(x == 0, upper, first)

    outs = [((8, own_in, columns), LOW)] + [((part, width), LOW)] * 2 + [((some, width), LOW)] * 2
    scratch = [pltpu.VMEM(keep.shape, LOW)]
    args = (keep, got, first_in, first_down, first_out, place)
    return simple(kernel, "owner_pieces", outs, *args, smem=(5,), scratch=scratch)


def own_gradients(shards, down_mine, down_far, out_one, out_two, mixed, scalars, bias_local, place):
    own_in = shards.shape[1]
    part, width = down_mine.shape
    some = out_one.shape[0]
    vocab = bias_local.shape[1]

    def kernel(shard_ref, mine_ref, far_ref, one_ref, two_ref, mixed_ref, scalar_ref, bias_ref, place_ref, qkv_ref, up_ref, down_ref, out_ref, mixed_out, last_ref):
        y = place_ref[0]
        for yy in range(2):
            for kk in range(2):
                for cc in range(2):
                    number = (yy * 2 + kk) * 2 + cc
                    start = ((cc * 2 + kk) * 2 + yy) * LANES
                    for j in range(3):
                        qkv_ref[:, j * width + start : j * width + start + LANES] = shard_ref[
                            number, :, j * LANES : (j + 1) * LANES
                        ].astype(F32)
                    for j in range(4):
                        start = (j // 2 * 8 + kk * 4 + j % 2 * 2 + cc) * 2 * part + yy * part
                        up_ref[:, start : start + part] = shard_ref[
                            number, :, (3 + j) * LANES : (4 + j) * LANES
                        ].astype(F32)
        mine, far = mine_ref[...].astype(F32), far_ref[...].astype(F32)
        down_ref[:part, :] = jnp.where(y == 0, mine, far)
        down_ref[part:, :] = jnp.where(y == 0, far, mine)
        one, two = one_ref[...].astype(F32), two_ref[...].astype(F32)
        out_ref[:some, :] = jnp.where(y == 0, one, two)
        out_ref[some:, :] = jnp.where(y == 0, two, one)
        mixed = jnp.sum(mixed_ref[...], 0)
        mixed_out[...] = mixed

        def squares(value):
            return jnp.sum(jnp.sum(value * value, 0, keepdims=True), 1, keepdims=True)

        total = squares(qkv_ref[...]) + squares(up_ref[...])
        total = total + squares(down_ref[...]) + squares(out_ref[...]) + squares(mixed[:vocab])
        total = total + jnp.where(y == 1, squares(mixed[vocab:]), 0.0)
        lane = lax.broadcasted_iota(jnp.int32, (1, LANES), 1)
        penalty = jnp.where(y == 0, scalar_ref[0:1, 2:3], 0.0)
        bias = jnp.concatenate([bias_ref[...], jnp.zeros((1, LANES - vocab), F32)], 1)
        row = jnp.where(lane == 0, total, jnp.where(lane == 1, penalty, 0.0))
        last_ref[...] = row + pltpu.roll(bias, vocab, 1)

    outs = [
        ((own_in, 3 * width), F32),
        ((own_in, 4 * width), F32),
        ((2 * part, width), F32),
        ((2 * some, width), F32),
        (mixed.shape[1:], F32),
        ((1, LANES), F32),
    ]
    args = (shards, down_mine, down_far, out_one, out_two, mixed, scalars, bias_local, place)
    return simple(kernel, "own_gradients", outs, *args, smem=(8,))


def fast_input_backward(pieces, x_low, dy, vec, down_sum, bias_up, table_local, place):
    rows, width = dy.shape
    part = bias_up.shape[1] // 4
    total = vec.shape[1]
    owners = 32
    vocab = width // owners

    def kernel(p0, p1, p2, p3, x_ref, dy_ref, vec_ref, sum_ref, up_ref, table_ref, place_ref, low_ref, mixed_ref, grad_ref):
        d_norm = p0[...] + p1[...].astype(F32) + p2[...].astype(F32) + p3[...].astype(F32)
        gain = vec_ref[1:2, :width]
        _, normed, inverse = layer_norm(x_ref[...].astype(F32), gain, 0.0)
        low_ref[...] = (dy_ref[...] + norm_back(d_norm, normed, inverse, gain)).astype(LOW)
        grad_ref[:, :width] = jnp.sum(d_norm * normed, 0, keepdims=True)
        grad_ref[:, width : 2 * width] = jnp.sum(d_norm, 0, keepdims=True)
        grad_ref[:, 2 * width : 3 * width] = sum_ref[...]
        grad_ref[:, 3 * width :] = jnp.zeros((1, total - 3 * width), F32)
        y, k, c = place_ref[0], place_ref[2], place_ref[4]
        for j in range(4):
            start = unit_start(width, j, y, k, c, part)
            grad_ref[:, pl.ds(start, part)] = up_ref[:, j * part : (j + 1) * part]
        mixed_ref[:, vocab:, :] = jnp.zeros((owners, mixed_ref.shape[1] - vocab, LANES), F32)
        for owner in range(owners):
            mixed_ref[owner, :vocab, :] = table_ref[owner * vocab : (owner + 1) * vocab, :]
        first_half = lax.broadcasted_iota(jnp.int32, (1, LANES), 1) < LANES // 2
        for pair in range(owners // 4):
            at = pair * 7 * LANES
            tiles = [grad_ref[:, at + q * LANES : at + (q + 1) * LANES] for q in range(7)]
            turned = [pltpu.roll(tile, LANES // 2, 1) for tile in tiles[3:]]
            even = tiles[:3] + [jnp.where(first_half, tiles[3], 0.0)]
            odd = [jnp.where(first_half, turned[q], turned[q + 1]) for q in range(3)]
            odd = odd + [jnp.where(first_half, turned[3], 0.0)]
            for side, lines in enumerate((even, odd)):
                for q in range(4):
                    owner = owners // 2 + 2 * pair + side
                    mixed_ref[owner, vocab + q : vocab + q + 1, :] = lines[q]

    outs = [((rows, width), LOW), ((owners, vocab + 8, LANES), F32)]
    args = (*pieces, x_low, dy, vec, down_sum, bias_up, table_local, place)
    scratch = [pltpu.VMEM((1, total), F32)]
    return simple(kernel, "input_backward", outs, *args, smem=(10,), scratch=scratch)


def last_sums(dh_all, last_all, rows_sum, normed, inverse, vec, mixed, place):
    vocab, width = rows_sum.shape
    total = vec.shape[1]
    chunk = 448
    devices = dh_all.shape[0]

    def kernel(dh_all_ref, last_ref, sum_ref, norm_ref, inv_ref, vec_ref, mixed_ref, place_ref, scalar_ref, vector_ref, table_ref, dh_ref, all_ref, emb_ref):
        y, me = place_ref[0], place_ref[5]
        for h in range(2):
            for x in range(2):
                for kk in range(2):
                    here = slice(kk * vocab, (kk + 1) * vocab)
                    block = jnp.zeros((vocab, LANES), F32)
                    for yy in range(2):
                        for k in range(2):
                            for c in range(2):
                                device = (((yy * 2 + h) * 2 + k) * 2 + x) * 2 + c
                                block = block + dh_all_ref[device, here, :].astype(F32)
                    start = (h * 4 + kk * 2 + x) * LANES
                    dh_ref[:, start : start + LANES] = block
        for device in range(devices):
            yy, i = device // (devices // 2), device % (devices // 2)
            start = 3 * width + i * 2 * LANES + yy * LANES
            all_ref[:, start : start + LANES] = dh_all_ref[
                device, 2 * vocab : 2 * vocab + 1, :
            ].astype(F32)
        dh = dh_ref[...]
        normed = norm_ref[...]
        rows = sum_ref[...]
        embed = rows + norm_back(dh, normed, inv_ref[...], vec_ref[0:1, :width])
        emb_ref[...] = embed
        all_ref[:, :width] = jnp.sum(dh * normed, 0, keepdims=True)
        all_ref[:, width : 2 * width] = jnp.sum(dh, 0, keepdims=True)
        all_ref[:, 2 * width : 3 * width] = jnp.sum(rows, 0, keepdims=True)
        scalars = jnp.sum(last_ref[...], 0, keepdims=True)
        lane = lax.broadcasted_iota(jnp.int32, (1, LANES), 1)
        bias = jnp.where((lane >= vocab) & (lane < 2 * vocab), scalars, 0.0)
        squares = jnp.sum(jnp.where(lane == 0, scalars, 0.0)) + jnp.sum(bias * bias)
        squares = squares + jnp.sum(embed * embed)
        vector = all_ref[...]
        squares = squares + jnp.sum(vector * vector)
        scalar_ref[...] = jnp.where(lane == 0, squares, scalars)
        odd = lax.rem(me, 2)
        start = pl.multiple_of(me * chunk - odd * (LANES // 2), LANES)
        mine = all_ref[:, pl.ds(start, chunk + LANES // 2)]
        mine = jnp.where(odd == 0, mine, pltpu.roll(mine, chunk, 1))
        far = jnp.concatenate([mixed_ref[vocab + q : vocab + q + 1, :] for q in range(4)], 1)
        vector_ref[...] = jnp.where(y == 0, mine, far)[:, :chunk]
        number = y * (devices // 2) + me
        block = emb_ref[:, pl.ds(pl.multiple_of(number // 4 * LANES, LANES), LANES)]
        block = pltpu.roll(block, lax.rem(LANES - lax.rem(number, 4) * vocab, LANES), 1)
        padded = jnp.concatenate([block, jnp.zeros((LANES - vocab, LANES), F32)], 0).T[:vocab, :]
        lane = lax.broadcasted_iota(jnp.int32, (vocab, LANES), 1)
        mixed = pltpu.roll(mixed_ref[:vocab, :], vocab, 1)
        table_ref[...] = jnp.where(lane < vocab, padded, mixed)

    args = (dh_all, last_all, rows_sum, normed, inverse, vec, mixed, place)
    outs = [((1, LANES), F32), ((1, chunk), F32), ((vocab, LANES), F32)]
    scratch = [
        pltpu.VMEM((vocab, width), F32),
        pltpu.VMEM((1, total), F32),
        pltpu.VMEM((vocab, width), F32),
    ]
    return simple(kernel, "last_sums", outs, *args, smem=(7,), scratch=scratch)


def body_fast(
    tokens,
    lengths,
    counted,
    partners,
    qkv_weight,
    out_weight,
    up_weight,
    down_weight,
    vectors,
    tables,
    head_bias,
    *states,
):
    y, h, k, x, c = (lax.axis_index(a) for a in ALL)
    me = lax.axis_index(PLANE)
    place = scalars_of(y, h, k, x, c, me)
    slots = tokens.shape[1]
    vocab = head_bias.shape[0]
    plane, everyone = 16, 32

    rows = jnp.concatenate(
        [
            jnp.pad(tables.T.astype(LOW), ((0, 0), (0, LANES - tables.shape[0]))),
            jnp.pad(vectors[0].astype(LOW), (0, 16 * LANES - vectors.shape[1])).reshape(16, LANES),
        ],
        0,
    )
    meta = jnp.concatenate([tokens, jnp.pad(lengths, ((0, 0), (0, slots - lengths.shape[1])))], 1)
    shards, down_keep, down_send, out_one, out_two = cut_weights(
        qkv_weight[0], up_weight[0], down_weight[0], out_weight[0], place
    )
    shards = trade(shards, ("y", "k", "c"))
    table_all = spread(rows, ALL)
    meta = jnp.concatenate([meta] + [flip(meta, ("k", "c"), (dk, dc)) for dc, dk in NEAR], 0)
    down_far = flip(down_send, ("y",), (1,))
    routes = [[], []]
    for device in range(everyone):
        yy, hh, kk, xx, cc = (device >> 4, device >> 3 & 1, device >> 2 & 1, device >> 1 & 1, device & 1)
        owner = cc * 8 + kk * 4 + yy * 2 + hh
        for step in range(2):
            routes[step].append(((xx ^ step) * plane + owner, device))
    out_one = lax.ppermute(out_one, ALL, routes[0])
    out_two = lax.ppermute(out_two, ALL, routes[1])
    bias, rope, hot, target_hot, seq_weight, seq_count = slot_tables(
        meta, counted, place, rope_constant(slots)
    )
    low_tables, vec, h0, normed0, inverse0, part = token_products(table_all, shards, place)
    upper, tail = shard_rows(shards, down_keep, down_far, out_one, out_two, place)
    parts = [part] + [flip(part, ("h", "x"), bits) for bits in NEAR]
    tails = across(tail)

    keep, send, qkv0, att0, act0, slope0, w_out0, w_down0 = first_group_forward(
        parts, tails, vec, place, hot, rope, bias
    )
    x_low, h_low = first_finish_rows(group_sums(keep, send), hot, low_tables, vec)

    uppers = across(upper)
    keep, send, hs, qkv, att, act, slope, w_in, w_out, w_down = group_forward(
        group_pieces(h_low), uppers, vec, place, rope, bias
    )
    normed_f, inverse_f, final_low, logp, sums = fast_loss_forward(
        x_low,
        group_sums(keep, send),
        vec,
        low_tables,
        head_bias,
        target_hot,
        seq_weight,
        seq_count,
    )
    sums = spread(sums, ALL).reshape(everyone, LANES)
    dy, dy_low, table_local, bias_local, down_sum, scalars = fast_loss_backward(
        sums,
        partners,
        place,
        normed_f,
        inverse_f,
        final_low,
        logp,
        low_tables,
        target_hot,
        seq_weight,
        plane,
        seq_count.shape[0],
    )

    keep, send, d_rows, d_in, bias_up = group_backward(
        group_pieces(dy_low), qkv, slope, w_in, w_out, w_down, rope, bias
    )
    terms = group_sums(keep, send)
    hs, d_in, act, att, d_rows, _ = together(hs, d_in, act, att, d_rows, terms[0])
    keep, send = weight_gradients(hs, d_in, act, att, d_rows, place)
    terms[0], send = together(terms[0], send)
    got = flip(send, ("x",), (1,))
    own_low, mixed = fast_input_backward(
        terms, x_low, dy, vec, down_sum, bias_up, table_local, place
    )

    pieces = group_pieces(own_low)
    mixed = trade(mixed, ALL)
    messages = first_group_backward(
        pieces, qkv0, att0, slope0, w_out0, w_down0, hot, rope, bias, place
    )
    parts = [messages[0]] + [flip(m, ("h", "x"), bits) for m, bits in zip(messages[1:], NEAR)]
    got, mixed, _ = together(got, mixed, messages[0])
    mine, send = add_and_split(keep, got, place)
    got = flip(send, ("h",), (1,))
    first_in, first_down, first_out, dh, rows_sum = token_gradients(
        parts, h0, shards, act0, place
    )
    dh_all = spread(dh, ALL)
    shards, down_mine, down_send, out_one, out_two = owner_pieces(
        mine, got, first_in, first_down, first_out, place
    )
    shards = trade(shards, ("y", "k", "c"))
    down_far = flip(down_send, ("y",), (1,))
    out_one = lax.ppermute(out_one, ALL, [(b, a) for a, b in routes[0]])
    out_two = lax.ppermute(out_two, ALL, [(b, a) for a, b in routes[1]])
    qkv_grad, up_grad, down_grad, out_grad, mixed, last = own_gradients(
        shards, down_mine, down_far, out_one, out_two, mixed, scalars, bias_local, place
    )
    last_all = spread(last, ALL).reshape(everyone, LANES)
    totals, vector_grad, table_grad = last_sums(
        dh_all, last_all, rows_sum, normed0, inverse0, vec, mixed, place
    )
    penalty = totals[0, 1]
    bias_grad = totals[0, vocab : 2 * vocab]
    grad_norm = jnp.sqrt(totals[0, 0])
    factor = jnp.minimum(1.0, CLIP_AT / grad_norm)
    grads = (
        qkv_grad[None],
        out_grad[None],
        up_grad[None],
        down_grad[None],
        vector_grad,
        table_grad[:, : tables.shape[0]].T,
        bias_grad,
    )
    masters = (qkv_weight, out_weight, up_weight, down_weight, vectors, tables, head_bias)
    rates = (RATE_MAT, RATE_OUT, RATE_MAT, RATE_MAT, RATE_VEC, RATE_VEC, RATE_VEC)
    decays = (DECAY, DECAY, DECAY, DECAY, 0.0, 0.0, 0.0)
    results = []
    for number in range(7):
        results.extend(
            adam(
                masters[number],
                states[number],
                states[7 + number],
                grads[number] * factor,
                rates[number],
                decays[number],
            )
        )
    loss_parts = jnp.stack([scalars[0, 0], scalars[0, 1], penalty])
    return (grad_norm, loss_parts, *results)


def body(
    tokens,
    lengths,
    counted,
    partners,
    qkv_weight,
    out_weight,
    up_weight,
    down_weight,
    vectors,
    tables,
    head_bias,
    qkv_moment,
    out_moment,
    up_moment,
    down_moment,
    vector_moment,
    table_moment,
    bias_moment,
    qkv_square,
    out_square,
    up_square,
    down_square,
    vector_square,
    table_square,
    bias_square,
):
    sections = lax.axis_size("y")
    spans = lax.axis_size("h")
    plane = lax.axis_size(PLANE)
    everyone = sections * plane
    y, h, k, x, c = (lax.axis_index(a) for a in ALL)
    me = lax.axis_index(PLANE)
    group = Group(sections, spans)
    micro, slots = tokens.shape
    per_pack = lengths.shape[1]
    width = qkv_weight.shape[2] // 3
    hidden = up_weight.shape[2]
    vocab = head_bias.shape[0]
    own_in = qkv_weight.shape[1]
    own_out = out_weight.shape[1]
    own_ff = down_weight.shape[1]
    shares = 4 * sections
    heads = width // HEAD
    shard_heads = heads // shares
    shard_width = width // shares
    shard_ff = hidden // shares
    rows = micro * slots // sections
    block_rows = micro * slots
    group_rows = 4 * block_rows
    group_packs = 4 * micro
    own_packs = max(1, rows // slots)
    own_pack_rows = min(rows, slots)

    low_qkv = qkv_weight[0].astype(LOW)
    low_out = out_weight[0].astype(LOW)
    low_up = up_weight[0].astype(LOW)
    low_down = down_weight[0].astype(LOW)

    table_part = tables.shape[1]
    vector_part = vectors.shape[1]
    small = jnp.concatenate(
        [
            tables.astype(LOW).reshape(-1),
            vectors[0].astype(LOW),
            lengths.astype(LOW).reshape(-1),
        ]
    )
    small_all = spread(small, ALL)
    cut_one = tables.size
    cut_two = cut_one + vector_part
    table_low = (
        small_all[:, :cut_one]
        .reshape(everyone, tables.shape[0], table_part)
        .transpose(1, 0, 2)
        .reshape(tables.shape[0], width)
    )
    vec_low = small_all[:, cut_one:cut_two].reshape(sections, plane * vector_part)
    vec_all = vec_low.astype(F32)
    lengths_all = small_all[:, cut_two:].astype(jnp.int32)
    embed = table_low[:vocab].astype(F32)
    head_low = table_low[vocab : 2 * vocab]
    final_gain = table_low[2 * vocab].astype(F32)
    final_bias = table_low[2 * vocab + 1].astype(F32)
    out_bias = head_bias.astype(LOW).astype(F32)

    segment, position = jax.vmap(lambda row: pack_layout(row, slots))(lengths)
    target = jnp.concatenate([tokens[:, 1:], jnp.zeros((micro, 1), jnp.int32)], 1)
    same = jnp.concatenate([segment[:, 1:] == segment[:, :-1], jnp.zeros((micro, 1), bool)], 1)
    weight = (same & (counted == 1)).astype(F32)
    sequence = segment + per_pack * jnp.arange(micro, dtype=jnp.int32)[:, None]

    def own(array):
        return lax.dynamic_slice_in_dim(array.reshape((block_rows,) + array.shape[2:]), y * rows, rows, 0)

    own_target = own(target)
    own_weight = own(weight)
    own_sequence = own(sequence)
    first_pack = (y * rows) // slots

    def packs_of(array):
        return lax.dynamic_slice_in_dim(array, first_pack, own_packs, 0)

    pack_tokens = packs_of(tokens)
    pack_segment = packs_of(segment)
    pack_position = packs_of(position)
    own_tokens = own(tokens).reshape(own_packs, own_pack_rows)
    own_segment = own(segment).reshape(own_packs, own_pack_rows)
    own_position = own(position).reshape(own_packs, own_pack_rows)
    pack_index = jnp.broadcast_to(jnp.arange(slots, dtype=jnp.int32), (own_packs, slots))
    own_index = (
        jnp.broadcast_to(jnp.arange(own_pack_rows, dtype=jnp.int32), (own_packs, own_pack_rows))
        + (y * rows) % slots
    )
    own_mask = (own_segment[:, :, None] == pack_segment[:, None, :]) & (
        pack_index[:, None, :] <= own_index[:, :, None]
    )
    target_hot = one_hot(own_target, vocab, F32)
    local_seqs = micro * per_pack
    seq_weight = one_hot(own_sequence, local_seqs, F32) * own_weight[:, None]
    seq_count = jnp.sum(
        one_hot(sequence.reshape(-1), local_seqs, F32) * weight.reshape(-1)[:, None], 0
    )
    hot_pack = one_hot(pack_tokens.reshape(-1), vocab, LOW)
    hot_own = one_hot(own_tokens.reshape(-1), vocab, LOW)
    own_bias = jnp.where(own_mask, 0.0, -1e30).reshape(rows, slots)
    own_rope = rope_rows(own_position.reshape(-1))
    pack_rope = own_rope if rows % slots == 0 else rope_rows(pack_position.reshape(-1))

    lengths_plane = lengths_all.reshape(sections, spans, 2, 2, 2, micro * per_pack)[0]
    lengths_group = pick(lengths_plane, h)[:, :, :, :]
    lengths_group = lax.dynamic_index_in_dim(lengths_group, x, 1, keepdims=False)

    parts = []
    for dc in range(2):
        for dk in range(2):
            block_lengths = pick(pick(lengths_group, (k - dk) % 2), (c - dc) % 2)
            parts.append(block_lengths.reshape(micro, per_pack))
    group_lengths = jnp.concatenate(parts, 0)
    group_segment, group_position = jax.vmap(lambda row: pack_layout(row, slots))(group_lengths)
    turn = (y - jnp.arange(sections)) % sections

    def by_offset(array):
        cut = array.reshape((4, sections, rows) + array.shape[2:])
        return jnp.take(cut, turn, axis=1).reshape((4 * sections * rows,) + array.shape[2:])

    if rows % slots == 0:
        group_segment = by_offset(group_segment).reshape(group_packs, slots)
        group_position = by_offset(group_position).reshape(group_packs, slots)
    group_index = jnp.arange(slots, dtype=jnp.int32)
    group_mask = (group_segment[:, :, None] == group_segment[:, None, :]) & (
        group_index[None, :] <= group_index[:, None]
    )
    group_bias = jnp.where(group_mask, 0.0, -1e30).reshape(group_rows, slots)
    group_rope = rope_rows(group_position.reshape(-1))

    def to_group(value):
        got = group.gather(value).reshape((4, sections, rows) + value.shape[1:])
        if rows % slots:
            got = jnp.take(got, turn, axis=1)
        return got.reshape((group_rows,) + value.shape[1:])

    def from_group(keep, send):
        def cut(value):
            value = value.reshape((2, sections, rows) + value.shape[1:])
            if rows % slots:
                value = jnp.take(value, turn, axis=1)
            return value.reshape((2 * sections, rows) + value.shape[3:])

        return group.scatter(cut(keep), cut(send))

    part_ff = own_ff // sections

    def columns_by_shard(qkv_rows, up_rows):
        cut_qkv = qkv_rows.reshape(own_in, 3, 2, 2, sections, shard_width)
        cut_up = up_rows.reshape(own_in, spans, 2, 2, 2, sections, part_ff)
        pieces = []
        for cc in range(2):
            for kk in range(2):
                for yy in range(sections):
                    pieces.append(
                        jnp.concatenate(
                            [cut_qkv[:, j, cc, kk, yy] for j in range(3)]
                            + [
                                cut_up[:, hh, kk, xx, cc, yy]
                                for hh in range(spans)
                                for xx in range(2)
                            ],
                            1,
                        )
                    )
        return jnp.stack(pieces).reshape((2, 2, sections) + pieces[0].shape)

    def columns_back(shards):
        cut = shards[..., : 3 * shard_width].reshape(2, 2, sections, own_in, 3, shard_width)
        qkv_rows = cut.transpose(3, 4, 0, 1, 2, 5).reshape(own_in, 3 * width)
        cut = shards[..., 3 * shard_width :].reshape(
            2, 2, sections, own_in, spans, 2, part_ff
        )
        up_rows = cut.transpose(3, 4, 1, 5, 0, 2, 6).reshape(own_in, hidden)
        return (qkv_rows, up_rows)

    small_out = width // everyone

    def out_routes(layer):
        routes = [[] for _ in range(sections)]
        for yy in range(sections):
            for hh in range(spans):
                for kk in range(2):
                    for xx in range(2):
                        for cc in range(2):
                            share = (cc * 2 + kk) * sections + yy
                            number = share * (2 * spans) + hh * 2 + xx
                            device = yy * plane + ((hh * 2 + kk) * 2 + xx) * 2 + cc
                            owner = layer * plane + number // sections
                            routes[number % sections].append((owner, device))
        return routes

    share_index = (c * 2 + k) * sections + y
    out_part = (share_index * (2 * spans) + h * 2 + x) % sections

    by_shard = columns_by_shard(low_qkv, low_up)
    give = shift(pick(by_shard, 1 - c), "c", 1)
    over_c = ordered(pick(by_shard, c), give, c, 1)
    give = shift(pick(over_c, 1 - k), "k", 1)
    over_k = ordered(pick(over_c, k), give, k, 0)

    gain0, bias0 = vec_all[0, :width], vec_all[0, width : 2 * width]
    bias_down0, bias_up0 = vec_all[0, 2 * width : 3 * width], vec_all[0, 3 * width :]
    h0_full, normed0, inverse0 = layer_norm(embed, gain0, bias0)
    h0 = h0_full.astype(LOW)
    pair_rows = 2 * own_in
    h0_here = jnp.concatenate(
        [
            lax.dynamic_slice_in_dim(h0, ((h * 2 + kk) * 2 + x) * pair_rows, pair_rows, 1)
            for kk in range(2)
        ],
        1,
    )
    both = [
        mm(h0_here, over_k[:, :, yy].reshape(4 * own_in, -1)) for yy in range(sections)
    ]
    spread_over = 2 * spans
    token_rows = vocab // spread_over
    proj_part = jnp.concatenate([part[:, : 3 * shard_width] for part in both], 1)
    proj_part = proj_part.reshape(spread_over, -1, own_ff)
    u_part = jnp.stack(
        [
            jnp.concatenate(
                [
                    part[:, 3 * shard_width + j * part_ff : 3 * shard_width + (j + 1) * part_ff]
                    for part in both
                ],
                1,
            )
            for j in range(spread_over)
        ]
    )
    mixed = jnp.sum(trade(jnp.concatenate([u_part, proj_part], 1), ("h", "x")), 0)
    u_own = mixed[:vocab] + lax.dynamic_slice_in_dim(bias_up0, me * own_ff, own_ff, 0)
    proj_own = mixed[vocab:]
    a0, slope0 = gelu_pair(u_own)
    a0 = a0.astype(LOW)
    ffn_part = jnp.where(y == 0, mm(a0, low_down), 0.0)
    for yy in range(1, sections):
        got = lax.ppermute(proj_own, "y", [(0, yy)])
        proj_own = jnp.where(y == yy, got, proj_own)
    proj_all = spread(proj_own, PLANE)
    ffn_cols = trade(ffn_part.reshape(vocab, everyone, -1).transpose(1, 0, 2), ALL)
    ffn_cols = jnp.sum(ffn_cols, 0)
    proj_table = (
        proj_all.reshape(spans, 2, 2, 2, token_rows, sections, 3, shard_width)
        .transpose(0, 2, 4, 6, 3, 1, 5, 7)
        .reshape(vocab, 3 * width)
    )
    ffn_table = spread(ffn_cols, ALL).transpose(1, 0, 2).reshape(vocab, width)
    query0, keys0, values0, att0 = first_forward(
        proj_table, hot_own, hot_pack, own_rope, pack_rope, own_bias, own_packs
    )

    first_out = low_out
    for yy in range(1, sections):
        got = lax.ppermute(low_out, "y", [(0, yy)])
        first_out = jnp.where(y == yy, got, first_out)
    pieces = jnp.stack([first_out] + [shift(first_out, "h", s) for s in range(1, spans)])
    pieces = jnp.take(pieces, (h - jnp.arange(spans)) % spans, axis=0)
    pieces = after(pieces, h0)
    pieces = ordered(pieces, after(shift(pieces, "k", 1), mixed), k, 1)
    pieces = ordered(pieces, after(shift(pieces, "x", 1), proj_table), x, 2)
    pieces = ordered(pieces, after(shift(pieces, "c", 1), att0), c, 3)
    first_out = pieces.reshape(width, width)

    stay = embed + ffn_table + bias_down0
    x_low, h_low = first_finish(
        att0, first_out, hot_own, stay, vec_all[1, :width], vec_all[1, width : 2 * width]
    )

    shard_weights = []
    for layer in range(1, sections):
        cut_down = low_down.reshape(sections, part_ff, width)
        down_piece = cut_down[layer]
        for yy in range(sections):
            if yy != layer:
                got = lax.ppermute(cut_down[yy], "y", [(layer, yy)])
                down_piece = jnp.where(y == yy, got, down_piece)
        cut_out = low_out.reshape(sections, small_out, width)
        out_piece = jnp.zeros((small_out, width), LOW)
        for p, route in enumerate(out_routes(layer)):
            got = lax.ppermute(cut_out[p], ALL, route)
            out_piece = jnp.where(out_part == p, got, out_piece)
        tail = jnp.concatenate([down_piece, out_piece], 0)
        tail = across_gather(tail, x, h0, ffn_part, att0)
        w_down = tail[:, :, :part_ff].reshape(shard_ff, width)
        w_out = tail[:, :, part_ff:].reshape(shard_width, width)
        mine = over_k[:, :, layer]
        for yy in range(sections):
            if yy != layer:
                got = lax.ppermute(over_k[:, :, yy], "y", [(layer, yy)])
                mine = jnp.where(y == yy, got, mine)
        whole = across_gather(mine, x, mixed, proj_table, h_low)
        w_in = whole.transpose(0, 2, 1, 3, 4, 5).reshape(width, -1)
        if shard_width < LANES:
            pad = LANES - shard_width
            cut = [w_in[:, j * shard_width : (j + 1) * shard_width] for j in range(3)]
            cut = [jnp.pad(piece, ((0, 0), (0, pad))) for piece in cut]
            w_in = jnp.concatenate(cut + [w_in[:, 3 * shard_width :]], 1)
            w_out = jnp.pad(w_out, ((0, pad), (0, 0)))
        shard_weights.append((w_in, w_out, w_down))

    kept = []
    for layer in range(1, sections):
        w_in, w_out, w_down = shard_weights[layer - 1]
        vec = vec_all[layer]
        gain, bias, bias_down = (vec[j * width : (j + 1) * width] for j in range(3))
        cut = vec[3 * width :].reshape(spans, 2, 2, 2, sections, part_ff)
        cut = lax.dynamic_index_in_dim(cut, k, 1, keepdims=False)
        cut = lax.dynamic_index_in_dim(cut, c, 2, keepdims=False)
        bias_up = lax.dynamic_index_in_dim(cut, y, 2, keepdims=False).reshape(shard_ff)
        if layer > 1:
            x_low = xs.astype(LOW)
            h_low = layer_norm(x_low.astype(F32), gain, bias)[0].astype(LOW)
        hs = to_group(h_low)
        keep, send, qkv, att, act, slope = upper_forward(
            hs, w_in, w_out, w_down, bias_up, group_rope, group_bias, slots
        )
        kept.append((x_low, gain, bias, hs, qkv, att, act, slope))
        pieces = from_group(keep, send)
        if layer < sections - 1:
            xs = x_low.astype(F32) + sum(piece.astype(F32) for piece in pieces) + bias_down

    normed_f, inverse_f, final_low, logp, lik_sum = loss_forward(
        x_low, pieces, bias_down, final_gain, final_bias, head_low, out_bias, target_hot, seq_weight
    )
    sums = spread(jnp.concatenate([lik_sum[0], seq_count]), ALL)
    dy, own_low, table_local, bias_local, down_sum, scalars = loss_backward(
        sums,
        partners,
        me[None],
        normed_f,
        inverse_f,
        final_low,
        logp,
        head_low,
        final_gain,
        target_hot,
        seq_weight,
        plane,
    )
    loss_total, count_total = scalars[0, 0], scalars[0, 1]
    penalty_local = jnp.where(y == 0, scalars[0, 2], 0.0)
    bias_local = bias_local[0]

    def finish_shards(layer, out_grad, down_grad, in_grad, first, second, last):
        tail = jnp.concatenate(
            [
                down_grad.reshape(spans, 2, part_ff, width),
                out_grad.reshape(spans, 2, small_out, width),
            ],
            2,
        )
        tail = across_scatter(tail, x, first, second, last).astype(LOW)
        down_piece, out_piece = tail[:part_ff], tail[part_ff:]
        down_rows = jnp.stack(
            [
                down_piece if yy == layer else lax.ppermute(down_piece, "y", [(yy, layer)])
                for yy in range(sections)
            ]
        ).reshape(own_ff, width)
        out_rows = jnp.stack(
            [
                lax.ppermute(out_piece, ALL, [(b, a) for a, b in route])
                for route in out_routes(layer)
            ]
        ).reshape(own_out, width)
        inner = in_grad.reshape(spans, 2, 2, 2, own_in, -1).transpose(0, 2, 1, 3, 4, 5)
        inner = across_scatter(inner, x, first, second, last).astype(LOW)
        keep = pick(inner, k)
        give = shift(pick(inner, 1 - k), "k", 1)
        over_k = ordered(keep, give, k, 1)
        keep = pick(over_k, c)
        give = shift(pick(over_k, 1 - c), "c", 1)
        over_c = ordered(keep, give, c, 0)
        shards = jnp.stack(
            [
                over_c if yy == layer else lax.ppermute(over_c, "y", [(yy, layer)])
                for yy in range(sections)
            ],
            2,
        )
        qkv_rows, up_rows = columns_back(shards)
        return (qkv_rows, out_rows, up_rows, down_rows)

    pending = []
    vector_locals = []
    for layer in range(sections - 1, 0, -1):
        w_in, w_out, w_down = shard_weights[layer - 1]
        x_low, gain, bias, hs, qkv, att, act, slope = kept[layer - 1]
        d_rows = to_group(own_low)
        keep, send, d_in, bias_up_grad = upper_backward(
            d_rows, qkv, slope, w_in, w_out, w_down, group_rope, group_bias, slots
        )
        pieces = from_group(keep, send)
        above = dy
        own_low, vec_sums, dyb_token = input_backward(pieces, x_low, dy, gain, hot_own)
        dy = own_low.astype(F32)
        att, act, hs, d_in, d_rows = lax.optimization_barrier((att, act, hs, d_in, d_rows, keep))[:5]
        out_grad = t_mm(att, d_rows)[:shard_width]
        down_grad = t_mm(act, d_rows)
        in_grad = t_mm(hs, d_in)
        if shard_width < LANES:
            cut = [in_grad[:, j * LANES : j * LANES + shard_width] for j in range(3)]
            in_grad = jnp.concatenate(cut + [in_grad[:, 3 * LANES :]], 1)
        bias_up_grad = bias_up_grad.reshape(spans, 2, part_ff)
        place = (
            (jnp.arange(2) == k)[None, :, None, None, None, None]
            & (jnp.arange(2) == c)[None, None, None, :, None, None]
            & (jnp.arange(sections) == y)[None, None, None, None, :, None]
        )
        bias_up_grad = jnp.where(place, bias_up_grad[:, None, :, None, None, :], 0.0)
        vector_locals.append(
            jnp.concatenate([vec_sums[0], vec_sums[1], down_sum[0], bias_up_grad.reshape(-1)])
        )
        down_sum = vec_sums[2:3]
        pending.append((layer, out_grad, down_grad, in_grad, keep))
    vector_locals = vector_locals[::-1]

    dyb_cols = trade(dyb_token.reshape(vocab, everyone, -1).transpose(1, 0, 2), ALL)
    dq_token, dk_token, dv_token, first_out_grad = first_backward(
        own_low,
        query0,
        keys0,
        values0,
        att0,
        hot_own,
        hot_pack,
        own_rope,
        pack_rope,
        own_bias,
        first_out,
        own_packs,
    )
    dyb_cols = jnp.sum(after(dyb_cols, first_out_grad), 0)
    dyb_sum = spread(dyb_cols, ALL).transpose(1, 0, 2).reshape(vocab, width)
    token_part = jnp.concatenate([dq_token, dk_token, dv_token], 1)
    token_cols = trade(token_part.reshape(vocab, everyone, -1).transpose(1, 0, 2), ALL)
    token_cols = jnp.sum(token_cols, 0).astype(LOW)
    du_own = (mm_exact(dyb_sum, low_down, ((1,), (1,))) * slope0).astype(LOW)
    du_sum = spread(du_own, PLANE).transpose(1, 0, 2).reshape(vocab, hidden)
    dproj_sum = spread(token_cols, ALL).transpose(1, 0, 2).reshape(vocab, 3 * width)
    dh_own = mm_t(dproj_sum, low_qkv) + mm_t(du_sum, low_up)

    shard_grads = [None] * sections
    for layer, out_grad, down_grad, in_grad, keep in pending:
        shard_grads[layer] = finish_shards(
            layer, out_grad, down_grad, in_grad, own_low, first_out_grad, du_own
        )
    vector_cut = jnp.stack([jnp.zeros_like(vector_locals[0])] + vector_locals)
    vector_cut = vector_cut.reshape(everyone, vector_part)
    table_cut = table_local.reshape(-1, everyone, table_part).transpose(1, 0, 2)
    mixed = jnp.concatenate([vector_cut, table_cut.reshape(everyone, -1)], 1)
    mixed = jnp.sum(trade(after(mixed, first_out_grad), ALL), 0)
    h0_own = lax.dynamic_slice_in_dim(h0, me * own_in, own_in, 1)
    down_first = mm_exact(a0, dyb_sum, ((0,), (0,)))
    qkv_first = t_mm(h0_own, dproj_sum)
    up_first = t_mm(h0_own, du_sum)
    part = first_out_grad.reshape(spans, 2, 2, 2, own_out, width)
    part = jnp.moveaxis(part, 3, 0)
    part = pick(part, c) + shift(pick(part, 1 - c).astype(LOW), "c", 1).astype(F32)
    part = jnp.moveaxis(part, 2, 0)
    part = pick(part, x) + shift(pick(part, 1 - x).astype(LOW), "x", 1).astype(F32)
    part = jnp.moveaxis(part, 1, 0)
    part = pick(part, k) + shift(pick(part, 1 - k).astype(LOW), "k", 1).astype(F32)
    total = pick(part, h)
    for s in range(1, spans):
        total = total + shift(pick(part, (h + s) % spans).astype(LOW), "h", s).astype(F32)
    out_first = total
    for yy in range(1, sections):
        out_first = out_first + lax.ppermute(total.astype(LOW), "y", [(yy, 0)]).astype(F32)

    first = (qkv_first, out_first, up_first, down_first)
    grads = []
    for number in range(4):
        grad = first[number]
        for layer in range(1, sections):
            grad = jnp.where(y == layer, shard_grads[layer][number].astype(F32), grad)
        grads.append(grad[None])
    mixed_vector = mixed[:vector_part]
    mixed_table = mixed[vector_part:].reshape(-1, table_part)

    squares = sum((jnp.sum(g * g) for g in grads)) + jnp.sum(mixed_table * mixed_table)
    squares = squares + jnp.where(y == 0, 0.0, jnp.sum(mixed_vector * mixed_vector))
    up_sum = jnp.sum(du_sum.astype(F32), 0)
    down_sum = jnp.sum(dyb_sum, 0)
    squares = squares + jnp.where(
        (y == 0) & (me == 0), jnp.sum(up_sum * up_sum) + jnp.sum(down_sum * down_sum), 0.0
    )
    last = jnp.concatenate([squares[None], penalty_local[None], bias_local])
    last = jnp.pad(last, (0, (-last.shape[0]) % own_in)).reshape(-1, own_in)
    last = spread(jnp.concatenate([dh_own, last], 0), ALL)
    dh = last[:plane, :vocab].transpose(1, 0, 2).reshape(vocab, width)
    last = jnp.sum(last[:, vocab:], 0).reshape(-1)
    embed_grad = dyb_sum + norm_back(dh, normed0, inverse0, gain0)
    gain_grad, shift_grad = jnp.sum(dh * normed0, 0), jnp.sum(dh, 0)
    vector_first = jnp.concatenate([gain_grad, shift_grad, down_sum, up_sum])
    vector_own = lax.dynamic_slice_in_dim(vector_first, me * vector_part, vector_part, 0)
    vector_grad = jnp.where(y == 0, vector_own, mixed_vector)
    number = y * plane + me
    embed_own = lax.dynamic_slice_in_dim(embed_grad, number * table_part, table_part, 1)
    table_grad = jnp.concatenate([embed_own, mixed_table], 0)
    penalty = last[1]
    bias_grad = last[2 : 2 + vocab]
    squares = last[0] + jnp.sum(embed_grad * embed_grad) + jnp.sum(bias_grad * bias_grad)
    squares = squares + jnp.sum(gain_grad * gain_grad) + jnp.sum(shift_grad * shift_grad)
    grad_norm = jnp.sqrt(squares)
    factor = jnp.minimum(1.0, CLIP_AT / grad_norm)
    grads = grads + [vector_grad[None], table_grad, bias_grad]
    masters = (qkv_weight, out_weight, up_weight, down_weight, vectors, tables, head_bias)
    moments = (
        qkv_moment,
        out_moment,
        up_moment,
        down_moment,
        vector_moment,
        table_moment,
        bias_moment,
    )
    squares_in = (
        qkv_square,
        out_square,
        up_square,
        down_square,
        vector_square,
        table_square,
        bias_square,
    )
    rates = (RATE_MAT, RATE_OUT, RATE_MAT, RATE_MAT, RATE_VEC, RATE_VEC, RATE_VEC)
    decays = (DECAY, DECAY, DECAY, DECAY, 0.0, 0.0, 0.0)
    results = []
    for number in range(7):
        results.extend(
            adam(
                masters[number],
                moments[number],
                squares_in[number],
                grads[number] * factor,
                rates[number],
                decays[number],
            )
        )
    loss_parts = jnp.stack([loss_total, count_total, penalty])
    return (grad_norm, loss_parts, *results)


def solution(mesh):
    sections, plane = mesh.shape["section"], mesh.shape["dp"]
    fine = Mesh(mesh.devices.reshape(sections, plane // 8, 2, 2, 2), ALL)
    matrix = P("y", PLANE, None)
    vector = P("y", PLANE)
    table = P(None, ALL)
    states = (matrix, matrix, matrix, matrix, vector, table, P())
    results = []
    for spec in states:
        results.extend([spec] * 3)
    chosen = body_fast if (sections, plane) == (2, 16) else body
    return jax.shard_map(
        chosen,
        mesh=fine,
        in_specs=(P(PLANE, None), P(PLANE, None), P(PLANE, None), P(PLANE))
        + states
        + states
        + states,
        out_specs=(P(), P(), *results),
        check_vma=False,
    )
```

```python
import math

import jax
import jax.numpy as jnp
import numpy as np
from jax import lax
from jax.experimental import pallas as pl
from jax.experimental.pallas import tpu as pltpu
from jax.sharding import Mesh
from jax.sharding import PartitionSpec as P

HEAD = 64
ROT = 32
STEP = 10

EPS_NORM = 1e-05
PENALTY = 2.0
CLIP_AT = 0.02
RATE_MAT = 0.02
RATE_OUT = 0.1
RATE_VEC = 0.2
BETA_ONE = 0.9
BETA_TWO = 0.95
EPS_ADAM = 1e-08
DECAY = 0.1
GELU_C = 0.7978845608028654

ALL = ("y", "h", "k", "x", "c")
PLANE = ("h", "k", "x", "c")
LOW = jnp.bfloat16
F32 = jnp.float32
EXACT = lax.Precision.HIGHEST


def mm(left, right):
    return jnp.dot(left, right, preferred_element_type=F32)


def mm_t(left, right):
    return lax.dot_general(left, right, (((1,), (1,)), ((), ())), preferred_element_type=F32)


def t_mm(left, right):
    return lax.dot_general(left, right, (((0,), (0,)), ((), ())), preferred_element_type=F32)


def mm_exact(left, right, dims):
    return lax.dot_general(
        left.astype(F32), right.astype(F32), (dims, ((), ())), precision=EXACT
    )


def pick(array, index):
    return lax.dynamic_index_in_dim(array, index, 0, keepdims=False)


def spread(value, axes):
    many = lax.axis_size(axes)
    return lax.all_to_all(jnp.broadcast_to(value[None], (many,) + value.shape), axes, 0, 0, tiled=True)


def trade(pieces, axes):
    return lax.all_to_all(pieces, axes, 0, 0, tiled=True)


def shift(value, axis, by):
    many = lax.axis_size(axis)
    return lax.ppermute(value, axis, [(i, (i + by) % many) for i in range(many)])


def after(value, *earlier):
    return lax.optimization_barrier((value,) + earlier)[0]


def together(*values):
    return lax.optimization_barrier(values)


def ordered(own, other, bit, axis):
    return jnp.stack(
        [jnp.where(bit == 0, own, other), jnp.where(bit == 0, other, own)], axis
    )


def layer_norm(x, gain, bias):
    mean = jnp.mean(x, -1, keepdims=True)
    centred = x - mean
    inverse = lax.rsqrt(jnp.mean(centred * centred, -1, keepdims=True) + EPS_NORM)
    normed = centred * inverse
    return (normed * gain + bias, normed, inverse)


def norm_back(grad, normed, inverse, gain):
    scaled = grad * gain
    return inverse * (
        scaled
        - jnp.mean(scaled, -1, keepdims=True)
        - normed * jnp.mean(scaled * normed, -1, keepdims=True)
    )


def gelu_pair(value):
    inner = jnp.tanh(GELU_C * (value + 0.044715 * value * value * value))
    result = 0.5 * value * (1.0 + inner)
    slope = 0.5 * (1.0 + inner) + 0.5 * value * (1.0 - inner * inner) * GELU_C * (
        1.0 + 3.0 * 0.044715 * value * value
    )
    return (result, slope)


def one_hot(row, vocab, dtype):
    return (row[:, None] == jnp.arange(vocab, dtype=jnp.int32)[None, :]).astype(dtype)


def pack_layout(lengths_row, slots):
    ends = jnp.cumsum(lengths_row)
    starts = ends - lengths_row
    index = jnp.arange(slots, dtype=jnp.int32)
    segment = jnp.sum((index[:, None] >= ends[None, :]).astype(jnp.int32), 1)
    member = segment[:, None] == jnp.arange(lengths_row.shape[0], dtype=jnp.int32)[None, :]
    position = index - jnp.sum(jnp.where(member, starts[None, :], 0), 1)
    return (segment, position)


LANES = 128
VMEM_LIMIT = 28 * 1024 * 1024
VMEM_MOST = 60 * 1024 * 1024
SCALE = 1.0 / math.sqrt(HEAD)


def rope_rows(position):
    half = ROT // 2
    freq = 10000.0 ** (-2.0 * jnp.arange(half, dtype=F32) / ROT)
    angle = position.astype(F32)[:, None] * freq
    cosine, sine = (jnp.cos(angle), jnp.sin(angle))
    none, one = (jnp.zeros_like(sine), jnp.ones_like(sine))
    many = LANES // HEAD
    rest = HEAD // half - 2
    return jnp.stack(
        [
            jnp.concatenate(([cosine, cosine] + [one] * rest) * many, 1),
            jnp.concatenate(([-sine, none] + [none] * rest) * many, 1),
            jnp.concatenate(([none, sine] + [none] * rest) * many, 1),
        ]
    )


def turn_by(value, rope, sign):
    above = pltpu.roll(value, LANES - ROT // 2, 1)
    below = pltpu.roll(value, ROT // 2, 1)
    return value * rope[0] + sign * (above * rope[1] + below * rope[2])


def head_lanes(shape):
    lane = lax.broadcasted_iota(jnp.int32, shape, 1)
    return [(lane // HEAD) == number for number in range(LANES // HEAD)]


def soft(query, keys, bias):
    scores = mm_t(query, keys) * SCALE + bias
    expo = jnp.exp(scores - jnp.max(scores, -1, keepdims=True))
    return expo / jnp.sum(expo, -1, keepdims=True)


def attend_pair(query, keys, values, bias):
    out = jnp.zeros(query.shape, F32)
    nothing = jnp.zeros((), LOW)
    for mine_q, mine_k in zip(head_lanes(query.shape), head_lanes(keys.shape)):
        probs = soft(jnp.where(mine_q, query, nothing), keys, bias).astype(LOW)
        out = out + mm(probs, jnp.where(mine_k, values, nothing))
    return out.astype(LOW)


def attend_pair_back(d_out, query, keys, values, bias):
    d_query = jnp.zeros(query.shape, F32)
    d_keys = jnp.zeros(keys.shape, F32)
    d_values = jnp.zeros(keys.shape, F32)
    nothing = jnp.zeros((), LOW)
    for mine_q, mine_k in zip(head_lanes(query.shape), head_lanes(keys.shape)):
        query_h = jnp.where(mine_q, query, nothing)
        d_out_h = jnp.where(mine_q, d_out, nothing)
        probs = soft(query_h, keys, bias)
        d_values = d_values + t_mm(probs.astype(LOW), d_out_h)
        d_probs = mm_t(d_out_h, values)
        d_scores = probs * (d_probs - jnp.sum(probs * d_probs, -1, keepdims=True))
        d_scores = d_scores.astype(LOW)
        d_query = d_query + mm(d_scores, jnp.where(mine_k, keys, nothing))
        d_keys = d_keys + t_mm(d_scores, query_h)
    return (d_query * SCALE, d_keys * SCALE, d_values)


def whole_spec(shape):
    return pl.BlockSpec(shape, lambda *_: (0,) * len(shape))


def params(limit=VMEM_LIMIT):
    return pltpu.CompilerParams(vmem_limit_bytes=limit)


def upper_forward(hs, w_in, w_out, w_down, bias_up, rope, bias, slots):
    total, width = hs.shape
    lanes, units = (w_out.shape[0], w_down.shape[0])
    step = total // 2

    def kernel(h_ref, win_ref, wout_ref, wdown_ref, bup_ref, rope_ref, bias_ref, keep_ref, send_ref, qkv_ref, att_ref, act_ref, slope_ref):
        h = h_ref[...]
        proj = mm(h, win_ref[:, : 3 * lanes])
        for g in range(lanes // LANES):
            spans = [slice(j * lanes + g * LANES, j * lanes + (g + 1) * LANES) for j in range(3)]
            qkv_ref[:, spans[0]] = turn_by(proj[:, spans[0]], rope_ref, 1.0).astype(LOW)
            qkv_ref[:, spans[1]] = turn_by(proj[:, spans[1]], rope_ref, 1.0).astype(LOW)
            qkv_ref[:, spans[2]] = proj[:, spans[2]].astype(LOW)
            for pack in range(step // slots):
                here = slice(pack * slots, (pack + 1) * slots)
                q, k, v = (qkv_ref[here, spans[j]] for j in range(3))
                att_ref[here, g * LANES : (g + 1) * LANES] = attend_pair(q, k, v, bias_ref[here, :])
        act, slope = gelu_pair(mm(h, win_ref[:, 3 * lanes :]) + bup_ref[...])
        act = act.astype(LOW)
        act_ref[...] = act
        slope_ref[...] = slope
        out = mm(att_ref[...], wout_ref[...]) + mm(act, wdown_ref[...])

        @pl.when(pl.program_id(0) == 0)
        def _():
            send_ref[...] = out.astype(LOW)

        @pl.when(pl.program_id(0) == 1)
        def _():
            keep_ref[...] = out

    def by_rows(columns):
        return pl.BlockSpec((step, columns), lambda s: (1 - s, 0))

    return pl.pallas_call(
        kernel,
        grid=(2,),
        in_specs=[
            by_rows(width),
            whole_spec(w_in.shape),
            whole_spec(w_out.shape),
            whole_spec(w_down.shape),
            whole_spec((1, units)),
            pl.BlockSpec((3, step, LANES), lambda s: (0, 1 - s, 0)),
            by_rows(slots),
        ],
        out_specs=[
            whole_spec((step, width)),
            whole_spec((step, width)),
            by_rows(3 * lanes),
            by_rows(lanes),
            by_rows(units),
            by_rows(units),
        ],
        out_shape=[
            jax.ShapeDtypeStruct((step, width), F32),
            jax.ShapeDtypeStruct((step, width), LOW),
            jax.ShapeDtypeStruct((total, 3 * lanes), LOW),
            jax.ShapeDtypeStruct((total, lanes), LOW),
            jax.ShapeDtypeStruct((total, units), LOW),
            jax.ShapeDtypeStruct((total, units), F32),
        ],
        compiler_params=params(),
        name="upper_forward",
    )(hs, w_in, w_out, w_down, bias_up[None], rope, bias)


def upper_backward(d_rows, qkv, slope, w_in, w_out, w_down, rope, bias, slots):
    total, width = d_rows.shape
    lanes, units = (w_out.shape[0], w_down.shape[0])
    step = total // 2

    def kernel(d_ref, qkv_ref, slope_ref, win_ref, wout_ref, wdown_ref, rope_ref, bias_ref, keep_ref, send_ref, din_ref, sum_ref):
        d_out = d_ref[...]
        d_att = mm_t(d_out, wout_ref[...]).astype(LOW)
        d_pre = (mm_t(d_out, wdown_ref[...]) * slope_ref[...]).astype(LOW)
        din_ref[:, 3 * lanes :] = d_pre
        sums = jnp.sum(d_pre.astype(F32), 0, keepdims=True)
        for g in range(lanes // LANES):
            spans = [slice(j * lanes + g * LANES, j * lanes + (g + 1) * LANES) for j in range(3)]
            for pack in range(step // slots):
                here = slice(pack * slots, (pack + 1) * slots)
                q, k, v = (qkv_ref[here, spans[j]] for j in range(3))
                dq, dk, dv = attend_pair_back(
                    d_att[here, g * LANES : (g + 1) * LANES], q, k, v, bias_ref[here, :]
                )
                turned = [rope_ref[j, here, :] for j in range(3)]
                din_ref[here, spans[0]] = turn_by(dq, turned, -1.0).astype(LOW)
                din_ref[here, spans[1]] = turn_by(dk, turned, -1.0).astype(LOW)
                din_ref[here, spans[2]] = dv.astype(LOW)
        d_norm = mm_t(din_ref[...], win_ref[...])

        @pl.when(pl.program_id(0) == 0)
        def _():
            send_ref[...] = d_norm.astype(LOW)
            sum_ref[...] = sums

        @pl.when(pl.program_id(0) == 1)
        def _():
            keep_ref[...] = d_norm
            sum_ref[...] += sums

    def by_rows(columns):
        return pl.BlockSpec((step, columns), lambda s: (1 - s, 0))

    return pl.pallas_call(
        kernel,
        grid=(2,),
        in_specs=[
            by_rows(width),
            by_rows(3 * lanes),
            by_rows(units),
            whole_spec(w_in.shape),
            whole_spec(w_out.shape),
            whole_spec(w_down.shape),
            pl.BlockSpec((3, step, LANES), lambda s: (0, 1 - s, 0)),
            by_rows(slots),
        ],
        out_specs=[
            whole_spec((step, width)),
            whole_spec((step, width)),
            by_rows(3 * lanes + units),
            whole_spec((1, units)),
        ],
        out_shape=[
            jax.ShapeDtypeStruct((step, width), F32),
            jax.ShapeDtypeStruct((step, width), LOW),
            jax.ShapeDtypeStruct((total, 3 * lanes + units), LOW),
            jax.ShapeDtypeStruct((1, units), F32),
        ],
        compiler_params=params(),
        name="upper_backward",
    )(d_rows, qkv, slope, w_in, w_out, w_down, rope, bias)


def exact_rows(hot, table):
    high = table.astype(LOW)
    rest = table - high.astype(F32)
    middle = rest.astype(LOW)
    lowest = (rest - middle.astype(F32)).astype(LOW)
    return mm(hot, high) + (mm(hot, middle) + mm(hot, lowest))


def first_forward(table, hot_own, hot_pack, rope_own, rope_pack, bias, packs):
    vocab = table.shape[0]
    width = table.shape[1] // 3
    pairs = width // LANES
    own_rows = hot_own.shape[0] // packs
    pack_rows = hot_pack.shape[0] // packs

    def kernel(tq_ref, tk_ref, tv_ref, hot_ref, hotp_ref, ro_ref, rp_ref, bias_ref, q_ref, k_ref, v_ref, att_ref):
        hot = hot_ref[...]
        hotp = hotp_ref[...]
        q = turn_by(exact_rows(hot, tq_ref[...]), ro_ref, 1.0).astype(LOW)
        k = turn_by(exact_rows(hotp, tk_ref[...]), rp_ref, 1.0).astype(LOW)
        v = mm(hotp, tv_ref[...].astype(LOW)).astype(LOW)
        q_ref[...] = q
        k_ref[...] = k
        v_ref[...] = v
        att_ref[...] = attend_pair(q, k, v, bias_ref[...])

    def table_spec(which):
        return pl.BlockSpec((vocab, LANES), lambda p, j: (0, which * pairs + j))

    def rows_spec(many, columns):
        return pl.BlockSpec((many, columns), lambda p, j: (p, 0))

    def rope_spec(many):
        return pl.BlockSpec((3, many, LANES), lambda p, j: (0, p, 0))

    def pair_spec(many):
        return pl.BlockSpec((many, LANES), lambda p, j: (p, j))

    owned, packed = (hot_own.shape[0], hot_pack.shape[0])
    return pl.pallas_call(
        kernel,
        grid=(packs, pairs),
        in_specs=[
            table_spec(0),
            table_spec(1),
            table_spec(2),
            rows_spec(own_rows, vocab),
            rows_spec(pack_rows, vocab),
            rope_spec(own_rows),
            rope_spec(pack_rows),
            rows_spec(own_rows, pack_rows),
        ],
        out_specs=[
            pair_spec(own_rows),
            pair_spec(pack_rows),
            pair_spec(pack_rows),
            pair_spec(own_rows),
        ],
        out_shape=[
            jax.ShapeDtypeStruct((owned, width), LOW),
            jax.ShapeDtypeStruct((packed, width), LOW),
            jax.ShapeDtypeStruct((packed, width), LOW),
            jax.ShapeDtypeStruct((owned, width), LOW),
        ],
        compiler_params=params(),
        name="first_forward",
    )(table, table, table, hot_own, hot_pack, rope_own, rope_pack, bias)


def cost(microseconds):
    return pl.CostEstimate(flops=max(1, int(microseconds * 1e9 * 1.0)), bytes_accessed=0, transcendentals=0)


def simple(kernel, name, outs, *args, smem=(), us=1.0, scratch=(), behind=(), limit=VMEM_LIMIT):
    specs = [
        pl.BlockSpec(memory_space=pltpu.SMEM) if i in smem else whole_spec(arg.shape)
        for i, arg in enumerate(args)
    ]
    many, unread = (len(args), len(behind))

    def run(*refs):
        kernel(*refs[:many], *refs[many + unread :])

    return pl.pallas_call(
        run,
        grid=(1,),
        in_specs=specs + [pl.BlockSpec(memory_space=pl.ANY)] * unread,
        out_specs=[whole_spec(shape) for shape, _ in outs],
        out_shape=[jax.ShapeDtypeStruct(shape, kind) for shape, kind in outs],
        scratch_shapes=list(scratch),
        compiler_params=params(limit),
        cost_estimate=cost(us),
        name=name,
    )(*args, *behind)


def first_finish(att, first_out, hot, stay, gain, bias):
    rows, width = att.shape

    def kernel(att_ref, out_ref, hot_ref, stay_ref, gain_ref, bias_ref, x_ref, h_ref):
        x = mm(att_ref[...], out_ref[...]) + exact_rows(hot_ref[...], stay_ref[...])
        x = x.astype(LOW)
        x_ref[...] = x
        h_ref[...] = layer_norm(x.astype(F32), gain_ref[...], bias_ref[...])[0].astype(LOW)

    outs = [((rows, width), LOW), ((rows, width), LOW)]
    return simple(kernel, "first_finish", outs, att, first_out, hot, stay, gain[None], bias[None])


def loss_forward(base, pieces, bias_down, gain, bias, head_low, out_bias, target_hot, seq_weight):
    rows, width = base.shape
    vocab = head_low.shape[0]
    seqs = seq_weight.shape[1]

    def kernel(x_ref, *refs):
        piece_refs = refs[: len(pieces)]
        down_ref, gain_ref, bias_ref, head_ref, hbias_ref, hot_ref, seq_ref = refs[len(pieces) : -5]
        norm_ref, inv_ref, final_ref, logp_ref, lik_ref = refs[-5:]
        x = x_ref[...].astype(F32)
        for ref in piece_refs:
            x = x + ref[...].astype(F32)
        out, normed, inverse = layer_norm(x + down_ref[...], gain_ref[...], bias_ref[...])
        norm_ref[...] = normed
        inv_ref[...] = inverse
        final = out.astype(LOW)
        final_ref[...] = final
        logits = mm_t(final, head_ref[...]) + hbias_ref[...]
        top = jnp.max(logits, -1, keepdims=True)
        logp = logits - (top + jnp.log(jnp.sum(jnp.exp(logits - top), -1, keepdims=True)))
        logp_ref[...] = logp
        picked = jnp.sum(hot_ref[...] * logp, 1, keepdims=True)
        lik_ref[...] = jnp.sum(seq_ref[...] * picked, 0, keepdims=True)

    outs = [
        ((rows, width), F32),
        ((rows, 1), F32),
        ((rows, width), LOW),
        ((rows, vocab), F32),
        ((1, seqs), F32),
    ]
    return simple(
        kernel,
        "loss_forward",
        outs,
        base,
        *pieces,
        bias_down[None],
        gain[None],
        bias[None],
        head_low,
        out_bias[None],
        target_hot,
        seq_weight,
    )


def loss_backward(sums, partners, place, normed, inverse, final_low, logp, head_low, gain, target_hot, seq_weight, plane):
    rows, width = normed.shape
    vocab = head_low.shape[0]
    seqs = seq_weight.shape[1]
    devices = sums.shape[0]
    total_seqs = plane * seqs

    def kernel(sums_ref, partner_ref, place_ref, norm_ref, inv_ref, final_ref, logp_ref, head_ref, gain_ref, hot_ref, seq_ref, dy_ref, low_ref, table_ref, bias_ref, down_ref, scalar_ref):
        got = sums_ref[...]
        row = lax.broadcasted_iota(jnp.int32, got.shape, 0)
        column = lax.broadcasted_iota(jnp.int32, got.shape, 1)
        owner = lax.rem(row, plane)
        is_sum = column < seqs
        is_count = (column >= seqs) & (row < plane)
        loss = -jnp.sum(jnp.where(is_sum, got, 0.0))
        count = jnp.sum(jnp.where(is_count, got, 0.0))

        def likelihood(device, number):
            here = owner == device
            amount = jnp.sum(jnp.where(here & is_count & (column == seqs + number), got, 0.0))
            amount = jnp.maximum(amount, 1.0)
            total = jnp.sum(jnp.where(here & (column == number), got, 0.0))
            return (total / amount, amount)

        coeff = jnp.zeros((rows, 1), F32)
        penalty = 0.0
        for number in range(seqs):
            mine, amount = likelihood(place_ref[0], number)
            partner = partner_ref[number]
            other, _ = likelihood(partner // seqs, lax.rem(partner, seqs))
            differ = mine - other
            penalty = penalty + 0.5 * differ * differ
            term = -1.0 / count + PENALTY * 2.0 * differ / total_seqs / amount
            coeff = coeff + seq_ref[:, number : number + 1] * term
        d_logits = (coeff * (hot_ref[...] - jnp.exp(logp_ref[...]))).astype(LOW)
        d_final = mm(d_logits, head_ref[...])
        normed = norm_ref[...]
        dy = norm_back(d_final, normed, inv_ref[...], gain_ref[...])
        dy_ref[...] = dy
        low = dy.astype(LOW)
        low_ref[...] = low
        table_ref[:vocab, :] = t_mm(d_logits, final_ref[...])
        table_ref[vocab : vocab + 1, :] = jnp.sum(d_final * normed, 0, keepdims=True)
        table_ref[vocab + 1 : vocab + 2, :] = jnp.sum(d_final, 0, keepdims=True)
        bias_ref[...] = jnp.sum(d_logits.astype(F32), 0, keepdims=True)
        down_ref[...] = jnp.sum(low.astype(F32), 0, keepdims=True)
        lane = lax.broadcasted_iota(jnp.int32, (1, LANES), 1)
        scalar_ref[...] = jnp.where(lane == 0, loss, jnp.where(lane == 1, count, penalty))

    outs = [
        ((rows, width), F32),
        ((rows, width), LOW),
        ((vocab + 2, width), F32),
        ((1, vocab), F32),
        ((1, width), F32),
        ((1, LANES), F32),
    ]
    return simple(
        kernel,
        "loss_backward",
        outs,
        sums,
        partners,
        place,
        normed,
        inverse,
        final_low,
        logp,
        head_low,
        gain[None],
        target_hot,
        seq_weight,
        smem=(1, 2),
    )


def input_backward(pieces, x_low, dy, gain, hot):
    rows, width = dy.shape
    vocab = hot.shape[1]

    def kernel(*refs):
        piece_refs = refs[: len(pieces)]
        x_ref, dy_ref, gain_ref, hot_ref, low_ref, vec_ref, token_ref = refs[len(pieces) :]
        d_norm = piece_refs[0][...]
        for ref in piece_refs[1:]:
            d_norm = d_norm + ref[...].astype(F32)
        gain_row = gain_ref[...]
        _, normed, inverse = layer_norm(x_ref[...].astype(F32), gain_row, 0.0)
        low = (dy_ref[...] + norm_back(d_norm, normed, inverse, gain_row)).astype(LOW)
        low_ref[...] = low
        vec_ref[0:1, :] = jnp.sum(d_norm * normed, 0, keepdims=True)
        vec_ref[1:2, :] = jnp.sum(d_norm, 0, keepdims=True)
        vec_ref[2:3, :] = jnp.sum(low.astype(F32), 0, keepdims=True)
        token_ref[...] = t_mm(hot_ref[...], low)

    outs = [((rows, width), LOW), ((3, width), F32), ((vocab, width), F32)]
    return simple(kernel, "input_backward", outs, *pieces, x_low, dy, gain[None], hot)


def first_backward(d_rows, query, keys, values, att, hot_own, hot_pack, rope_own, rope_pack, bias, first_out, packs):
    width = first_out.shape[0]
    vocab = hot_own.shape[1]
    pairs = width // LANES
    own_rows = hot_own.shape[0] // packs
    pack_rows = hot_pack.shape[0] // packs

    def kernel(d_ref, q_ref, k_ref, v_ref, att_ref, hot_ref, hotp_ref, ro_ref, rp_ref, bias_ref, out_ref, tq_ref, tk_ref, tv_ref, grad_ref):
        d_out = d_ref[...]
        d_att = mm_t(d_out, out_ref[...]).astype(LOW)
        dq, dk, dv = attend_pair_back(d_att, q_ref[...], k_ref[...], v_ref[...], bias_ref[...])
        dq = turn_by(dq, ro_ref, -1.0).astype(LOW)
        dk = turn_by(dk, rp_ref, -1.0).astype(LOW)
        hot = hot_ref[...]
        hotp = hotp_ref[...]
        parts = (t_mm(hot, dq), t_mm(hotp, dk), t_mm(hotp, dv.astype(LOW)), t_mm(att_ref[...], d_out))
        refs = (tq_ref, tk_ref, tv_ref, grad_ref)

        @pl.when(pl.program_id(1) == 0)
        def _():
            for ref, part in zip(refs, parts):
                ref[...] = part

        @pl.when(pl.program_id(1) > 0)
        def _():
            for ref, part in zip(refs, parts):
                ref[...] += part

    def rows_spec(many, columns):
        return pl.BlockSpec((many, columns), lambda j, p: (p, 0))

    def rope_spec(many):
        return pl.BlockSpec((3, many, LANES), lambda j, p: (0, p, 0))

    def pair_spec(many):
        return pl.BlockSpec((many, LANES), lambda j, p: (p, j))

    token_spec = pl.BlockSpec((vocab, LANES), lambda j, p: (0, j))
    return pl.pallas_call(
        kernel,
        grid=(pairs, packs),
        in_specs=[
            rows_spec(own_rows, width),
            pair_spec(own_rows),
            pair_spec(pack_rows),
            pair_spec(pack_rows),
            pair_spec(own_rows),
            rows_spec(own_rows, vocab),
            rows_spec(pack_rows, vocab),
            rope_spec(own_rows),
            rope_spec(pack_rows),
            rows_spec(own_rows, pack_rows),
            pl.BlockSpec((LANES, width), lambda j, p: (j, 0)),
        ],
        out_specs=[
            token_spec,
            token_spec,
            token_spec,
            pl.BlockSpec((LANES, width), lambda j, p: (j, 0)),
        ],
        out_shape=[
            jax.ShapeDtypeStruct((vocab, width), F32),
            jax.ShapeDtypeStruct((vocab, width), F32),
            jax.ShapeDtypeStruct((vocab, width), F32),
            jax.ShapeDtypeStruct((width, width), F32),
        ],
        compiler_params=params(),
        cost_estimate=cost(10.5),
        name="first_backward",
    )(d_rows, query, keys, values, att, hot_own, hot_pack, rope_own, rope_pack, bias, first_out)


def adam(weight, first, second, grad, rate, decay):
    first_new = BETA_ONE * first + (1.0 - BETA_ONE) * grad
    second_new = BETA_TWO * second + (1.0 - BETA_TWO) * grad * grad
    update = (
        first_new
        / (1.0 - BETA_ONE**STEP)
        / (jnp.sqrt(second_new / (1.0 - BETA_TWO**STEP)) + EPS_ADAM)
    )
    return (first_new, second_new, weight - rate * (update + decay * weight))


class Group:
    def __init__(self, sections, spans):
        self.sections = sections
        self.spans = spans
        self.offsets = [(dk, dy) for dk in range(2) for dy in range(sections)]

    def route(self, dk, dy, sign):
        s = self.sections
        return [
            (a * 2 + b, ((a + sign * dy) % s) * 2 + (b + sign * dk) % 2)
            for a in range(s)
            for b in range(2)
        ]

    def gather(self, value):
        pieces = []
        for dk, dy in self.offsets:
            piece = value
            if (dk, dy) != (0, 0):
                piece = lax.ppermute(value, ("y", "k"), self.route(dk, dy, 1))
            pieces.append(piece)
        mine = jnp.stack(pieces)
        return jnp.stack([mine, shift(mine, "c", 1)])

    def scatter(self, keep, send):
        mine = keep + shift(send, "c", 1).astype(F32)
        pieces = [mine[0]]
        for number, (dk, dy) in enumerate(self.offsets):
            if (dk, dy) != (0, 0):
                pieces.append(
                    lax.ppermute(mine[number].astype(LOW), ("y", "k"), self.route(dk, dy, -1))
                )
        return pieces


def across_gather(piece, x, first, second, last):
    spans = lax.axis_size("h")
    h = lax.axis_index("h")
    piece = after(piece, first)
    if spans == 2:
        both = ordered(piece, after(shift(piece, "h", 1), second), h, 0)
    else:
        stacked = jnp.stack([piece] + [shift(piece, "h", s) for s in range(1, spans)])
        both = jnp.take(stacked, (h - jnp.arange(spans)) % spans, axis=0)
    return ordered(both, after(shift(both, "x", 1), last), x, 1)


def across_scatter(parts, x, first, second, last):
    spans = lax.axis_size("h")
    h = lax.axis_index("h")
    flipped = jnp.swapaxes(parts, 0, 1)
    away = shift(after(pick(flipped, 1 - x).astype(LOW), first), "x", 1)
    mine = pick(flipped, x) + after(away, second).astype(F32)
    total = pick(mine, h)
    for s in range(1, spans):
        away = shift(pick(mine, (h + s) % spans).astype(LOW), "h", s)
        total = total + after(away, last).astype(F32)
    return total


def scalars_of(*values):
    return jnp.stack([jnp.asarray(v, jnp.int32) for v in values])


def flip(value, axes, bits):
    mask = 0
    for bit in bits:
        mask = 2 * mask + bit
    many = 2 ** len(bits)
    return lax.ppermute(value, axes, [(i, i ^ mask) for i in range(many)])


NEAR = [(0, 1), (1, 0), (1, 1)]
def fast_loss_forward(base, pieces, vec, low_tables, out_bias, target_hot, seq_weight, seq_count):
    rows, width = base.shape
    vocab = target_hot.shape[1]

    def kernel(x_ref, p0, p1, p2, p3, vec_ref, low_ref, hbias_ref, hot_ref, seq_ref, count_ref, norm_ref, inv_ref, final_ref, logp_ref, sums_ref):
        x = x_ref[...].astype(F32) + p0[...]
        x = x + p1[...].astype(F32) + p2[...].astype(F32) + p3[...].astype(F32)
        gain = low_ref[2 * vocab : 2 * vocab + 1, :].astype(F32)
        bias = low_ref[2 * vocab + 1 : 2 * vocab + 2, :].astype(F32)
        out, normed, inverse = layer_norm(x + vec_ref[1:2, 2 * width : 3 * width], gain, bias)
        norm_ref[...] = normed
        inv_ref[...] = inverse
        final = out.astype(LOW)
        final_ref[...] = final
        logits = mm_t(final, low_ref[vocab : 2 * vocab, :]) + hbias_ref[...].astype(LOW).astype(F32)
        top = jnp.max(logits, -1, keepdims=True)
        logp = logits - (top + jnp.log(jnp.sum(jnp.exp(logits - top), -1, keepdims=True)))
        logp_ref[...] = logp
        picked = jnp.sum(hot_ref[...] * logp, 1, keepdims=True)
        row = jnp.sum(seq_ref[...] * picked, 0, keepdims=True)
        counts = count_ref[...]
        line = lax.broadcasted_iota(jnp.int32, counts.shape, 0)
        lane = lax.broadcasted_iota(jnp.int32, counts.shape, 1)
        seqs = counts.shape[0]
        row = row + jnp.sum(jnp.where(lane == line + seqs, counts, 0.0), 0, keepdims=True)
        sums_ref[...] = row

    outs = [
        ((rows, width), F32),
        ((rows, 1), F32),
        ((rows, width), LOW),
        ((rows, vocab), F32),
        ((1, LANES), F32),
    ]
    return simple(
        kernel,
        "loss_forward",
        outs,
        base,
        *pieces,
        vec,
        low_tables,
        out_bias[None],
        target_hot,
        seq_weight,
        seq_count,
    )


def fast_loss_backward(sums, partners, place, normed, inverse, final_low, logp, low_tables, target_hot, seq_weight, plane, seqs):
    rows, width = normed.shape
    vocab = target_hot.shape[1]
    total_seqs = plane * seqs

    def kernel(sums_ref, partner_ref, place_ref, norm_ref, inv_ref, final_ref, logp_ref, low_ref, hot_ref, seq_ref, dy_ref, low_out_ref, table_ref, ends_ref, bias_ref, down_ref, scalar_ref):
        got = sums_ref[...]
        row = lax.broadcasted_iota(jnp.int32, got.shape, 0)
        column = lax.broadcasted_iota(jnp.int32, got.shape, 1)
        owner = lax.rem(row, plane)
        is_sum = column < seqs
        is_count = (column >= seqs) & (column < 2 * seqs) & (row < plane)
        loss = -jnp.sum(jnp.where(is_sum, got, 0.0))
        count = jnp.sum(jnp.where(is_count, got, 0.0))

        def likelihood(device, number):
            here = owner == device
            amount = jnp.sum(jnp.where(here & is_count & (column == seqs + number), got, 0.0))
            amount = jnp.maximum(amount, 1.0)
            total = jnp.sum(jnp.where(here & (column == number), got, 0.0))
            return (total / amount, amount)

        coeff = jnp.zeros((rows, 1), F32)
        penalty = 0.0
        for number in range(seqs):
            mine, amount = likelihood(place_ref[5], number)
            partner = partner_ref[number]
            other, _ = likelihood(partner // seqs, lax.rem(partner, seqs))
            differ = mine - other
            penalty = penalty + 0.5 * differ * differ
            term = -1.0 / count + PENALTY * 2.0 * differ / total_seqs / amount
            coeff = coeff + seq_ref[:, number : number + 1] * term
        d_logits = (coeff * (hot_ref[...] - jnp.exp(logp_ref[...]))).astype(LOW)
        d_final = mm(d_logits, low_ref[vocab : 2 * vocab, :])
        normed = norm_ref[...]
        gain = low_ref[2 * vocab : 2 * vocab + 1, :].astype(F32)
        dy = norm_back(d_final, normed, inv_ref[...], gain)
        dy_ref[...] = dy
        low = dy.astype(LOW)
        low_out_ref[...] = low
        line = lax.broadcasted_iota(jnp.int32, (8, width), 0)
        ends = jnp.where(
            line == 0,
            jnp.sum(d_final * normed, 0, keepdims=True),
            jnp.where(line == 1, jnp.sum(d_final, 0, keepdims=True), 0.0),
        )
        ends_ref[...] = ends
        grads = jnp.concatenate(
            [t_mm(d_logits, final_ref[...]), jnp.zeros((LANES - vocab, width), F32)], 0
        )
        table_ref[...] = grads.T
        bias_ref[...] = jnp.sum(d_logits.astype(F32), 0, keepdims=True)
        down_ref[...] = jnp.sum(low.astype(F32), 0, keepdims=True)
        lane = lax.broadcasted_iota(jnp.int32, (1, LANES), 1)
        scalar_ref[...] = jnp.where(lane == 0, loss, jnp.where(lane == 1, count, penalty))

    outs = [
        ((rows, width), F32),
        ((rows, width), LOW),
        ((width, LANES), F32),
        ((8, width), F32),
        ((1, vocab), F32),
        ((1, width), F32),
        ((1, LANES), F32),
    ]
    return simple(
        kernel,
        "loss_backward",
        outs,
        sums,
        partners,
        place,
        normed,
        inverse,
        final_low,
        logp,
        low_tables,
        target_hot,
        seq_weight,
        smem=(1, 2),
    )


def rope_constant(slots):
    half = ROT // 2
    freq = np.float32(10000.0) ** (np.float32(-2.0) * np.arange(half, dtype=np.float32) / ROT)
    angle = np.arange(slots, dtype=np.float32)[:, None] * freq.astype(np.float32)
    cosine = np.cos(angle.astype(np.float64)).astype(np.float32)
    sine = np.sin(angle.astype(np.float64)).astype(np.float32)
    none, one = (np.zeros_like(sine), np.ones_like(sine))
    many = LANES // HEAD
    rest = HEAD // half - 2
    return np.stack(
        [
            np.concatenate(([cosine, cosine] + [one] * rest) * many, 1),
            np.concatenate(([-sine, none] + [none] * rest) * many, 1),
            np.concatenate(([none, sine] + [none] * rest) * many, 1),
        ]
    )


TOKEN_ROW = 36
VECTOR_ROW = 12
SHARD = 7 * LANES
MIXED = 4 * LANES
ROWS = 48
FLIPS = [(0, 0), (0, 1), (1, 0), (1, 1)]
CUBE = [(dy, dk, dc) for dy in range(2) for dk, dc in FLIPS]


def cube_flips(pieces):
    return [pieces[0]] + [
        flip(piece, ("y", "k", "c"), bits) for piece, bits in zip(pieces[1:], CUBE[1:])
    ]


def cube_number(place_ref, bits):
    y, k, c = (place_ref[axis] for axis in (0, 2, 4))
    return ((y + bits[0]) % 2 * 2 + (k + bits[1]) % 2) * 2 + (c + bits[2]) % 2


def row_spots(number):
    spots = []
    done = 0
    while done < ROWS:
        at = number * ROWS + done
        many = min(ROWS - done, 64 - at % 64)
        spots.append((done, many, at // 64, at % 64))
        done += many
    return spots


def cut_first(tables, vectors, tokens, lengths, down, out, place):
    features, table_rows = tables.shape
    chunk = vectors.shape[1]
    own_ff, width = down.shape
    part = own_ff // 2
    some = out.shape[0] // 2
    packs, per_pack = lengths.shape

    def kernel(tab_ref, vec_ref, tok_ref, len_ref, down_ref, out_ref, place_ref, rows_ref, keep_ref, send_ref, one_ref, two_ref):
        y = place_ref[0]
        table = jnp.concatenate(
            [tab_ref[...], jnp.zeros((features, LANES - table_rows), F32)], 1
        )
        rows_ref[:features, :] = table.astype(LOW)
        rest = chunk - 3 * LANES
        ends = jnp.concatenate(
            [vec_ref[:, 3 * LANES :], jnp.zeros((1, LANES - rest), F32)], 1
        )
        sizes = [len_ref[p : p + 1, :].astype(F32) for p in range(packs)]
        sizes = jnp.concatenate(sizes + [jnp.zeros((1, LANES - packs * per_pack), F32)], 1)
        lines = [vec_ref[:, j * LANES : (j + 1) * LANES] for j in range(3)] + [ends]
        lines = lines + [tok_ref[p : p + 1, :].astype(F32) for p in range(packs)] + [sizes]
        line = lax.broadcasted_iota(jnp.int32, (16, LANES), 0)
        tail = jnp.zeros((16, LANES), F32)
        for number, value in enumerate(lines):
            tail = jnp.where(line == number, value, tail)
        rows_ref[features:, :] = tail.astype(LOW)
        keep_ref[...] = down_ref[pl.ds(pl.multiple_of(y * part, part), part), :].astype(LOW)
        send_ref[...] = down_ref[pl.ds(pl.multiple_of((1 - y) * part, part), part), :].astype(LOW)
        one_ref[...] = out_ref[pl.ds(pl.multiple_of(y * some, some), some), :].astype(LOW)
        two_ref[...] = out_ref[pl.ds(pl.multiple_of((1 - y) * some, some), some), :].astype(LOW)

    outs = [((ROWS, LANES), LOW)] + [((part, width), LOW)] * 2 + [((some, width), LOW)] * 2
    args = (tables, vectors, tokens, lengths, down, out, place)
    return simple(kernel, "cut_first", outs, *args, smem=(6,), limit=VMEM_MOST)


def cut_weights(qkv, up, rows, behind):
    own_in, width = (qkv.shape[0], up.shape[1] // 4)
    own_ff = width // 4
    part = own_ff // 2

    def kernel(qkv_ref, up_ref, r0, r1, r2, r3, shard_ref):
        for dest in range(8):
            yy, kk, cc = dest >> 2, dest >> 1 & 1, dest & 1
            start = ((cc * 2 + kk) * 2 + yy) * LANES
            for j in range(3):
                shard_ref[dest, :, j * LANES : (j + 1) * LANES] = qkv_ref[
                    :, j * width + start : j * width + start + LANES
                ].astype(LOW)
            for j in range(4):
                start = (j // 2 * 8 + kk * 4 + j % 2 * 2 + cc) * own_ff + yy * part
                shard_ref[dest, :, (3 + j) * LANES : (4 + j) * LANES] = up_ref[
                    :, start : start + part
                ].astype(LOW)
        for number, ref in enumerate((r0, r1, r2, r3)):
            for row, many, tile, at in row_spots(number):
                value = ref[row : row + many, :]
                start = SHARD + tile * LANES
                for dest in range(8):
                    shard_ref[dest, at : at + many, start : start + LANES] = value

    outs = [((8, own_in, SHARD + 3 * LANES), LOW)]
    return simple(kernel, "cut_weights", outs, qkv, up, *rows, behind=behind)[0]


def unpack_rows(shards, place):
    def kernel(shard_ref, place_ref, rows_ref):
        h, x = place_ref[1], place_ref[3]
        for source in range(8):
            yy, kk, cc = source >> 2, source >> 1 & 1, source & 1
            for number, (dh, dx) in enumerate(FLIPS):
                device = (((yy * 2 + (h + dh) % 2) * 2 + kk) * 2 + (x + dx) % 2) * 2 + cc
                for row, many, tile, at in row_spots(number):
                    start = SHARD + tile * LANES
                    rows_ref[device, row : row + many, :] = shard_ref[
                        source, at : at + many, start : start + LANES
                    ]

    return simple(kernel, "unpack_rows", [((32, ROWS, LANES), LOW)], shards, place, smem=(1,))[0]


def slot_tables(tables, counted, place, rope_of_position, behind):
    slots = counted.shape[1]
    per_pack = 4
    seqs = 2 * per_pack
    packs = 8

    def kernel(tab_ref, count_ref, place_ref, table_ref, bias_ref, rope_ref, hot_ref, target_ref, seqw_ref, seqc_ref):
        y, h, k, x, c = (place_ref[j] for j in range(5))
        row = lax.broadcasted_iota(jnp.int32, (slots, slots), 0)
        column = lax.broadcasted_iota(jnp.int32, (slots, slots), 1)
        lane = lax.broadcasted_iota(jnp.int32, (1, slots), 1)

        def ends_of(lengths, pack):
            first = pack * per_pack
            return [
                jnp.sum(
                    jnp.where((lane >= first) & (lane <= first + j), lengths, 0.0), 1, keepdims=True
                )
                for j in range(per_pack)
            ]

        def segments(ends, index):
            number = jnp.zeros(index.shape, jnp.int32)
            for end in ends:
                number = number + (index.astype(F32) >= end).astype(jnp.int32)
            return number

        for block in range(4):
            dc, dk = FLIPS[block]
            device = ((h * 2 + (k + dk) % 2) * 2 + x) * 2 + (c + dc) % 2
            lines = tab_ref[device, TOKEN_ROW : TOKEN_ROW + 4, :].astype(F32)
            lengths = lines[2:3]
            for dy in range(2):
                pack = lax.rem(y + dy, 2)
                here = pl.ds((block * 2 + dy) * slots, slots)
                ends = ends_of(lengths, pack)
                by_row, by_column = segments(ends, row), segments(ends, column)
                seen = (by_row == by_column) & (column <= row)
                bias_ref[here, :] = jnp.where(seen, 0.0, -1e30)
                start = jnp.zeros((slots, slots), F32)
                for j in range(1, per_pack):
                    start = jnp.where(by_row == j, ends[j - 1], start)
                position = row.astype(F32) - start
                hot = jnp.where(column.astype(F32) == position, 1.0, 0.0).astype(LOW)
                for part in range(3):
                    rope_ref[part, here, :] = exact_rows(hot, table_ref[part])
                token = jnp.where(pack == 0, lines[0:1], lines[1:2])
                hot = jnp.where(row.astype(F32) == token, 1.0, 0.0)
                hot_ref[here, :] = hot.T[:, : hot_ref.shape[1]].astype(LOW)
        lines = tab_ref[((h * 2 + k) * 2 + x) * 2 + c, TOKEN_ROW : TOKEN_ROW + 4, :].astype(F32)
        counts = jnp.zeros((seqs, slots), F32)
        seq_line = lax.broadcasted_iota(jnp.int32, (seqs, slots), 0)
        for pack in range(2):
            number = segments(ends_of(lines[2:3], pack), lane)
            following = pltpu.roll(number.astype(F32), slots - 1, 1)
            same = (following == number.astype(F32)) & (lane < slots - 1)
            weight = jnp.where(same & (count_ref[pack : pack + 1, :] == 1), 1.0, 0.0)
            by_seq = jnp.where(seq_line == number + pack * per_pack, weight, 0.0)
            counts = counts + by_seq

            @pl.when(pack == y)
            def _():
                target = pltpu.roll(lines[pack : pack + 1], slots - 1, 1)
                hot = jnp.where(row.astype(F32) == target, 1.0, 0.0)
                target_ref[...] = hot.T[:, : target_ref.shape[1]]
                padded = jnp.concatenate([by_seq, jnp.zeros((slots - seqs, slots), F32)], 0)
                seqw_ref[...] = padded.T

        seqc_ref[...] = jnp.broadcast_to(jnp.sum(counts, 1, keepdims=True), (seqs, LANES))

    outs = [
        ((packs * slots, slots), F32),
        ((3, packs * slots, LANES), F32),
        ((packs * slots, 32), LOW),
        ((slots, 32), F32),
        ((slots, LANES), F32),
        ((seqs, LANES), F32),
    ]
    args = (tables, counted, place, rope_of_position)
    return simple(kernel, "slot_tables", outs, *args, smem=(2,), us=2.0, behind=behind)


def token_products(tables, weights, place):
    vocab = 32
    devices, _, lanes = tables.shape
    width = devices * vocab
    own_in, columns = weights.shape[1], SHARD
    total = devices // 2 * 448

    def kernel(tab_ref, w_ref, place_ref, low_ref, vec_ref, h_ref, norm_ref, inv_ref, part_ref):
        h, x = place_ref[1], place_ref[3]
        flat = tab_ref[:, :vocab, :].astype(F32).reshape(width, lanes).T
        low_ref[...] = flat.astype(LOW)
        first_half = lax.broadcasted_iota(jnp.int32, (1, LANES), 1) < LANES // 2
        for pair in range(devices // 2):
            line, at = pair // (devices // 4), pair % (devices // 4) * 7 * LANES
            even = tab_ref[2 * pair, vocab : vocab + 4, :].astype(F32)
            odd = pltpu.roll(tab_ref[2 * pair + 1, vocab : vocab + 4, :].astype(F32), LANES // 2, 1)
            for q in range(7):
                if q < 3:
                    value = even[q : q + 1]
                elif q == 3:
                    value = jnp.where(first_half, even[3:4], odd[0:1])
                else:
                    value = jnp.where(first_half, odd[q - 4 : q - 3], odd[q - 3 : q - 2])
                vec_ref[line : line + 1, at + q * LANES : at + (q + 1) * LANES] = value
        out, normed, inverse = layer_norm(
            flat[:vocab], vec_ref[0:1, :width], vec_ref[0:1, width : 2 * width]
        )
        norm_ref[...] = normed
        inv_ref[...] = inverse
        h_ref[...] = out.astype(LOW)
        rows = 2 * own_in
        sums = jnp.zeros((vocab, columns), F32)
        for kk in range(2):
            start = pl.multiple_of(((h * 2 + kk) * 2 + x) * rows, LANES)
            block = w_ref[2 * kk : 2 * kk + 2, :, :columns].reshape(rows, columns)
            sums = sums + mm(h_ref[:, pl.ds(start, rows)], block)
        part_ref[...] = sums

    outs = [
        ((lanes, width), LOW),
        ((2, total), F32),
        ((vocab, width), LOW),
        ((vocab, width), F32),
        ((vocab, 1), F32),
        ((vocab, columns), F32),
    ]
    return simple(kernel, "token_products", outs, tables, weights, place, smem=(2,))


def first_rows(down_keep, down_far, out_one, out_two, place):
    part, width = down_keep.shape
    some = out_one.shape[0]

    def kernel(keep_ref, far_ref, one_ref, two_ref, place_ref, rows_ref):
        y, x = place_ref[0], place_ref[3]
        rows_ref[:part, :] = jnp.where(y == 0, keep_ref[...], far_ref[...])
        rows_ref[part:, :] = jnp.where(x == 0, one_ref[...], two_ref[...])

    outs = [((part + some, width), LOW)]
    args = (down_keep, down_far, out_one, out_two, place)
    return simple(kernel, "first_rows", outs, *args, smem=(4,))[0]


def upper_rows(weights, down_keep, down_far, out_one, out_two, place):
    part, width = down_keep.shape
    some = out_one.shape[0]
    own_in, columns = weights.shape[1], SHARD

    def kernel(w_ref, keep_ref, far_ref, one_ref, two_ref, place_ref, *piece_refs):
        y, x = place_ref[0], place_ref[3]
        for j in range(4):
            ref = piece_refs[j // 2]
            ref[j % 2 * own_in : (j % 2 + 1) * own_in, :columns] = w_ref[4 + j, :, :columns]
        out = jnp.where(x == 0, two_ref[...], one_ref[...])
        for j in range(8):
            ref = piece_refs[j // 4]
            here = slice(j % 4 * some, (j % 4 + 1) * some)
            ref[here, columns:] = out[:, j * LANES : (j + 1) * LANES]
        piece_refs[2][...] = jnp.where(y == 0, far_ref[...], keep_ref[...])

    outs = [((part, width), LOW)] * 3
    args = (weights, down_keep, down_far, out_one, out_two, place)
    return simple(kernel, "upper_rows", outs, *args, smem=(5,))


def across(value):
    far = flip(value, ("h",), (1,))
    return [value, flip(value, ("x",), (1,)), far, flip(far, ("x",), (1,))]


def group_pieces(value):
    near = [value] + [flip(value, ("y", "k"), (dy, dk)) for dk, dy in NEAR]
    return near + [flip(piece, ("c",), (1,)) for piece in near]


def group_sums(keep, send, behind=()):
    got = flip(send, ("c",), (1,))
    rows, width = (keep.shape[0] // 4, keep.shape[1])

    def kernel(keep_ref, got_ref, *refs):
        for j, ref in enumerate(refs):
            here = slice(j * rows, (j + 1) * rows)
            ref[...] = (keep_ref[here, :] + got_ref[here, :].astype(F32)).astype(ref.dtype)

    outs = [((rows, width), F32)] + [((rows, width), LOW)] * 3
    mine = simple(kernel, "group_sums", outs, keep, got, behind=behind)
    return [mine[0]] + [flip(piece, ("y", "k"), (dy, dk)) for piece, (dk, dy) in zip(mine[1:], NEAR)]


def block_of(place_ref, number):
    dh, dx = FLIPS[number]
    return (place_ref[1] + dh) % 2 * 2 + (place_ref[3] + dx) % 2


def first_group_forward(parts, tails, vec, place, hot, rope, bias, behind):
    vocab, columns = parts[0].shape
    total, slots = bias.shape
    tail_rows, width = tails[0].shape
    part = LANES
    some = tail_rows - part
    units = 4 * part
    step = total // 2

    def kernel(*refs):
        refs = refs[:11] + refs[11 + len(behind) :]
        part_refs, tail_refs = refs[:2], refs[2:6]
        vec_ref, place_ref, hot_ref, rope_ref, bias_ref = refs[6:11]
        keep_ref, send_ref, qkv_ref, att_ref, act_ref, slope_ref, wout_ref, wdown_ref = refs[11:19]
        table_ref, ffn_ref = refs[19:]
        first = pl.program_id(0) == 0

        @pl.when(first)
        def _():
            for number, ref in enumerate(tail_refs):
                block = block_of(place_ref, number)
                wdown_ref[pl.ds(pl.multiple_of(block * part, part), part), :] = ref[:part, :]
                wout_ref[pl.ds(pl.multiple_of(block * some, some), some), :] = ref[part:, :]
            sums = part_refs[0][...] + part_refs[1][...]
            table_ref[...] = sums[:, : 3 * LANES]
            y, k, c = place_ref[0], place_ref[2], place_ref[4]
            bias_up = jnp.concatenate(
                [
                    vec_ref[0:1, pl.ds(unit_start(width, j, y, k, c, part), part)]
                    for j in range(4)
                ],
                1,
            )
            act, slope = gelu_pair(sums[:, 3 * LANES :] + bias_up)
            act = act.astype(LOW)
            act_ref[...] = act
            slope_ref[...] = slope
            ffn_ref[...] = mm(act, wdown_ref[...])

        for pack in range(step // slots):
            here = slice(pack * slots, (pack + 1) * slots)
            hot_here = hot_ref[here, :]
            rope_here = [rope_ref[j, here, :] for j in range(3)]
            q = turn_by(exact_rows(hot_here, table_ref[:, :LANES]), rope_here, 1.0).astype(LOW)
            k = turn_by(
                exact_rows(hot_here, table_ref[:, LANES : 2 * LANES]), rope_here, 1.0
            ).astype(LOW)
            v = mm(hot_here, table_ref[:, 2 * LANES :].astype(LOW)).astype(LOW)
            qkv_ref[here, :LANES] = q
            qkv_ref[here, LANES : 2 * LANES] = k
            qkv_ref[here, 2 * LANES :] = v
            att_ref[here, :] = attend_pair(q, k, v, bias_ref[here, :])
        out = mm(att_ref[...], wout_ref[...]) + exact_rows(hot_ref[...], ffn_ref[...])

        @pl.when(first)
        def _():
            send_ref[...] = out.astype(LOW)

        @pl.when(jnp.logical_not(first))
        def _():
            keep_ref[...] = out

    def by_rows(columns):
        return pl.BlockSpec((step, columns), lambda s: (1 - s, 0))

    args = (*parts, *tails, vec)
    return pl.pallas_call(
        kernel,
        grid=(2,),
        in_specs=[whole_spec(arg.shape) for arg in args]
        + [
            pl.BlockSpec(memory_space=pltpu.SMEM),
            by_rows(vocab),
            pl.BlockSpec((3, step, LANES), lambda s: (0, 1 - s, 0)),
            by_rows(slots),
        ]
        + [pl.BlockSpec(memory_space=pl.ANY)] * len(behind),
        out_specs=[
            whole_spec((step, width)),
            whole_spec((step, width)),
            by_rows(3 * LANES),
            by_rows(LANES),
            whole_spec((vocab, units)),
            whole_spec((vocab, units)),
            whole_spec((4 * some, width)),
            whole_spec((units, width)),
        ],
        out_shape=[
            jax.ShapeDtypeStruct((step, width), F32),
            jax.ShapeDtypeStruct((step, width), LOW),
            jax.ShapeDtypeStruct((total, 3 * LANES), LOW),
            jax.ShapeDtypeStruct((total, LANES), LOW),
            jax.ShapeDtypeStruct((vocab, units), LOW),
            jax.ShapeDtypeStruct((vocab, units), F32),
            jax.ShapeDtypeStruct((4 * some, width), LOW),
            jax.ShapeDtypeStruct((units, width), LOW),
        ],
        scratch_shapes=[pltpu.VMEM((vocab, 3 * LANES), F32), pltpu.VMEM((vocab, width), F32)],
        compiler_params=params(),
        cost_estimate=cost(9),
        name="first_group_forward",
    )(*args, place, hot, rope, bias, *behind)


def unit_start(width, j, y, k, c, part):
    unit = (j // 2 * 8 + k * 4 + j % 2 * 2 + c) * 2 * part + y * part
    return pl.multiple_of(3 * width + unit, LANES)


def first_finish_rows(pieces, hot, low_tables, vec, behind):
    rows, width = pieces[0].shape
    vocab = hot.shape[1]

    def kernel(p0, p1, p2, p3, hot_ref, low_ref, vec_ref, x_ref, h_ref):
        stay = low_ref[:vocab, :].astype(F32) + vec_ref[0:1, 2 * width : 3 * width]
        x = exact_rows(hot_ref[:rows, :], stay) + p0[...]
        x = x + p1[...].astype(F32) + p2[...].astype(F32) + p3[...].astype(F32)
        x = x.astype(LOW)
        x_ref[...] = x
        h_ref[...] = layer_norm(
            x.astype(F32), vec_ref[1:2, :width], vec_ref[1:2, width : 2 * width]
        )[0].astype(LOW)

    outs = [((rows, width), LOW), ((rows, width), LOW)]
    return simple(kernel, "first_finish", outs, *pieces, hot, low_tables, vec, behind=behind)


def group_forward(pieces, shards, vec, place, rope, bias):
    slots, width = pieces[0].shape
    total = slots * len(pieces)
    step = total // 2
    part = LANES
    units, columns = 4 * part, 7 * LANES
    some = part // 4

    def kernel(*refs):
        piece_refs, shard_refs = refs[:8], refs[8:20]
        vec_ref, place_ref, rope_ref, bias_ref = refs[20:24]
        keep_ref, send_ref, h_ref, qkv_ref, att_ref, act_ref, slope_ref = refs[24:31]
        win_ref, wout_ref, wdown_ref = refs[31:]
        half = 1 - pl.program_id(0)

        @pl.when(half == 1)
        def _():
            for number in range(4):
                three = shard_refs[3 * number : 3 * number + 3]
                block = block_of(place_ref, number)
                for kk in range(2):
                    start = (block // 2 * 4 + kk * 2 + block % 2) * part
                    here = pl.ds(pl.multiple_of(start, part), part)
                    win_ref[here, :] = three[kk][:, :columns]
                here = pl.ds(pl.multiple_of(block * some, some), some)
                for j in range(8):
                    there = slice(j % 4 * some, (j % 4 + 1) * some)
                    wout_ref[here, j * LANES : (j + 1) * LANES] = three[j // 4][there, columns:]
                here = pl.ds(pl.multiple_of(block * part, part), part)
                wdown_ref[here, :] = three[2][...]

        for s in range(2):

            @pl.when(half == s)
            def _():
                for j in range(4):
                    h_ref[j * slots : (j + 1) * slots, :] = piece_refs[4 * s + j][...]

        h = h_ref[...]
        proj = mm(h, win_ref[:, : 3 * LANES])
        spans = [slice(j * LANES, (j + 1) * LANES) for j in range(3)]
        qkv_ref[:, spans[0]] = turn_by(proj[:, spans[0]], rope_ref, 1.0).astype(LOW)
        qkv_ref[:, spans[1]] = turn_by(proj[:, spans[1]], rope_ref, 1.0).astype(LOW)
        qkv_ref[:, spans[2]] = proj[:, spans[2]].astype(LOW)
        for pack in range(step // slots):
            here = slice(pack * slots, (pack + 1) * slots)
            q, k, v = (qkv_ref[here, spans[j]] for j in range(3))
            att_ref[here, :] = attend_pair(q, k, v, bias_ref[here, :])
        y, k, c = place_ref[0], place_ref[2], place_ref[4]
        bias_up = jnp.concatenate(
            [vec_ref[1:2, pl.ds(unit_start(width, j, y, k, c, part), part)] for j in range(4)], 1
        )
        act, slope = gelu_pair(mm(h, win_ref[:, 3 * LANES :]) + bias_up)
        act = act.astype(LOW)
        act_ref[...] = act
        slope_ref[...] = slope
        out = mm(att_ref[...], wout_ref[...]) + mm(act, wdown_ref[...])

        @pl.when(half == 1)
        def _():
            send_ref[...] = out.astype(LOW)

        @pl.when(half == 0)
        def _():
            keep_ref[...] = out

    def by_rows(columns):
        return pl.BlockSpec((step, columns), lambda s: (1 - s, 0))

    args = (*pieces, *shards, vec)
    shapes = [
        ((step, width), F32),
        ((step, width), LOW),
        ((total, width), LOW),
        ((total, 3 * LANES), LOW),
        ((total, LANES), LOW),
        ((total, units), LOW),
        ((total, units), F32),
        ((width, columns), LOW),
        ((LANES, width), LOW),
        ((units, width), LOW),
    ]
    return pl.pallas_call(
        kernel,
        grid=(2,),
        in_specs=[whole_spec(arg.shape) for arg in args]
        + [
            pl.BlockSpec(memory_space=pltpu.SMEM),
            pl.BlockSpec((3, step, LANES), lambda s: (0, 1 - s, 0)),
            by_rows(slots),
        ],
        out_specs=[
            whole_spec(shape) if number < 2 or number > 6 else by_rows(shape[1])
            for number, (shape, _) in enumerate(shapes)
        ],
        out_shape=[jax.ShapeDtypeStruct(shape, kind) for shape, kind in shapes],
        compiler_params=params(),
        cost_estimate=cost(12.5),
        name="group_forward",
    )(*args, place, rope, bias)


def group_backward(pieces, qkv, slope, w_in, w_out, w_down, rope, bias):
    slots, width = pieces[0].shape
    total = slots * len(pieces)
    units = w_down.shape[0]
    step = total // 2

    def kernel(*refs):
        piece_refs = refs[:8]
        win_ref, wout_ref, wdown_ref, qkv_ref, slope_ref, rope_ref, bias_ref = refs[8:15]
        keep_ref, send_ref, d_ref, din_ref, sum_ref = refs[15:]
        half = 1 - pl.program_id(0)
        for s in range(2):

            @pl.when(half == s)
            def _():
                for j in range(4):
                    d_ref[j * slots : (j + 1) * slots, :] = piece_refs[4 * s + j][...]

        d_out = d_ref[...]
        d_att = mm_t(d_out, wout_ref[...]).astype(LOW)
        d_pre = (mm_t(d_out, wdown_ref[...]) * slope_ref[...]).astype(LOW)
        din_ref[:, 3 * LANES :] = d_pre
        sums = jnp.sum(d_pre.astype(F32), 0, keepdims=True)
        spans = [slice(j * LANES, (j + 1) * LANES) for j in range(3)]
        for pack in range(step // slots):
            here = slice(pack * slots, (pack + 1) * slots)
            q, k, v = (qkv_ref[here, spans[j]] for j in range(3))
            dq, dk, dv = attend_pair_back(d_att[here, :], q, k, v, bias_ref[here, :])
            turned = [rope_ref[j, here, :] for j in range(3)]
            din_ref[here, spans[0]] = turn_by(dq, turned, -1.0).astype(LOW)
            din_ref[here, spans[1]] = turn_by(dk, turned, -1.0).astype(LOW)
            din_ref[here, spans[2]] = dv.astype(LOW)
        d_norm = mm_t(din_ref[...], win_ref[...])

        @pl.when(half == 1)
        def _():
            send_ref[...] = d_norm.astype(LOW)
            sum_ref[...] = sums

        @pl.when(half == 0)
        def _():
            keep_ref[...] = d_norm
            sum_ref[...] += sums

    def by_rows(columns):
        return pl.BlockSpec((step, columns), lambda s: (1 - s, 0))

    args = (*pieces, w_in, w_out, w_down)
    return pl.pallas_call(
        kernel,
        grid=(2,),
        in_specs=[whole_spec(arg.shape) for arg in args]
        + [
            by_rows(3 * LANES),
            by_rows(units),
            pl.BlockSpec((3, step, LANES), lambda s: (0, 1 - s, 0)),
            by_rows(slots),
        ],
        out_specs=[
            whole_spec((step, width)),
            whole_spec((step, width)),
            by_rows(width),
            by_rows(3 * LANES + units),
            whole_spec((1, units)),
        ],
        out_shape=[
            jax.ShapeDtypeStruct((step, width), F32),
            jax.ShapeDtypeStruct((step, width), LOW),
            jax.ShapeDtypeStruct((total, width), LOW),
            jax.ShapeDtypeStruct((total, 3 * LANES + units), LOW),
            jax.ShapeDtypeStruct((1, units), F32),
        ],
        compiler_params=params(),
        cost_estimate=cost(13.4),
        name="group_backward",
    )(*args, qkv, slope, rope, bias)


def weight_gradients(hs, d_in, act, att, d_rows, place):
    width = hs.shape[1]
    columns = d_in.shape[1]
    block = LANES
    some = LANES // 4

    def kernel(h_ref, din_ref, act_ref, att_ref, d_ref, place_ref, *refs):
        out_ref = refs[6]
        x = place_ref[3]
        h = pl.program_id(0)

        @pl.when(h == 0)
        def _():
            out_ref[...] = t_mm(att_ref[...], d_ref[...])

        d_in = din_ref[...]
        d_rows = d_ref[...]
        for three, xx in ((refs[:3], x), (refs[3:6], 1 - x)):
            for k in range(2):
                start = pl.multiple_of(((h * 2 + k) * 2 + xx) * block, LANES)
                grad = t_mm(h_ref[:, pl.ds(start, block)], d_in)
                three[k][0, :, :columns] = grad.astype(three[k].dtype)
            start = pl.multiple_of((h * 2 + xx) * some, some)
            grad = out_ref[pl.ds(start, some), :]
            for j in range(8):
                here = slice(j % 4 * some, (j % 4 + 1) * some)
                three[j // 4][0, here, columns:] = grad[:, j * LANES : (j + 1) * LANES].astype(
                    three[j // 4].dtype
                )
            start = pl.multiple_of((h * 2 + xx) * block, LANES)
            three[2][0] = t_mm(act_ref[:, pl.ds(start, block)], d_rows).astype(three[2].dtype)

    args = (hs, d_in, act, att, d_rows)
    shape = (2, block, width)
    return pl.pallas_call(
        kernel,
        grid=(2,),
        in_specs=[whole_spec(arg.shape) for arg in args]
        + [pl.BlockSpec(memory_space=pltpu.SMEM)],
        out_specs=[pl.BlockSpec((1,) + shape[1:], lambda h: (h, 0, 0))] * 6,
        out_shape=[jax.ShapeDtypeStruct(shape, kind) for kind in (F32,) * 3 + (LOW,) * 3],
        scratch_shapes=[pltpu.VMEM((LANES, width), F32)],
        compiler_params=params(),
        cost_estimate=cost(5.0),
        name="weight_gradients",
    )(*args, place)


def add_split(keep_ref, got_ref, place_ref, mine_ref, send_ref):
    b = place_ref[1]
    mine_ref[...] = keep_ref[b] + got_ref[b].astype(F32)
    send_ref[...] = (keep_ref[1 - b] + got_ref[1 - b].astype(F32)).astype(LOW)


def split_two(total):
    high = total.astype(LOW)
    return (high, (total - high.astype(F32)).astype(LOW))


def first_group_backward(pieces, qkv, att, slope, w_out, w_down, hot, rope, bias, mixed, keep, got, place, behind):
    slots, width = pieces[0].shape
    total = slots * len(pieces)
    vocab = hot.shape[1]
    units = w_down.shape[0]
    some = LANES // 4
    columns = 3 * LANES + units + width

    def kernel(*refs):
        piece_refs = refs[:8]
        qkv_ref, att_ref, slope_ref, wout_ref, wdown_ref, hot_ref, rope_ref, bias_ref = refs[8:16]
        mixed_ref, keep_ref, got_ref, place_ref = refs[16:20]
        out_refs, mine_ref, send_ref, sum_ref, grad_ref = refs[20:22], *refs[22:]
        sum_ref[...] = jnp.zeros(sum_ref.shape, F32)
        grad_ref[...] = jnp.zeros(grad_ref.shape, F32)
        spans = [slice(j * LANES, (j + 1) * LANES) for j in range(3)]
        for pack, ref in enumerate(piece_refs):
            here = slice(pack * slots, (pack + 1) * slots)
            d_out = ref[...]
            hot_here = hot_ref[here, :]
            d_att = mm_t(d_out, wout_ref[...]).astype(LOW)
            q, k, v = (qkv_ref[here, spans[j]] for j in range(3))
            dq, dk, dv = attend_pair_back(d_att, q, k, v, bias_ref[here, :])
            turned = [rope_ref[j, here, :] for j in range(3)]
            sum_ref[:, spans[0]] += t_mm(hot_here, turn_by(dq, turned, -1.0).astype(LOW))
            sum_ref[:, spans[1]] += t_mm(hot_here, turn_by(dk, turned, -1.0).astype(LOW))
            sum_ref[:, spans[2]] += t_mm(hot_here, dv.astype(LOW))
            sum_ref[:, 3 * LANES + units :] += t_mm(hot_here, d_out)
            grad_ref[...] += t_mm(att_ref[here, :], d_out)
        high, rest = split_two(sum_ref[:, 3 * LANES + units :])
        down = wdown_ref[...]
        sum_ref[:, 3 * LANES : 3 * LANES + units] = (
            mm_t(high, down) + mm_t(rest, down)
        ) * slope_ref[...]
        for ref, xx in zip(out_refs, (place_ref[3], 1 - place_ref[3])):
            ref[:, :columns] = sum_ref[...].astype(ref.dtype)
            for h in range(2):
                at = columns + h * (width + MIXED)
                start = pl.multiple_of((h * 2 + xx) * some, some)
                ref[:, at : at + width] = grad_ref[pl.ds(start, some), :].astype(ref.dtype)
                for dest in range(8):
                    device = (((dest // 4 * 2 + h) * 2 + dest // 2 % 2) * 2 + xx) * 2 + dest % 2
                    here = slice(dest % 2 * 16, dest % 2 * 16 + 16)
                    start = at + width + dest // 2 * LANES
                    ref[here, start : start + LANES] = mixed_ref[device].astype(ref.dtype)
        add_split(keep_ref, got_ref, place_ref, mine_ref, send_ref)

    wide = columns + 2 * (width + MIXED)
    shape = keep.shape[1:]
    outs = [((vocab, wide), F32), ((vocab, wide), LOW)] + [(shape, F32), (shape, LOW)]
    args = (*pieces, qkv, att, slope, w_out, w_down, hot, rope, bias, mixed, keep, got, place)
    scratch = [pltpu.VMEM((vocab, columns), F32), pltpu.VMEM((LANES, width), F32)]
    return simple(
        kernel,
        "first_group_backward",
        outs,
        *args,
        smem=(19,),
        scratch=scratch,
        us=9.0,
        behind=behind,
    )


def fold(keep, got, down, down_far, place):
    vocab = keep.shape[0]
    by_h = 1024 + MIXED
    columns = keep.shape[1] - 2 * by_h

    def kernel(keep_ref, got_ref, one_ref, two_ref, place_ref, mine_ref, send_ref, down_ref):
        down_ref[...] = (one_ref[...] + two_ref[...].astype(F32)).astype(LOW)
        same = keep_ref[:, :columns] + got_ref[:, :columns].astype(F32)
        mine_ref[:, :columns] = same
        send_ref[:, :columns] = same.astype(LOW)
        for ref, h in ((mine_ref, place_ref[1]), (send_ref, 1 - place_ref[1])):
            here = pl.ds(pl.multiple_of(columns + h * by_h, LANES), by_h)
            ref[:, columns:] = (keep_ref[:, here] + got_ref[:, here].astype(F32)).astype(ref.dtype)

    shape = (vocab, columns + by_h)
    outs = [(shape, F32), (shape, LOW), (down.shape, LOW)]
    return simple(kernel, "fold", outs, keep, got, down, down_far, place, smem=(4,))


def add_two(one, two):
    def kernel(one_ref, two_ref, out_ref):
        out_ref[...] = one_ref[...] + two_ref[...]

    return simple(kernel, "add_two", [(one.shape, one.dtype)], one, two)[0]


def token_gradients(parts, h0, weights, act, act_far, place, behind):
    vocab, width = h0.shape
    own_in, shard = weights.shape[1], SHARD
    units = act.shape[1]
    part = units // 4

    def kernel(p0, p1, h_ref, w_ref, act_ref, other_ref, place_ref, in_ref, down_ref, out_ref, dh_ref, rows_ref, mixed_ref, act_out):
        total = p0[...] + p1[...].astype(F32)
        rows = total[:, shard : shard + width]
        rows_ref[...] = rows
        out_ref[...] = total[:, shard + width : shard + 2 * width].astype(LOW)
        for dest in range(8):
            start = shard + 2 * width + dest // 2 * LANES
            here = slice(dest % 2 * 16, dest % 2 * 16 + 16)
            mixed_ref[dest] = total[here, start : start + LANES]
        high, rest = split_two(total[:, :shard])
        h, x = place_ref[1], place_ref[3]
        two = 2 * own_in
        for kk in range(2):
            start = pl.multiple_of(((h * 2 + kk) * 2 + x) * two, LANES)
            mine = h_ref[:, pl.ds(start, two)]
            grad = t_mm(mine, high) + t_mm(mine, rest)
            in_ref[2 * kk : 2 * kk + 2] = grad.astype(LOW).reshape(2, own_in, shard)
            block = w_ref[2 * kk : 2 * kk + 2, :, :shard].reshape(two, shard)
            dh_ref[kk * vocab : (kk + 1) * vocab, :] = mm_t(high, block) + mm_t(rest, block)
        act_out[...] = total[:, 3 * LANES : shard]
        start = pl.multiple_of((h * 2 + x) * part, LANES)
        bias = jnp.sum(act_out[:, pl.ds(start, part)], 0, keepdims=True)
        dh_ref[2 * vocab :, :] = jnp.broadcast_to(bias, (8, LANES))
        high, rest = split_two(rows)
        for j, ref in enumerate((act_ref, other_ref)):
            mine = ref[:, pl.ds(start, part)]
            down_ref[j * part : (j + 1) * part, :] = t_mm(mine, high) + t_mm(mine, rest)

    outs = [
        ((4, own_in, shard), LOW),
        ((2 * part, width), F32),
        ((vocab, width), LOW),
        ((2 * vocab + 8, LANES), F32),
        ((vocab, width), F32),
        ((8, 16, LANES), F32),
    ]
    scratch = [pltpu.VMEM((vocab, units), F32)]
    args = (*parts, h0, weights, act, act_far, place)
    return simple(
        kernel, "token_gradients", outs, *args, smem=(6,), scratch=scratch, behind=behind
    )


def owner_pieces(keeps, gots, down, first_in, first_down, first_out, dh, mixed, scalars, bias_local, place):
    rows, width = keeps[0].shape
    own_in, columns = first_in.shape[1:]
    some = first_out.shape[0]
    vocab = bias_local.shape[1]

    def kernel(k0, k1, g0, g1, upper_ref, in_ref, down_ref, out_ref, dh_ref, mixed_ref, scalar_ref, bias_ref, place_ref, shard_ref, one_ref, two_ref, last_ref, sum_ref):
        y, x = place_ref[0], place_ref[3]
        for j, (keep, got) in enumerate(((k0, g0), (k1, g1))):
            sum_ref[j * rows : (j + 1) * rows, :] = (keep[...] + got[...].astype(F32)).astype(LOW)
        lane = lax.broadcasted_iota(jnp.int32, (vocab, LANES), 1)
        for number in range(8):
            if number < 4:
                shard_ref[number, :, :columns] = in_ref[number]
            else:
                here = slice((number - 4) * own_in, (number - 3) * own_in)
                shard_ref[number, :, :columns] = sum_ref[here, :columns]
            block = dh_ref[number // 4 * vocab : (number // 4 + 1) * vocab, :]
            if number % 4:
                block = pltpu.roll(block, LANES - number % 4 * vocab, 1)
            high = block.astype(LOW).astype(F32)
            rest = pltpu.roll(block - high, vocab, 1)
            both = jnp.where(lane < vocab, high, jnp.where(lane < 2 * vocab, rest, 0.0))
            shard_ref[number, :vocab, columns:] = both.astype(LOW)
            high, rest = split_two(mixed_ref[number])
            shard_ref[number, vocab : vocab + 16, columns:] = high
            shard_ref[number, vocab + 16 :, columns:] = rest
        for j in range(width // LANES):
            here = slice(j * LANES, (j + 1) * LANES)
            upper = sum_ref[j * some : (j + 1) * some, columns:]
            first = out_ref[:, here]
            one_ref[:, here] = jnp.where(x == 0, first, upper)
            two_ref[:, here] = jnp.where(x == 0, upper, first)

        def squares(value):
            value = value.astype(F32)
            return jnp.sum(jnp.sum(value * value, 0, keepdims=True), 1, keepdims=True)

        total = squares(sum_ref[...]) + squares(upper_ref[...]) + squares(out_ref[...])
        total = total + jnp.where(y == 0, squares(down_ref[...]), 0.0)
        for j in range(4):
            total = total + squares(in_ref[j])
        lane = lax.broadcasted_iota(jnp.int32, (1, LANES), 1)
        penalty = jnp.where(y == 0, scalar_ref[0:1, 2:3], 0.0)
        bias = jnp.concatenate([bias_ref[...], jnp.zeros((1, LANES - vocab), F32)], 1)
        row = jnp.where(lane == 0, total, jnp.where(lane == 1, penalty, 0.0))
        last_ref[...] = row + pltpu.roll(bias, vocab, 1)

    outs = [((8, own_in, columns + LANES), LOW)]
    outs = outs + [((some, width), LOW)] * 2
    outs = outs + [((1, LANES), F32)]
    scratch = [pltpu.VMEM((2 * rows, width), LOW)]
    args = (*keeps, *gots, down, first_in, first_down, first_out, dh, mixed, scalars, bias_local, place)
    return simple(kernel, "owner_pieces", outs, *args, smem=(12,), scratch=scratch)


def norm_sums(shards, dh, last, place, behind):
    vocab = 32

    def kernel(shard_ref, dh_ref, last_ref, place_ref, all_ref, mixed_ref, out_ref):
        total = jnp.sum(shard_ref[:, :vocab, SHARD:].astype(F32), 0)
        total = total + pltpu.roll(total, LANES - vocab, 1)
        lane = lax.broadcasted_iota(jnp.int32, (8, LANES), 1)
        packed = total[:8]
        for group in range(1, 4):
            moved = pltpu.roll(total[group * 8 : (group + 1) * 8], group * vocab, 1)
            packed = jnp.where(lane >= group * vocab, moved, packed)
        out_ref[:8, :] = packed
        mixed = jnp.sum(shard_ref[:, vocab : vocab + 16, SHARD:].astype(F32), 0)
        mixed = mixed + jnp.sum(shard_ref[:, vocab + 16 :, SHARD:].astype(F32), 0)
        mixed_ref[...] = mixed
        line = lax.broadcasted_iota(jnp.int32, (16, LANES), 0)
        counted = (line < VECTOR_ROW) | (place_ref[0] == 1)
        squares = jnp.where(counted, mixed * mixed, 0.0)
        squares = jnp.sum(jnp.sum(squares, 0, keepdims=True), 1, keepdims=True)
        first = lax.broadcasted_iota(jnp.int32, (1, LANES), 1) == 0
        row = last_ref[...] + jnp.where(first, squares, 0.0)
        line = lax.broadcasted_iota(jnp.int32, (8, LANES), 0)
        out_ref[8:, :] = jnp.where(line == 0, row, dh_ref[2 * vocab :, :])
        all_ref[...] = jnp.broadcast_to(out_ref[...][None], all_ref.shape)

    outs = [((32, 16, LANES), F32), ((16, LANES), F32)]
    scratch = [pltpu.VMEM((16, LANES), F32)]
    args = (shards, dh, last, place)
    return simple(kernel, "norm_sums", outs, *args, smem=(3,), scratch=scratch, behind=behind)


def own_gradients(shards, first_down, down_mine, down_far, out_one, out_two, place):
    own_in = shards.shape[1]
    part, width = down_mine.shape
    some = out_one.shape[0]

    def kernel(shard_ref, first_ref, mine_ref, far_ref, one_ref, two_ref, place_ref, qkv_ref, up_ref, down_ref, out_ref):
        y = place_ref[0]
        for number in range(8):
            yy, kk, cc = number >> 2, number >> 1 & 1, number & 1
            start = ((cc * 2 + kk) * 2 + yy) * LANES
            for j in range(3):
                qkv_ref[:, j * width + start : j * width + start + LANES] = shard_ref[
                    number, :, j * LANES : (j + 1) * LANES
                ].astype(F32)
            for j in range(4):
                start = (j // 2 * 8 + kk * 4 + j % 2 * 2 + cc) * 2 * part + yy * part
                up_ref[:, start : start + part] = shard_ref[
                    number, :, (3 + j) * LANES : (4 + j) * LANES
                ].astype(F32)
        mine, far = mine_ref[...].astype(F32), far_ref[...].astype(F32)
        down_ref[:part, :] = jnp.where(y == 0, first_ref[:part, :], far)
        down_ref[part:, :] = jnp.where(y == 0, first_ref[part:, :], mine)
        one, two = one_ref[...].astype(F32), two_ref[...].astype(F32)
        out_ref[:some, :] = jnp.where(y == 0, one, two)
        out_ref[some:, :] = jnp.where(y == 0, two, one)

    outs = [
        ((own_in, 3 * width), F32),
        ((own_in, 4 * width), F32),
        ((2 * part, width), F32),
        ((2 * some, width), F32),
    ]
    args = (shards, first_down, down_mine, down_far, out_one, out_two, place)
    return simple(kernel, "own_gradients", outs, *args, smem=(6,))


def fast_input_backward(pieces, x_low, dy, vec, down_sum, bias_up, table_local, ends_local, keeps, gots, later, place):
    rows, width = dy.shape
    part = bias_up.shape[1] // 4
    total = vec.shape[1]
    owners = 32
    vocab = width // owners

    def kernel(p0, p1, p2, p3, x_ref, dy_ref, vec_ref, sum_ref, up_ref, table_ref, ends_ref, k0, k1, g0, g1, later_ref, place_ref, low_ref, mixed_ref, m0, m1, s0, s1, pass_ref, grad_ref):
        add_split(k0, g0, place_ref, m0, s0)
        add_split(k1, g1, place_ref, m1, s1)
        pass_ref[...] = later_ref[...]
        d_norm = p0[...] + p1[...].astype(F32) + p2[...].astype(F32) + p3[...].astype(F32)
        gain = vec_ref[1:2, :width]
        _, normed, inverse = layer_norm(x_ref[...].astype(F32), gain, 0.0)
        low_ref[...] = (dy_ref[...] + norm_back(d_norm, normed, inverse, gain)).astype(LOW)
        grad_ref[:, :width] = jnp.sum(d_norm * normed, 0, keepdims=True)
        grad_ref[:, width : 2 * width] = jnp.sum(d_norm, 0, keepdims=True)
        grad_ref[:, 2 * width : 3 * width] = sum_ref[...]
        grad_ref[:, 3 * width :] = jnp.zeros((1, total - 3 * width), F32)
        y, k, c = place_ref[0], place_ref[2], place_ref[4]
        for j in range(4):
            start = unit_start(width, j, y, k, c, part)
            grad_ref[:, pl.ds(start, part)] = up_ref[:, j * part : (j + 1) * part]
        mixed_ref[:, 8:, :] = jnp.zeros((owners, 8, LANES), F32)
        lane = lax.broadcasted_iota(jnp.int32, (8, LANES), 1)
        for owner in range(owners):
            rows_here = jnp.zeros((8, LANES), F32)
            for group in range(4):
                start = owner * vocab + group * 8
                value = table_ref[start : start + 8, :]
                if group:
                    value = pltpu.roll(value, group * vocab, 1)
                mine = (lane >= group * vocab) & (lane < (group + 1) * vocab)
                rows_here = jnp.where(mine, value, rows_here)
            mixed_ref[owner, :8, :] = rows_here
            block = ends_ref[:, owner // 4 * LANES : (owner // 4 + 1) * LANES]
            if owner % 4:
                block = pltpu.roll(block, LANES - owner % 4 * vocab, 1)
            mine = lax.broadcasted_iota(jnp.int32, (2, LANES), 1) < vocab
            mixed_ref[owner, 8:10, :] = jnp.where(mine, block[:2], 0.0)
        first_half = lax.broadcasted_iota(jnp.int32, (1, LANES), 1) < LANES // 2
        for pair in range(owners // 4):
            at = pair * 7 * LANES
            tiles = [grad_ref[:, at + q * LANES : at + (q + 1) * LANES] for q in range(7)]
            turned = [pltpu.roll(tile, LANES // 2, 1) for tile in tiles[3:]]
            even = tiles[:3] + [jnp.where(first_half, tiles[3], 0.0)]
            odd = [jnp.where(first_half, turned[q], turned[q + 1]) for q in range(3)]
            odd = odd + [jnp.where(first_half, turned[3], 0.0)]
            for side, lines in enumerate((even, odd)):
                for q in range(4):
                    owner = owners // 2 + 2 * pair + side
                    mixed_ref[owner, VECTOR_ROW + q : VECTOR_ROW + q + 1, :] = lines[q]

    outs = [((rows, width), LOW), ((owners, 16, LANES), F32)]
    shape = later.shape[1:]
    outs = outs + [(shape, F32)] * 2 + [(shape, LOW)] * 2 + [(later.shape, LOW)]
    args = (*pieces, x_low, dy, vec, down_sum, bias_up, table_local, ends_local, *keeps, *gots, later, place)
    scratch = [pltpu.VMEM((1, total), F32)]
    return simple(kernel, "input_backward", outs, *args, smem=(16,), scratch=scratch, us=2.0)


def pack_states(vectors, tables, biases, behind):
    features, table_rows = tables[0].shape
    chunk = vectors[0].shape[1]
    many = features + 8

    def kernel(*refs):
        out_ref = refs[9]
        for number in range(3):
            vec_ref, tab_ref, bias_ref = refs[number], refs[3 + number], refs[6 + number]
            start = number * many
            pad = jnp.zeros((features, LANES - table_rows), F32)
            out_ref[start : start + features, :] = jnp.concatenate([tab_ref[...], pad], 1)
            lines = [vec_ref[:, j * LANES : (j + 1) * LANES] for j in range(3)]
            rest = chunk - 3 * LANES
            ends = jnp.concatenate(
                [vec_ref[:, 3 * LANES :], jnp.zeros((1, LANES - rest), F32)], 1
            )
            bias = bias_ref[...]
            bias = jnp.concatenate([bias, jnp.zeros((1, LANES - bias.shape[1]), F32)], 1)
            line = lax.broadcasted_iota(jnp.int32, (8, LANES), 0)
            tail = jnp.zeros((8, LANES), F32)
            for row, value in enumerate(lines + [ends, bias]):
                tail = jnp.where(line == row, value, tail)
            out_ref[start + features : start + many, :] = tail

    args = (*vectors, *tables, *biases)
    return simple(kernel, "pack_states", [((3 * many, LANES), F32)], *args, behind=behind)[0]


def last_sums(dh_all, rows_sum, normed, inverse, vec, mixed, scalars, place, packed, chunk, table_rows):
    vocab, width = rows_sum.shape
    total = vec.shape[1]
    devices = dh_all.shape[0]

    def kernel(*refs):
        dh_all_ref, sum_ref, norm_ref, inv_ref, vec_ref, mixed_ref, known_ref, place_ref = refs[:8]
        packed_ref, scalar_ref, norm_ref_out, parts_ref = refs[8:12]
        vector_outs, table_outs, bias_outs = refs[12:15], refs[15:18], refs[18:21]
        dh_ref, all_ref, emb_ref = refs[21:]
        many = vocab + 8
        table_ins = [packed_ref[j * many : j * many + vocab, :table_rows] for j in range(3)]
        tails = [packed_ref[j * many + vocab : (j + 1) * many, :] for j in range(3)]
        vector_ins = [
            jnp.concatenate([tail[row : row + 1] for row in range(4)], 1)[:, :chunk] for tail in tails
        ]
        bias_ins = [tail[4:5, :vocab] for tail in tails]
        y, me = place_ref[0], place_ref[5]
        scalars = jnp.zeros((1, LANES), F32)
        lane = lax.broadcasted_iota(jnp.int32, (8, LANES), 1)
        for h in range(2):
            for x in range(2):
                for yy in range(2):
                    start = (h * 4 + yy * 2 + x) * LANES
                    tiles = [jnp.zeros((8, LANES), F32)] * 4
                    for spot in range(4):
                        device = ((yy * 2 + h) * 2 + spot // 2) * 4 + x * 2 + spot % 2
                        packed = dh_all_ref[device, :8, :]
                        mine = (lane >= spot * vocab) & (lane < (spot + 1) * vocab)
                        for group in range(4):
                            by = (spot - group) * vocab % LANES
                            moved = pltpu.roll(packed, by, 1) if by else packed
                            tiles[group] = jnp.where(mine, moved, tiles[group])
                        ends = dh_all_ref[device, 8:, :]
                        scalars = scalars + ends[0:1]
                        unit = 3 * width + device % 16 * 2 * LANES + yy * LANES
                        all_ref[:, unit : unit + LANES] = ends[1:2]
                    for group in range(4):
                        dh_ref[group * 8 : (group + 1) * 8, start : start + LANES] = tiles[group]
        dh = dh_ref[...]
        normed = norm_ref[...]
        rows = sum_ref[...]
        embed = rows + norm_back(dh, normed, inv_ref[...], vec_ref[0:1, :width])
        emb_ref[...] = embed
        all_ref[:, :width] = jnp.sum(dh * normed, 0, keepdims=True)
        all_ref[:, width : 2 * width] = jnp.sum(dh, 0, keepdims=True)
        all_ref[:, 2 * width : 3 * width] = jnp.sum(rows, 0, keepdims=True)
        lane = lax.broadcasted_iota(jnp.int32, (1, LANES), 1)
        bias = jnp.where((lane >= vocab) & (lane < 2 * vocab), scalars, 0.0)
        vector = all_ref[...]

        def squares(value):
            return jnp.sum(jnp.sum(value * value, 0, keepdims=True), 1, keepdims=True)

        total_squares = scalars[:, 0:1] + squares(bias) + squares(embed) + squares(vector)
        norm = jnp.sqrt(total_squares)
        factor = jnp.minimum(1.0, CLIP_AT / norm)
        known = known_ref[...]
        row = jnp.where(lane == 0, norm, jnp.where(lane == 1, known[:, 0:1], known[:, 1:2]))
        row = jnp.where(lane == 3, scalars[:, 1:2], row)
        scalar_ref[...] = jnp.where(lane == 4, factor, row)
        norm_ref_out[...] = norm
        parts_ref[...] = row[:, 1:4]

        def update(ins, outs, grad):
            new = adam(*ins, grad * factor, RATE_VEC, 0.0)
            for ref, value in zip(outs, new):
                ref[...] = value

        odd = lax.rem(me, 2)
        start = pl.multiple_of(me * chunk - odd * (LANES // 2), LANES)
        mine = all_ref[:, pl.ds(start, chunk + LANES // 2)]
        mine = jnp.where(odd == 0, mine, pltpu.roll(mine, chunk, 1))
        far = jnp.concatenate(
            [mixed_ref[VECTOR_ROW + q : VECTOR_ROW + q + 1, :] for q in range(4)], 1
        )
        update(vector_ins, vector_outs, jnp.where(y == 0, mine, far)[:, :chunk])
        number = y * (devices // 2) + me
        block = emb_ref[:, pl.ds(pl.multiple_of(number // 4 * LANES, LANES), LANES)]
        block = pltpu.roll(block, lax.rem(LANES - lax.rem(number, 4) * vocab, LANES), 1)
        padded = jnp.concatenate([block, jnp.zeros((LANES - vocab, LANES), F32)], 0).T[:vocab, :]
        wide = lax.broadcasted_iota(jnp.int32, (vocab, LANES), 1)
        head = jnp.concatenate(
            [mixed_ref[:8, :]]
            + [pltpu.roll(mixed_ref[:8, :], LANES - group * vocab, 1) for group in range(1, 4)],
            0,
        )
        ends = jnp.concatenate([mixed_ref[8:16, :], jnp.zeros((LANES - 8, LANES), F32)], 0).T[:vocab]
        grad = jnp.where(wide < vocab, padded, pltpu.roll(head, vocab, 1))
        grad = jnp.where(wide < 2 * vocab, grad, pltpu.roll(ends, 2 * vocab, 1))
        update(table_ins, table_outs, grad[:, :table_rows])
        update(bias_ins, bias_outs, pltpu.roll(bias, LANES - vocab, 1)[:, :vocab])

    args = (dh_all, rows_sum, normed, inverse, vec, mixed, scalars, place, packed)
    outs = [((1, LANES), F32), ((1, 1), F32), ((1, 3), F32)] + [((1, chunk), F32)] * 3 + [((vocab, table_rows), F32)] * 3
    outs = outs + [((1, vocab), F32)] * 3
    scratch = [
        pltpu.VMEM((vocab, width), F32),
        pltpu.VMEM((1, total), F32),
        pltpu.VMEM((vocab, width), F32),
    ]
    return simple(
        kernel, "last_sums", outs, *args, smem=(7,), scratch=scratch, limit=VMEM_MOST
    )


def update_all(scalars, grads, weights, firsts, seconds, rates):
    steps = 4
    shapes = [weight.shape for weight in weights]

    def kernel(scalar_ref, *refs):
        factor = scalar_ref[:, 4:5]
        for j, rate in enumerate(rates):
            grad_ref, weight_ref, first_ref, second_ref = (refs[part * 4 + j] for part in range(4))
            new = adam(
                weight_ref[0],
                first_ref[0],
                second_ref[0],
                grad_ref[...] * factor,
                rate,
                DECAY,
            )
            for part, value in enumerate(new):
                refs[16 + j * 3 + part][0] = value

    def spec(shape, lead):
        rows, columns = shape[-2:]
        block, where = (rows // steps, columns), lambda s: (s, 0)
        if lead:
            return pl.BlockSpec((1,) + block, lambda s: (0,) + where(s))
        return pl.BlockSpec(block, where)

    return pl.pallas_call(
        kernel,
        grid=(steps,),
        in_specs=[pl.BlockSpec((1, LANES), lambda s: (0, 0))]
        + [spec(shape, False) for shape in shapes]
        + [spec(shape, True) for shape in shapes] * 3,
        out_specs=[spec(shape, True) for shape in shapes for _ in range(3)],
        out_shape=[jax.ShapeDtypeStruct(shape, F32) for shape in shapes for _ in range(3)],
        compiler_params=params(VMEM_MOST),
        cost_estimate=cost(6.0),
        name="update_all",
    )(scalars, *grads, *weights, *firsts, *seconds)


def body_fast(
    tokens,
    lengths,
    counted,
    partners,
    qkv_weight,
    out_weight,
    up_weight,
    down_weight,
    vectors,
    tables,
    head_bias,
    *states,
):
    y, h, k, x, c = (lax.axis_index(a) for a in ALL)
    me = lax.axis_index(PLANE)
    place = scalars_of(y, h, k, x, c, me)
    slots = tokens.shape[1]
    vocab = head_bias.shape[0]
    plane, everyone = 16, 32

    rows, down_keep, down_send, out_one, out_two = cut_first(
        tables.T, vectors, tokens, lengths, down_weight[0], out_weight[0], place
    )
    down_far = flip(down_send, ("y",), (1,))
    routes = [[], []]
    for device in range(everyone):
        yy, hh, kk, xx, cc = (device >> 4, device >> 3 & 1, device >> 2 & 1, device >> 1 & 1, device & 1)
        owner = cc * 8 + kk * 4 + yy * 2 + hh
        for step in range(2):
            routes[step].append(((xx ^ step) * plane + owner, device))
    out_one = lax.ppermute(out_one, ALL, routes[0])
    out_two = lax.ppermute(out_two, ALL, routes[1])
    rows = [rows] + [flip(rows, ("h", "x"), bits) for bits in NEAR]
    tail = first_rows(down_keep, down_far, out_one, out_two, place)
    tails = across(tail)
    shards = cut_weights(qkv_weight[0], up_weight[0], rows, (tail,))
    shards = trade(shards, ("y", "k", "c"))
    table_all = unpack_rows(shards, place)
    low_tables, vec, h0, normed0, inverse0, part = token_products(table_all, shards, place)
    uppers = upper_rows(shards, down_keep, down_far, out_one, out_two, place)
    nears = [flip(piece, ("x",), (1,)) for piece in uppers]
    fars = [flip(piece, ("h",), (1,)) for piece in uppers]
    crosses = [flip(piece, ("x",), (1,)) for piece in fars]
    part = add_two(part, flip(part, ("x",), (1,)))
    parts = [part, flip(part, ("h",), (1,))]
    bias, rope, hot, target_hot, seq_weight, seq_count = slot_tables(
        table_all, counted, place, rope_constant(slots), (part,)
    )

    packed = pack_states(
        (vectors, states[4], states[11]),
        (tables.T, states[5].T, states[12].T),
        (head_bias[None], states[6][None], states[13][None]),
        (seq_count,),
    )

    keep, send, qkv0, att0, act0, slope0, w_out0, w_down0 = first_group_forward(
        parts, tails, vec, place, hot, rope, bias, (fars[0],nears[0],nears[1])
    )
    act_far = flip(act0, ("y",), (1,))
    pieces = group_sums(keep, send, ())
    x_low, h_low = first_finish_rows(pieces, hot, low_tables, vec, (fars[1], crosses[0]))

    uppers = [*uppers, *nears, *fars, *crosses]
    keep, send, hs, qkv, att, act, slope, w_in, w_out, w_down = group_forward(
        group_pieces(h_low), uppers, vec, place, rope, bias
    )
    normed_f, inverse_f, final_low, logp, sums = fast_loss_forward(
        x_low,
        group_sums(keep, send),
        vec,
        low_tables,
        head_bias,
        target_hot,
        seq_weight,
        seq_count,
    )
    sums = spread(sums, ALL).reshape(everyone, LANES)
    dy, dy_low, table_local, ends_local, bias_local, down_sum, scalars = fast_loss_backward(
        sums,
        partners,
        place,
        normed_f,
        inverse_f,
        final_low,
        logp,
        low_tables,
        target_hot,
        seq_weight,
        plane,
        seq_count.shape[0],
    )

    keep, send, d_rows, d_in, bias_up = group_backward(
        group_pieces(dy_low), qkv, slope, w_in, w_out, w_down, rope, bias
    )
    keep_1, keep_2, keep_0, send_1, send_2, send_0 = weight_gradients(
        hs, d_in, act, att, d_rows, place
    )
    gots = [flip(piece, ("x",), (1,)) for piece in (send_0, send_1)]
    terms = group_sums(keep, send, (send_0,))
    own_low, mixed, mine_0, mine_1, send_0, send_1, send_2 = fast_input_backward(
        terms,
        x_low,
        dy,
        vec,
        down_sum,
        bias_up,
        table_local,
        ends_local,
        (keep_0, keep_1),
        gots,
        send_2,
        place,
    )

    pieces = group_pieces(own_low)
    got_2 = flip(send_2, ("x",), (1,))
    far_0, far_1 = (flip(piece, ("h",), (1,)) for piece in (send_0, send_1))
    keep, send, mine_2, send_2 = first_group_backward(
        pieces,
        qkv0,
        att0,
        slope0,
        w_out0,
        w_down0,
        hot,
        rope,
        bias,
        mixed,
        keep_2,
        got_2,
        place,
        (far_0,),
    )
    far_2 = flip(send_2, ("h",), (1,))
    part, send, down_mine = fold(keep, flip(send, ("x",), (1,)), mine_0, far_0, place)
    down_far = lax.ppermute(down_mine, "y", [(0, 1)])
    parts = [part, flip(send, ("h",), (1,))]
    first_in, first_down, first_out, dh, rows_sum, mixed = token_gradients(
        parts, h0, shards, act0, act_far, place, (far_2,)
    )
    shards, out_one, out_two, last = owner_pieces(
        (mine_1, mine_2),
        (far_1, far_2),
        down_mine,
        first_in,
        first_down,
        first_out,
        dh,
        mixed,
        scalars,
        bias_local,
        place,
    )
    out_one = lax.ppermute(out_one, ALL, [(b, a) for a, b in routes[0]])
    out_two = lax.ppermute(out_two, ALL, [(b, a) for a, b in routes[1]])
    shards = trade(shards, ("y", "k", "c"))
    qkv_grad, up_grad, down_grad, out_grad = own_gradients(
        shards, first_down, down_mine, down_far, out_one, out_two, place
    )
    sums, mixed = norm_sums(shards, dh, last, place, ())
    scalars, norm, parts, *small = last_sums(
        trade(sums, ALL),
        rows_sum,
        normed0,
        inverse0,
        vec,
        mixed,
        scalars,
        place,
        packed,
        vectors.shape[1],
        tables.shape[0],
    )
    results = update_all(
        scalars,
        (qkv_grad, out_grad, up_grad, down_grad),
        (qkv_weight, out_weight, up_weight, down_weight),
        states[:4],
        states[7:11],
        (RATE_MAT, RATE_OUT, RATE_MAT, RATE_MAT),
    )
    results = list(results)
    results.extend(small[:3])
    results.extend(value.T for value in small[3:6])
    results.extend(value[0] for value in small[6:])
    return (norm.reshape(()), parts.reshape(3), *results)


def body(
    tokens,
    lengths,
    counted,
    partners,
    qkv_weight,
    out_weight,
    up_weight,
    down_weight,
    vectors,
    tables,
    head_bias,
    qkv_moment,
    out_moment,
    up_moment,
    down_moment,
    vector_moment,
    table_moment,
    bias_moment,
    qkv_square,
    out_square,
    up_square,
    down_square,
    vector_square,
    table_square,
    bias_square,
):
    sections = lax.axis_size("y")
    spans = lax.axis_size("h")
    plane = lax.axis_size(PLANE)
    everyone = sections * plane
    y, h, k, x, c = (lax.axis_index(a) for a in ALL)
    me = lax.axis_index(PLANE)
    group = Group(sections, spans)
    micro, slots = tokens.shape
    per_pack = lengths.shape[1]
    width = qkv_weight.shape[2] // 3
    hidden = up_weight.shape[2]
    vocab = head_bias.shape[0]
    own_in = qkv_weight.shape[1]
    own_out = out_weight.shape[1]
    own_ff = down_weight.shape[1]
    shares = 4 * sections
    heads = width // HEAD
    shard_heads = heads // shares
    shard_width = width // shares
    shard_ff = hidden // shares
    rows = micro * slots // sections
    block_rows = micro * slots
    group_rows = 4 * block_rows
    group_packs = 4 * micro
    own_packs = max(1, rows // slots)
    own_pack_rows = min(rows, slots)

    low_qkv = qkv_weight[0].astype(LOW)
    low_out = out_weight[0].astype(LOW)
    low_up = up_weight[0].astype(LOW)
    low_down = down_weight[0].astype(LOW)

    table_part = tables.shape[1]
    vector_part = vectors.shape[1]
    small = jnp.concatenate(
        [
            tables.astype(LOW).reshape(-1),
            vectors[0].astype(LOW),
            lengths.astype(LOW).reshape(-1),
        ]
    )
    small_all = spread(small, ALL)
    cut_one = tables.size
    cut_two = cut_one + vector_part
    table_low = (
        small_all[:, :cut_one]
        .reshape(everyone, tables.shape[0], table_part)
        .transpose(1, 0, 2)
        .reshape(tables.shape[0], width)
    )
    vec_low = small_all[:, cut_one:cut_two].reshape(sections, plane * vector_part)
    vec_all = vec_low.astype(F32)
    lengths_all = small_all[:, cut_two:].astype(jnp.int32)
    embed = table_low[:vocab].astype(F32)
    head_low = table_low[vocab : 2 * vocab]
    final_gain = table_low[2 * vocab].astype(F32)
    final_bias = table_low[2 * vocab + 1].astype(F32)
    out_bias = head_bias.astype(LOW).astype(F32)

    segment, position = jax.vmap(lambda row: pack_layout(row, slots))(lengths)
    target = jnp.concatenate([tokens[:, 1:], jnp.zeros((micro, 1), jnp.int32)], 1)
    same = jnp.concatenate([segment[:, 1:] == segment[:, :-1], jnp.zeros((micro, 1), bool)], 1)
    weight = (same & (counted == 1)).astype(F32)
    sequence = segment + per_pack * jnp.arange(micro, dtype=jnp.int32)[:, None]

    def own(array):
        return lax.dynamic_slice_in_dim(array.reshape((block_rows,) + array.shape[2:]), y * rows, rows, 0)

    own_target = own(target)
    own_weight = own(weight)
    own_sequence = own(sequence)
    first_pack = (y * rows) // slots

    def packs_of(array):
        return lax.dynamic_slice_in_dim(array, first_pack, own_packs, 0)

    pack_tokens = packs_of(tokens)
    pack_segment = packs_of(segment)
    pack_position = packs_of(position)
    own_tokens = own(tokens).reshape(own_packs, own_pack_rows)
    own_segment = own(segment).reshape(own_packs, own_pack_rows)
    own_position = own(position).reshape(own_packs, own_pack_rows)
    pack_index = jnp.broadcast_to(jnp.arange(slots, dtype=jnp.int32), (own_packs, slots))
    own_index = (
        jnp.broadcast_to(jnp.arange(own_pack_rows, dtype=jnp.int32), (own_packs, own_pack_rows))
        + (y * rows) % slots
    )
    own_mask = (own_segment[:, :, None] == pack_segment[:, None, :]) & (
        pack_index[:, None, :] <= own_index[:, :, None]
    )
    target_hot = one_hot(own_target, vocab, F32)
    local_seqs = micro * per_pack
    seq_weight = one_hot(own_sequence, local_seqs, F32) * own_weight[:, None]
    seq_count = jnp.sum(
        one_hot(sequence.reshape(-1), local_seqs, F32) * weight.reshape(-1)[:, None], 0
    )
    hot_pack = one_hot(pack_tokens.reshape(-1), vocab, LOW)
    hot_own = one_hot(own_tokens.reshape(-1), vocab, LOW)
    own_bias = jnp.where(own_mask, 0.0, -1e30).reshape(rows, slots)
    own_rope = rope_rows(own_position.reshape(-1))
    pack_rope = own_rope if rows % slots == 0 else rope_rows(pack_position.reshape(-1))

    lengths_plane = lengths_all.reshape(sections, spans, 2, 2, 2, micro * per_pack)[0]
    lengths_group = pick(lengths_plane, h)[:, :, :, :]
    lengths_group = lax.dynamic_index_in_dim(lengths_group, x, 1, keepdims=False)

    parts = []
    for dc in range(2):
        for dk in range(2):
            block_lengths = pick(pick(lengths_group, (k - dk) % 2), (c - dc) % 2)
            parts.append(block_lengths.reshape(micro, per_pack))
    group_lengths = jnp.concatenate(parts, 0)
    group_segment, group_position = jax.vmap(lambda row: pack_layout(row, slots))(group_lengths)
    turn = (y - jnp.arange(sections)) % sections

    def by_offset(array):
        cut = array.reshape((4, sections, rows) + array.shape[2:])
        return jnp.take(cut, turn, axis=1).reshape((4 * sections * rows,) + array.shape[2:])

    if rows % slots == 0:
        group_segment = by_offset(group_segment).reshape(group_packs, slots)
        group_position = by_offset(group_position).reshape(group_packs, slots)
    group_index = jnp.arange(slots, dtype=jnp.int32)
    group_mask = (group_segment[:, :, None] == group_segment[:, None, :]) & (
        group_index[None, :] <= group_index[:, None]
    )
    group_bias = jnp.where(group_mask, 0.0, -1e30).reshape(group_rows, slots)
    group_rope = rope_rows(group_position.reshape(-1))

    def to_group(value):
        got = group.gather(value).reshape((4, sections, rows) + value.shape[1:])
        if rows % slots:
            got = jnp.take(got, turn, axis=1)
        return got.reshape((group_rows,) + value.shape[1:])

    def from_group(keep, send):
        def cut(value):
            value = value.reshape((2, sections, rows) + value.shape[1:])
            if rows % slots:
                value = jnp.take(value, turn, axis=1)
            return value.reshape((2 * sections, rows) + value.shape[3:])

        return group.scatter(cut(keep), cut(send))

    part_ff = own_ff // sections

    def columns_by_shard(qkv_rows, up_rows):
        cut_qkv = qkv_rows.reshape(own_in, 3, 2, 2, sections, shard_width)
        cut_up = up_rows.reshape(own_in, spans, 2, 2, 2, sections, part_ff)
        pieces = []
        for cc in range(2):
            for kk in range(2):
                for yy in range(sections):
                    pieces.append(
                        jnp.concatenate(
                            [cut_qkv[:, j, cc, kk, yy] for j in range(3)]
                            + [
                                cut_up[:, hh, kk, xx, cc, yy]
                                for hh in range(spans)
                                for xx in range(2)
                            ],
                            1,
                        )
                    )
        return jnp.stack(pieces).reshape((2, 2, sections) + pieces[0].shape)

    def columns_back(shards):
        cut = shards[..., : 3 * shard_width].reshape(2, 2, sections, own_in, 3, shard_width)
        qkv_rows = cut.transpose(3, 4, 0, 1, 2, 5).reshape(own_in, 3 * width)
        cut = shards[..., 3 * shard_width :].reshape(
            2, 2, sections, own_in, spans, 2, part_ff
        )
        up_rows = cut.transpose(3, 4, 1, 5, 0, 2, 6).reshape(own_in, hidden)
        return (qkv_rows, up_rows)

    small_out = width // everyone

    def out_routes(layer):
        routes = [[] for _ in range(sections)]
        for yy in range(sections):
            for hh in range(spans):
                for kk in range(2):
                    for xx in range(2):
                        for cc in range(2):
                            share = (cc * 2 + kk) * sections + yy
                            number = share * (2 * spans) + hh * 2 + xx
                            device = yy * plane + ((hh * 2 + kk) * 2 + xx) * 2 + cc
                            owner = layer * plane + number // sections
                            routes[number % sections].append((owner, device))
        return routes

    share_index = (c * 2 + k) * sections + y
    out_part = (share_index * (2 * spans) + h * 2 + x) % sections

    by_shard = columns_by_shard(low_qkv, low_up)
    give = shift(pick(by_shard, 1 - c), "c", 1)
    over_c = ordered(pick(by_shard, c), give, c, 1)
    give = shift(pick(over_c, 1 - k), "k", 1)
    over_k = ordered(pick(over_c, k), give, k, 0)

    gain0, bias0 = vec_all[0, :width], vec_all[0, width : 2 * width]
    bias_down0, bias_up0 = vec_all[0, 2 * width : 3 * width], vec_all[0, 3 * width :]
    h0_full, normed0, inverse0 = layer_norm(embed, gain0, bias0)
    h0 = h0_full.astype(LOW)
    pair_rows = 2 * own_in
    h0_here = jnp.concatenate(
        [
            lax.dynamic_slice_in_dim(h0, ((h * 2 + kk) * 2 + x) * pair_rows, pair_rows, 1)
            for kk in range(2)
        ],
        1,
    )
    both = [
        mm(h0_here, over_k[:, :, yy].reshape(4 * own_in, -1)) for yy in range(sections)
    ]
    spread_over = 2 * spans
    token_rows = vocab // spread_over
    proj_part = jnp.concatenate([part[:, : 3 * shard_width] for part in both], 1)
    proj_part = proj_part.reshape(spread_over, -1, own_ff)
    u_part = jnp.stack(
        [
            jnp.concatenate(
                [
                    part[:, 3 * shard_width + j * part_ff : 3 * shard_width + (j + 1) * part_ff]
                    for part in both
                ],
                1,
            )
            for j in range(spread_over)
        ]
    )
    mixed = jnp.sum(trade(jnp.concatenate([u_part, proj_part], 1), ("h", "x")), 0)
    u_own = mixed[:vocab] + lax.dynamic_slice_in_dim(bias_up0, me * own_ff, own_ff, 0)
    proj_own = mixed[vocab:]
    a0, slope0 = gelu_pair(u_own)
    a0 = a0.astype(LOW)
    ffn_part = jnp.where(y == 0, mm(a0, low_down), 0.0)
    for yy in range(1, sections):
        got = lax.ppermute(proj_own, "y", [(0, yy)])
        proj_own = jnp.where(y == yy, got, proj_own)
    proj_all = spread(proj_own, PLANE)
    ffn_cols = trade(ffn_part.reshape(vocab, everyone, -1).transpose(1, 0, 2), ALL)
    ffn_cols = jnp.sum(ffn_cols, 0)
    proj_table = (
        proj_all.reshape(spans, 2, 2, 2, token_rows, sections, 3, shard_width)
        .transpose(0, 2, 4, 6, 3, 1, 5, 7)
        .reshape(vocab, 3 * width)
    )
    ffn_table = spread(ffn_cols, ALL).transpose(1, 0, 2).reshape(vocab, width)
    query0, keys0, values0, att0 = first_forward(
        proj_table, hot_own, hot_pack, own_rope, pack_rope, own_bias, own_packs
    )

    first_out = low_out
    for yy in range(1, sections):
        got = lax.ppermute(low_out, "y", [(0, yy)])
        first_out = jnp.where(y == yy, got, first_out)
    pieces = jnp.stack([first_out] + [shift(first_out, "h", s) for s in range(1, spans)])
    pieces = jnp.take(pieces, (h - jnp.arange(spans)) % spans, axis=0)
    pieces = after(pieces, h0)
    pieces = ordered(pieces, after(shift(pieces, "k", 1), mixed), k, 1)
    pieces = ordered(pieces, after(shift(pieces, "x", 1), proj_table), x, 2)
    pieces = ordered(pieces, after(shift(pieces, "c", 1), att0), c, 3)
    first_out = pieces.reshape(width, width)

    stay = embed + ffn_table + bias_down0
    x_low, h_low = first_finish(
        att0, first_out, hot_own, stay, vec_all[1, :width], vec_all[1, width : 2 * width]
    )

    shard_weights = []
    for layer in range(1, sections):
        cut_down = low_down.reshape(sections, part_ff, width)
        down_piece = cut_down[layer]
        for yy in range(sections):
            if yy != layer:
                got = lax.ppermute(cut_down[yy], "y", [(layer, yy)])
                down_piece = jnp.where(y == yy, got, down_piece)
        cut_out = low_out.reshape(sections, small_out, width)
        out_piece = jnp.zeros((small_out, width), LOW)
        for p, route in enumerate(out_routes(layer)):
            got = lax.ppermute(cut_out[p], ALL, route)
            out_piece = jnp.where(out_part == p, got, out_piece)
        tail = jnp.concatenate([down_piece, out_piece], 0)
        tail = across_gather(tail, x, h0, ffn_part, att0)
        w_down = tail[:, :, :part_ff].reshape(shard_ff, width)
        w_out = tail[:, :, part_ff:].reshape(shard_width, width)
        mine = over_k[:, :, layer]
        for yy in range(sections):
            if yy != layer:
                got = lax.ppermute(over_k[:, :, yy], "y", [(layer, yy)])
                mine = jnp.where(y == yy, got, mine)
        whole = across_gather(mine, x, mixed, proj_table, h_low)
        w_in = whole.transpose(0, 2, 1, 3, 4, 5).reshape(width, -1)
        if shard_width < LANES:
            pad = LANES - shard_width
            cut = [w_in[:, j * shard_width : (j + 1) * shard_width] for j in range(3)]
            cut = [jnp.pad(piece, ((0, 0), (0, pad))) for piece in cut]
            w_in = jnp.concatenate(cut + [w_in[:, 3 * shard_width :]], 1)
            w_out = jnp.pad(w_out, ((0, pad), (0, 0)))
        shard_weights.append((w_in, w_out, w_down))

    kept = []
    for layer in range(1, sections):
        w_in, w_out, w_down = shard_weights[layer - 1]
        vec = vec_all[layer]
        gain, bias, bias_down = (vec[j * width : (j + 1) * width] for j in range(3))
        cut = vec[3 * width :].reshape(spans, 2, 2, 2, sections, part_ff)
        cut = lax.dynamic_index_in_dim(cut, k, 1, keepdims=False)
        cut = lax.dynamic_index_in_dim(cut, c, 2, keepdims=False)
        bias_up = lax.dynamic_index_in_dim(cut, y, 2, keepdims=False).reshape(shard_ff)
        if layer > 1:
            x_low = xs.astype(LOW)
            h_low = layer_norm(x_low.astype(F32), gain, bias)[0].astype(LOW)
        hs = to_group(h_low)
        keep, send, qkv, att, act, slope = upper_forward(
            hs, w_in, w_out, w_down, bias_up, group_rope, group_bias, slots
        )
        kept.append((x_low, gain, bias, hs, qkv, att, act, slope))
        pieces = from_group(keep, send)
        if layer < sections - 1:
            xs = x_low.astype(F32) + sum(piece.astype(F32) for piece in pieces) + bias_down

    normed_f, inverse_f, final_low, logp, lik_sum = loss_forward(
        x_low, pieces, bias_down, final_gain, final_bias, head_low, out_bias, target_hot, seq_weight
    )
    sums = spread(jnp.concatenate([lik_sum[0], seq_count]), ALL)
    dy, own_low, table_local, bias_local, down_sum, scalars = loss_backward(
        sums,
        partners,
        me[None],
        normed_f,
        inverse_f,
        final_low,
        logp,
        head_low,
        final_gain,
        target_hot,
        seq_weight,
        plane,
    )
    loss_total, count_total = scalars[0, 0], scalars[0, 1]
    penalty_local = jnp.where(y == 0, scalars[0, 2], 0.0)
    bias_local = bias_local[0]

    def finish_shards(layer, out_grad, down_grad, in_grad, first, second, last):
        tail = jnp.concatenate(
            [
                down_grad.reshape(spans, 2, part_ff, width),
                out_grad.reshape(spans, 2, small_out, width),
            ],
            2,
        )
        tail = across_scatter(tail, x, first, second, last).astype(LOW)
        down_piece, out_piece = tail[:part_ff], tail[part_ff:]
        down_rows = jnp.stack(
            [
                down_piece if yy == layer else lax.ppermute(down_piece, "y", [(yy, layer)])
                for yy in range(sections)
            ]
        ).reshape(own_ff, width)
        out_rows = jnp.stack(
            [
                lax.ppermute(out_piece, ALL, [(b, a) for a, b in route])
                for route in out_routes(layer)
            ]
        ).reshape(own_out, width)
        inner = in_grad.reshape(spans, 2, 2, 2, own_in, -1).transpose(0, 2, 1, 3, 4, 5)
        inner = across_scatter(inner, x, first, second, last).astype(LOW)
        keep = pick(inner, k)
        give = shift(pick(inner, 1 - k), "k", 1)
        over_k = ordered(keep, give, k, 1)
        keep = pick(over_k, c)
        give = shift(pick(over_k, 1 - c), "c", 1)
        over_c = ordered(keep, give, c, 0)
        shards = jnp.stack(
            [
                over_c if yy == layer else lax.ppermute(over_c, "y", [(yy, layer)])
                for yy in range(sections)
            ],
            2,
        )
        qkv_rows, up_rows = columns_back(shards)
        return (qkv_rows, out_rows, up_rows, down_rows)

    pending = []
    vector_locals = []
    for layer in range(sections - 1, 0, -1):
        w_in, w_out, w_down = shard_weights[layer - 1]
        x_low, gain, bias, hs, qkv, att, act, slope = kept[layer - 1]
        d_rows = to_group(own_low)
        keep, send, d_in, bias_up_grad = upper_backward(
            d_rows, qkv, slope, w_in, w_out, w_down, group_rope, group_bias, slots
        )
        pieces = from_group(keep, send)
        above = dy
        own_low, vec_sums, dyb_token = input_backward(pieces, x_low, dy, gain, hot_own)
        dy = own_low.astype(F32)
        att, act, hs, d_in, d_rows = lax.optimization_barrier((att, act, hs, d_in, d_rows, keep))[:5]
        out_grad = t_mm(att, d_rows)[:shard_width]
        down_grad = t_mm(act, d_rows)
        in_grad = t_mm(hs, d_in)
        if shard_width < LANES:
            cut = [in_grad[:, j * LANES : j * LANES + shard_width] for j in range(3)]
            in_grad = jnp.concatenate(cut + [in_grad[:, 3 * LANES :]], 1)
        bias_up_grad = bias_up_grad.reshape(spans, 2, part_ff)
        place = (
            (jnp.arange(2) == k)[None, :, None, None, None, None]
            & (jnp.arange(2) == c)[None, None, None, :, None, None]
            & (jnp.arange(sections) == y)[None, None, None, None, :, None]
        )
        bias_up_grad = jnp.where(place, bias_up_grad[:, None, :, None, None, :], 0.0)
        vector_locals.append(
            jnp.concatenate([vec_sums[0], vec_sums[1], down_sum[0], bias_up_grad.reshape(-1)])
        )
        down_sum = vec_sums[2:3]
        pending.append((layer, out_grad, down_grad, in_grad, keep))
    vector_locals = vector_locals[::-1]

    dyb_cols = trade(dyb_token.reshape(vocab, everyone, -1).transpose(1, 0, 2), ALL)
    dq_token, dk_token, dv_token, first_out_grad = first_backward(
        own_low,
        query0,
        keys0,
        values0,
        att0,
        hot_own,
        hot_pack,
        own_rope,
        pack_rope,
        own_bias,
        first_out,
        own_packs,
    )
    dyb_cols = jnp.sum(after(dyb_cols, first_out_grad), 0)
    dyb_sum = spread(dyb_cols, ALL).transpose(1, 0, 2).reshape(vocab, width)
    token_part = jnp.concatenate([dq_token, dk_token, dv_token], 1)
    token_cols = trade(token_part.reshape(vocab, everyone, -1).transpose(1, 0, 2), ALL)
    token_cols = jnp.sum(token_cols, 0).astype(LOW)
    du_own = (mm_exact(dyb_sum, low_down, ((1,), (1,))) * slope0).astype(LOW)
    du_sum = spread(du_own, PLANE).transpose(1, 0, 2).reshape(vocab, hidden)
    dproj_sum = spread(token_cols, ALL).transpose(1, 0, 2).reshape(vocab, 3 * width)
    dh_own = mm_t(dproj_sum, low_qkv) + mm_t(du_sum, low_up)

    shard_grads = [None] * sections
    for layer, out_grad, down_grad, in_grad, keep in pending:
        shard_grads[layer] = finish_shards(
            layer, out_grad, down_grad, in_grad, own_low, first_out_grad, du_own
        )
    vector_cut = jnp.stack([jnp.zeros_like(vector_locals[0])] + vector_locals)
    vector_cut = vector_cut.reshape(everyone, vector_part)
    table_cut = table_local.reshape(-1, everyone, table_part).transpose(1, 0, 2)
    mixed = jnp.concatenate([vector_cut, table_cut.reshape(everyone, -1)], 1)
    mixed = jnp.sum(trade(after(mixed, first_out_grad), ALL), 0)
    h0_own = lax.dynamic_slice_in_dim(h0, me * own_in, own_in, 1)
    down_first = mm_exact(a0, dyb_sum, ((0,), (0,)))
    qkv_first = t_mm(h0_own, dproj_sum)
    up_first = t_mm(h0_own, du_sum)
    part = first_out_grad.reshape(spans, 2, 2, 2, own_out, width)
    part = jnp.moveaxis(part, 3, 0)
    part = pick(part, c) + shift(pick(part, 1 - c).astype(LOW), "c", 1).astype(F32)
    part = jnp.moveaxis(part, 2, 0)
    part = pick(part, x) + shift(pick(part, 1 - x).astype(LOW), "x", 1).astype(F32)
    part = jnp.moveaxis(part, 1, 0)
    part = pick(part, k) + shift(pick(part, 1 - k).astype(LOW), "k", 1).astype(F32)
    total = pick(part, h)
    for s in range(1, spans):
        total = total + shift(pick(part, (h + s) % spans).astype(LOW), "h", s).astype(F32)
    out_first = total
    for yy in range(1, sections):
        out_first = out_first + lax.ppermute(total.astype(LOW), "y", [(yy, 0)]).astype(F32)

    first = (qkv_first, out_first, up_first, down_first)
    grads = []
    for number in range(4):
        grad = first[number]
        for layer in range(1, sections):
            grad = jnp.where(y == layer, shard_grads[layer][number].astype(F32), grad)
        grads.append(grad[None])
    mixed_vector = mixed[:vector_part]
    mixed_table = mixed[vector_part:].reshape(-1, table_part)

    squares = sum((jnp.sum(g * g) for g in grads)) + jnp.sum(mixed_table * mixed_table)
    squares = squares + jnp.where(y == 0, 0.0, jnp.sum(mixed_vector * mixed_vector))
    up_sum = jnp.sum(du_sum.astype(F32), 0)
    down_sum = jnp.sum(dyb_sum, 0)
    squares = squares + jnp.where(
        (y == 0) & (me == 0), jnp.sum(up_sum * up_sum) + jnp.sum(down_sum * down_sum), 0.0
    )
    last = jnp.concatenate([squares[None], penalty_local[None], bias_local])
    last = jnp.pad(last, (0, (-last.shape[0]) % own_in)).reshape(-1, own_in)
    last = spread(jnp.concatenate([dh_own, last], 0), ALL)
    dh = last[:plane, :vocab].transpose(1, 0, 2).reshape(vocab, width)
    last = jnp.sum(last[:, vocab:], 0).reshape(-1)
    embed_grad = dyb_sum + norm_back(dh, normed0, inverse0, gain0)
    gain_grad, shift_grad = jnp.sum(dh * normed0, 0), jnp.sum(dh, 0)
    vector_first = jnp.concatenate([gain_grad, shift_grad, down_sum, up_sum])
    vector_own = lax.dynamic_slice_in_dim(vector_first, me * vector_part, vector_part, 0)
    vector_grad = jnp.where(y == 0, vector_own, mixed_vector)
    number = y * plane + me
    embed_own = lax.dynamic_slice_in_dim(embed_grad, number * table_part, table_part, 1)
    table_grad = jnp.concatenate([embed_own, mixed_table], 0)
    penalty = last[1]
    bias_grad = last[2 : 2 + vocab]
    squares = last[0] + jnp.sum(embed_grad * embed_grad) + jnp.sum(bias_grad * bias_grad)
    squares = squares + jnp.sum(gain_grad * gain_grad) + jnp.sum(shift_grad * shift_grad)
    grad_norm = jnp.sqrt(squares)
    factor = jnp.minimum(1.0, CLIP_AT / grad_norm)
    grads = grads + [vector_grad[None], table_grad, bias_grad]
    masters = (qkv_weight, out_weight, up_weight, down_weight, vectors, tables, head_bias)
    moments = (
        qkv_moment,
        out_moment,
        up_moment,
        down_moment,
        vector_moment,
        table_moment,
        bias_moment,
    )
    squares_in = (
        qkv_square,
        out_square,
        up_square,
        down_square,
        vector_square,
        table_square,
        bias_square,
    )
    rates = (RATE_MAT, RATE_OUT, RATE_MAT, RATE_MAT, RATE_VEC, RATE_VEC, RATE_VEC)
    decays = (DECAY, DECAY, DECAY, DECAY, 0.0, 0.0, 0.0)
    results = []
    for number in range(7):
        results.extend(
            adam(
                masters[number],
                moments[number],
                squares_in[number],
                grads[number] * factor,
                rates[number],
                decays[number],
            )
        )
    loss_parts = jnp.stack([loss_total, count_total, penalty])
    return (grad_norm, loss_parts, *results)


def solution(mesh):
    sections, plane = mesh.shape["section"], mesh.shape["dp"]
    fine = Mesh(mesh.devices.reshape(sections, plane // 8, 2, 2, 2), ALL)
    matrix = P("y", PLANE, None)
    vector = P("y", PLANE)
    table = P(None, ALL)
    states = (matrix, matrix, matrix, matrix, vector, table, P())
    results = []
    for spec in states:
        results.extend([spec] * 3)
    chosen = body_fast if (sections, plane) == (2, 16) else body
    return jax.shard_map(
        chosen,
        mesh=fine,
        in_specs=(P(PLANE, None), P(PLANE, None), P(PLANE, None), P(PLANE))
        + states
        + states
        + states,
        out_specs=(P(), P(), *results),
        check_vma=False,
    )
```

```python
import math

import jax
import jax.numpy as jnp
import numpy as np
from jax import lax
from jax.experimental import pallas as pl
from jax.experimental.pallas import tpu as pltpu
from jax.sharding import Mesh
from jax.sharding import PartitionSpec as P

HEAD = 64
ROT = 32
STEP = 10

EPS_NORM = 1e-05
PENALTY = 2.0
CLIP_AT = 0.02
RATE_MAT = 0.02
RATE_OUT = 0.1
RATE_VEC = 0.2
BETA_ONE = 0.9
BETA_TWO = 0.95
EPS_ADAM = 1e-08
DECAY = 0.1
GELU_C = 0.7978845608028654

ALL = ("y", "h", "k", "x", "c")
PLANE = ("h", "k", "x", "c")
LOW = jnp.bfloat16
F32 = jnp.float32
EXACT = lax.Precision.HIGHEST


def mm(left, right):
    return jnp.dot(left, right, preferred_element_type=F32)


def mm_t(left, right):
    return lax.dot_general(left, right, (((1,), (1,)), ((), ())), preferred_element_type=F32)


def t_mm(left, right):
    return lax.dot_general(left, right, (((0,), (0,)), ((), ())), preferred_element_type=F32)


def mm_exact(left, right, dims):
    return lax.dot_general(
        left.astype(F32), right.astype(F32), (dims, ((), ())), precision=EXACT
    )


def pick(array, index):
    return lax.dynamic_index_in_dim(array, index, 0, keepdims=False)


def spread(value, axes):
    many = lax.axis_size(axes)
    return lax.all_to_all(jnp.broadcast_to(value[None], (many,) + value.shape), axes, 0, 0, tiled=True)


def trade(pieces, axes):
    return lax.all_to_all(pieces, axes, 0, 0, tiled=True)


def shift(value, axis, by):
    many = lax.axis_size(axis)
    return lax.ppermute(value, axis, [(i, (i + by) % many) for i in range(many)])


def after(value, *earlier):
    return lax.optimization_barrier((value,) + earlier)[0]


def together(*values):
    return lax.optimization_barrier(values)


def ordered(own, other, bit, axis):
    return jnp.stack(
        [jnp.where(bit == 0, own, other), jnp.where(bit == 0, other, own)], axis
    )


def layer_norm(x, gain, bias):
    mean = jnp.mean(x, -1, keepdims=True)
    centred = x - mean
    inverse = lax.rsqrt(jnp.mean(centred * centred, -1, keepdims=True) + EPS_NORM)
    normed = centred * inverse
    return (normed * gain + bias, normed, inverse)


def norm_back(grad, normed, inverse, gain):
    scaled = grad * gain
    return inverse * (
        scaled
        - jnp.mean(scaled, -1, keepdims=True)
        - normed * jnp.mean(scaled * normed, -1, keepdims=True)
    )


def gelu_pair(value):
    inner = jnp.tanh(GELU_C * (value + 0.044715 * value * value * value))
    result = 0.5 * value * (1.0 + inner)
    slope = 0.5 * (1.0 + inner) + 0.5 * value * (1.0 - inner * inner) * GELU_C * (
        1.0 + 3.0 * 0.044715 * value * value
    )
    return (result, slope)


def one_hot(row, vocab, dtype):
    return (row[:, None] == jnp.arange(vocab, dtype=jnp.int32)[None, :]).astype(dtype)


def pack_layout(lengths_row, slots):
    ends = jnp.cumsum(lengths_row)
    starts = ends - lengths_row
    index = jnp.arange(slots, dtype=jnp.int32)
    segment = jnp.sum((index[:, None] >= ends[None, :]).astype(jnp.int32), 1)
    member = segment[:, None] == jnp.arange(lengths_row.shape[0], dtype=jnp.int32)[None, :]
    position = index - jnp.sum(jnp.where(member, starts[None, :], 0), 1)
    return (segment, position)


LANES = 128
VMEM_LIMIT = 28 * 1024 * 1024
VMEM_MOST = 60 * 1024 * 1024
SCALE = 1.0 / math.sqrt(HEAD)


def rope_rows(position):
    half = ROT // 2
    freq = 10000.0 ** (-2.0 * jnp.arange(half, dtype=F32) / ROT)
    angle = position.astype(F32)[:, None] * freq
    cosine, sine = (jnp.cos(angle), jnp.sin(angle))
    none, one = (jnp.zeros_like(sine), jnp.ones_like(sine))
    many = LANES // HEAD
    rest = HEAD // half - 2
    return jnp.stack(
        [
            jnp.concatenate(([cosine, cosine] + [one] * rest) * many, 1),
            jnp.concatenate(([-sine, none] + [none] * rest) * many, 1),
            jnp.concatenate(([none, sine] + [none] * rest) * many, 1),
        ]
    )


def turn_by(value, rope, sign):
    above = pltpu.roll(value, LANES - ROT // 2, 1)
    below = pltpu.roll(value, ROT // 2, 1)
    return value * rope[0] + sign * (above * rope[1] + below * rope[2])


def head_lanes(shape):
    lane = lax.broadcasted_iota(jnp.int32, shape, 1)
    return [(lane // HEAD) == number for number in range(LANES // HEAD)]


def soft(query, keys, bias):
    scores = mm_t(query, keys) * SCALE + bias
    expo = jnp.exp(scores - jnp.max(scores, -1, keepdims=True))
    return expo / jnp.sum(expo, -1, keepdims=True)


def attend_pair(query, keys, values, bias):
    out = jnp.zeros(query.shape, F32)
    nothing = jnp.zeros((), LOW)
    for mine_q, mine_k in zip(head_lanes(query.shape), head_lanes(keys.shape)):
        probs = soft(jnp.where(mine_q, query, nothing), keys, bias).astype(LOW)
        out = out + mm(probs, jnp.where(mine_k, values, nothing))
    return out.astype(LOW)


def attend_pair_back(d_out, query, keys, values, bias):
    d_query = jnp.zeros(query.shape, F32)
    d_keys = jnp.zeros(keys.shape, F32)
    d_values = jnp.zeros(keys.shape, F32)
    nothing = jnp.zeros((), LOW)
    for mine_q, mine_k in zip(head_lanes(query.shape), head_lanes(keys.shape)):
        query_h = jnp.where(mine_q, query, nothing)
        d_out_h = jnp.where(mine_q, d_out, nothing)
        probs = soft(query_h, keys, bias)
        d_values = d_values + t_mm(probs.astype(LOW), d_out_h)
        d_probs = mm_t(d_out_h, values)
        d_scores = probs * (d_probs - jnp.sum(probs * d_probs, -1, keepdims=True))
        d_scores = d_scores.astype(LOW)
        d_query = d_query + mm(d_scores, jnp.where(mine_k, keys, nothing))
        d_keys = d_keys + t_mm(d_scores, query_h)
    return (d_query * SCALE, d_keys * SCALE, d_values)


def whole_spec(shape):
    return pl.BlockSpec(shape, lambda *_: (0,) * len(shape))


def params(limit=VMEM_LIMIT):
    return pltpu.CompilerParams(vmem_limit_bytes=limit)


def upper_forward(hs, w_in, w_out, w_down, bias_up, rope, bias, slots):
    total, width = hs.shape
    lanes, units = (w_out.shape[0], w_down.shape[0])
    step = total // 2

    def kernel(h_ref, win_ref, wout_ref, wdown_ref, bup_ref, rope_ref, bias_ref, keep_ref, send_ref, qkv_ref, att_ref, act_ref, slope_ref):
        h = h_ref[...]
        proj = mm(h, win_ref[:, : 3 * lanes])
        for g in range(lanes // LANES):
            spans = [slice(j * lanes + g * LANES, j * lanes + (g + 1) * LANES) for j in range(3)]
            qkv_ref[:, spans[0]] = turn_by(proj[:, spans[0]], rope_ref, 1.0).astype(LOW)
            qkv_ref[:, spans[1]] = turn_by(proj[:, spans[1]], rope_ref, 1.0).astype(LOW)
            qkv_ref[:, spans[2]] = proj[:, spans[2]].astype(LOW)
            for pack in range(step // slots):
                here = slice(pack * slots, (pack + 1) * slots)
                q, k, v = (qkv_ref[here, spans[j]] for j in range(3))
                att_ref[here, g * LANES : (g + 1) * LANES] = attend_pair(q, k, v, bias_ref[here, :])
        act, slope = gelu_pair(mm(h, win_ref[:, 3 * lanes :]) + bup_ref[...])
        act = act.astype(LOW)
        act_ref[...] = act
        slope_ref[...] = slope
        out = mm(att_ref[...], wout_ref[...]) + mm(act, wdown_ref[...])

        @pl.when(pl.program_id(0) == 0)
        def _():
            send_ref[...] = out.astype(LOW)

        @pl.when(pl.program_id(0) == 1)
        def _():
            keep_ref[...] = out

    def by_rows(columns):
        return pl.BlockSpec((step, columns), lambda s: (1 - s, 0))

    return pl.pallas_call(
        kernel,
        grid=(2,),
        in_specs=[
            by_rows(width),
            whole_spec(w_in.shape),
            whole_spec(w_out.shape),
            whole_spec(w_down.shape),
            whole_spec((1, units)),
            pl.BlockSpec((3, step, LANES), lambda s: (0, 1 - s, 0)),
            by_rows(slots),
        ],
        out_specs=[
            whole_spec((step, width)),
            whole_spec((step, width)),
            by_rows(3 * lanes),
            by_rows(lanes),
            by_rows(units),
            by_rows(units),
        ],
        out_shape=[
            jax.ShapeDtypeStruct((step, width), F32),
            jax.ShapeDtypeStruct((step, width), LOW),
            jax.ShapeDtypeStruct((total, 3 * lanes), LOW),
            jax.ShapeDtypeStruct((total, lanes), LOW),
            jax.ShapeDtypeStruct((total, units), LOW),
            jax.ShapeDtypeStruct((total, units), F32),
        ],
        compiler_params=params(),
        name="upper_forward",
    )(hs, w_in, w_out, w_down, bias_up[None], rope, bias)


def upper_backward(d_rows, qkv, slope, w_in, w_out, w_down, rope, bias, slots):
    total, width = d_rows.shape
    lanes, units = (w_out.shape[0], w_down.shape[0])
    step = total // 2

    def kernel(d_ref, qkv_ref, slope_ref, win_ref, wout_ref, wdown_ref, rope_ref, bias_ref, keep_ref, send_ref, din_ref, sum_ref):
        d_out = d_ref[...]
        d_att = mm_t(d_out, wout_ref[...]).astype(LOW)
        d_pre = (mm_t(d_out, wdown_ref[...]) * slope_ref[...]).astype(LOW)
        din_ref[:, 3 * lanes :] = d_pre
        sums = jnp.sum(d_pre.astype(F32), 0, keepdims=True)
        for g in range(lanes // LANES):
            spans = [slice(j * lanes + g * LANES, j * lanes + (g + 1) * LANES) for j in range(3)]
            for pack in range(step // slots):
                here = slice(pack * slots, (pack + 1) * slots)
                q, k, v = (qkv_ref[here, spans[j]] for j in range(3))
                dq, dk, dv = attend_pair_back(
                    d_att[here, g * LANES : (g + 1) * LANES], q, k, v, bias_ref[here, :]
                )
                turned = [rope_ref[j, here, :] for j in range(3)]
                din_ref[here, spans[0]] = turn_by(dq, turned, -1.0).astype(LOW)
                din_ref[here, spans[1]] = turn_by(dk, turned, -1.0).astype(LOW)
                din_ref[here, spans[2]] = dv.astype(LOW)
        d_norm = mm_t(din_ref[...], win_ref[...])

        @pl.when(pl.program_id(0) == 0)
        def _():
            send_ref[...] = d_norm.astype(LOW)
            sum_ref[...] = sums

        @pl.when(pl.program_id(0) == 1)
        def _():
            keep_ref[...] = d_norm
            sum_ref[...] += sums

    def by_rows(columns):
        return pl.BlockSpec((step, columns), lambda s: (1 - s, 0))

    return pl.pallas_call(
        kernel,
        grid=(2,),
        in_specs=[
            by_rows(width),
            by_rows(3 * lanes),
            by_rows(units),
            whole_spec(w_in.shape),
            whole_spec(w_out.shape),
            whole_spec(w_down.shape),
            pl.BlockSpec((3, step, LANES), lambda s: (0, 1 - s, 0)),
            by_rows(slots),
        ],
        out_specs=[
            whole_spec((step, width)),
            whole_spec((step, width)),
            by_rows(3 * lanes + units),
            whole_spec((1, units)),
        ],
        out_shape=[
            jax.ShapeDtypeStruct((step, width), F32),
            jax.ShapeDtypeStruct((step, width), LOW),
            jax.ShapeDtypeStruct((total, 3 * lanes + units), LOW),
            jax.ShapeDtypeStruct((1, units), F32),
        ],
        compiler_params=params(),
        name="upper_backward",
    )(d_rows, qkv, slope, w_in, w_out, w_down, rope, bias)


def exact_rows(hot, table):
    high = table.astype(LOW)
    rest = table - high.astype(F32)
    middle = rest.astype(LOW)
    lowest = (rest - middle.astype(F32)).astype(LOW)
    return mm(hot, high) + (mm(hot, middle) + mm(hot, lowest))


def first_forward(table, hot_own, hot_pack, rope_own, rope_pack, bias, packs):
    vocab = table.shape[0]
    width = table.shape[1] // 3
    pairs = width // LANES
    own_rows = hot_own.shape[0] // packs
    pack_rows = hot_pack.shape[0] // packs

    def kernel(tq_ref, tk_ref, tv_ref, hot_ref, hotp_ref, ro_ref, rp_ref, bias_ref, q_ref, k_ref, v_ref, att_ref):
        hot = hot_ref[...]
        hotp = hotp_ref[...]
        q = turn_by(exact_rows(hot, tq_ref[...]), ro_ref, 1.0).astype(LOW)
        k = turn_by(exact_rows(hotp, tk_ref[...]), rp_ref, 1.0).astype(LOW)
        v = mm(hotp, tv_ref[...].astype(LOW)).astype(LOW)
        q_ref[...] = q
        k_ref[...] = k
        v_ref[...] = v
        att_ref[...] = attend_pair(q, k, v, bias_ref[...])

    def table_spec(which):
        return pl.BlockSpec((vocab, LANES), lambda p, j: (0, which * pairs + j))

    def rows_spec(many, columns):
        return pl.BlockSpec((many, columns), lambda p, j: (p, 0))

    def rope_spec(many):
        return pl.BlockSpec((3, many, LANES), lambda p, j: (0, p, 0))

    def pair_spec(many):
        return pl.BlockSpec((many, LANES), lambda p, j: (p, j))

    owned, packed = (hot_own.shape[0], hot_pack.shape[0])
    return pl.pallas_call(
        kernel,
        grid=(packs, pairs),
        in_specs=[
            table_spec(0),
            table_spec(1),
            table_spec(2),
            rows_spec(own_rows, vocab),
            rows_spec(pack_rows, vocab),
            rope_spec(own_rows),
            rope_spec(pack_rows),
            rows_spec(own_rows, pack_rows),
        ],
        out_specs=[
            pair_spec(own_rows),
            pair_spec(pack_rows),
            pair_spec(pack_rows),
            pair_spec(own_rows),
        ],
        out_shape=[
            jax.ShapeDtypeStruct((owned, width), LOW),
            jax.ShapeDtypeStruct((packed, width), LOW),
            jax.ShapeDtypeStruct((packed, width), LOW),
            jax.ShapeDtypeStruct((owned, width), LOW),
        ],
        compiler_params=params(),
        name="first_forward",
    )(table, table, table, hot_own, hot_pack, rope_own, rope_pack, bias)


def cost(microseconds):
    return pl.CostEstimate(flops=max(1, int(microseconds * 1e9 * 1.0)), bytes_accessed=0, transcendentals=0)


def simple(kernel, name, outs, *args, smem=(), us=1.0, scratch=(), behind=(), limit=VMEM_LIMIT):
    specs = [
        pl.BlockSpec(memory_space=pltpu.SMEM) if i in smem else whole_spec(arg.shape)
        for i, arg in enumerate(args)
    ]
    many, unread = (len(args), len(behind))

    def run(*refs):
        kernel(*refs[:many], *refs[many + unread :])

    return pl.pallas_call(
        run,
        grid=(1,),
        in_specs=specs + [pl.BlockSpec(memory_space=pl.ANY)] * unread,
        out_specs=[whole_spec(shape) for shape, _ in outs],
        out_shape=[jax.ShapeDtypeStruct(shape, kind) for shape, kind in outs],
        scratch_shapes=list(scratch),
        compiler_params=params(limit),
        cost_estimate=cost(us),
        name=name,
    )(*args, *behind)


def first_finish(att, first_out, hot, stay, gain, bias):
    rows, width = att.shape

    def kernel(att_ref, out_ref, hot_ref, stay_ref, gain_ref, bias_ref, x_ref, h_ref):
        x = mm(att_ref[...], out_ref[...]) + exact_rows(hot_ref[...], stay_ref[...])
        x = x.astype(LOW)
        x_ref[...] = x
        h_ref[...] = layer_norm(x.astype(F32), gain_ref[...], bias_ref[...])[0].astype(LOW)

    outs = [((rows, width), LOW), ((rows, width), LOW)]
    return simple(kernel, "first_finish", outs, att, first_out, hot, stay, gain[None], bias[None])


def loss_forward(base, pieces, bias_down, gain, bias, head_low, out_bias, target_hot, seq_weight):
    rows, width = base.shape
    vocab = head_low.shape[0]
    seqs = seq_weight.shape[1]

    def kernel(x_ref, *refs):
        piece_refs = refs[: len(pieces)]
        down_ref, gain_ref, bias_ref, head_ref, hbias_ref, hot_ref, seq_ref = refs[len(pieces) : -5]
        norm_ref, inv_ref, final_ref, logp_ref, lik_ref = refs[-5:]
        x = x_ref[...].astype(F32)
        for ref in piece_refs:
            x = x + ref[...].astype(F32)
        out, normed, inverse = layer_norm(x + down_ref[...], gain_ref[...], bias_ref[...])
        norm_ref[...] = normed
        inv_ref[...] = inverse
        final = out.astype(LOW)
        final_ref[...] = final
        logits = mm_t(final, head_ref[...]) + hbias_ref[...]
        top = jnp.max(logits, -1, keepdims=True)
        logp = logits - (top + jnp.log(jnp.sum(jnp.exp(logits - top), -1, keepdims=True)))
        logp_ref[...] = logp
        picked = jnp.sum(hot_ref[...] * logp, 1, keepdims=True)
        lik_ref[...] = jnp.sum(seq_ref[...] * picked, 0, keepdims=True)

    outs = [
        ((rows, width), F32),
        ((rows, 1), F32),
        ((rows, width), LOW),
        ((rows, vocab), F32),
        ((1, seqs), F32),
    ]
    return simple(
        kernel,
        "loss_forward",
        outs,
        base,
        *pieces,
        bias_down[None],
        gain[None],
        bias[None],
        head_low,
        out_bias[None],
        target_hot,
        seq_weight,
    )


def loss_backward(sums, partners, place, normed, inverse, final_low, logp, head_low, gain, target_hot, seq_weight, plane):
    rows, width = normed.shape
    vocab = head_low.shape[0]
    seqs = seq_weight.shape[1]
    devices = sums.shape[0]
    total_seqs = plane * seqs

    def kernel(sums_ref, partner_ref, place_ref, norm_ref, inv_ref, final_ref, logp_ref, head_ref, gain_ref, hot_ref, seq_ref, dy_ref, low_ref, table_ref, bias_ref, down_ref, scalar_ref):
        got = sums_ref[...]
        row = lax.broadcasted_iota(jnp.int32, got.shape, 0)
        column = lax.broadcasted_iota(jnp.int32, got.shape, 1)
        owner = lax.rem(row, plane)
        is_sum = column < seqs
        is_count = (column >= seqs) & (row < plane)
        loss = -jnp.sum(jnp.where(is_sum, got, 0.0))
        count = jnp.sum(jnp.where(is_count, got, 0.0))

        def likelihood(device, number):
            here = owner == device
            amount = jnp.sum(jnp.where(here & is_count & (column == seqs + number), got, 0.0))
            amount = jnp.maximum(amount, 1.0)
            total = jnp.sum(jnp.where(here & (column == number), got, 0.0))
            return (total / amount, amount)

        coeff = jnp.zeros((rows, 1), F32)
        penalty = 0.0
        for number in range(seqs):
            mine, amount = likelihood(place_ref[0], number)
            partner = partner_ref[number]
            other, _ = likelihood(partner // seqs, lax.rem(partner, seqs))
            differ = mine - other
            penalty = penalty + 0.5 * differ * differ
            term = -1.0 / count + PENALTY * 2.0 * differ / total_seqs / amount
            coeff = coeff + seq_ref[:, number : number + 1] * term
        d_logits = (coeff * (hot_ref[...] - jnp.exp(logp_ref[...]))).astype(LOW)
        d_final = mm(d_logits, head_ref[...])
        normed = norm_ref[...]
        dy = norm_back(d_final, normed, inv_ref[...], gain_ref[...])
        dy_ref[...] = dy
        low = dy.astype(LOW)
        low_ref[...] = low
        table_ref[:vocab, :] = t_mm(d_logits, final_ref[...])
        table_ref[vocab : vocab + 1, :] = jnp.sum(d_final * normed, 0, keepdims=True)
        table_ref[vocab + 1 : vocab + 2, :] = jnp.sum(d_final, 0, keepdims=True)
        bias_ref[...] = jnp.sum(d_logits.astype(F32), 0, keepdims=True)
        down_ref[...] = jnp.sum(low.astype(F32), 0, keepdims=True)
        lane = lax.broadcasted_iota(jnp.int32, (1, LANES), 1)
        scalar_ref[...] = jnp.where(lane == 0, loss, jnp.where(lane == 1, count, penalty))

    outs = [
        ((rows, width), F32),
        ((rows, width), LOW),
        ((vocab + 2, width), F32),
        ((1, vocab), F32),
        ((1, width), F32),
        ((1, LANES), F32),
    ]
    return simple(
        kernel,
        "loss_backward",
        outs,
        sums,
        partners,
        place,
        normed,
        inverse,
        final_low,
        logp,
        head_low,
        gain[None],
        target_hot,
        seq_weight,
        smem=(1, 2),
    )


def input_backward(pieces, x_low, dy, gain, hot):
    rows, width = dy.shape
    vocab = hot.shape[1]

    def kernel(*refs):
        piece_refs = refs[: len(pieces)]
        x_ref, dy_ref, gain_ref, hot_ref, low_ref, vec_ref, token_ref = refs[len(pieces) :]
        d_norm = piece_refs[0][...]
        for ref in piece_refs[1:]:
            d_norm = d_norm + ref[...].astype(F32)
        gain_row = gain_ref[...]
        _, normed, inverse = layer_norm(x_ref[...].astype(F32), gain_row, 0.0)
        low = (dy_ref[...] + norm_back(d_norm, normed, inverse, gain_row)).astype(LOW)
        low_ref[...] = low
        vec_ref[0:1, :] = jnp.sum(d_norm * normed, 0, keepdims=True)
        vec_ref[1:2, :] = jnp.sum(d_norm, 0, keepdims=True)
        vec_ref[2:3, :] = jnp.sum(low.astype(F32), 0, keepdims=True)
        token_ref[...] = t_mm(hot_ref[...], low)

    outs = [((rows, width), LOW), ((3, width), F32), ((vocab, width), F32)]
    return simple(kernel, "input_backward", outs, *pieces, x_low, dy, gain[None], hot)


def first_backward(d_rows, query, keys, values, att, hot_own, hot_pack, rope_own, rope_pack, bias, first_out, packs):
    width = first_out.shape[0]
    vocab = hot_own.shape[1]
    pairs = width // LANES
    own_rows = hot_own.shape[0] // packs
    pack_rows = hot_pack.shape[0] // packs

    def kernel(d_ref, q_ref, k_ref, v_ref, att_ref, hot_ref, hotp_ref, ro_ref, rp_ref, bias_ref, out_ref, tq_ref, tk_ref, tv_ref, grad_ref):
        d_out = d_ref[...]
        d_att = mm_t(d_out, out_ref[...]).astype(LOW)
        dq, dk, dv = attend_pair_back(d_att, q_ref[...], k_ref[...], v_ref[...], bias_ref[...])
        dq = turn_by(dq, ro_ref, -1.0).astype(LOW)
        dk = turn_by(dk, rp_ref, -1.0).astype(LOW)
        hot = hot_ref[...]
        hotp = hotp_ref[...]
        parts = (t_mm(hot, dq), t_mm(hotp, dk), t_mm(hotp, dv.astype(LOW)), t_mm(att_ref[...], d_out))
        refs = (tq_ref, tk_ref, tv_ref, grad_ref)

        @pl.when(pl.program_id(1) == 0)
        def _():
            for ref, part in zip(refs, parts):
                ref[...] = part

        @pl.when(pl.program_id(1) > 0)
        def _():
            for ref, part in zip(refs, parts):
                ref[...] += part

    def rows_spec(many, columns):
        return pl.BlockSpec((many, columns), lambda j, p: (p, 0))

    def rope_spec(many):
        return pl.BlockSpec((3, many, LANES), lambda j, p: (0, p, 0))

    def pair_spec(many):
        return pl.BlockSpec((many, LANES), lambda j, p: (p, j))

    token_spec = pl.BlockSpec((vocab, LANES), lambda j, p: (0, j))
    return pl.pallas_call(
        kernel,
        grid=(pairs, packs),
        in_specs=[
            rows_spec(own_rows, width),
            pair_spec(own_rows),
            pair_spec(pack_rows),
            pair_spec(pack_rows),
            pair_spec(own_rows),
            rows_spec(own_rows, vocab),
            rows_spec(pack_rows, vocab),
            rope_spec(own_rows),
            rope_spec(pack_rows),
            rows_spec(own_rows, pack_rows),
            pl.BlockSpec((LANES, width), lambda j, p: (j, 0)),
        ],
        out_specs=[
            token_spec,
            token_spec,
            token_spec,
            pl.BlockSpec((LANES, width), lambda j, p: (j, 0)),
        ],
        out_shape=[
            jax.ShapeDtypeStruct((vocab, width), F32),
            jax.ShapeDtypeStruct((vocab, width), F32),
            jax.ShapeDtypeStruct((vocab, width), F32),
            jax.ShapeDtypeStruct((width, width), F32),
        ],
        compiler_params=params(),
        cost_estimate=cost(10.5),
        name="first_backward",
    )(d_rows, query, keys, values, att, hot_own, hot_pack, rope_own, rope_pack, bias, first_out)


def adam(weight, first, second, grad, rate, decay):
    first_new = BETA_ONE * first + (1.0 - BETA_ONE) * grad
    second_new = BETA_TWO * second + (1.0 - BETA_TWO) * grad * grad
    update = (
        first_new
        / (1.0 - BETA_ONE**STEP)
        / (jnp.sqrt(second_new / (1.0 - BETA_TWO**STEP)) + EPS_ADAM)
    )
    return (first_new, second_new, weight - rate * (update + decay * weight))


class Group:
    def __init__(self, sections, spans):
        self.sections = sections
        self.spans = spans
        self.offsets = [(dk, dy) for dk in range(2) for dy in range(sections)]

    def route(self, dk, dy, sign):
        s = self.sections
        return [
            (a * 2 + b, ((a + sign * dy) % s) * 2 + (b + sign * dk) % 2)
            for a in range(s)
            for b in range(2)
        ]

    def gather(self, value):
        pieces = []
        for dk, dy in self.offsets:
            piece = value
            if (dk, dy) != (0, 0):
                piece = lax.ppermute(value, ("y", "k"), self.route(dk, dy, 1))
            pieces.append(piece)
        mine = jnp.stack(pieces)
        return jnp.stack([mine, shift(mine, "c", 1)])

    def scatter(self, keep, send):
        mine = keep + shift(send, "c", 1).astype(F32)
        pieces = [mine[0]]
        for number, (dk, dy) in enumerate(self.offsets):
            if (dk, dy) != (0, 0):
                pieces.append(
                    lax.ppermute(mine[number].astype(LOW), ("y", "k"), self.route(dk, dy, -1))
                )
        return pieces


def across_gather(piece, x, first, second, last):
    spans = lax.axis_size("h")
    h = lax.axis_index("h")
    piece = after(piece, first)
    if spans == 2:
        both = ordered(piece, after(shift(piece, "h", 1), second), h, 0)
    else:
        stacked = jnp.stack([piece] + [shift(piece, "h", s) for s in range(1, spans)])
        both = jnp.take(stacked, (h - jnp.arange(spans)) % spans, axis=0)
    return ordered(both, after(shift(both, "x", 1), last), x, 1)


def across_scatter(parts, x, first, second, last):
    spans = lax.axis_size("h")
    h = lax.axis_index("h")
    flipped = jnp.swapaxes(parts, 0, 1)
    away = shift(after(pick(flipped, 1 - x).astype(LOW), first), "x", 1)
    mine = pick(flipped, x) + after(away, second).astype(F32)
    total = pick(mine, h)
    for s in range(1, spans):
        away = shift(pick(mine, (h + s) % spans).astype(LOW), "h", s)
        total = total + after(away, last).astype(F32)
    return total


def scalars_of(*values):
    return jnp.stack([jnp.asarray(v, jnp.int32) for v in values])


def flip(value, axes, bits):
    mask = 0
    for bit in bits:
        mask = 2 * mask + bit
    many = 2 ** len(bits)
    return lax.ppermute(value, axes, [(i, i ^ mask) for i in range(many)])


NEAR = [(0, 1), (1, 0), (1, 1)]
def fast_loss_forward(base, pieces, vec, low_tables, out_bias, target_hot, seq_weight, seq_count):
    rows, width = base.shape
    vocab = target_hot.shape[1]

    def kernel(x_ref, p0, p1, p2, p3, vec_ref, low_ref, hbias_ref, hot_ref, seq_ref, count_ref, norm_ref, inv_ref, final_ref, logp_ref, sums_ref):
        x = x_ref[...].astype(F32) + p0[...]
        x = x + p1[...].astype(F32) + p2[...].astype(F32) + p3[...].astype(F32)
        gain = low_ref[2 * vocab : 2 * vocab + 1, :].astype(F32)
        bias = low_ref[2 * vocab + 1 : 2 * vocab + 2, :].astype(F32)
        out, normed, inverse = layer_norm(x + vec_ref[1:2, 2 * width : 3 * width], gain, bias)
        norm_ref[...] = normed
        inv_ref[...] = inverse
        final = out.astype(LOW)
        final_ref[...] = final
        logits = mm_t(final, low_ref[vocab : 2 * vocab, :]) + hbias_ref[...].astype(LOW).astype(F32)
        top = jnp.max(logits, -1, keepdims=True)
        logp = logits - (top + jnp.log(jnp.sum(jnp.exp(logits - top), -1, keepdims=True)))
        logp_ref[...] = logp
        picked = jnp.sum(hot_ref[...] * logp, 1, keepdims=True)
        row = jnp.sum(seq_ref[...] * picked, 0, keepdims=True)
        counts = count_ref[...]
        line = lax.broadcasted_iota(jnp.int32, counts.shape, 0)
        lane = lax.broadcasted_iota(jnp.int32, counts.shape, 1)
        seqs = counts.shape[0]
        row = row + jnp.sum(jnp.where(lane == line + seqs, counts, 0.0), 0, keepdims=True)
        sums_ref[...] = row

    outs = [
        ((rows, width), F32),
        ((rows, 1), F32),
        ((rows, width), LOW),
        ((rows, vocab), F32),
        ((1, LANES), F32),
    ]
    return simple(
        kernel,
        "loss_forward",
        outs,
        base,
        *pieces,
        vec,
        low_tables,
        out_bias[None],
        target_hot,
        seq_weight,
        seq_count,
    )


def fast_loss_backward(sums, partners, place, normed, inverse, final_low, logp, low_tables, target_hot, seq_weight, plane, seqs):
    rows, width = normed.shape
    vocab = target_hot.shape[1]
    total_seqs = plane * seqs

    def kernel(sums_ref, partner_ref, place_ref, norm_ref, inv_ref, final_ref, logp_ref, low_ref, hot_ref, seq_ref, dy_ref, low_out_ref, table_ref, ends_ref, bias_ref, down_ref, scalar_ref):
        got = sums_ref[...]
        row = lax.broadcasted_iota(jnp.int32, got.shape, 0)
        column = lax.broadcasted_iota(jnp.int32, got.shape, 1)
        owner = lax.rem(row, plane)
        is_sum = column < seqs
        is_count = (column >= seqs) & (column < 2 * seqs) & (row < plane)
        loss = -jnp.sum(jnp.where(is_sum, got, 0.0))
        count = jnp.sum(jnp.where(is_count, got, 0.0))

        def likelihood(device, number):
            here = owner == device
            amount = jnp.sum(jnp.where(here & is_count & (column == seqs + number), got, 0.0))
            amount = jnp.maximum(amount, 1.0)
            total = jnp.sum(jnp.where(here & (column == number), got, 0.0))
            return (total / amount, amount)

        coeff = jnp.zeros((rows, 1), F32)
        penalty = 0.0
        for number in range(seqs):
            mine, amount = likelihood(place_ref[5], number)
            partner = partner_ref[number]
            other, _ = likelihood(partner // seqs, lax.rem(partner, seqs))
            differ = mine - other
            penalty = penalty + 0.5 * differ * differ
            term = -1.0 / count + PENALTY * 2.0 * differ / total_seqs / amount
            coeff = coeff + seq_ref[:, number : number + 1] * term
        d_logits = (coeff * (hot_ref[...] - jnp.exp(logp_ref[...]))).astype(LOW)
        d_final = mm(d_logits, low_ref[vocab : 2 * vocab, :])
        normed = norm_ref[...]
        gain = low_ref[2 * vocab : 2 * vocab + 1, :].astype(F32)
        dy = norm_back(d_final, normed, inv_ref[...], gain)
        dy_ref[...] = dy
        low = dy.astype(LOW)
        low_out_ref[...] = low
        line = lax.broadcasted_iota(jnp.int32, (8, width), 0)
        ends = jnp.where(
            line == 0,
            jnp.sum(d_final * normed, 0, keepdims=True),
            jnp.where(line == 1, jnp.sum(d_final, 0, keepdims=True), 0.0),
        )
        ends_ref[...] = ends
        grads = jnp.concatenate(
            [t_mm(d_logits, final_ref[...]), jnp.zeros((LANES - vocab, width), F32)], 0
        )
        table_ref[...] = grads.T
        bias_ref[...] = jnp.sum(d_logits.astype(F32), 0, keepdims=True)
        down_ref[...] = jnp.sum(low.astype(F32), 0, keepdims=True)
        lane = lax.broadcasted_iota(jnp.int32, (1, LANES), 1)
        scalar_ref[...] = jnp.where(lane == 0, loss, jnp.where(lane == 1, count, penalty))

    outs = [
        ((rows, width), F32),
        ((rows, width), LOW),
        ((width, LANES), F32),
        ((8, width), F32),
        ((1, vocab), F32),
        ((1, width), F32),
        ((1, LANES), F32),
    ]
    return simple(
        kernel,
        "loss_backward",
        outs,
        sums,
        partners,
        place,
        normed,
        inverse,
        final_low,
        logp,
        low_tables,
        target_hot,
        seq_weight,
        smem=(1, 2),
    )


def rope_constant(slots):
    half = ROT // 2
    freq = np.float32(10000.0) ** (np.float32(-2.0) * np.arange(half, dtype=np.float32) / ROT)
    angle = np.arange(slots, dtype=np.float32)[:, None] * freq.astype(np.float32)
    cosine = np.cos(angle.astype(np.float64)).astype(np.float32)
    sine = np.sin(angle.astype(np.float64)).astype(np.float32)
    none, one = (np.zeros_like(sine), np.ones_like(sine))
    many = LANES // HEAD
    rest = HEAD // half - 2
    return np.stack(
        [
            np.concatenate(([cosine, cosine] + [one] * rest) * many, 1),
            np.concatenate(([-sine, none] + [none] * rest) * many, 1),
            np.concatenate(([none, sine] + [none] * rest) * many, 1),
        ]
    )


TOKEN_ROW = 36
VECTOR_ROW = 12
SHARD = 7 * LANES
MIXED = 4 * LANES
ROWS = 48
FLIPS = [(0, 0), (0, 1), (1, 0), (1, 1)]
CUBE = [(dy, dk, dc) for dy in range(2) for dk, dc in FLIPS]


def cube_flips(pieces):
    return [pieces[0]] + [
        flip(piece, ("y", "k", "c"), bits) for piece, bits in zip(pieces[1:], CUBE[1:])
    ]


def cube_number(place_ref, bits):
    y, k, c = (place_ref[axis] for axis in (0, 2, 4))
    return ((y + bits[0]) % 2 * 2 + (k + bits[1]) % 2) * 2 + (c + bits[2]) % 2


def row_spots(number):
    spots = []
    done = 0
    while done < ROWS:
        at = number * ROWS + done
        many = min(ROWS - done, 64 - at % 64)
        spots.append((done, many, at // 64, at % 64))
        done += many
    return spots


def cut_first(tables, vectors, tokens, lengths, down, out, place):
    features, table_rows = tables.shape
    chunk = vectors.shape[1]
    own_ff, width = down.shape
    part = own_ff // 2
    some = out.shape[0] // 2
    packs, per_pack = lengths.shape

    def kernel(tab_ref, vec_ref, tok_ref, len_ref, down_ref, out_ref, place_ref, rows_ref, keep_ref, send_ref, one_ref, two_ref):
        y = place_ref[0]
        table = jnp.concatenate(
            [tab_ref[...], jnp.zeros((features, LANES - table_rows), F32)], 1
        )
        rows_ref[:features, :] = table.astype(LOW)
        rest = chunk - 3 * LANES
        ends = jnp.concatenate(
            [vec_ref[:, 3 * LANES :], jnp.zeros((1, LANES - rest), F32)], 1
        )
        sizes = [len_ref[p : p + 1, :].astype(F32) for p in range(packs)]
        sizes = jnp.concatenate(sizes + [jnp.zeros((1, LANES - packs * per_pack), F32)], 1)
        lines = [vec_ref[:, j * LANES : (j + 1) * LANES] for j in range(3)] + [ends]
        lines = lines + [tok_ref[p : p + 1, :].astype(F32) for p in range(packs)] + [sizes]
        line = lax.broadcasted_iota(jnp.int32, (16, LANES), 0)
        tail = jnp.zeros((16, LANES), F32)
        for number, value in enumerate(lines):
            tail = jnp.where(line == number, value, tail)
        rows_ref[features:, :] = tail.astype(LOW)
        keep_ref[...] = down_ref[pl.ds(pl.multiple_of(y * part, part), part), :].astype(LOW)
        send_ref[...] = down_ref[pl.ds(pl.multiple_of((1 - y) * part, part), part), :].astype(LOW)
        one_ref[...] = out_ref[pl.ds(pl.multiple_of(y * some, some), some), :].astype(LOW)
        two_ref[...] = out_ref[pl.ds(pl.multiple_of((1 - y) * some, some), some), :].astype(LOW)

    outs = [((ROWS, LANES), LOW)] + [((part, width), LOW)] * 2 + [((some, width), LOW)] * 2
    args = (tables, vectors, tokens, lengths, down, out, place)
    return simple(kernel, "cut_first", outs, *args, smem=(6,), limit=VMEM_MOST)


def cut_weights(qkv, up, rows, behind):
    own_in, width = (qkv.shape[0], up.shape[1] // 4)
    own_ff = width // 4
    part = own_ff // 2

    def kernel(qkv_ref, up_ref, r0, r1, r2, r3, shard_ref):
        for dest in range(8):
            yy, kk, cc = dest >> 2, dest >> 1 & 1, dest & 1
            start = ((cc * 2 + kk) * 2 + yy) * LANES
            for j in range(3):
                shard_ref[dest, :, j * LANES : (j + 1) * LANES] = qkv_ref[
                    :, j * width + start : j * width + start + LANES
                ].astype(LOW)
            for j in range(4):
                start = (j // 2 * 8 + kk * 4 + j % 2 * 2 + cc) * own_ff + yy * part
                shard_ref[dest, :, (3 + j) * LANES : (4 + j) * LANES] = up_ref[
                    :, start : start + part
                ].astype(LOW)
        for number, ref in enumerate((r0, r1, r2, r3)):
            for row, many, tile, at in row_spots(number):
                value = ref[row : row + many, :]
                start = SHARD + tile * LANES
                for dest in range(8):
                    shard_ref[dest, at : at + many, start : start + LANES] = value

    outs = [((8, own_in, SHARD + 3 * LANES), LOW)]
    return simple(kernel, "cut_weights", outs, qkv, up, *rows, behind=behind)[0]


def unpack_rows(shards, place):
    def kernel(shard_ref, place_ref, rows_ref):
        h, x = place_ref[1], place_ref[3]
        for source in range(8):
            yy, kk, cc = source >> 2, source >> 1 & 1, source & 1
            for number, (dh, dx) in enumerate(FLIPS):
                device = (((yy * 2 + (h + dh) % 2) * 2 + kk) * 2 + (x + dx) % 2) * 2 + cc
                for row, many, tile, at in row_spots(number):
                    start = SHARD + tile * LANES
                    rows_ref[device, row : row + many, :] = shard_ref[
                        source, at : at + many, start : start + LANES
                    ]

    return simple(kernel, "unpack_rows", [((32, ROWS, LANES), LOW)], shards, place, smem=(1,))[0]


def slot_tables(tables, counted, place, rope_of_position, behind):
    slots = counted.shape[1]
    per_pack = 4
    seqs = 2 * per_pack
    packs = 8

    def kernel(tab_ref, count_ref, place_ref, table_ref, bias_ref, rope_ref, hot_ref, target_ref, seqw_ref, seqc_ref):
        y, h, k, x, c = (place_ref[j] for j in range(5))
        row = lax.broadcasted_iota(jnp.int32, (slots, slots), 0)
        column = lax.broadcasted_iota(jnp.int32, (slots, slots), 1)
        lane = lax.broadcasted_iota(jnp.int32, (1, slots), 1)

        def ends_of(lengths, pack):
            first = pack * per_pack
            return [
                jnp.sum(
                    jnp.where((lane >= first) & (lane <= first + j), lengths, 0.0), 1, keepdims=True
                )
                for j in range(per_pack)
            ]

        def segments(ends, index):
            number = jnp.zeros(index.shape, jnp.int32)
            for end in ends:
                number = number + (index.astype(F32) >= end).astype(jnp.int32)
            return number

        for block in range(4):
            dc, dk = FLIPS[block]
            device = ((h * 2 + (k + dk) % 2) * 2 + x) * 2 + (c + dc) % 2
            lines = tab_ref[device, TOKEN_ROW : TOKEN_ROW + 4, :].astype(F32)
            lengths = lines[2:3]
            for dy in range(2):
                pack = lax.rem(y + dy, 2)
                here = pl.ds((block * 2 + dy) * slots, slots)
                ends = ends_of(lengths, pack)
                by_row, by_column = segments(ends, row), segments(ends, column)
                seen = (by_row == by_column) & (column <= row)
                bias_ref[here, :] = jnp.where(seen, 0.0, -1e30)
                start = jnp.zeros((slots, slots), F32)
                for j in range(1, per_pack):
                    start = jnp.where(by_row == j, ends[j - 1], start)
                position = row.astype(F32) - start
                hot = jnp.where(column.astype(F32) == position, 1.0, 0.0).astype(LOW)
                for part in range(3):
                    rope_ref[part, here, :] = exact_rows(hot, table_ref[part])
                token = jnp.where(pack == 0, lines[0:1], lines[1:2])
                hot = jnp.where(row.astype(F32) == token, 1.0, 0.0)
                hot_ref[here, :] = hot.T[:, : hot_ref.shape[1]].astype(LOW)
        lines = tab_ref[((h * 2 + k) * 2 + x) * 2 + c, TOKEN_ROW : TOKEN_ROW + 4, :].astype(F32)
        counts = jnp.zeros((seqs, slots), F32)
        seq_line = lax.broadcasted_iota(jnp.int32, (seqs, slots), 0)
        for pack in range(2):
            number = segments(ends_of(lines[2:3], pack), lane)
            following = pltpu.roll(number.astype(F32), slots - 1, 1)
            same = (following == number.astype(F32)) & (lane < slots - 1)
            weight = jnp.where(same & (count_ref[pack : pack + 1, :] == 1), 1.0, 0.0)
            by_seq = jnp.where(seq_line == number + pack * per_pack, weight, 0.0)
            counts = counts + by_seq

            @pl.when(pack == y)
            def _():
                target = pltpu.roll(lines[pack : pack + 1], slots - 1, 1)
                hot = jnp.where(row.astype(F32) == target, 1.0, 0.0)
                target_ref[...] = hot.T[:, : target_ref.shape[1]]
                padded = jnp.concatenate([by_seq, jnp.zeros((slots - seqs, slots), F32)], 0)
                seqw_ref[...] = padded.T

        seqc_ref[...] = jnp.broadcast_to(jnp.sum(counts, 1, keepdims=True), (seqs, LANES))

    outs = [
        ((packs * slots, slots), F32),
        ((3, packs * slots, LANES), F32),
        ((packs * slots, 32), LOW),
        ((slots, 32), F32),
        ((slots, LANES), F32),
        ((seqs, LANES), F32),
    ]
    args = (tables, counted, place, rope_of_position)
    return simple(kernel, "slot_tables", outs, *args, smem=(2,), us=2.0, behind=behind)


def token_products(tables, weights, place):
    vocab = 32
    devices, _, lanes = tables.shape
    width = devices * vocab
    own_in, columns = weights.shape[1], SHARD
    total = devices // 2 * 448

    def kernel(tab_ref, w_ref, place_ref, low_ref, vec_ref, h_ref, norm_ref, inv_ref, part_ref):
        h, x = place_ref[1], place_ref[3]
        flat = tab_ref[:, :vocab, :].astype(F32).reshape(width, lanes).T
        low_ref[...] = flat.astype(LOW)
        first_half = lax.broadcasted_iota(jnp.int32, (1, LANES), 1) < LANES // 2
        for pair in range(devices // 2):
            line, at = pair // (devices // 4), pair % (devices // 4) * 7 * LANES
            even = tab_ref[2 * pair, vocab : vocab + 4, :].astype(F32)
            odd = pltpu.roll(tab_ref[2 * pair + 1, vocab : vocab + 4, :].astype(F32), LANES // 2, 1)
            for q in range(7):
                if q < 3:
                    value = even[q : q + 1]
                elif q == 3:
                    value = jnp.where(first_half, even[3:4], odd[0:1])
                else:
                    value = jnp.where(first_half, odd[q - 4 : q - 3], odd[q - 3 : q - 2])
                vec_ref[line : line + 1, at + q * LANES : at + (q + 1) * LANES] = value
        out, normed, inverse = layer_norm(
            flat[:vocab], vec_ref[0:1, :width], vec_ref[0:1, width : 2 * width]
        )
        norm_ref[...] = normed
        inv_ref[...] = inverse
        h_ref[...] = out.astype(LOW)
        rows = 2 * own_in
        sums = jnp.zeros((vocab, columns), F32)
        for kk in range(2):
            start = pl.multiple_of(((h * 2 + kk) * 2 + x) * rows, LANES)
            block = w_ref[2 * kk : 2 * kk + 2, :, :columns].reshape(rows, columns)
            sums = sums + mm(h_ref[:, pl.ds(start, rows)], block)
        part_ref[...] = sums

    outs = [
        ((lanes, width), LOW),
        ((2, total), F32),
        ((vocab, width), LOW),
        ((vocab, width), F32),
        ((vocab, 1), F32),
        ((vocab, columns), F32),
    ]
    return simple(kernel, "token_products", outs, tables, weights, place, smem=(2,))


def first_rows(down_keep, down_far, out_one, out_two, place):
    part, width = down_keep.shape
    some = out_one.shape[0]

    def kernel(keep_ref, far_ref, one_ref, two_ref, place_ref, rows_ref):
        y, x = place_ref[0], place_ref[3]
        rows_ref[:part, :] = jnp.where(y == 0, keep_ref[...], far_ref[...])
        rows_ref[part:, :] = jnp.where(x == 0, one_ref[...], two_ref[...])

    outs = [((part + some, width), LOW)]
    args = (down_keep, down_far, out_one, out_two, place)
    return simple(kernel, "first_rows", outs, *args, smem=(4,))[0]


def upper_rows(weights, down_keep, down_far, out_one, out_two, place):
    part, width = down_keep.shape
    some = out_one.shape[0]
    own_in, columns = weights.shape[1], SHARD

    def kernel(w_ref, keep_ref, far_ref, one_ref, two_ref, place_ref, *piece_refs):
        y, x = place_ref[0], place_ref[3]
        for j in range(4):
            ref = piece_refs[j // 2]
            ref[j % 2 * own_in : (j % 2 + 1) * own_in, :columns] = w_ref[4 + j, :, :columns]
        out = jnp.where(x == 0, two_ref[...], one_ref[...])
        for j in range(8):
            ref = piece_refs[j // 4]
            here = slice(j % 4 * some, (j % 4 + 1) * some)
            ref[here, columns:] = out[:, j * LANES : (j + 1) * LANES]
        piece_refs[2][...] = jnp.where(y == 0, far_ref[...], keep_ref[...])

    outs = [((part, width), LOW)] * 3
    args = (weights, down_keep, down_far, out_one, out_two, place)
    return simple(kernel, "upper_rows", outs, *args, smem=(5,))


def across(value):
    far = flip(value, ("h",), (1,))
    return [value, flip(value, ("x",), (1,)), far, flip(far, ("x",), (1,))]


def group_pieces(value):
    near = [value] + [flip(value, ("y", "k"), (dy, dk)) for dk, dy in NEAR]
    return near + [flip(piece, ("c",), (1,)) for piece in near]


def group_sums(keep, send, behind=()):
    got = flip(send, ("c",), (1,))
    rows, width = (keep.shape[0] // 4, keep.shape[1])

    def kernel(keep_ref, got_ref, *refs):
        for j, ref in enumerate(refs):
            here = slice(j * rows, (j + 1) * rows)
            ref[...] = (keep_ref[here, :] + got_ref[here, :].astype(F32)).astype(ref.dtype)

    outs = [((rows, width), F32)] + [((rows, width), LOW)] * 3
    mine = simple(kernel, "group_sums", outs, keep, got, behind=behind)
    return [mine[0]] + [flip(piece, ("y", "k"), (dy, dk)) for piece, (dk, dy) in zip(mine[1:], NEAR)]


def block_of(place_ref, number):
    dh, dx = FLIPS[number]
    return (place_ref[1] + dh) % 2 * 2 + (place_ref[3] + dx) % 2


def first_group_forward(parts, tails, vec, place, hot, rope, bias, behind):
    vocab, columns = parts[0].shape
    total, slots = bias.shape
    tail_rows, width = tails[0].shape
    part = LANES
    some = tail_rows - part
    units = 4 * part
    step = total // 2

    def kernel(*refs):
        refs = refs[:11] + refs[11 + len(behind) :]
        part_refs, tail_refs = refs[:2], refs[2:6]
        vec_ref, place_ref, hot_ref, rope_ref, bias_ref = refs[6:11]
        keep_ref, send_ref, qkv_ref, att_ref, act_ref, slope_ref, wout_ref, wdown_ref = refs[11:19]
        table_ref, ffn_ref = refs[19:]
        first = pl.program_id(0) == 0

        @pl.when(first)
        def _():
            for number, ref in enumerate(tail_refs):
                block = block_of(place_ref, number)
                wdown_ref[pl.ds(pl.multiple_of(block * part, part), part), :] = ref[:part, :]
                wout_ref[pl.ds(pl.multiple_of(block * some, some), some), :] = ref[part:, :]
            sums = part_refs[0][...] + part_refs[1][...]
            table_ref[...] = sums[:, : 3 * LANES]
            y, k, c = place_ref[0], place_ref[2], place_ref[4]
            bias_up = jnp.concatenate(
                [
                    vec_ref[0:1, pl.ds(unit_start(width, j, y, k, c, part), part)]
                    for j in range(4)
                ],
                1,
            )
            act, slope = gelu_pair(sums[:, 3 * LANES :] + bias_up)
            act = act.astype(LOW)
            act_ref[...] = act
            slope_ref[...] = slope
            ffn_ref[...] = mm(act, wdown_ref[...])

        for pack in range(step // slots):
            here = slice(pack * slots, (pack + 1) * slots)
            hot_here = hot_ref[here, :]
            rope_here = [rope_ref[j, here, :] for j in range(3)]
            q = turn_by(exact_rows(hot_here, table_ref[:, :LANES]), rope_here, 1.0).astype(LOW)
            k = turn_by(
                exact_rows(hot_here, table_ref[:, LANES : 2 * LANES]), rope_here, 1.0
            ).astype(LOW)
            v = mm(hot_here, table_ref[:, 2 * LANES :].astype(LOW)).astype(LOW)
            qkv_ref[here, :LANES] = q
            qkv_ref[here, LANES : 2 * LANES] = k
            qkv_ref[here, 2 * LANES :] = v
            att_ref[here, :] = attend_pair(q, k, v, bias_ref[here, :])
        out = mm(att_ref[...], wout_ref[...]) + exact_rows(hot_ref[...], ffn_ref[...])

        @pl.when(first)
        def _():
            send_ref[...] = out.astype(LOW)

        @pl.when(jnp.logical_not(first))
        def _():
            keep_ref[...] = out

    def by_rows(columns):
        return pl.BlockSpec((step, columns), lambda s: (1 - s, 0))

    args = (*parts, *tails, vec)
    return pl.pallas_call(
        kernel,
        grid=(2,),
        in_specs=[whole_spec(arg.shape) for arg in args]
        + [
            pl.BlockSpec(memory_space=pltpu.SMEM),
            by_rows(vocab),
            pl.BlockSpec((3, step, LANES), lambda s: (0, 1 - s, 0)),
            by_rows(slots),
        ]
        + [pl.BlockSpec(memory_space=pl.ANY)] * len(behind),
        out_specs=[
            whole_spec((step, width)),
            whole_spec((step, width)),
            by_rows(3 * LANES),
            by_rows(LANES),
            whole_spec((vocab, units)),
            whole_spec((vocab, units)),
            whole_spec((4 * some, width)),
            whole_spec((units, width)),
        ],
        out_shape=[
            jax.ShapeDtypeStruct((step, width), F32),
            jax.ShapeDtypeStruct((step, width), LOW),
            jax.ShapeDtypeStruct((total, 3 * LANES), LOW),
            jax.ShapeDtypeStruct((total, LANES), LOW),
            jax.ShapeDtypeStruct((vocab, units), LOW),
            jax.ShapeDtypeStruct((vocab, units), F32),
            jax.ShapeDtypeStruct((4 * some, width), LOW),
            jax.ShapeDtypeStruct((units, width), LOW),
        ],
        scratch_shapes=[pltpu.VMEM((vocab, 3 * LANES), F32), pltpu.VMEM((vocab, width), F32)],
        compiler_params=params(),
        cost_estimate=cost(9),
        name="first_group_forward",
    )(*args, place, hot, rope, bias, *behind)


def unit_start(width, j, y, k, c, part):
    unit = (j // 2 * 8 + k * 4 + j % 2 * 2 + c) * 2 * part + y * part
    return pl.multiple_of(3 * width + unit, LANES)


def first_finish_rows(pieces, hot, low_tables, vec, behind):
    rows, width = pieces[0].shape
    vocab = hot.shape[1]

    def kernel(p0, p1, p2, p3, hot_ref, low_ref, vec_ref, x_ref, h_ref):
        stay = low_ref[:vocab, :].astype(F32) + vec_ref[0:1, 2 * width : 3 * width]
        x = exact_rows(hot_ref[:rows, :], stay) + p0[...]
        x = x + p1[...].astype(F32) + p2[...].astype(F32) + p3[...].astype(F32)
        x = x.astype(LOW)
        x_ref[...] = x
        h_ref[...] = layer_norm(
            x.astype(F32), vec_ref[1:2, :width], vec_ref[1:2, width : 2 * width]
        )[0].astype(LOW)

    outs = [((rows, width), LOW), ((rows, width), LOW)]
    return simple(kernel, "first_finish", outs, *pieces, hot, low_tables, vec, behind=behind)


def group_forward(pieces, shards, vec, place, rope, bias):
    slots, width = pieces[0].shape
    total = slots * len(pieces)
    step = total // 2
    part = LANES
    units, columns = 4 * part, 7 * LANES
    some = part // 4

    def kernel(*refs):
        piece_refs, shard_refs = refs[:8], refs[8:20]
        vec_ref, place_ref, rope_ref, bias_ref = refs[20:24]
        keep_ref, send_ref, h_ref, qkv_ref, att_ref, act_ref, slope_ref = refs[24:31]
        win_ref, wout_ref, wdown_ref = refs[31:]
        half = 1 - pl.program_id(0)

        @pl.when(half == 1)
        def _():
            for number in range(4):
                three = shard_refs[3 * number : 3 * number + 3]
                block = block_of(place_ref, number)
                for kk in range(2):
                    start = (block // 2 * 4 + kk * 2 + block % 2) * part
                    here = pl.ds(pl.multiple_of(start, part), part)
                    win_ref[here, :] = three[kk][:, :columns]
                here = pl.ds(pl.multiple_of(block * some, some), some)
                for j in range(8):
                    there = slice(j % 4 * some, (j % 4 + 1) * some)
                    wout_ref[here, j * LANES : (j + 1) * LANES] = three[j // 4][there, columns:]
                here = pl.ds(pl.multiple_of(block * part, part), part)
                wdown_ref[here, :] = three[2][...]

        for s in range(2):

            @pl.when(half == s)
            def _():
                for j in range(4):
                    h_ref[j * slots : (j + 1) * slots, :] = piece_refs[4 * s + j][...]

        h = h_ref[...]
        proj = mm(h, win_ref[:, : 3 * LANES])
        spans = [slice(j * LANES, (j + 1) * LANES) for j in range(3)]
        qkv_ref[:, spans[0]] = turn_by(proj[:, spans[0]], rope_ref, 1.0).astype(LOW)
        qkv_ref[:, spans[1]] = turn_by(proj[:, spans[1]], rope_ref, 1.0).astype(LOW)
        qkv_ref[:, spans[2]] = proj[:, spans[2]].astype(LOW)
        for pack in range(step // slots):
            here = slice(pack * slots, (pack + 1) * slots)
            q, k, v = (qkv_ref[here, spans[j]] for j in range(3))
            att_ref[here, :] = attend_pair(q, k, v, bias_ref[here, :])
        y, k, c = place_ref[0], place_ref[2], place_ref[4]
        bias_up = jnp.concatenate(
            [vec_ref[1:2, pl.ds(unit_start(width, j, y, k, c, part), part)] for j in range(4)], 1
        )
        act, slope = gelu_pair(mm(h, win_ref[:, 3 * LANES :]) + bias_up)
        act = act.astype(LOW)
        act_ref[...] = act
        slope_ref[...] = slope
        out = mm(att_ref[...], wout_ref[...]) + mm(act, wdown_ref[...])

        @pl.when(half == 1)
        def _():
            send_ref[...] = out.astype(LOW)

        @pl.when(half == 0)
        def _():
            keep_ref[...] = out

    def by_rows(columns):
        return pl.BlockSpec((step, columns), lambda s: (1 - s, 0))

    args = (*pieces, *shards, vec)
    shapes = [
        ((step, width), F32),
        ((step, width), LOW),
        ((total, width), LOW),
        ((total, 3 * LANES), LOW),
        ((total, LANES), LOW),
        ((total, units), LOW),
        ((total, units), F32),
        ((width, columns), LOW),
        ((LANES, width), LOW),
        ((units, width), LOW),
    ]
    return pl.pallas_call(
        kernel,
        grid=(2,),
        in_specs=[whole_spec(arg.shape) for arg in args]
        + [
            pl.BlockSpec(memory_space=pltpu.SMEM),
            pl.BlockSpec((3, step, LANES), lambda s: (0, 1 - s, 0)),
            by_rows(slots),
        ],
        out_specs=[
            whole_spec(shape) if number < 2 or number > 6 else by_rows(shape[1])
            for number, (shape, _) in enumerate(shapes)
        ],
        out_shape=[jax.ShapeDtypeStruct(shape, kind) for shape, kind in shapes],
        compiler_params=params(),
        cost_estimate=cost(12.5),
        name="group_forward",
    )(*args, place, rope, bias)


def group_backward(pieces, qkv, slope, w_in, w_out, w_down, rope, bias):
    slots, width = pieces[0].shape
    total = slots * len(pieces)
    units = w_down.shape[0]
    step = total // 2

    def kernel(*refs):
        piece_refs = refs[:8]
        win_ref, wout_ref, wdown_ref, qkv_ref, slope_ref, rope_ref, bias_ref = refs[8:15]
        keep_ref, send_ref, d_ref, din_ref, sum_ref = refs[15:]
        half = 1 - pl.program_id(0)
        for s in range(2):

            @pl.when(half == s)
            def _():
                for j in range(4):
                    d_ref[j * slots : (j + 1) * slots, :] = piece_refs[4 * s + j][...]

        d_out = d_ref[...]
        d_att = mm_t(d_out, wout_ref[...]).astype(LOW)
        d_pre = (mm_t(d_out, wdown_ref[...]) * slope_ref[...]).astype(LOW)
        din_ref[:, 3 * LANES :] = d_pre
        sums = jnp.sum(d_pre.astype(F32), 0, keepdims=True)
        spans = [slice(j * LANES, (j + 1) * LANES) for j in range(3)]
        for pack in range(step // slots):
            here = slice(pack * slots, (pack + 1) * slots)
            q, k, v = (qkv_ref[here, spans[j]] for j in range(3))
            dq, dk, dv = attend_pair_back(d_att[here, :], q, k, v, bias_ref[here, :])
            turned = [rope_ref[j, here, :] for j in range(3)]
            din_ref[here, spans[0]] = turn_by(dq, turned, -1.0).astype(LOW)
            din_ref[here, spans[1]] = turn_by(dk, turned, -1.0).astype(LOW)
            din_ref[here, spans[2]] = dv.astype(LOW)
        d_norm = mm_t(din_ref[...], win_ref[...])

        @pl.when(half == 1)
        def _():
            send_ref[...] = d_norm.astype(LOW)
            sum_ref[...] = sums

        @pl.when(half == 0)
        def _():
            keep_ref[...] = d_norm
            sum_ref[...] += sums

    def by_rows(columns):
        return pl.BlockSpec((step, columns), lambda s: (1 - s, 0))

    args = (*pieces, w_in, w_out, w_down)
    return pl.pallas_call(
        kernel,
        grid=(2,),
        in_specs=[whole_spec(arg.shape) for arg in args]
        + [
            by_rows(3 * LANES),
            by_rows(units),
            pl.BlockSpec((3, step, LANES), lambda s: (0, 1 - s, 0)),
            by_rows(slots),
        ],
        out_specs=[
            whole_spec((step, width)),
            whole_spec((step, width)),
            by_rows(width),
            by_rows(3 * LANES + units),
            whole_spec((1, units)),
        ],
        out_shape=[
            jax.ShapeDtypeStruct((step, width), F32),
            jax.ShapeDtypeStruct((step, width), LOW),
            jax.ShapeDtypeStruct((total, width), LOW),
            jax.ShapeDtypeStruct((total, 3 * LANES + units), LOW),
            jax.ShapeDtypeStruct((1, units), F32),
        ],
        compiler_params=params(),
        cost_estimate=cost(13.4),
        name="group_backward",
    )(*args, qkv, slope, rope, bias)


def weight_gradients(hs, d_in, act, att, d_rows, place):
    width = hs.shape[1]
    columns = d_in.shape[1]
    block = LANES
    some = LANES // 4

    def kernel(h_ref, din_ref, act_ref, att_ref, d_ref, place_ref, *refs):
        out_ref = refs[6]
        x = place_ref[3]
        h = pl.program_id(0)

        @pl.when(h == 0)
        def _():
            out_ref[...] = t_mm(att_ref[...], d_ref[...])

        d_in = din_ref[...]
        d_rows = d_ref[...]
        for three, xx in ((refs[:3], x), (refs[3:6], 1 - x)):
            for k in range(2):
                start = pl.multiple_of(((h * 2 + k) * 2 + xx) * block, LANES)
                grad = t_mm(h_ref[:, pl.ds(start, block)], d_in)
                three[k][0, :, :columns] = grad.astype(three[k].dtype)
            start = pl.multiple_of((h * 2 + xx) * some, some)
            grad = out_ref[pl.ds(start, some), :]
            for j in range(8):
                here = slice(j % 4 * some, (j % 4 + 1) * some)
                three[j // 4][0, here, columns:] = grad[:, j * LANES : (j + 1) * LANES].astype(
                    three[j // 4].dtype
                )
            start = pl.multiple_of((h * 2 + xx) * block, LANES)
            three[2][0] = t_mm(act_ref[:, pl.ds(start, block)], d_rows).astype(three[2].dtype)

    args = (hs, d_in, act, att, d_rows)
    shape = (2, block, width)
    return pl.pallas_call(
        kernel,
        grid=(2,),
        in_specs=[whole_spec(arg.shape) for arg in args]
        + [pl.BlockSpec(memory_space=pltpu.SMEM)],
        out_specs=[pl.BlockSpec((1,) + shape[1:], lambda h: (h, 0, 0))] * 6,
        out_shape=[jax.ShapeDtypeStruct(shape, kind) for kind in (F32,) * 3 + (LOW,) * 3],
        scratch_shapes=[pltpu.VMEM((LANES, width), F32)],
        compiler_params=params(),
        cost_estimate=cost(5.0),
        name="weight_gradients",
    )(*args, place)


def add_split(keep_ref, got_ref, place_ref, mine_ref, send_ref):
    b = place_ref[1]
    mine_ref[...] = keep_ref[b] + got_ref[b].astype(F32)
    send_ref[...] = (keep_ref[1 - b] + got_ref[1 - b].astype(F32)).astype(LOW)


def split_two(total):
    high = total.astype(LOW)
    return (high, (total - high.astype(F32)).astype(LOW))


def first_group_backward(pieces, qkv, att, slope, w_out, w_down, hot, rope, bias, mixed, keep, got, place, behind):
    slots, width = pieces[0].shape
    total = slots * len(pieces)
    vocab = hot.shape[1]
    units = w_down.shape[0]
    some = LANES // 4
    columns = 3 * LANES + units + width

    def kernel(*refs):
        piece_refs = refs[:8]
        qkv_ref, att_ref, slope_ref, wout_ref, wdown_ref, hot_ref, rope_ref, bias_ref = refs[8:16]
        mixed_ref, keep_ref, got_ref, place_ref = refs[16:20]
        out_refs, mine_ref, send_ref, sum_ref, grad_ref = refs[20:22], *refs[22:]
        sum_ref[...] = jnp.zeros(sum_ref.shape, F32)
        grad_ref[...] = jnp.zeros(grad_ref.shape, F32)
        spans = [slice(j * LANES, (j + 1) * LANES) for j in range(3)]
        for pack, ref in enumerate(piece_refs):
            here = slice(pack * slots, (pack + 1) * slots)
            d_out = ref[...]
            hot_here = hot_ref[here, :]
            d_att = mm_t(d_out, wout_ref[...]).astype(LOW)
            q, k, v = (qkv_ref[here, spans[j]] for j in range(3))
            dq, dk, dv = attend_pair_back(d_att, q, k, v, bias_ref[here, :])
            turned = [rope_ref[j, here, :] for j in range(3)]
            sum_ref[:, spans[0]] += t_mm(hot_here, turn_by(dq, turned, -1.0).astype(LOW))
            sum_ref[:, spans[1]] += t_mm(hot_here, turn_by(dk, turned, -1.0).astype(LOW))
            sum_ref[:, spans[2]] += t_mm(hot_here, dv.astype(LOW))
            sum_ref[:, 3 * LANES + units :] += t_mm(hot_here, d_out)
            grad_ref[...] += t_mm(att_ref[here, :], d_out)
        high, rest = split_two(sum_ref[:, 3 * LANES + units :])
        down = wdown_ref[...]
        sum_ref[:, 3 * LANES : 3 * LANES + units] = (
            mm_t(high, down) + mm_t(rest, down)
        ) * slope_ref[...]
        for ref, xx in zip(out_refs, (place_ref[3], 1 - place_ref[3])):
            ref[:, :columns] = sum_ref[...].astype(ref.dtype)
            for h in range(2):
                at = columns + h * (width + MIXED)
                start = pl.multiple_of((h * 2 + xx) * some, some)
                ref[:, at : at + width] = grad_ref[pl.ds(start, some), :].astype(ref.dtype)
                for dest in range(8):
                    device = (((dest // 4 * 2 + h) * 2 + dest // 2 % 2) * 2 + xx) * 2 + dest % 2
                    here = slice(dest % 2 * 16, dest % 2 * 16 + 16)
                    start = at + width + dest // 2 * LANES
                    ref[here, start : start + LANES] = mixed_ref[device].astype(ref.dtype)
        add_split(keep_ref, got_ref, place_ref, mine_ref, send_ref)

    wide = columns + 2 * (width + MIXED)
    shape = keep.shape[1:]
    outs = [((vocab, wide), F32), ((vocab, wide), LOW)] + [(shape, F32), (shape, LOW)]
    args = (*pieces, qkv, att, slope, w_out, w_down, hot, rope, bias, mixed, keep, got, place)
    scratch = [pltpu.VMEM((vocab, columns), F32), pltpu.VMEM((LANES, width), F32)]
    return simple(
        kernel,
        "first_group_backward",
        outs,
        *args,
        smem=(19,),
        scratch=scratch,
        us=9.0,
        behind=behind,
    )


def fold(keep, got, down, down_far, place, behind):
    vocab = keep.shape[0]
    by_h = 1024 + MIXED
    columns = keep.shape[1] - 2 * by_h

    def kernel(keep_ref, got_ref, one_ref, two_ref, place_ref, mine_ref, send_ref, down_ref):
        down_ref[...] = (one_ref[...] + two_ref[...].astype(F32)).astype(LOW)
        same = keep_ref[:, :columns] + got_ref[:, :columns].astype(F32)
        mine_ref[:, :columns] = same
        send_ref[:, :columns] = same.astype(LOW)
        for ref, h in ((mine_ref, place_ref[1]), (send_ref, 1 - place_ref[1])):
            here = pl.ds(pl.multiple_of(columns + h * by_h, LANES), by_h)
            ref[:, columns:] = (keep_ref[:, here] + got_ref[:, here].astype(F32)).astype(ref.dtype)

    shape = (vocab, columns + by_h)
    outs = [(shape, F32), (shape, LOW), (down.shape, LOW)]
    args = (keep, got, down, down_far, place)
    return simple(kernel, "fold", outs, *args, smem=(4,), behind=behind)


def add_two(one, two):
    def kernel(one_ref, two_ref, out_ref):
        out_ref[...] = one_ref[...] + two_ref[...]

    return simple(kernel, "add_two", [(one.shape, one.dtype)], one, two)[0]


def token_gradients(parts, h0, weights, act, act_far, place, behind):
    vocab, width = h0.shape
    own_in, shard = weights.shape[1], SHARD
    units = act.shape[1]
    part = units // 4

    def kernel(p0, p1, h_ref, w_ref, act_ref, other_ref, place_ref, in_ref, down_ref, out_ref, dh_ref, rows_ref, mixed_ref, act_out):
        total = p0[...] + p1[...].astype(F32)
        rows = total[:, shard : shard + width]
        rows_ref[...] = rows
        out_ref[...] = total[:, shard + width : shard + 2 * width].astype(LOW)
        for dest in range(8):
            start = shard + 2 * width + dest // 2 * LANES
            here = slice(dest % 2 * 16, dest % 2 * 16 + 16)
            mixed_ref[dest] = total[here, start : start + LANES]
        high, rest = split_two(total[:, :shard])
        h, x = place_ref[1], place_ref[3]
        two = 2 * own_in
        for kk in range(2):
            start = pl.multiple_of(((h * 2 + kk) * 2 + x) * two, LANES)
            mine = h_ref[:, pl.ds(start, two)]
            grad = t_mm(mine, high) + t_mm(mine, rest)
            in_ref[2 * kk : 2 * kk + 2] = grad.astype(LOW).reshape(2, own_in, shard)
            block = w_ref[2 * kk : 2 * kk + 2, :, :shard].reshape(two, shard)
            dh_ref[kk * vocab : (kk + 1) * vocab, :] = mm_t(high, block) + mm_t(rest, block)
        act_out[...] = total[:, 3 * LANES : shard]
        start = pl.multiple_of((h * 2 + x) * part, LANES)
        bias = jnp.sum(act_out[:, pl.ds(start, part)], 0, keepdims=True)
        dh_ref[2 * vocab :, :] = jnp.broadcast_to(bias, (8, LANES))
        high, rest = split_two(rows)
        for j, ref in enumerate((act_ref, other_ref)):
            mine = ref[:, pl.ds(start, part)]
            down_ref[j * part : (j + 1) * part, :] = t_mm(mine, high) + t_mm(mine, rest)

    outs = [
        ((4, own_in, shard), LOW),
        ((2 * part, width), F32),
        ((vocab, width), LOW),
        ((2 * vocab + 8, LANES), F32),
        ((vocab, width), F32),
        ((8, 16, LANES), F32),
    ]
    scratch = [pltpu.VMEM((vocab, units), F32)]
    args = (*parts, h0, weights, act, act_far, place)
    return simple(
        kernel, "token_gradients", outs, *args, smem=(6,), scratch=scratch, behind=behind
    )


def owner_pieces(keeps, gots, down, first_in, first_down, first_out, dh, mixed, scalars, bias_local, place):
    rows, width = keeps[0].shape
    own_in, columns = first_in.shape[1:]
    some = first_out.shape[0]
    vocab = bias_local.shape[1]

    def kernel(k0, k1, g0, g1, upper_ref, in_ref, down_ref, out_ref, dh_ref, mixed_ref, scalar_ref, bias_ref, place_ref, shard_ref, one_ref, two_ref, last_ref, sum_ref):
        y, x = place_ref[0], place_ref[3]
        for j, (keep, got) in enumerate(((k0, g0), (k1, g1))):
            sum_ref[j * rows : (j + 1) * rows, :] = (keep[...] + got[...].astype(F32)).astype(LOW)
        lane = lax.broadcasted_iota(jnp.int32, (vocab, LANES), 1)
        for number in range(8):
            if number < 4:
                shard_ref[number, :, :columns] = in_ref[number]
            else:
                here = slice((number - 4) * own_in, (number - 3) * own_in)
                shard_ref[number, :, :columns] = sum_ref[here, :columns]
            block = dh_ref[number // 4 * vocab : (number // 4 + 1) * vocab, :]
            if number % 4:
                block = pltpu.roll(block, LANES - number % 4 * vocab, 1)
            high = block.astype(LOW).astype(F32)
            rest = pltpu.roll(block - high, vocab, 1)
            both = jnp.where(lane < vocab, high, jnp.where(lane < 2 * vocab, rest, 0.0))
            shard_ref[number, :vocab, columns:] = both.astype(LOW)
            high, rest = split_two(mixed_ref[number])
            shard_ref[number, vocab : vocab + 16, columns:] = high
            shard_ref[number, vocab + 16 :, columns:] = rest
        for j in range(width // LANES):
            here = slice(j * LANES, (j + 1) * LANES)
            upper = sum_ref[j * some : (j + 1) * some, columns:]
            first = out_ref[:, here]
            one_ref[:, here] = jnp.where(x == 0, first, upper)
            two_ref[:, here] = jnp.where(x == 0, upper, first)

        def squares(value):
            value = value.astype(F32)
            return jnp.sum(jnp.sum(value * value, 0, keepdims=True), 1, keepdims=True)

        total = squares(sum_ref[...]) + squares(upper_ref[...]) + squares(out_ref[...])
        total = total + jnp.where(y == 0, squares(down_ref[...]), 0.0)
        for j in range(4):
            total = total + squares(in_ref[j])
        lane = lax.broadcasted_iota(jnp.int32, (1, LANES), 1)
        penalty = jnp.where(y == 0, scalar_ref[0:1, 2:3], 0.0)
        bias = jnp.concatenate([bias_ref[...], jnp.zeros((1, LANES - vocab), F32)], 1)
        row = jnp.where(lane == 0, total, jnp.where(lane == 1, penalty, 0.0))
        last_ref[...] = row + pltpu.roll(bias, vocab, 1)

    outs = [((8, own_in, columns + LANES), LOW)]
    outs = outs + [((some, width), LOW)] * 2
    outs = outs + [((1, LANES), F32)]
    scratch = [pltpu.VMEM((2 * rows, width), LOW)]
    args = (*keeps, *gots, down, first_in, first_down, first_out, dh, mixed, scalars, bias_local, place)
    return simple(kernel, "owner_pieces", outs, *args, smem=(12,), scratch=scratch)


def norm_sums(shards, dh, last, place, behind):
    vocab = 32

    def kernel(shard_ref, dh_ref, last_ref, place_ref, all_ref, mixed_ref, out_ref):
        total = jnp.sum(shard_ref[:, :vocab, SHARD:].astype(F32), 0)
        total = total + pltpu.roll(total, LANES - vocab, 1)
        lane = lax.broadcasted_iota(jnp.int32, (8, LANES), 1)
        packed = total[:8]
        for group in range(1, 4):
            moved = pltpu.roll(total[group * 8 : (group + 1) * 8], group * vocab, 1)
            packed = jnp.where(lane >= group * vocab, moved, packed)
        out_ref[:8, :] = packed
        mixed = jnp.sum(shard_ref[:, vocab : vocab + 16, SHARD:].astype(F32), 0)
        mixed = mixed + jnp.sum(shard_ref[:, vocab + 16 :, SHARD:].astype(F32), 0)
        mixed_ref[...] = mixed
        line = lax.broadcasted_iota(jnp.int32, (16, LANES), 0)
        counted = (line < VECTOR_ROW) | (place_ref[0] == 1)
        squares = jnp.where(counted, mixed * mixed, 0.0)
        squares = jnp.sum(jnp.sum(squares, 0, keepdims=True), 1, keepdims=True)
        first = lax.broadcasted_iota(jnp.int32, (1, LANES), 1) == 0
        row = last_ref[...] + jnp.where(first, squares, 0.0)
        line = lax.broadcasted_iota(jnp.int32, (8, LANES), 0)
        out_ref[8:, :] = jnp.where(line == 0, row, dh_ref[2 * vocab :, :])
        all_ref[...] = jnp.broadcast_to(out_ref[...][None], all_ref.shape)

    outs = [((32, 16, LANES), F32), ((16, LANES), F32)]
    scratch = [pltpu.VMEM((16, LANES), F32)]
    args = (shards, dh, last, place)
    return simple(kernel, "norm_sums", outs, *args, smem=(3,), scratch=scratch, behind=behind)


def update_all(scalars, shards, first_down, down_mine, down_far, out_one, out_two, place, weights, firsts, seconds, rates):
    steps = 4
    own_in = shards.shape[1]
    part, width = down_mine.shape
    some = out_one.shape[0]
    rows = own_in // steps

    def kernel(scalar_ref, shard_ref, first_ref, mine_ref, far_ref, one_ref, two_ref, place_ref, *refs):
        state_refs, out_refs = refs[:12], refs[12:24]
        qkv_ref, up_ref = refs[24:]
        y = place_ref[0]
        early = pl.program_id(0) < steps // 2
        factor = scalar_ref[:, 4:5]
        for number in range(8):
            yy, kk, cc = number >> 2, number >> 1 & 1, number & 1
            start = ((cc * 2 + kk) * 2 + yy) * LANES
            for j in range(3):
                qkv_ref[:, j * width + start : j * width + start + LANES] = shard_ref[
                    number, :, j * LANES : (j + 1) * LANES
                ].astype(F32)
            for j in range(4):
                start = (j // 2 * 8 + kk * 4 + j % 2 * 2 + cc) * 2 * part + yy * part
                up_ref[:, start : start + part] = shard_ref[
                    number, :, (3 + j) * LANES : (4 + j) * LANES
                ].astype(F32)
        upper = jnp.where(early, far_ref[...], mine_ref[...]).astype(F32)
        down = jnp.where(y == 0, first_ref[...], upper)
        out = jnp.where((y == 0) == early, one_ref[...], two_ref[...]).astype(F32)
        for j, (grad, rate) in enumerate(zip((qkv_ref[...], out, up_ref[...], down), rates)):
            new = adam(*(state_refs[part * 4 + j][0] for part in range(3)), grad * factor, rate, DECAY)
            for number, value in enumerate(new):
                out_refs[j * 3 + number][0] = value

    def own(shape):
        return pl.BlockSpec((1, shape[1] // steps, shape[2]), lambda s: (0, s, 0))

    def half(block, which):
        if which is None:
            return pl.BlockSpec(block, lambda s: (s % 2, 0))
        return pl.BlockSpec(block, lambda s: (jnp.clip(s - which, 0, 1), 0))

    shapes = [weight.shape for weight in weights]
    many = 2 * part // steps
    return pl.pallas_call(
        kernel,
        grid=(steps,),
        in_specs=[
            pl.BlockSpec((1, LANES), lambda s: (0, 0)),
            pl.BlockSpec((8, rows, shards.shape[2]), lambda s: (0, s, 0)),
            pl.BlockSpec((many, width), lambda s: (s, 0)),
            half((many, width), steps // 2),
            half((many, width), 0),
            half((2 * some // steps, width), None),
            half((2 * some // steps, width), None),
            pl.BlockSpec(memory_space=pltpu.SMEM),
        ]
        + [own(shape) for shape in shapes] * 3,
        out_specs=[own(shape) for shape in shapes for _ in range(3)],
        out_shape=[jax.ShapeDtypeStruct(shape, F32) for shape in shapes for _ in range(3)],
        scratch_shapes=[pltpu.VMEM((rows, 3 * width), F32), pltpu.VMEM((rows, 4 * width), F32)],
        compiler_params=params(VMEM_MOST),
        cost_estimate=cost(6.0),
        name="update_all",
    )(scalars, shards, first_down, down_mine, down_far, out_one, out_two, place, *weights, *firsts, *seconds)


def fast_input_backward(pieces, x_low, dy, vec, down_sum, bias_up, table_local, ends_local, keeps, gots, later, place):
    rows, width = dy.shape
    part = bias_up.shape[1] // 4
    total = vec.shape[1]
    owners = 32
    vocab = width // owners

    def kernel(p0, p1, p2, p3, x_ref, dy_ref, vec_ref, sum_ref, up_ref, table_ref, ends_ref, k0, k1, g0, g1, later_ref, place_ref, low_ref, mixed_ref, m0, m1, s0, s1, pass_ref, grad_ref):
        add_split(k0, g0, place_ref, m0, s0)
        add_split(k1, g1, place_ref, m1, s1)
        pass_ref[...] = later_ref[...]
        d_norm = p0[...] + p1[...].astype(F32) + p2[...].astype(F32) + p3[...].astype(F32)
        gain = vec_ref[1:2, :width]
        _, normed, inverse = layer_norm(x_ref[...].astype(F32), gain, 0.0)
        low_ref[...] = (dy_ref[...] + norm_back(d_norm, normed, inverse, gain)).astype(LOW)
        grad_ref[:, :width] = jnp.sum(d_norm * normed, 0, keepdims=True)
        grad_ref[:, width : 2 * width] = jnp.sum(d_norm, 0, keepdims=True)
        grad_ref[:, 2 * width : 3 * width] = sum_ref[...]
        grad_ref[:, 3 * width :] = jnp.zeros((1, total - 3 * width), F32)
        y, k, c = place_ref[0], place_ref[2], place_ref[4]
        for j in range(4):
            start = unit_start(width, j, y, k, c, part)
            grad_ref[:, pl.ds(start, part)] = up_ref[:, j * part : (j + 1) * part]
        mixed_ref[:, 8:, :] = jnp.zeros((owners, 8, LANES), F32)
        lane = lax.broadcasted_iota(jnp.int32, (8, LANES), 1)
        for owner in range(owners):
            rows_here = jnp.zeros((8, LANES), F32)
            for group in range(4):
                start = owner * vocab + group * 8
                value = table_ref[start : start + 8, :]
                if group:
                    value = pltpu.roll(value, group * vocab, 1)
                mine = (lane >= group * vocab) & (lane < (group + 1) * vocab)
                rows_here = jnp.where(mine, value, rows_here)
            mixed_ref[owner, :8, :] = rows_here
            block = ends_ref[:, owner // 4 * LANES : (owner // 4 + 1) * LANES]
            if owner % 4:
                block = pltpu.roll(block, LANES - owner % 4 * vocab, 1)
            mine = lax.broadcasted_iota(jnp.int32, (2, LANES), 1) < vocab
            mixed_ref[owner, 8:10, :] = jnp.where(mine, block[:2], 0.0)
        first_half = lax.broadcasted_iota(jnp.int32, (1, LANES), 1) < LANES // 2
        for pair in range(owners // 4):
            at = pair * 7 * LANES
            tiles = [grad_ref[:, at + q * LANES : at + (q + 1) * LANES] for q in range(7)]
            turned = [pltpu.roll(tile, LANES // 2, 1) for tile in tiles[3:]]
            even = tiles[:3] + [jnp.where(first_half, tiles[3], 0.0)]
            odd = [jnp.where(first_half, turned[q], turned[q + 1]) for q in range(3)]
            odd = odd + [jnp.where(first_half, turned[3], 0.0)]
            for side, lines in enumerate((even, odd)):
                for q in range(4):
                    owner = owners // 2 + 2 * pair + side
                    mixed_ref[owner, VECTOR_ROW + q : VECTOR_ROW + q + 1, :] = lines[q]

    outs = [((rows, width), LOW), ((owners, 16, LANES), F32)]
    shape = later.shape[1:]
    outs = outs + [(shape, F32)] * 2 + [(shape, LOW)] * 2 + [(later.shape, LOW)]
    args = (*pieces, x_low, dy, vec, down_sum, bias_up, table_local, ends_local, *keeps, *gots, later, place)
    scratch = [pltpu.VMEM((1, total), F32)]
    return simple(kernel, "input_backward", outs, *args, smem=(16,), scratch=scratch, us=2.0)


def pack_states(vectors, tables, biases, behind):
    features, table_rows = tables[0].shape
    chunk = vectors[0].shape[1]
    many = features + 8

    def kernel(*refs):
        out_ref = refs[9]
        for number in range(3):
            vec_ref, tab_ref, bias_ref = refs[number], refs[3 + number], refs[6 + number]
            start = number * many
            pad = jnp.zeros((features, LANES - table_rows), F32)
            out_ref[start : start + features, :] = jnp.concatenate([tab_ref[...], pad], 1)
            lines = [vec_ref[:, j * LANES : (j + 1) * LANES] for j in range(3)]
            rest = chunk - 3 * LANES
            ends = jnp.concatenate(
                [vec_ref[:, 3 * LANES :], jnp.zeros((1, LANES - rest), F32)], 1
            )
            bias = bias_ref[...]
            bias = jnp.concatenate([bias, jnp.zeros((1, LANES - bias.shape[1]), F32)], 1)
            line = lax.broadcasted_iota(jnp.int32, (8, LANES), 0)
            tail = jnp.zeros((8, LANES), F32)
            for row, value in enumerate(lines + [ends, bias]):
                tail = jnp.where(line == row, value, tail)
            out_ref[start + features : start + many, :] = tail

    args = (*vectors, *tables, *biases)
    return simple(kernel, "pack_states", [((3 * many, LANES), F32)], *args, behind=behind)[0]


def last_sums(dh_all, rows_sum, normed, inverse, vec, mixed, scalars, place, packed, chunk, table_rows):
    vocab, width = rows_sum.shape
    total = vec.shape[1]
    devices = dh_all.shape[0]

    def kernel(*refs):
        dh_all_ref, sum_ref, norm_ref, inv_ref, vec_ref, mixed_ref, known_ref, place_ref = refs[:8]
        packed_ref, scalar_ref, norm_ref_out, parts_ref = refs[8:12]
        vector_outs, table_outs, bias_outs = refs[12:15], refs[15:18], refs[18:21]
        dh_ref, all_ref, emb_ref = refs[21:]
        many = vocab + 8
        table_ins = [packed_ref[j * many : j * many + vocab, :table_rows] for j in range(3)]
        tails = [packed_ref[j * many + vocab : (j + 1) * many, :] for j in range(3)]
        vector_ins = [
            jnp.concatenate([tail[row : row + 1] for row in range(4)], 1)[:, :chunk] for tail in tails
        ]
        bias_ins = [tail[4:5, :vocab] for tail in tails]
        y, me = place_ref[0], place_ref[5]
        scalars = jnp.zeros((1, LANES), F32)
        lane = lax.broadcasted_iota(jnp.int32, (8, LANES), 1)
        for h in range(2):
            for x in range(2):
                for yy in range(2):
                    start = (h * 4 + yy * 2 + x) * LANES
                    tiles = [jnp.zeros((8, LANES), F32)] * 4
                    for spot in range(4):
                        device = ((yy * 2 + h) * 2 + spot // 2) * 4 + x * 2 + spot % 2
                        packed = dh_all_ref[device, :8, :]
                        mine = (lane >= spot * vocab) & (lane < (spot + 1) * vocab)
                        for group in range(4):
                            by = (spot - group) * vocab % LANES
                            moved = pltpu.roll(packed, by, 1) if by else packed
                            tiles[group] = jnp.where(mine, moved, tiles[group])
                        ends = dh_all_ref[device, 8:, :]
                        scalars = scalars + ends[0:1]
                        unit = 3 * width + device % 16 * 2 * LANES + yy * LANES
                        all_ref[:, unit : unit + LANES] = ends[1:2]
                    for group in range(4):
                        dh_ref[group * 8 : (group + 1) * 8, start : start + LANES] = tiles[group]
        dh = dh_ref[...]
        normed = norm_ref[...]
        rows = sum_ref[...]
        embed = rows + norm_back(dh, normed, inv_ref[...], vec_ref[0:1, :width])
        emb_ref[...] = embed
        all_ref[:, :width] = jnp.sum(dh * normed, 0, keepdims=True)
        all_ref[:, width : 2 * width] = jnp.sum(dh, 0, keepdims=True)
        all_ref[:, 2 * width : 3 * width] = jnp.sum(rows, 0, keepdims=True)
        lane = lax.broadcasted_iota(jnp.int32, (1, LANES), 1)
        bias = jnp.where((lane >= vocab) & (lane < 2 * vocab), scalars, 0.0)
        vector = all_ref[...]

        def squares(value):
            return jnp.sum(jnp.sum(value * value, 0, keepdims=True), 1, keepdims=True)

        total_squares = scalars[:, 0:1] + squares(bias) + squares(embed) + squares(vector)
        norm = jnp.sqrt(total_squares)
        factor = jnp.minimum(1.0, CLIP_AT / norm)
        known = known_ref[...]
        row = jnp.where(lane == 0, norm, jnp.where(lane == 1, known[:, 0:1], known[:, 1:2]))
        row = jnp.where(lane == 3, scalars[:, 1:2], row)
        scalar_ref[...] = jnp.where(lane == 4, factor, row)
        norm_ref_out[...] = norm
        parts_ref[...] = row[:, 1:4]

        def update(ins, outs, grad):
            new = adam(*ins, grad * factor, RATE_VEC, 0.0)
            for ref, value in zip(outs, new):
                ref[...] = value

        odd = lax.rem(me, 2)
        start = pl.multiple_of(me * chunk - odd * (LANES // 2), LANES)
        mine = all_ref[:, pl.ds(start, chunk + LANES // 2)]
        mine = jnp.where(odd == 0, mine, pltpu.roll(mine, chunk, 1))
        far = jnp.concatenate(
            [mixed_ref[VECTOR_ROW + q : VECTOR_ROW + q + 1, :] for q in range(4)], 1
        )
        update(vector_ins, vector_outs, jnp.where(y == 0, mine, far)[:, :chunk])
        number = y * (devices // 2) + me
        block = emb_ref[:, pl.ds(pl.multiple_of(number // 4 * LANES, LANES), LANES)]
        block = pltpu.roll(block, lax.rem(LANES - lax.rem(number, 4) * vocab, LANES), 1)
        padded = jnp.concatenate([block, jnp.zeros((LANES - vocab, LANES), F32)], 0).T[:vocab, :]
        wide = lax.broadcasted_iota(jnp.int32, (vocab, LANES), 1)
        head = jnp.concatenate(
            [mixed_ref[:8, :]]
            + [pltpu.roll(mixed_ref[:8, :], LANES - group * vocab, 1) for group in range(1, 4)],
            0,
        )
        ends = jnp.concatenate([mixed_ref[8:16, :], jnp.zeros((LANES - 8, LANES), F32)], 0).T[:vocab]
        grad = jnp.where(wide < vocab, padded, pltpu.roll(head, vocab, 1))
        grad = jnp.where(wide < 2 * vocab, grad, pltpu.roll(ends, 2 * vocab, 1))
        update(table_ins, table_outs, grad[:, :table_rows])
        update(bias_ins, bias_outs, pltpu.roll(bias, LANES - vocab, 1)[:, :vocab])

    args = (dh_all, rows_sum, normed, inverse, vec, mixed, scalars, place, packed)
    outs = [((1, LANES), F32), ((1, 1), F32), ((1, 3), F32)] + [((1, chunk), F32)] * 3 + [((vocab, table_rows), F32)] * 3
    outs = outs + [((1, vocab), F32)] * 3
    scratch = [
        pltpu.VMEM((vocab, width), F32),
        pltpu.VMEM((1, total), F32),
        pltpu.VMEM((vocab, width), F32),
    ]
    return simple(
        kernel, "last_sums", outs, *args, smem=(7,), scratch=scratch
    )


def body_fast(
    tokens,
    lengths,
    counted,
    partners,
    qkv_weight,
    out_weight,
    up_weight,
    down_weight,
    vectors,
    tables,
    head_bias,
    *states,
):
    y, h, k, x, c = (lax.axis_index(a) for a in ALL)
    me = lax.axis_index(PLANE)
    place = scalars_of(y, h, k, x, c, me)
    slots = tokens.shape[1]
    vocab = head_bias.shape[0]
    plane, everyone = 16, 32

    rows, down_keep, down_send, out_one, out_two = cut_first(
        tables.T, vectors, tokens, lengths, down_weight[0], out_weight[0], place
    )
    down_far = flip(down_send, ("y",), (1,))
    routes = [[], []]
    for device in range(everyone):
        yy, hh, kk, xx, cc = (device >> 4, device >> 3 & 1, device >> 2 & 1, device >> 1 & 1, device & 1)
        owner = cc * 8 + kk * 4 + yy * 2 + hh
        for step in range(2):
            routes[step].append(((xx ^ step) * plane + owner, device))
    out_one = lax.ppermute(out_one, ALL, routes[0])
    out_two = lax.ppermute(out_two, ALL, routes[1])
    rows = [rows] + [flip(rows, ("h", "x"), bits) for bits in NEAR]
    tail = first_rows(down_keep, down_far, out_one, out_two, place)
    tails = across(tail)
    shards = cut_weights(qkv_weight[0], up_weight[0], rows, (tail,))
    shards = trade(shards, ("y", "k", "c"))
    table_all = unpack_rows(shards, place)
    low_tables, vec, h0, normed0, inverse0, part = token_products(table_all, shards, place)
    uppers = upper_rows(shards, down_keep, down_far, out_one, out_two, place)
    nears = [flip(piece, ("x",), (1,)) for piece in uppers]
    fars = [flip(piece, ("h",), (1,)) for piece in uppers]
    crosses = [flip(piece, ("x",), (1,)) for piece in fars]
    part = add_two(part, flip(part, ("x",), (1,)))
    parts = [part, flip(part, ("h",), (1,))]
    bias, rope, hot, target_hot, seq_weight, seq_count = slot_tables(
        table_all, counted, place, rope_constant(slots), (part,)
    )

    packed = pack_states(
        (vectors, states[4], states[11]),
        (tables.T, states[5].T, states[12].T),
        (head_bias[None], states[6][None], states[13][None]),
        (seq_count,),
    )

    keep, send, qkv0, att0, act0, slope0, w_out0, w_down0 = first_group_forward(
        parts, tails, vec, place, hot, rope, bias, (fars[0], nears[0], nears[1])
    )
    act_far = flip(act0, ("y",), (1,))
    pieces = group_sums(keep, send, ())
    x_low, h_low = first_finish_rows(pieces, hot, low_tables, vec, (fars[1], crosses[0]))

    uppers = [*uppers, *nears, *fars, *crosses]
    keep, send, hs, qkv, att, act, slope, w_in, w_out, w_down = group_forward(
        group_pieces(h_low), uppers, vec, place, rope, bias
    )
    normed_f, inverse_f, final_low, logp, sums = fast_loss_forward(
        x_low,
        group_sums(keep, send),
        vec,
        low_tables,
        head_bias,
        target_hot,
        seq_weight,
        seq_count,
    )
    sums = spread(sums, ALL).reshape(everyone, LANES)
    dy, dy_low, table_local, ends_local, bias_local, down_sum, scalars = fast_loss_backward(
        sums,
        partners,
        place,
        normed_f,
        inverse_f,
        final_low,
        logp,
        low_tables,
        target_hot,
        seq_weight,
        plane,
        seq_count.shape[0],
    )

    keep, send, d_rows, d_in, bias_up = group_backward(
        group_pieces(dy_low), qkv, slope, w_in, w_out, w_down, rope, bias
    )
    keep_1, keep_2, keep_0, send_1, send_2, send_0 = weight_gradients(
        hs, d_in, act, att, d_rows, place
    )
    gots = [flip(piece, ("x",), (1,)) for piece in (send_0, send_1)]
    terms = group_sums(keep, send, (send_0,))
    own_low, mixed, mine_0, mine_1, send_0, send_1, send_2 = fast_input_backward(
        terms,
        x_low,
        dy,
        vec,
        down_sum,
        bias_up,
        table_local,
        ends_local,
        (keep_0, keep_1),
        gots,
        send_2,
        place,
    )

    pieces = group_pieces(own_low)
    got_2 = flip(send_2, ("x",), (1,))
    far_0, far_1 = (flip(piece, ("h",), (1,)) for piece in (send_0, send_1))
    keep, send, mine_2, send_2 = first_group_backward(
        pieces,
        qkv0,
        att0,
        slope0,
        w_out0,
        w_down0,
        hot,
        rope,
        bias,
        mixed,
        keep_2,
        got_2,
        place,
        (far_0,far_1),
    )
    far_2 = flip(send_2, ("h",), (1,))
    part, send, down_mine = fold(keep, flip(send, ("x",), (1,)), mine_0, far_0, place, ())
    down_far = lax.ppermute(down_mine, "y", [(0, 1)])
    parts = [part, flip(send, ("h",), (1,))]
    first_in, first_down, first_out, dh, rows_sum, mixed = token_gradients(
        parts, h0, shards, act0, act_far, place, (far_2,)
    )
    shards, out_one, out_two, last = owner_pieces(
        (mine_1, mine_2),
        (far_1, far_2),
        down_mine,
        first_in,
        first_down,
        first_out,
        dh,
        mixed,
        scalars,
        bias_local,
        place,
    )
    out_one = lax.ppermute(out_one, ALL, [(b, a) for a, b in routes[0]])
    out_two = lax.ppermute(out_two, ALL, [(b, a) for a, b in routes[1]])
    shards = trade(shards, ("y", "k", "c"))
    sums, mixed = norm_sums(shards, dh, last, place, ())
    scalars, norm, parts, *small = last_sums(
        trade(sums, ALL),
        rows_sum,
        normed0,
        inverse0,
        vec,
        mixed,
        scalars,
        place,
        packed,
        vectors.shape[1],
        tables.shape[0],
    )
    results = update_all(
        scalars,
        shards,
        first_down,
        down_mine,
        down_far,
        out_one,
        out_two,
        place,
        (qkv_weight, out_weight, up_weight, down_weight),
        states[:4],
        states[7:11],
        (RATE_MAT, RATE_OUT, RATE_MAT, RATE_MAT),
    )
    results = list(results)
    results.extend(small[:3])
    results.extend(value.T for value in small[3:6])
    results.extend(value[0] for value in small[6:])
    return (norm.reshape(()), parts.reshape(3), *results)


def body(
    tokens,
    lengths,
    counted,
    partners,
    qkv_weight,
    out_weight,
    up_weight,
    down_weight,
    vectors,
    tables,
    head_bias,
    qkv_moment,
    out_moment,
    up_moment,
    down_moment,
    vector_moment,
    table_moment,
    bias_moment,
    qkv_square,
    out_square,
    up_square,
    down_square,
    vector_square,
    table_square,
    bias_square,
):
    sections = lax.axis_size("y")
    spans = lax.axis_size("h")
    plane = lax.axis_size(PLANE)
    everyone = sections * plane
    y, h, k, x, c = (lax.axis_index(a) for a in ALL)
    me = lax.axis_index(PLANE)
    group = Group(sections, spans)
    micro, slots = tokens.shape
    per_pack = lengths.shape[1]
    width = qkv_weight.shape[2] // 3
    hidden = up_weight.shape[2]
    vocab = head_bias.shape[0]
    own_in = qkv_weight.shape[1]
    own_out = out_weight.shape[1]
    own_ff = down_weight.shape[1]
    shares = 4 * sections
    heads = width // HEAD
    shard_heads = heads // shares
    shard_width = width // shares
    shard_ff = hidden // shares
    rows = micro * slots // sections
    block_rows = micro * slots
    group_rows = 4 * block_rows
    group_packs = 4 * micro
    own_packs = max(1, rows // slots)
    own_pack_rows = min(rows, slots)

    low_qkv = qkv_weight[0].astype(LOW)
    low_out = out_weight[0].astype(LOW)
    low_up = up_weight[0].astype(LOW)
    low_down = down_weight[0].astype(LOW)

    table_part = tables.shape[1]
    vector_part = vectors.shape[1]
    small = jnp.concatenate(
        [
            tables.astype(LOW).reshape(-1),
            vectors[0].astype(LOW),
            lengths.astype(LOW).reshape(-1),
        ]
    )
    small_all = spread(small, ALL)
    cut_one = tables.size
    cut_two = cut_one + vector_part
    table_low = (
        small_all[:, :cut_one]
        .reshape(everyone, tables.shape[0], table_part)
        .transpose(1, 0, 2)
        .reshape(tables.shape[0], width)
    )
    vec_low = small_all[:, cut_one:cut_two].reshape(sections, plane * vector_part)
    vec_all = vec_low.astype(F32)
    lengths_all = small_all[:, cut_two:].astype(jnp.int32)
    embed = table_low[:vocab].astype(F32)
    head_low = table_low[vocab : 2 * vocab]
    final_gain = table_low[2 * vocab].astype(F32)
    final_bias = table_low[2 * vocab + 1].astype(F32)
    out_bias = head_bias.astype(LOW).astype(F32)

    segment, position = jax.vmap(lambda row: pack_layout(row, slots))(lengths)
    target = jnp.concatenate([tokens[:, 1:], jnp.zeros((micro, 1), jnp.int32)], 1)
    same = jnp.concatenate([segment[:, 1:] == segment[:, :-1], jnp.zeros((micro, 1), bool)], 1)
    weight = (same & (counted == 1)).astype(F32)
    sequence = segment + per_pack * jnp.arange(micro, dtype=jnp.int32)[:, None]

    def own(array):
        return lax.dynamic_slice_in_dim(array.reshape((block_rows,) + array.shape[2:]), y * rows, rows, 0)

    own_target = own(target)
    own_weight = own(weight)
    own_sequence = own(sequence)
    first_pack = (y * rows) // slots

    def packs_of(array):
        return lax.dynamic_slice_in_dim(array, first_pack, own_packs, 0)

    pack_tokens = packs_of(tokens)
    pack_segment = packs_of(segment)
    pack_position = packs_of(position)
    own_tokens = own(tokens).reshape(own_packs, own_pack_rows)
    own_segment = own(segment).reshape(own_packs, own_pack_rows)
    own_position = own(position).reshape(own_packs, own_pack_rows)
    pack_index = jnp.broadcast_to(jnp.arange(slots, dtype=jnp.int32), (own_packs, slots))
    own_index = (
        jnp.broadcast_to(jnp.arange(own_pack_rows, dtype=jnp.int32), (own_packs, own_pack_rows))
        + (y * rows) % slots
    )
    own_mask = (own_segment[:, :, None] == pack_segment[:, None, :]) & (
        pack_index[:, None, :] <= own_index[:, :, None]
    )
    target_hot = one_hot(own_target, vocab, F32)
    local_seqs = micro * per_pack
    seq_weight = one_hot(own_sequence, local_seqs, F32) * own_weight[:, None]
    seq_count = jnp.sum(
        one_hot(sequence.reshape(-1), local_seqs, F32) * weight.reshape(-1)[:, None], 0
    )
    hot_pack = one_hot(pack_tokens.reshape(-1), vocab, LOW)
    hot_own = one_hot(own_tokens.reshape(-1), vocab, LOW)
    own_bias = jnp.where(own_mask, 0.0, -1e30).reshape(rows, slots)
    own_rope = rope_rows(own_position.reshape(-1))
    pack_rope = own_rope if rows % slots == 0 else rope_rows(pack_position.reshape(-1))

    lengths_plane = lengths_all.reshape(sections, spans, 2, 2, 2, micro * per_pack)[0]
    lengths_group = pick(lengths_plane, h)[:, :, :, :]
    lengths_group = lax.dynamic_index_in_dim(lengths_group, x, 1, keepdims=False)

    parts = []
    for dc in range(2):
        for dk in range(2):
            block_lengths = pick(pick(lengths_group, (k - dk) % 2), (c - dc) % 2)
            parts.append(block_lengths.reshape(micro, per_pack))
    group_lengths = jnp.concatenate(parts, 0)
    group_segment, group_position = jax.vmap(lambda row: pack_layout(row, slots))(group_lengths)
    turn = (y - jnp.arange(sections)) % sections

    def by_offset(array):
        cut = array.reshape((4, sections, rows) + array.shape[2:])
        return jnp.take(cut, turn, axis=1).reshape((4 * sections * rows,) + array.shape[2:])

    if rows % slots == 0:
        group_segment = by_offset(group_segment).reshape(group_packs, slots)
        group_position = by_offset(group_position).reshape(group_packs, slots)
    group_index = jnp.arange(slots, dtype=jnp.int32)
    group_mask = (group_segment[:, :, None] == group_segment[:, None, :]) & (
        group_index[None, :] <= group_index[:, None]
    )
    group_bias = jnp.where(group_mask, 0.0, -1e30).reshape(group_rows, slots)
    group_rope = rope_rows(group_position.reshape(-1))

    def to_group(value):
        got = group.gather(value).reshape((4, sections, rows) + value.shape[1:])
        if rows % slots:
            got = jnp.take(got, turn, axis=1)
        return got.reshape((group_rows,) + value.shape[1:])

    def from_group(keep, send):
        def cut(value):
            value = value.reshape((2, sections, rows) + value.shape[1:])
            if rows % slots:
                value = jnp.take(value, turn, axis=1)
            return value.reshape((2 * sections, rows) + value.shape[3:])

        return group.scatter(cut(keep), cut(send))

    part_ff = own_ff // sections

    def columns_by_shard(qkv_rows, up_rows):
        cut_qkv = qkv_rows.reshape(own_in, 3, 2, 2, sections, shard_width)
        cut_up = up_rows.reshape(own_in, spans, 2, 2, 2, sections, part_ff)
        pieces = []
        for cc in range(2):
            for kk in range(2):
                for yy in range(sections):
                    pieces.append(
                        jnp.concatenate(
                            [cut_qkv[:, j, cc, kk, yy] for j in range(3)]
                            + [
                                cut_up[:, hh, kk, xx, cc, yy]
                                for hh in range(spans)
                                for xx in range(2)
                            ],
                            1,
                        )
                    )
        return jnp.stack(pieces).reshape((2, 2, sections) + pieces[0].shape)

    def columns_back(shards):
        cut = shards[..., : 3 * shard_width].reshape(2, 2, sections, own_in, 3, shard_width)
        qkv_rows = cut.transpose(3, 4, 0, 1, 2, 5).reshape(own_in, 3 * width)
        cut = shards[..., 3 * shard_width :].reshape(
            2, 2, sections, own_in, spans, 2, part_ff
        )
        up_rows = cut.transpose(3, 4, 1, 5, 0, 2, 6).reshape(own_in, hidden)
        return (qkv_rows, up_rows)

    small_out = width // everyone

    def out_routes(layer):
        routes = [[] for _ in range(sections)]
        for yy in range(sections):
            for hh in range(spans):
                for kk in range(2):
                    for xx in range(2):
                        for cc in range(2):
                            share = (cc * 2 + kk) * sections + yy
                            number = share * (2 * spans) + hh * 2 + xx
                            device = yy * plane + ((hh * 2 + kk) * 2 + xx) * 2 + cc
                            owner = layer * plane + number // sections
                            routes[number % sections].append((owner, device))
        return routes

    share_index = (c * 2 + k) * sections + y
    out_part = (share_index * (2 * spans) + h * 2 + x) % sections

    by_shard = columns_by_shard(low_qkv, low_up)
    give = shift(pick(by_shard, 1 - c), "c", 1)
    over_c = ordered(pick(by_shard, c), give, c, 1)
    give = shift(pick(over_c, 1 - k), "k", 1)
    over_k = ordered(pick(over_c, k), give, k, 0)

    gain0, bias0 = vec_all[0, :width], vec_all[0, width : 2 * width]
    bias_down0, bias_up0 = vec_all[0, 2 * width : 3 * width], vec_all[0, 3 * width :]
    h0_full, normed0, inverse0 = layer_norm(embed, gain0, bias0)
    h0 = h0_full.astype(LOW)
    pair_rows = 2 * own_in
    h0_here = jnp.concatenate(
        [
            lax.dynamic_slice_in_dim(h0, ((h * 2 + kk) * 2 + x) * pair_rows, pair_rows, 1)
            for kk in range(2)
        ],
        1,
    )
    both = [
        mm(h0_here, over_k[:, :, yy].reshape(4 * own_in, -1)) for yy in range(sections)
    ]
    spread_over = 2 * spans
    token_rows = vocab // spread_over
    proj_part = jnp.concatenate([part[:, : 3 * shard_width] for part in both], 1)
    proj_part = proj_part.reshape(spread_over, -1, own_ff)
    u_part = jnp.stack(
        [
            jnp.concatenate(
                [
                    part[:, 3 * shard_width + j * part_ff : 3 * shard_width + (j + 1) * part_ff]
                    for part in both
                ],
                1,
            )
            for j in range(spread_over)
        ]
    )
    mixed = jnp.sum(trade(jnp.concatenate([u_part, proj_part], 1), ("h", "x")), 0)
    u_own = mixed[:vocab] + lax.dynamic_slice_in_dim(bias_up0, me * own_ff, own_ff, 0)
    proj_own = mixed[vocab:]
    a0, slope0 = gelu_pair(u_own)
    a0 = a0.astype(LOW)
    ffn_part = jnp.where(y == 0, mm(a0, low_down), 0.0)
    for yy in range(1, sections):
        got = lax.ppermute(proj_own, "y", [(0, yy)])
        proj_own = jnp.where(y == yy, got, proj_own)
    proj_all = spread(proj_own, PLANE)
    ffn_cols = trade(ffn_part.reshape(vocab, everyone, -1).transpose(1, 0, 2), ALL)
    ffn_cols = jnp.sum(ffn_cols, 0)
    proj_table = (
        proj_all.reshape(spans, 2, 2, 2, token_rows, sections, 3, shard_width)
        .transpose(0, 2, 4, 6, 3, 1, 5, 7)
        .reshape(vocab, 3 * width)
    )
    ffn_table = spread(ffn_cols, ALL).transpose(1, 0, 2).reshape(vocab, width)
    query0, keys0, values0, att0 = first_forward(
        proj_table, hot_own, hot_pack, own_rope, pack_rope, own_bias, own_packs
    )

    first_out = low_out
    for yy in range(1, sections):
        got = lax.ppermute(low_out, "y", [(0, yy)])
        first_out = jnp.where(y == yy, got, first_out)
    pieces = jnp.stack([first_out] + [shift(first_out, "h", s) for s in range(1, spans)])
    pieces = jnp.take(pieces, (h - jnp.arange(spans)) % spans, axis=0)
    pieces = after(pieces, h0)
    pieces = ordered(pieces, after(shift(pieces, "k", 1), mixed), k, 1)
    pieces = ordered(pieces, after(shift(pieces, "x", 1), proj_table), x, 2)
    pieces = ordered(pieces, after(shift(pieces, "c", 1), att0), c, 3)
    first_out = pieces.reshape(width, width)

    stay = embed + ffn_table + bias_down0
    x_low, h_low = first_finish(
        att0, first_out, hot_own, stay, vec_all[1, :width], vec_all[1, width : 2 * width]
    )

    shard_weights = []
    for layer in range(1, sections):
        cut_down = low_down.reshape(sections, part_ff, width)
        down_piece = cut_down[layer]
        for yy in range(sections):
            if yy != layer:
                got = lax.ppermute(cut_down[yy], "y", [(layer, yy)])
                down_piece = jnp.where(y == yy, got, down_piece)
        cut_out = low_out.reshape(sections, small_out, width)
        out_piece = jnp.zeros((small_out, width), LOW)
        for p, route in enumerate(out_routes(layer)):
            got = lax.ppermute(cut_out[p], ALL, route)
            out_piece = jnp.where(out_part == p, got, out_piece)
        tail = jnp.concatenate([down_piece, out_piece], 0)
        tail = across_gather(tail, x, h0, ffn_part, att0)
        w_down = tail[:, :, :part_ff].reshape(shard_ff, width)
        w_out = tail[:, :, part_ff:].reshape(shard_width, width)
        mine = over_k[:, :, layer]
        for yy in range(sections):
            if yy != layer:
                got = lax.ppermute(over_k[:, :, yy], "y", [(layer, yy)])
                mine = jnp.where(y == yy, got, mine)
        whole = across_gather(mine, x, mixed, proj_table, h_low)
        w_in = whole.transpose(0, 2, 1, 3, 4, 5).reshape(width, -1)
        if shard_width < LANES:
            pad = LANES - shard_width
            cut = [w_in[:, j * shard_width : (j + 1) * shard_width] for j in range(3)]
            cut = [jnp.pad(piece, ((0, 0), (0, pad))) for piece in cut]
            w_in = jnp.concatenate(cut + [w_in[:, 3 * shard_width :]], 1)
            w_out = jnp.pad(w_out, ((0, pad), (0, 0)))
        shard_weights.append((w_in, w_out, w_down))

    kept = []
    for layer in range(1, sections):
        w_in, w_out, w_down = shard_weights[layer - 1]
        vec = vec_all[layer]
        gain, bias, bias_down = (vec[j * width : (j + 1) * width] for j in range(3))
        cut = vec[3 * width :].reshape(spans, 2, 2, 2, sections, part_ff)
        cut = lax.dynamic_index_in_dim(cut, k, 1, keepdims=False)
        cut = lax.dynamic_index_in_dim(cut, c, 2, keepdims=False)
        bias_up = lax.dynamic_index_in_dim(cut, y, 2, keepdims=False).reshape(shard_ff)
        if layer > 1:
            x_low = xs.astype(LOW)
            h_low = layer_norm(x_low.astype(F32), gain, bias)[0].astype(LOW)
        hs = to_group(h_low)
        keep, send, qkv, att, act, slope = upper_forward(
            hs, w_in, w_out, w_down, bias_up, group_rope, group_bias, slots
        )
        kept.append((x_low, gain, bias, hs, qkv, att, act, slope))
        pieces = from_group(keep, send)
        if layer < sections - 1:
            xs = x_low.astype(F32) + sum(piece.astype(F32) for piece in pieces) + bias_down

    normed_f, inverse_f, final_low, logp, lik_sum = loss_forward(
        x_low, pieces, bias_down, final_gain, final_bias, head_low, out_bias, target_hot, seq_weight
    )
    sums = spread(jnp.concatenate([lik_sum[0], seq_count]), ALL)
    dy, own_low, table_local, bias_local, down_sum, scalars = loss_backward(
        sums,
        partners,
        me[None],
        normed_f,
        inverse_f,
        final_low,
        logp,
        head_low,
        final_gain,
        target_hot,
        seq_weight,
        plane,
    )
    loss_total, count_total = scalars[0, 0], scalars[0, 1]
    penalty_local = jnp.where(y == 0, scalars[0, 2], 0.0)
    bias_local = bias_local[0]

    def finish_shards(layer, out_grad, down_grad, in_grad, first, second, last):
        tail = jnp.concatenate(
            [
                down_grad.reshape(spans, 2, part_ff, width),
                out_grad.reshape(spans, 2, small_out, width),
            ],
            2,
        )
        tail = across_scatter(tail, x, first, second, last).astype(LOW)
        down_piece, out_piece = tail[:part_ff], tail[part_ff:]
        down_rows = jnp.stack(
            [
                down_piece if yy == layer else lax.ppermute(down_piece, "y", [(yy, layer)])
                for yy in range(sections)
            ]
        ).reshape(own_ff, width)
        out_rows = jnp.stack(
            [
                lax.ppermute(out_piece, ALL, [(b, a) for a, b in route])
                for route in out_routes(layer)
            ]
        ).reshape(own_out, width)
        inner = in_grad.reshape(spans, 2, 2, 2, own_in, -1).transpose(0, 2, 1, 3, 4, 5)
        inner = across_scatter(inner, x, first, second, last).astype(LOW)
        keep = pick(inner, k)
        give = shift(pick(inner, 1 - k), "k", 1)
        over_k = ordered(keep, give, k, 1)
        keep = pick(over_k, c)
        give = shift(pick(over_k, 1 - c), "c", 1)
        over_c = ordered(keep, give, c, 0)
        shards = jnp.stack(
            [
                over_c if yy == layer else lax.ppermute(over_c, "y", [(yy, layer)])
                for yy in range(sections)
            ],
            2,
        )
        qkv_rows, up_rows = columns_back(shards)
        return (qkv_rows, out_rows, up_rows, down_rows)

    pending = []
    vector_locals = []
    for layer in range(sections - 1, 0, -1):
        w_in, w_out, w_down = shard_weights[layer - 1]
        x_low, gain, bias, hs, qkv, att, act, slope = kept[layer - 1]
        d_rows = to_group(own_low)
        keep, send, d_in, bias_up_grad = upper_backward(
            d_rows, qkv, slope, w_in, w_out, w_down, group_rope, group_bias, slots
        )
        pieces = from_group(keep, send)
        above = dy
        own_low, vec_sums, dyb_token = input_backward(pieces, x_low, dy, gain, hot_own)
        dy = own_low.astype(F32)
        att, act, hs, d_in, d_rows = lax.optimization_barrier((att, act, hs, d_in, d_rows, keep))[:5]
        out_grad = t_mm(att, d_rows)[:shard_width]
        down_grad = t_mm(act, d_rows)
        in_grad = t_mm(hs, d_in)
        if shard_width < LANES:
            cut = [in_grad[:, j * LANES : j * LANES + shard_width] for j in range(3)]
            in_grad = jnp.concatenate(cut + [in_grad[:, 3 * LANES :]], 1)
        bias_up_grad = bias_up_grad.reshape(spans, 2, part_ff)
        place = (
            (jnp.arange(2) == k)[None, :, None, None, None, None]
            & (jnp.arange(2) == c)[None, None, None, :, None, None]
            & (jnp.arange(sections) == y)[None, None, None, None, :, None]
        )
        bias_up_grad = jnp.where(place, bias_up_grad[:, None, :, None, None, :], 0.0)
        vector_locals.append(
            jnp.concatenate([vec_sums[0], vec_sums[1], down_sum[0], bias_up_grad.reshape(-1)])
        )
        down_sum = vec_sums[2:3]
        pending.append((layer, out_grad, down_grad, in_grad, keep))
    vector_locals = vector_locals[::-1]

    dyb_cols = trade(dyb_token.reshape(vocab, everyone, -1).transpose(1, 0, 2), ALL)
    dq_token, dk_token, dv_token, first_out_grad = first_backward(
        own_low,
        query0,
        keys0,
        values0,
        att0,
        hot_own,
        hot_pack,
        own_rope,
        pack_rope,
        own_bias,
        first_out,
        own_packs,
    )
    dyb_cols = jnp.sum(after(dyb_cols, first_out_grad), 0)
    dyb_sum = spread(dyb_cols, ALL).transpose(1, 0, 2).reshape(vocab, width)
    token_part = jnp.concatenate([dq_token, dk_token, dv_token], 1)
    token_cols = trade(token_part.reshape(vocab, everyone, -1).transpose(1, 0, 2), ALL)
    token_cols = jnp.sum(token_cols, 0).astype(LOW)
    du_own = (mm_exact(dyb_sum, low_down, ((1,), (1,))) * slope0).astype(LOW)
    du_sum = spread(du_own, PLANE).transpose(1, 0, 2).reshape(vocab, hidden)
    dproj_sum = spread(token_cols, ALL).transpose(1, 0, 2).reshape(vocab, 3 * width)
    dh_own = mm_t(dproj_sum, low_qkv) + mm_t(du_sum, low_up)

    shard_grads = [None] * sections
    for layer, out_grad, down_grad, in_grad, keep in pending:
        shard_grads[layer] = finish_shards(
            layer, out_grad, down_grad, in_grad, own_low, first_out_grad, du_own
        )
    vector_cut = jnp.stack([jnp.zeros_like(vector_locals[0])] + vector_locals)
    vector_cut = vector_cut.reshape(everyone, vector_part)
    table_cut = table_local.reshape(-1, everyone, table_part).transpose(1, 0, 2)
    mixed = jnp.concatenate([vector_cut, table_cut.reshape(everyone, -1)], 1)
    mixed = jnp.sum(trade(after(mixed, first_out_grad), ALL), 0)
    h0_own = lax.dynamic_slice_in_dim(h0, me * own_in, own_in, 1)
    down_first = mm_exact(a0, dyb_sum, ((0,), (0,)))
    qkv_first = t_mm(h0_own, dproj_sum)
    up_first = t_mm(h0_own, du_sum)
    part = first_out_grad.reshape(spans, 2, 2, 2, own_out, width)
    part = jnp.moveaxis(part, 3, 0)
    part = pick(part, c) + shift(pick(part, 1 - c).astype(LOW), "c", 1).astype(F32)
    part = jnp.moveaxis(part, 2, 0)
    part = pick(part, x) + shift(pick(part, 1 - x).astype(LOW), "x", 1).astype(F32)
    part = jnp.moveaxis(part, 1, 0)
    part = pick(part, k) + shift(pick(part, 1 - k).astype(LOW), "k", 1).astype(F32)
    total = pick(part, h)
    for s in range(1, spans):
        total = total + shift(pick(part, (h + s) % spans).astype(LOW), "h", s).astype(F32)
    out_first = total
    for yy in range(1, sections):
        out_first = out_first + lax.ppermute(total.astype(LOW), "y", [(yy, 0)]).astype(F32)

    first = (qkv_first, out_first, up_first, down_first)
    grads = []
    for number in range(4):
        grad = first[number]
        for layer in range(1, sections):
            grad = jnp.where(y == layer, shard_grads[layer][number].astype(F32), grad)
        grads.append(grad[None])
    mixed_vector = mixed[:vector_part]
    mixed_table = mixed[vector_part:].reshape(-1, table_part)

    squares = sum((jnp.sum(g * g) for g in grads)) + jnp.sum(mixed_table * mixed_table)
    squares = squares + jnp.where(y == 0, 0.0, jnp.sum(mixed_vector * mixed_vector))
    up_sum = jnp.sum(du_sum.astype(F32), 0)
    down_sum = jnp.sum(dyb_sum, 0)
    squares = squares + jnp.where(
        (y == 0) & (me == 0), jnp.sum(up_sum * up_sum) + jnp.sum(down_sum * down_sum), 0.0
    )
    last = jnp.concatenate([squares[None], penalty_local[None], bias_local])
    last = jnp.pad(last, (0, (-last.shape[0]) % own_in)).reshape(-1, own_in)
    last = spread(jnp.concatenate([dh_own, last], 0), ALL)
    dh = last[:plane, :vocab].transpose(1, 0, 2).reshape(vocab, width)
    last = jnp.sum(last[:, vocab:], 0).reshape(-1)
    embed_grad = dyb_sum + norm_back(dh, normed0, inverse0, gain0)
    gain_grad, shift_grad = jnp.sum(dh * normed0, 0), jnp.sum(dh, 0)
    vector_first = jnp.concatenate([gain_grad, shift_grad, down_sum, up_sum])
    vector_own = lax.dynamic_slice_in_dim(vector_first, me * vector_part, vector_part, 0)
    vector_grad = jnp.where(y == 0, vector_own, mixed_vector)
    number = y * plane + me
    embed_own = lax.dynamic_slice_in_dim(embed_grad, number * table_part, table_part, 1)
    table_grad = jnp.concatenate([embed_own, mixed_table], 0)
    penalty = last[1]
    bias_grad = last[2 : 2 + vocab]
    squares = last[0] + jnp.sum(embed_grad * embed_grad) + jnp.sum(bias_grad * bias_grad)
    squares = squares + jnp.sum(gain_grad * gain_grad) + jnp.sum(shift_grad * shift_grad)
    grad_norm = jnp.sqrt(squares)
    factor = jnp.minimum(1.0, CLIP_AT / grad_norm)
    grads = grads + [vector_grad[None], table_grad, bias_grad]
    masters = (qkv_weight, out_weight, up_weight, down_weight, vectors, tables, head_bias)
    moments = (
        qkv_moment,
        out_moment,
        up_moment,
        down_moment,
        vector_moment,
        table_moment,
        bias_moment,
    )
    squares_in = (
        qkv_square,
        out_square,
        up_square,
        down_square,
        vector_square,
        table_square,
        bias_square,
    )
    rates = (RATE_MAT, RATE_OUT, RATE_MAT, RATE_MAT, RATE_VEC, RATE_VEC, RATE_VEC)
    decays = (DECAY, DECAY, DECAY, DECAY, 0.0, 0.0, 0.0)
    results = []
    for number in range(7):
        results.extend(
            adam(
                masters[number],
                moments[number],
                squares_in[number],
                grads[number] * factor,
                rates[number],
                decays[number],
            )
        )
    loss_parts = jnp.stack([loss_total, count_total, penalty])
    return (grad_norm, loss_parts, *results)


def solution(mesh):
    sections, plane = mesh.shape["section"], mesh.shape["dp"]
    fine = Mesh(mesh.devices.reshape(sections, plane // 8, 2, 2, 2), ALL)
    matrix = P("y", PLANE, None)
    vector = P("y", PLANE)
    table = P(None, ALL)
    states = (matrix, matrix, matrix, matrix, vector, table, P())
    results = []
    for spec in states:
        results.extend([spec] * 3)
    chosen = body_fast if (sections, plane) == (2, 16) else body
    return jax.shard_map(
        chosen,
        mesh=fine,
        in_specs=(P(PLANE, None), P(PLANE, None), P(PLANE, None), P(PLANE))
        + states
        + states
        + states,
        out_specs=(P(), P(), *results),
        check_vma=False,
    )
```

```python
import math

import jax
import jax.numpy as jnp
import numpy as np
from jax import lax
from jax.experimental import pallas as pl
from jax.experimental.pallas import tpu as pltpu
from jax.sharding import Mesh
from jax.sharding import PartitionSpec as P

HEAD = 64
ROT = 32
STEP = 10

EPS_NORM = 1e-05
PENALTY = 2.0
CLIP_AT = 0.02
RATE_MAT = 0.02
RATE_OUT = 0.1
RATE_VEC = 0.2
BETA_ONE = 0.9
BETA_TWO = 0.95
EPS_ADAM = 1e-08
DECAY = 0.1
GELU_C = 0.7978845608028654

ALL = ("y", "h", "k", "x", "c")
PLANE = ("h", "k", "x", "c")
LOW = jnp.bfloat16
F32 = jnp.float32
EXACT = lax.Precision.HIGHEST


def mm(left, right):
    return jnp.dot(left, right, preferred_element_type=F32)


def mm_t(left, right):
    return lax.dot_general(left, right, (((1,), (1,)), ((), ())), preferred_element_type=F32)


def t_mm(left, right):
    return lax.dot_general(left, right, (((0,), (0,)), ((), ())), preferred_element_type=F32)


def mm_exact(left, right, dims):
    return lax.dot_general(
        left.astype(F32), right.astype(F32), (dims, ((), ())), precision=EXACT
    )


def pick(array, index):
    return lax.dynamic_index_in_dim(array, index, 0, keepdims=False)


def spread(value, axes):
    many = lax.axis_size(axes)
    return lax.all_to_all(jnp.broadcast_to(value[None], (many,) + value.shape), axes, 0, 0, tiled=True)


def trade(pieces, axes):
    return lax.all_to_all(pieces, axes, 0, 0, tiled=True)


def shift(value, axis, by):
    many = lax.axis_size(axis)
    return lax.ppermute(value, axis, [(i, (i + by) % many) for i in range(many)])


def after(value, *earlier):
    return lax.optimization_barrier((value,) + earlier)[0]


def together(*values):
    return lax.optimization_barrier(values)


def ordered(own, other, bit, axis):
    return jnp.stack(
        [jnp.where(bit == 0, own, other), jnp.where(bit == 0, other, own)], axis
    )


def layer_norm(x, gain, bias):
    mean = jnp.mean(x, -1, keepdims=True)
    centred = x - mean
    inverse = lax.rsqrt(jnp.mean(centred * centred, -1, keepdims=True) + EPS_NORM)
    normed = centred * inverse
    return (normed * gain + bias, normed, inverse)


def norm_back(grad, normed, inverse, gain):
    scaled = grad * gain
    return inverse * (
        scaled
        - jnp.mean(scaled, -1, keepdims=True)
        - normed * jnp.mean(scaled * normed, -1, keepdims=True)
    )


def gelu_pair(value):
    inner = jnp.tanh(GELU_C * (value + 0.044715 * value * value * value))
    result = 0.5 * value * (1.0 + inner)
    slope = 0.5 * (1.0 + inner) + 0.5 * value * (1.0 - inner * inner) * GELU_C * (
        1.0 + 3.0 * 0.044715 * value * value
    )
    return (result, slope)


def one_hot(row, vocab, dtype):
    return (row[:, None] == jnp.arange(vocab, dtype=jnp.int32)[None, :]).astype(dtype)


def pack_layout(lengths_row, slots):
    ends = jnp.cumsum(lengths_row)
    starts = ends - lengths_row
    index = jnp.arange(slots, dtype=jnp.int32)
    segment = jnp.sum((index[:, None] >= ends[None, :]).astype(jnp.int32), 1)
    member = segment[:, None] == jnp.arange(lengths_row.shape[0], dtype=jnp.int32)[None, :]
    position = index - jnp.sum(jnp.where(member, starts[None, :], 0), 1)
    return (segment, position)


LANES = 128
VMEM_LIMIT = 25 * 1024 * 1024
VMEM_MOST = 60 * 1024 * 1024
SCALE = 1.0 / math.sqrt(HEAD)


def rope_rows(position):
    half = ROT // 2
    freq = 10000.0 ** (-2.0 * jnp.arange(half, dtype=F32) / ROT)
    angle = position.astype(F32)[:, None] * freq
    cosine, sine = (jnp.cos(angle), jnp.sin(angle))
    none, one = (jnp.zeros_like(sine), jnp.ones_like(sine))
    many = LANES // HEAD
    rest = HEAD // half - 2
    return jnp.stack(
        [
            jnp.concatenate(([cosine, cosine] + [one] * rest) * many, 1),
            jnp.concatenate(([-sine, none] + [none] * rest) * many, 1),
            jnp.concatenate(([none, sine] + [none] * rest) * many, 1),
        ]
    )


def turn_by(value, rope, sign):
    above = pltpu.roll(value, LANES - ROT // 2, 1)
    below = pltpu.roll(value, ROT // 2, 1)
    return value * rope[0] + sign * (above * rope[1] + below * rope[2])


def head_lanes(shape):
    lane = lax.broadcasted_iota(jnp.int32, shape, 1)
    return [(lane // HEAD) == number for number in range(LANES // HEAD)]


def soft(query, keys, bias):
    scores = mm_t(query, keys) * SCALE + bias
    expo = jnp.exp(scores - jnp.max(scores, -1, keepdims=True))
    return expo / jnp.sum(expo, -1, keepdims=True)


def attend_pair(query, keys, values, bias):
    out = jnp.zeros(query.shape, F32)
    nothing = jnp.zeros((), LOW)
    for mine_q, mine_k in zip(head_lanes(query.shape), head_lanes(keys.shape)):
        probs = soft(jnp.where(mine_q, query, nothing), keys, bias).astype(LOW)
        out = out + mm(probs, jnp.where(mine_k, values, nothing))
    return out.astype(LOW)


def attend_pair_back(d_out, query, keys, values, bias):
    d_query = jnp.zeros(query.shape, F32)
    d_keys = jnp.zeros(keys.shape, F32)
    d_values = jnp.zeros(keys.shape, F32)
    nothing = jnp.zeros((), LOW)
    for mine_q, mine_k in zip(head_lanes(query.shape), head_lanes(keys.shape)):
        query_h = jnp.where(mine_q, query, nothing)
        d_out_h = jnp.where(mine_q, d_out, nothing)
        probs = soft(query_h, keys, bias)
        d_values = d_values + t_mm(probs.astype(LOW), d_out_h)
        d_probs = mm_t(d_out_h, values)
        d_scores = probs * (d_probs - jnp.sum(probs * d_probs, -1, keepdims=True))
        d_scores = d_scores.astype(LOW)
        d_query = d_query + mm(d_scores, jnp.where(mine_k, keys, nothing))
        d_keys = d_keys + t_mm(d_scores, query_h)
    return (d_query * SCALE, d_keys * SCALE, d_values)


def whole_spec(shape):
    return pl.BlockSpec(shape, lambda *_: (0,) * len(shape))


def params(limit=VMEM_LIMIT):
    return pltpu.CompilerParams(vmem_limit_bytes=limit)


def upper_forward(hs, w_in, w_out, w_down, bias_up, rope, bias, slots):
    total, width = hs.shape
    lanes, units = (w_out.shape[0], w_down.shape[0])
    step = total // 2

    def kernel(h_ref, win_ref, wout_ref, wdown_ref, bup_ref, rope_ref, bias_ref, keep_ref, send_ref, qkv_ref, att_ref, act_ref, slope_ref):
        h = h_ref[...]
        proj = mm(h, win_ref[:, : 3 * lanes])
        for g in range(lanes // LANES):
            spans = [slice(j * lanes + g * LANES, j * lanes + (g + 1) * LANES) for j in range(3)]
            qkv_ref[:, spans[0]] = turn_by(proj[:, spans[0]], rope_ref, 1.0).astype(LOW)
            qkv_ref[:, spans[1]] = turn_by(proj[:, spans[1]], rope_ref, 1.0).astype(LOW)
            qkv_ref[:, spans[2]] = proj[:, spans[2]].astype(LOW)
            for pack in range(step // slots):
                here = slice(pack * slots, (pack + 1) * slots)
                q, k, v = (qkv_ref[here, spans[j]] for j in range(3))
                att_ref[here, g * LANES : (g + 1) * LANES] = attend_pair(q, k, v, bias_ref[here, :])
        act, slope = gelu_pair(mm(h, win_ref[:, 3 * lanes :]) + bup_ref[...])
        act = act.astype(LOW)
        act_ref[...] = act
        slope_ref[...] = slope
        out = mm(att_ref[...], wout_ref[...]) + mm(act, wdown_ref[...])

        @pl.when(pl.program_id(0) == 0)
        def _():
            send_ref[...] = out.astype(LOW)

        @pl.when(pl.program_id(0) == 1)
        def _():
            keep_ref[...] = out

    def by_rows(columns):
        return pl.BlockSpec((step, columns), lambda s: (1 - s, 0))

    return pl.pallas_call(
        kernel,
        grid=(2,),
        in_specs=[
            by_rows(width),
            whole_spec(w_in.shape),
            whole_spec(w_out.shape),
            whole_spec(w_down.shape),
            whole_spec((1, units)),
            pl.BlockSpec((3, step, LANES), lambda s: (0, 1 - s, 0)),
            by_rows(slots),
        ],
        out_specs=[
            whole_spec((step, width)),
            whole_spec((step, width)),
            by_rows(3 * lanes),
            by_rows(lanes),
            by_rows(units),
            by_rows(units),
        ],
        out_shape=[
            jax.ShapeDtypeStruct((step, width), F32),
            jax.ShapeDtypeStruct((step, width), LOW),
            jax.ShapeDtypeStruct((total, 3 * lanes), LOW),
            jax.ShapeDtypeStruct((total, lanes), LOW),
            jax.ShapeDtypeStruct((total, units), LOW),
            jax.ShapeDtypeStruct((total, units), F32),
        ],
        compiler_params=params(),
        name="upper_forward",
    )(hs, w_in, w_out, w_down, bias_up[None], rope, bias)


def upper_backward(d_rows, qkv, slope, w_in, w_out, w_down, rope, bias, slots):
    total, width = d_rows.shape
    lanes, units = (w_out.shape[0], w_down.shape[0])
    step = total // 2

    def kernel(d_ref, qkv_ref, slope_ref, win_ref, wout_ref, wdown_ref, rope_ref, bias_ref, keep_ref, send_ref, din_ref, sum_ref):
        d_out = d_ref[...]
        d_att = mm_t(d_out, wout_ref[...]).astype(LOW)
        d_pre = (mm_t(d_out, wdown_ref[...]) * slope_ref[...]).astype(LOW)
        din_ref[:, 3 * lanes :] = d_pre
        sums = jnp.sum(d_pre.astype(F32), 0, keepdims=True)
        for g in range(lanes // LANES):
            spans = [slice(j * lanes + g * LANES, j * lanes + (g + 1) * LANES) for j in range(3)]
            for pack in range(step // slots):
                here = slice(pack * slots, (pack + 1) * slots)
                q, k, v = (qkv_ref[here, spans[j]] for j in range(3))
                dq, dk, dv = attend_pair_back(
                    d_att[here, g * LANES : (g + 1) * LANES], q, k, v, bias_ref[here, :]
                )
                turned = [rope_ref[j, here, :] for j in range(3)]
                din_ref[here, spans[0]] = turn_by(dq, turned, -1.0).astype(LOW)
                din_ref[here, spans[1]] = turn_by(dk, turned, -1.0).astype(LOW)
                din_ref[here, spans[2]] = dv.astype(LOW)
        d_norm = mm_t(din_ref[...], win_ref[...])

        @pl.when(pl.program_id(0) == 0)
        def _():
            send_ref[...] = d_norm.astype(LOW)
            sum_ref[...] = sums

        @pl.when(pl.program_id(0) == 1)
        def _():
            keep_ref[...] = d_norm
            sum_ref[...] += sums

    def by_rows(columns):
        return pl.BlockSpec((step, columns), lambda s: (1 - s, 0))

    return pl.pallas_call(
        kernel,
        grid=(2,),
        in_specs=[
            by_rows(width),
            by_rows(3 * lanes),
            by_rows(units),
            whole_spec(w_in.shape),
            whole_spec(w_out.shape),
            whole_spec(w_down.shape),
            pl.BlockSpec((3, step, LANES), lambda s: (0, 1 - s, 0)),
            by_rows(slots),
        ],
        out_specs=[
            whole_spec((step, width)),
            whole_spec((step, width)),
            by_rows(3 * lanes + units),
            whole_spec((1, units)),
        ],
        out_shape=[
            jax.ShapeDtypeStruct((step, width), F32),
            jax.ShapeDtypeStruct((step, width), LOW),
            jax.ShapeDtypeStruct((total, 3 * lanes + units), LOW),
            jax.ShapeDtypeStruct((1, units), F32),
        ],
        compiler_params=params(),
        name="upper_backward",
    )(d_rows, qkv, slope, w_in, w_out, w_down, rope, bias)


def exact_rows(hot, table):
    high = table.astype(LOW)
    rest = table - high.astype(F32)
    middle = rest.astype(LOW)
    lowest = (rest - middle.astype(F32)).astype(LOW)
    return mm(hot, high) + (mm(hot, middle) + mm(hot, lowest))


def first_forward(table, hot_own, hot_pack, rope_own, rope_pack, bias, packs):
    vocab = table.shape[0]
    width = table.shape[1] // 3
    pairs = width // LANES
    own_rows = hot_own.shape[0] // packs
    pack_rows = hot_pack.shape[0] // packs

    def kernel(tq_ref, tk_ref, tv_ref, hot_ref, hotp_ref, ro_ref, rp_ref, bias_ref, q_ref, k_ref, v_ref, att_ref):
        hot = hot_ref[...]
        hotp = hotp_ref[...]
        q = turn_by(exact_rows(hot, tq_ref[...]), ro_ref, 1.0).astype(LOW)
        k = turn_by(exact_rows(hotp, tk_ref[...]), rp_ref, 1.0).astype(LOW)
        v = mm(hotp, tv_ref[...].astype(LOW)).astype(LOW)
        q_ref[...] = q
        k_ref[...] = k
        v_ref[...] = v
        att_ref[...] = attend_pair(q, k, v, bias_ref[...])

    def table_spec(which):
        return pl.BlockSpec((vocab, LANES), lambda p, j: (0, which * pairs + j))

    def rows_spec(many, columns):
        return pl.BlockSpec((many, columns), lambda p, j: (p, 0))

    def rope_spec(many):
        return pl.BlockSpec((3, many, LANES), lambda p, j: (0, p, 0))

    def pair_spec(many):
        return pl.BlockSpec((many, LANES), lambda p, j: (p, j))

    owned, packed = (hot_own.shape[0], hot_pack.shape[0])
    return pl.pallas_call(
        kernel,
        grid=(packs, pairs),
        in_specs=[
            table_spec(0),
            table_spec(1),
            table_spec(2),
            rows_spec(own_rows, vocab),
            rows_spec(pack_rows, vocab),
            rope_spec(own_rows),
            rope_spec(pack_rows),
            rows_spec(own_rows, pack_rows),
        ],
        out_specs=[
            pair_spec(own_rows),
            pair_spec(pack_rows),
            pair_spec(pack_rows),
            pair_spec(own_rows),
        ],
        out_shape=[
            jax.ShapeDtypeStruct((owned, width), LOW),
            jax.ShapeDtypeStruct((packed, width), LOW),
            jax.ShapeDtypeStruct((packed, width), LOW),
            jax.ShapeDtypeStruct((owned, width), LOW),
        ],
        compiler_params=params(),
        name="first_forward",
    )(table, table, table, hot_own, hot_pack, rope_own, rope_pack, bias)


def cost(microseconds):
    return pl.CostEstimate(flops=max(1, int(microseconds * 1e9 * 1.0)), bytes_accessed=0, transcendentals=0)


def simple(kernel, name, outs, *args, smem=(), us=1.0, scratch=(), behind=(), limit=VMEM_LIMIT):
    specs = [
        pl.BlockSpec(memory_space=pltpu.SMEM) if i in smem else whole_spec(arg.shape)
        for i, arg in enumerate(args)
    ]
    many, unread = (len(args), len(behind))

    def run(*refs):
        kernel(*refs[:many], *refs[many + unread :])

    return pl.pallas_call(
        run,
        grid=(1,),
        in_specs=specs + [pl.BlockSpec(memory_space=pl.ANY)] * unread,
        out_specs=[whole_spec(shape) for shape, _ in outs],
        out_shape=[jax.ShapeDtypeStruct(shape, kind) for shape, kind in outs],
        scratch_shapes=list(scratch),
        compiler_params=params(limit),
        cost_estimate=cost(us),
        name=name,
    )(*args, *behind)


def first_finish(att, first_out, hot, stay, gain, bias):
    rows, width = att.shape

    def kernel(att_ref, out_ref, hot_ref, stay_ref, gain_ref, bias_ref, x_ref, h_ref):
        x = mm(att_ref[...], out_ref[...]) + exact_rows(hot_ref[...], stay_ref[...])
        x = x.astype(LOW)
        x_ref[...] = x
        h_ref[...] = layer_norm(x.astype(F32), gain_ref[...], bias_ref[...])[0].astype(LOW)

    outs = [((rows, width), LOW), ((rows, width), LOW)]
    return simple(kernel, "first_finish", outs, att, first_out, hot, stay, gain[None], bias[None])


def loss_forward(base, pieces, bias_down, gain, bias, head_low, out_bias, target_hot, seq_weight):
    rows, width = base.shape
    vocab = head_low.shape[0]
    seqs = seq_weight.shape[1]

    def kernel(x_ref, *refs):
        piece_refs = refs[: len(pieces)]
        down_ref, gain_ref, bias_ref, head_ref, hbias_ref, hot_ref, seq_ref = refs[len(pieces) : -5]
        norm_ref, inv_ref, final_ref, logp_ref, lik_ref = refs[-5:]
        x = x_ref[...].astype(F32)
        for ref in piece_refs:
            x = x + ref[...].astype(F32)
        out, normed, inverse = layer_norm(x + down_ref[...], gain_ref[...], bias_ref[...])
        norm_ref[...] = normed
        inv_ref[...] = inverse
        final = out.astype(LOW)
        final_ref[...] = final
        logits = mm_t(final, head_ref[...]) + hbias_ref[...]
        top = jnp.max(logits, -1, keepdims=True)
        logp = logits - (top + jnp.log(jnp.sum(jnp.exp(logits - top), -1, keepdims=True)))
        logp_ref[...] = logp
        picked = jnp.sum(hot_ref[...] * logp, 1, keepdims=True)
        lik_ref[...] = jnp.sum(seq_ref[...] * picked, 0, keepdims=True)

    outs = [
        ((rows, width), F32),
        ((rows, 1), F32),
        ((rows, width), LOW),
        ((rows, vocab), F32),
        ((1, seqs), F32),
    ]
    return simple(
        kernel,
        "loss_forward",
        outs,
        base,
        *pieces,
        bias_down[None],
        gain[None],
        bias[None],
        head_low,
        out_bias[None],
        target_hot,
        seq_weight,
    )


def loss_backward(sums, partners, place, normed, inverse, final_low, logp, head_low, gain, target_hot, seq_weight, plane):
    rows, width = normed.shape
    vocab = head_low.shape[0]
    seqs = seq_weight.shape[1]
    devices = sums.shape[0]
    total_seqs = plane * seqs

    def kernel(sums_ref, partner_ref, place_ref, norm_ref, inv_ref, final_ref, logp_ref, head_ref, gain_ref, hot_ref, seq_ref, dy_ref, low_ref, table_ref, bias_ref, down_ref, scalar_ref):
        got = sums_ref[...]
        row = lax.broadcasted_iota(jnp.int32, got.shape, 0)
        column = lax.broadcasted_iota(jnp.int32, got.shape, 1)
        owner = lax.rem(row, plane)
        is_sum = column < seqs
        is_count = (column >= seqs) & (row < plane)
        loss = -jnp.sum(jnp.where(is_sum, got, 0.0))
        count = jnp.sum(jnp.where(is_count, got, 0.0))

        def likelihood(device, number):
            here = owner == device
            amount = jnp.sum(jnp.where(here & is_count & (column == seqs + number), got, 0.0))
            amount = jnp.maximum(amount, 1.0)
            total = jnp.sum(jnp.where(here & (column == number), got, 0.0))
            return (total / amount, amount)

        coeff = jnp.zeros((rows, 1), F32)
        penalty = 0.0
        for number in range(seqs):
            mine, amount = likelihood(place_ref[0], number)
            partner = partner_ref[number]
            other, _ = likelihood(partner // seqs, lax.rem(partner, seqs))
            differ = mine - other
            penalty = penalty + 0.5 * differ * differ
            term = -1.0 / count + PENALTY * 2.0 * differ / total_seqs / amount
            coeff = coeff + seq_ref[:, number : number + 1] * term
        d_logits = (coeff * (hot_ref[...] - jnp.exp(logp_ref[...]))).astype(LOW)
        d_final = mm(d_logits, head_ref[...])
        normed = norm_ref[...]
        dy = norm_back(d_final, normed, inv_ref[...], gain_ref[...])
        dy_ref[...] = dy
        low = dy.astype(LOW)
        low_ref[...] = low
        table_ref[:vocab, :] = t_mm(d_logits, final_ref[...])
        table_ref[vocab : vocab + 1, :] = jnp.sum(d_final * normed, 0, keepdims=True)
        table_ref[vocab + 1 : vocab + 2, :] = jnp.sum(d_final, 0, keepdims=True)
        bias_ref[...] = jnp.sum(d_logits.astype(F32), 0, keepdims=True)
        down_ref[...] = jnp.sum(low.astype(F32), 0, keepdims=True)
        lane = lax.broadcasted_iota(jnp.int32, (1, LANES), 1)
        scalar_ref[...] = jnp.where(lane == 0, loss, jnp.where(lane == 1, count, penalty))

    outs = [
        ((rows, width), F32),
        ((rows, width), LOW),
        ((vocab + 2, width), F32),
        ((1, vocab), F32),
        ((1, width), F32),
        ((1, LANES), F32),
    ]
    return simple(
        kernel,
        "loss_backward",
        outs,
        sums,
        partners,
        place,
        normed,
        inverse,
        final_low,
        logp,
        head_low,
        gain[None],
        target_hot,
        seq_weight,
        smem=(1, 2),
    )


def input_backward(pieces, x_low, dy, gain, hot):
    rows, width = dy.shape
    vocab = hot.shape[1]

    def kernel(*refs):
        piece_refs = refs[: len(pieces)]
        x_ref, dy_ref, gain_ref, hot_ref, low_ref, vec_ref, token_ref = refs[len(pieces) :]
        d_norm = piece_refs[0][...]
        for ref in piece_refs[1:]:
            d_norm = d_norm + ref[...].astype(F32)
        gain_row = gain_ref[...]
        _, normed, inverse = layer_norm(x_ref[...].astype(F32), gain_row, 0.0)
        low = (dy_ref[...] + norm_back(d_norm, normed, inverse, gain_row)).astype(LOW)
        low_ref[...] = low
        vec_ref[0:1, :] = jnp.sum(d_norm * normed, 0, keepdims=True)
        vec_ref[1:2, :] = jnp.sum(d_norm, 0, keepdims=True)
        vec_ref[2:3, :] = jnp.sum(low.astype(F32), 0, keepdims=True)
        token_ref[...] = t_mm(hot_ref[...], low)

    outs = [((rows, width), LOW), ((3, width), F32), ((vocab, width), F32)]
    return simple(kernel, "input_backward", outs, *pieces, x_low, dy, gain[None], hot)


def first_backward(d_rows, query, keys, values, att, hot_own, hot_pack, rope_own, rope_pack, bias, first_out, packs):
    width = first_out.shape[0]
    vocab = hot_own.shape[1]
    pairs = width // LANES
    own_rows = hot_own.shape[0] // packs
    pack_rows = hot_pack.shape[0] // packs

    def kernel(d_ref, q_ref, k_ref, v_ref, att_ref, hot_ref, hotp_ref, ro_ref, rp_ref, bias_ref, out_ref, tq_ref, tk_ref, tv_ref, grad_ref):
        d_out = d_ref[...]
        d_att = mm_t(d_out, out_ref[...]).astype(LOW)
        dq, dk, dv = attend_pair_back(d_att, q_ref[...], k_ref[...], v_ref[...], bias_ref[...])
        dq = turn_by(dq, ro_ref, -1.0).astype(LOW)
        dk = turn_by(dk, rp_ref, -1.0).astype(LOW)
        hot = hot_ref[...]
        hotp = hotp_ref[...]
        parts = (t_mm(hot, dq), t_mm(hotp, dk), t_mm(hotp, dv.astype(LOW)), t_mm(att_ref[...], d_out))
        refs = (tq_ref, tk_ref, tv_ref, grad_ref)

        @pl.when(pl.program_id(1) == 0)
        def _():
            for ref, part in zip(refs, parts):
                ref[...] = part

        @pl.when(pl.program_id(1) > 0)
        def _():
            for ref, part in zip(refs, parts):
                ref[...] += part

    def rows_spec(many, columns):
        return pl.BlockSpec((many, columns), lambda j, p: (p, 0))

    def rope_spec(many):
        return pl.BlockSpec((3, many, LANES), lambda j, p: (0, p, 0))

    def pair_spec(many):
        return pl.BlockSpec((many, LANES), lambda j, p: (p, j))

    token_spec = pl.BlockSpec((vocab, LANES), lambda j, p: (0, j))
    return pl.pallas_call(
        kernel,
        grid=(pairs, packs),
        in_specs=[
            rows_spec(own_rows, width),
            pair_spec(own_rows),
            pair_spec(pack_rows),
            pair_spec(pack_rows),
            pair_spec(own_rows),
            rows_spec(own_rows, vocab),
            rows_spec(pack_rows, vocab),
            rope_spec(own_rows),
            rope_spec(pack_rows),
            rows_spec(own_rows, pack_rows),
            pl.BlockSpec((LANES, width), lambda j, p: (j, 0)),
        ],
        out_specs=[
            token_spec,
            token_spec,
            token_spec,
            pl.BlockSpec((LANES, width), lambda j, p: (j, 0)),
        ],
        out_shape=[
            jax.ShapeDtypeStruct((vocab, width), F32),
            jax.ShapeDtypeStruct((vocab, width), F32),
            jax.ShapeDtypeStruct((vocab, width), F32),
            jax.ShapeDtypeStruct((width, width), F32),
        ],
        compiler_params=params(),
        cost_estimate=cost(10.5),
        name="first_backward",
    )(d_rows, query, keys, values, att, hot_own, hot_pack, rope_own, rope_pack, bias, first_out)


def adam(weight, first, second, grad, rate, decay):
    first_new = BETA_ONE * first + (1.0 - BETA_ONE) * grad
    second_new = BETA_TWO * second + (1.0 - BETA_TWO) * grad * grad
    update = (
        first_new
        / (1.0 - BETA_ONE**STEP)
        / (jnp.sqrt(second_new / (1.0 - BETA_TWO**STEP)) + EPS_ADAM)
    )
    return (first_new, second_new, weight - rate * (update + decay * weight))


class Group:
    def __init__(self, sections, spans):
        self.sections = sections
        self.spans = spans
        self.offsets = [(dk, dy) for dk in range(2) for dy in range(sections)]

    def route(self, dk, dy, sign):
        s = self.sections
        return [
            (a * 2 + b, ((a + sign * dy) % s) * 2 + (b + sign * dk) % 2)
            for a in range(s)
            for b in range(2)
        ]

    def gather(self, value):
        pieces = []
        for dk, dy in self.offsets:
            piece = value
            if (dk, dy) != (0, 0):
                piece = lax.ppermute(value, ("y", "k"), self.route(dk, dy, 1))
            pieces.append(piece)
        mine = jnp.stack(pieces)
        return jnp.stack([mine, shift(mine, "c", 1)])

    def scatter(self, keep, send):
        mine = keep + shift(send, "c", 1).astype(F32)
        pieces = [mine[0]]
        for number, (dk, dy) in enumerate(self.offsets):
            if (dk, dy) != (0, 0):
                pieces.append(
                    lax.ppermute(mine[number].astype(LOW), ("y", "k"), self.route(dk, dy, -1))
                )
        return pieces


def across_gather(piece, x, first, second, last):
    spans = lax.axis_size("h")
    h = lax.axis_index("h")
    piece = after(piece, first)
    if spans == 2:
        both = ordered(piece, after(shift(piece, "h", 1), second), h, 0)
    else:
        stacked = jnp.stack([piece] + [shift(piece, "h", s) for s in range(1, spans)])
        both = jnp.take(stacked, (h - jnp.arange(spans)) % spans, axis=0)
    return ordered(both, after(shift(both, "x", 1), last), x, 1)


def across_scatter(parts, x, first, second, last):
    spans = lax.axis_size("h")
    h = lax.axis_index("h")
    flipped = jnp.swapaxes(parts, 0, 1)
    away = shift(after(pick(flipped, 1 - x).astype(LOW), first), "x", 1)
    mine = pick(flipped, x) + after(away, second).astype(F32)
    total = pick(mine, h)
    for s in range(1, spans):
        away = shift(pick(mine, (h + s) % spans).astype(LOW), "h", s)
        total = total + after(away, last).astype(F32)
    return total


def scalars_of(*values):
    return jnp.stack([jnp.asarray(v, jnp.int32) for v in values])


def flip(value, axes, bits):
    mask = 0
    for bit in bits:
        mask = 2 * mask + bit
    many = 2 ** len(bits)
    return lax.ppermute(value, axes, [(i, i ^ mask) for i in range(many)])


NEAR = [(0, 1), (1, 0), (1, 1)]
def fast_loss_forward(base, pieces, vec, low_tables, out_bias, target_hot, seq_weight, seq_count):
    rows, width = base.shape
    vocab = target_hot.shape[1]

    def kernel(x_ref, p0, p1, p2, p3, vec_ref, low_ref, hbias_ref, hot_ref, seq_ref, count_ref, norm_ref, inv_ref, final_ref, logp_ref, sums_ref):
        x = x_ref[...].astype(F32) + p0[...]
        x = x + p1[...].astype(F32) + p2[...].astype(F32) + p3[...].astype(F32)
        gain = low_ref[2 * vocab : 2 * vocab + 1, :].astype(F32)
        bias = low_ref[2 * vocab + 1 : 2 * vocab + 2, :].astype(F32)
        out, normed, inverse = layer_norm(x + vec_ref[1:2, 2 * width : 3 * width], gain, bias)
        norm_ref[...] = normed
        inv_ref[...] = inverse
        final = out.astype(LOW)
        final_ref[...] = final
        logits = mm_t(final, low_ref[vocab : 2 * vocab, :]) + hbias_ref[...].astype(LOW).astype(F32)
        top = jnp.max(logits, -1, keepdims=True)
        logp = logits - (top + jnp.log(jnp.sum(jnp.exp(logits - top), -1, keepdims=True)))
        logp_ref[...] = logp
        picked = jnp.sum(hot_ref[...] * logp, 1, keepdims=True)
        row = jnp.sum(seq_ref[...] * picked, 0, keepdims=True)
        counts = count_ref[...]
        line = lax.broadcasted_iota(jnp.int32, counts.shape, 0)
        lane = lax.broadcasted_iota(jnp.int32, counts.shape, 1)
        seqs = counts.shape[0]
        row = row + jnp.sum(jnp.where(lane == line + seqs, counts, 0.0), 0, keepdims=True)
        sums_ref[...] = row

    outs = [
        ((rows, width), F32),
        ((rows, 1), F32),
        ((rows, width), LOW),
        ((rows, vocab), F32),
        ((1, LANES), F32),
    ]
    return simple(
        kernel,
        "loss_forward",
        outs,
        base,
        *pieces,
        vec,
        low_tables,
        out_bias[None],
        target_hot,
        seq_weight,
        seq_count,
    )


def loss_tables(d_logits, final_low, normed, low_tables):
    vocab = d_logits.shape[1]
    rows, width = normed.shape

    def kernel(logit_ref, final_ref, norm_ref, low_ref, table_ref, ends_ref):
        d_logits = logit_ref[...]
        d_final = mm(d_logits, low_ref[vocab : 2 * vocab, :])
        line = lax.broadcasted_iota(jnp.int32, (8, width), 0)
        ends_ref[...] = jnp.where(
            line == 0,
            jnp.sum(d_final * norm_ref[...], 0, keepdims=True),
            jnp.where(line == 1, jnp.sum(d_final, 0, keepdims=True), 0.0),
        )
        grads = jnp.concatenate(
            [t_mm(d_logits, final_ref[...]), jnp.zeros((LANES - vocab, width), F32)], 0
        )
        table_ref[...] = grads.T

    outs = [((width, LANES), F32), ((8, width), F32)]
    return simple(kernel, "loss_tables", outs, d_logits, final_low, normed, low_tables)


def fast_loss_backward(sums, partners, place, normed, inverse, final_low, logp, low_tables, target_hot, seq_weight, plane, seqs):
    rows, width = normed.shape
    vocab = target_hot.shape[1]
    total_seqs = plane * seqs

    def kernel(sums_ref, partner_ref, place_ref, norm_ref, inv_ref, final_ref, logp_ref, low_ref, hot_ref, seq_ref, dy_ref, low_out_ref, logit_ref, bias_ref, down_ref, scalar_ref):
        lik = sums_ref[:plane, :] + sums_ref[plane:, :]
        counts = sums_ref[:plane, :]
        row = lax.broadcasted_iota(jnp.int32, lik.shape, 0)
        lanes = lax.broadcasted_iota(jnp.int32, lik.shape, 1)
        lane = lax.broadcasted_iota(jnp.int32, (1, LANES), 1)

        def all_of(value):
            return jnp.sum(jnp.sum(value, 0, keepdims=True), 1, keepdims=True)

        loss = -all_of(jnp.where(lanes < seqs, lik, 0.0))
        count = all_of(jnp.where((lanes >= seqs) & (lanes < 2 * seqs), counts, 0.0))
        amounts = jnp.maximum(pltpu.roll(counts, LANES - seqs, 1), 1.0)
        means = lik / amounts

        def line_of(value, device):
            return jnp.sum(jnp.where(row == device, value, 0.0), 0, keepdims=True)

        other = jnp.zeros((1, LANES), F32)
        for number in range(seqs):
            partner = partner_ref[number]
            line = line_of(means, partner // seqs)
            by = lax.rem(number + LANES - lax.rem(partner, seqs), LANES)
            other = jnp.where(lane == number, pltpu.roll(line, by, 1), other)
        differ = jnp.where(lane < seqs, line_of(means, place_ref[5]) - other, 0.0)
        penalty = 0.5 * all_of(differ * differ)
        amount = line_of(amounts, place_ref[5])
        term = -1.0 / count + PENALTY * 2.0 * differ / total_seqs / amount
        term = jnp.where(lane < seqs, term, 0.0)
        coeff = jnp.sum(seq_ref[...] * term, 1, keepdims=True)
        d_logits = (coeff * (hot_ref[...] - jnp.exp(logp_ref[...]))).astype(LOW)
        d_final = mm(d_logits, low_ref[vocab : 2 * vocab, :])
        normed = norm_ref[...]
        gain = low_ref[2 * vocab : 2 * vocab + 1, :].astype(F32)
        dy = norm_back(d_final, normed, inv_ref[...], gain)
        dy_ref[...] = dy
        low = dy.astype(LOW)
        low_out_ref[...] = low
        logit_ref[...] = d_logits
        bias_ref[...] = jnp.sum(d_logits.astype(F32), 0, keepdims=True)
        down_ref[...] = jnp.sum(low.astype(F32), 0, keepdims=True)
        lane = lax.broadcasted_iota(jnp.int32, (1, LANES), 1)
        scalar_ref[...] = jnp.where(lane == 0, loss, jnp.where(lane == 1, count, penalty))

    outs = [
        ((rows, width), F32),
        ((rows, width), LOW),
        ((rows, vocab), LOW),
        ((1, vocab), F32),
        ((1, width), F32),
        ((1, LANES), F32),
    ]
    return simple(
        kernel,
        "loss_backward",
        outs,
        sums,
        partners,
        place,
        normed,
        inverse,
        final_low,
        logp,
        low_tables,
        target_hot,
        seq_weight,
        smem=(1, 2),
    )


def rope_constant(slots):
    half = ROT // 2
    freq = np.float32(10000.0) ** (np.float32(-2.0) * np.arange(half, dtype=np.float32) / ROT)
    angle = np.arange(slots, dtype=np.float32)[:, None] * freq.astype(np.float32)
    cosine = np.cos(angle.astype(np.float64)).astype(np.float32)
    sine = np.sin(angle.astype(np.float64)).astype(np.float32)
    none, one = (np.zeros_like(sine), np.ones_like(sine))
    many = LANES // HEAD
    rest = HEAD // half - 2
    return np.stack(
        [
            np.concatenate(([cosine, cosine] + [one] * rest) * many, 1),
            np.concatenate(([-sine, none] + [none] * rest) * many, 1),
            np.concatenate(([none, sine] + [none] * rest) * many, 1),
        ]
    )


TOKEN_ROW = 36
VECTOR_ROW = 12
SHARD = 7 * LANES
MIXED = 4 * LANES
ROWS = 48
FLIPS = [(0, 0), (0, 1), (1, 0), (1, 1)]
CUBE = [(dy, dk, dc) for dy in range(2) for dk, dc in FLIPS]


def cube_flips(pieces):
    return [pieces[0]] + [
        flip(piece, ("y", "k", "c"), bits) for piece, bits in zip(pieces[1:], CUBE[1:])
    ]


def cube_number(place_ref, bits):
    y, k, c = (place_ref[axis] for axis in (0, 2, 4))
    return ((y + bits[0]) % 2 * 2 + (k + bits[1]) % 2) * 2 + (c + bits[2]) % 2


def row_spots(number):
    spots = []
    done = 0
    while done < ROWS:
        at = number * ROWS + done
        many = min(ROWS - done, 64 - at % 64)
        spots.append((done, many, at // 64, at % 64))
        done += many
    return spots


def cut_first(tables, vectors, tokens, lengths, down, out, place):
    features, table_rows = tables.shape
    chunk = vectors.shape[1]
    own_ff, width = down.shape
    part = own_ff // 2
    some = out.shape[0] // 2
    packs, per_pack = lengths.shape

    def kernel(tab_ref, vec_ref, tok_ref, len_ref, down_ref, out_ref, place_ref, rows_ref, keep_ref, send_ref, one_ref, two_ref):
        y = place_ref[0]
        table = jnp.concatenate(
            [tab_ref[...], jnp.zeros((features, LANES - table_rows), F32)], 1
        )
        rows_ref[:features, :] = table.astype(LOW)
        rest = chunk - 3 * LANES
        ends = jnp.concatenate(
            [vec_ref[:, 3 * LANES :], jnp.zeros((1, LANES - rest), F32)], 1
        )
        sizes = [len_ref[p : p + 1, :].astype(F32) for p in range(packs)]
        sizes = jnp.concatenate(sizes + [jnp.zeros((1, LANES - packs * per_pack), F32)], 1)
        lines = [vec_ref[:, j * LANES : (j + 1) * LANES] for j in range(3)] + [ends]
        lines = lines + [tok_ref[p : p + 1, :].astype(F32) for p in range(packs)] + [sizes]
        line = lax.broadcasted_iota(jnp.int32, (16, LANES), 0)
        tail = jnp.zeros((16, LANES), F32)
        for number, value in enumerate(lines):
            tail = jnp.where(line == number, value, tail)
        rows_ref[features:, :] = tail.astype(LOW)
        keep_ref[...] = down_ref[pl.ds(pl.multiple_of(y * part, part), part), :].astype(LOW)
        send_ref[...] = down_ref[pl.ds(pl.multiple_of((1 - y) * part, part), part), :].astype(LOW)
        one_ref[...] = out_ref[pl.ds(pl.multiple_of(y * some, some), some), :].astype(LOW)
        two_ref[...] = out_ref[pl.ds(pl.multiple_of((1 - y) * some, some), some), :].astype(LOW)

    outs = [((ROWS, LANES), LOW)] + [((part, width), LOW)] * 2 + [((some, width), LOW)] * 2
    args = (tables, vectors, tokens, lengths, down, out, place)
    return simple(kernel, "cut_first", outs, *args, smem=(6,), limit=VMEM_MOST)


def cut_weights(qkv, up, rows, behind):
    own_in, width = (qkv.shape[0], up.shape[1] // 4)
    own_ff = width // 4
    part = own_ff // 2

    def kernel(qkv_ref, up_ref, r0, r1, r2, r3, shard_ref):
        for dest in range(8):
            yy, kk, cc = dest >> 2, dest >> 1 & 1, dest & 1
            start = ((cc * 2 + kk) * 2 + yy) * LANES
            for j in range(3):
                shard_ref[dest, :, j * LANES : (j + 1) * LANES] = qkv_ref[
                    :, j * width + start : j * width + start + LANES
                ].astype(LOW)
            for j in range(4):
                start = (j // 2 * 8 + kk * 4 + j % 2 * 2 + cc) * own_ff + yy * part
                shard_ref[dest, :, (3 + j) * LANES : (4 + j) * LANES] = up_ref[
                    :, start : start + part
                ].astype(LOW)
        for number, ref in enumerate((r0, r1, r2, r3)):
            for row, many, tile, at in row_spots(number):
                value = ref[row : row + many, :]
                start = SHARD + tile * LANES
                for dest in range(8):
                    shard_ref[dest, at : at + many, start : start + LANES] = value

    outs = [((8, own_in, SHARD + 3 * LANES), LOW)]
    return simple(kernel, "cut_weights", outs, qkv, up, *rows, behind=behind)[0]


def unpack_rows(shards, place):
    def kernel(shard_ref, place_ref, rows_ref):
        h, x = place_ref[1], place_ref[3]
        for source in range(8):
            yy, kk, cc = source >> 2, source >> 1 & 1, source & 1
            for number, (dh, dx) in enumerate(FLIPS):
                device = (((yy * 2 + (h + dh) % 2) * 2 + kk) * 2 + (x + dx) % 2) * 2 + cc
                for row, many, tile, at in row_spots(number):
                    start = SHARD + tile * LANES
                    rows_ref[device, row : row + many, :] = shard_ref[
                        source, at : at + many, start : start + LANES
                    ]

    return simple(kernel, "unpack_rows", [((32, ROWS, LANES), LOW)], shards, place, smem=(1,))[0]


def slot_tables(tables, counted, place, rope_of_position, behind):
    slots = counted.shape[1]
    per_pack = 4
    seqs = 2 * per_pack
    packs = 8

    def kernel(tab_ref, count_ref, place_ref, table_ref, bias_ref, rope_ref, hot_ref, target_ref, seqw_ref, seqc_ref):
        y, h, k, x, c = (place_ref[j] for j in range(5))
        row = lax.broadcasted_iota(jnp.int32, (slots, slots), 0)
        column = lax.broadcasted_iota(jnp.int32, (slots, slots), 1)
        lane = lax.broadcasted_iota(jnp.int32, (1, slots), 1)

        def ends_of(lengths, pack):
            first = pack * per_pack
            return [
                jnp.sum(
                    jnp.where((lane >= first) & (lane <= first + j), lengths, 0.0), 1, keepdims=True
                )
                for j in range(per_pack)
            ]

        def segments(ends, index):
            number = jnp.zeros(index.shape, jnp.int32)
            for end in ends:
                number = number + (index.astype(F32) >= end).astype(jnp.int32)
            return number

        for block in range(4):
            dc, dk = FLIPS[block]
            device = ((h * 2 + (k + dk) % 2) * 2 + x) * 2 + (c + dc) % 2
            lines = tab_ref[device, TOKEN_ROW : TOKEN_ROW + 4, :].astype(F32)
            lengths = lines[2:3]
            for dy in range(2):
                pack = lax.rem(y + dy, 2)
                here = pl.ds((block * 2 + dy) * slots, slots)
                ends = ends_of(lengths, pack)
                by_row, by_column = segments(ends, row), segments(ends, column)
                seen = (by_row == by_column) & (column <= row)
                bias_ref[here, :] = jnp.where(seen, 0.0, -1e30)
                start = jnp.zeros((slots, slots), F32)
                for j in range(1, per_pack):
                    start = jnp.where(by_row == j, ends[j - 1], start)
                position = row.astype(F32) - start
                hot = jnp.where(column.astype(F32) == position, 1.0, 0.0).astype(LOW)
                for part in range(3):
                    rope_ref[part, here, :] = exact_rows(hot, table_ref[part])
                token = jnp.where(pack == 0, lines[0:1], lines[1:2])
                hot = jnp.where(row.astype(F32) == token, 1.0, 0.0)
                hot_ref[here, :] = hot.T[:, : hot_ref.shape[1]].astype(LOW)
        lines = tab_ref[((h * 2 + k) * 2 + x) * 2 + c, TOKEN_ROW : TOKEN_ROW + 4, :].astype(F32)
        counts = jnp.zeros((seqs, slots), F32)
        seq_line = lax.broadcasted_iota(jnp.int32, (seqs, slots), 0)
        for pack in range(2):
            number = segments(ends_of(lines[2:3], pack), lane)
            following = pltpu.roll(number.astype(F32), slots - 1, 1)
            same = (following == number.astype(F32)) & (lane < slots - 1)
            weight = jnp.where(same & (count_ref[pack : pack + 1, :] == 1), 1.0, 0.0)
            by_seq = jnp.where(seq_line == number + pack * per_pack, weight, 0.0)
            counts = counts + by_seq

            @pl.when(pack == y)
            def _():
                target = pltpu.roll(lines[pack : pack + 1], slots - 1, 1)
                hot = jnp.where(row.astype(F32) == target, 1.0, 0.0)
                target_ref[...] = hot.T[:, : target_ref.shape[1]]
                padded = jnp.concatenate([by_seq, jnp.zeros((slots - seqs, slots), F32)], 0)
                seqw_ref[...] = padded.T

        seqc_ref[...] = jnp.broadcast_to(jnp.sum(counts, 1, keepdims=True), (seqs, LANES))

    outs = [
        ((packs * slots, slots), F32),
        ((3, packs * slots, LANES), F32),
        ((packs * slots, 32), LOW),
        ((slots, 32), F32),
        ((slots, LANES), F32),
        ((seqs, LANES), F32),
    ]
    args = (tables, counted, place, rope_of_position)
    return simple(kernel, "slot_tables", outs, *args, smem=(2,), us=2.0, behind=behind)


def token_products(tables, weights, place):
    vocab = 32
    devices, _, lanes = tables.shape
    width = devices * vocab
    own_in, columns = weights.shape[1], SHARD
    total = devices // 2 * 448

    def kernel(tab_ref, w_ref, place_ref, low_ref, vec_ref, h_ref, norm_ref, inv_ref, part_ref):
        h, x = place_ref[1], place_ref[3]
        flat = tab_ref[:, :vocab, :].astype(F32).reshape(width, lanes).T
        low_ref[...] = flat.astype(LOW)
        first_half = lax.broadcasted_iota(jnp.int32, (1, LANES), 1) < LANES // 2
        for pair in range(devices // 2):
            line, at = pair // (devices // 4), pair % (devices // 4) * 7 * LANES
            even = tab_ref[2 * pair, vocab : vocab + 4, :].astype(F32)
            odd = pltpu.roll(tab_ref[2 * pair + 1, vocab : vocab + 4, :].astype(F32), LANES // 2, 1)
            for q in range(7):
                if q < 3:
                    value = even[q : q + 1]
                elif q == 3:
                    value = jnp.where(first_half, even[3:4], odd[0:1])
                else:
                    value = jnp.where(first_half, odd[q - 4 : q - 3], odd[q - 3 : q - 2])
                vec_ref[line : line + 1, at + q * LANES : at + (q + 1) * LANES] = value
        out, normed, inverse = layer_norm(
            flat[:vocab], vec_ref[0:1, :width], vec_ref[0:1, width : 2 * width]
        )
        norm_ref[...] = normed
        inv_ref[...] = inverse
        h_ref[...] = out.astype(LOW)
        rows = 2 * own_in
        sums = jnp.zeros((vocab, columns), F32)
        for kk in range(2):
            start = pl.multiple_of(((h * 2 + kk) * 2 + x) * rows, LANES)
            block = w_ref[2 * kk : 2 * kk + 2, :, :columns].reshape(rows, columns)
            sums = sums + mm(h_ref[:, pl.ds(start, rows)], block)
        part_ref[...] = sums

    outs = [
        ((lanes, width), LOW),
        ((2, total), F32),
        ((vocab, width), LOW),
        ((vocab, width), F32),
        ((vocab, 1), F32),
        ((vocab, columns), F32),
    ]
    return simple(kernel, "token_products", outs, tables, weights, place, smem=(2,))


def first_rows(down_keep, down_far, out_one, out_two, place):
    part, width = down_keep.shape
    some = out_one.shape[0]

    def kernel(keep_ref, far_ref, one_ref, two_ref, place_ref, rows_ref):
        y, x = place_ref[0], place_ref[3]
        rows_ref[:part, :] = jnp.where(y == 0, keep_ref[...], far_ref[...])
        rows_ref[part:, :] = jnp.where(x == 0, one_ref[...], two_ref[...])

    outs = [((part + some, width), LOW)]
    args = (down_keep, down_far, out_one, out_two, place)
    return simple(kernel, "first_rows", outs, *args, smem=(4,))[0]


def upper_rows(weights, down_keep, down_far, out_one, out_two, place):
    part, width = down_keep.shape
    some = out_one.shape[0]
    own_in, columns = weights.shape[1], SHARD

    def kernel(w_ref, keep_ref, far_ref, one_ref, two_ref, place_ref, *piece_refs):
        y, x = place_ref[0], place_ref[3]
        for j in range(4):
            ref = piece_refs[j // 2]
            ref[j % 2 * own_in : (j % 2 + 1) * own_in, :columns] = w_ref[4 + j, :, :columns]
        out = jnp.where(x == 0, two_ref[...], one_ref[...])
        for j in range(8):
            ref = piece_refs[j // 4]
            here = slice(j % 4 * some, (j % 4 + 1) * some)
            ref[here, columns:] = out[:, j * LANES : (j + 1) * LANES]
        piece_refs[2][...] = jnp.where(y == 0, far_ref[...], keep_ref[...])

    outs = [((part, width), LOW)] * 3
    args = (weights, down_keep, down_far, out_one, out_two, place)
    return simple(kernel, "upper_rows", outs, *args, smem=(5,))


def across(value):
    far = flip(value, ("h",), (1,))
    return [value, flip(value, ("x",), (1,)), far, flip(far, ("x",), (1,))]


def group_pieces(value):
    near = [value] + [flip(value, ("y", "k"), (dy, dk)) for dk, dy in NEAR]
    return near + [flip(piece, ("c",), (1,)) for piece in near]


def group_sums(keep, send, behind=()):
    got = flip(send, ("c",), (1,))
    rows, width = (keep.shape[0] // 4, keep.shape[1])

    def kernel(keep_ref, got_ref, *refs):
        for j, ref in enumerate(refs):
            here = slice(j * rows, (j + 1) * rows)
            ref[...] = (keep_ref[here, :] + got_ref[here, :].astype(F32)).astype(ref.dtype)

    outs = [((rows, width), F32)] + [((rows, width), LOW)] * 3
    mine = simple(kernel, "group_sums", outs, keep, got, behind=behind)
    return [mine[0]] + [flip(piece, ("y", "k"), (dy, dk)) for piece, (dk, dy) in zip(mine[1:], NEAR)]


def block_of(place_ref, number):
    dh, dx = FLIPS[number]
    return (place_ref[1] + dh) % 2 * 2 + (place_ref[3] + dx) % 2


def first_group_forward(parts, tails, vec, place, hot, rope, bias, behind):
    vocab, columns = parts[0].shape
    total, slots = bias.shape
    tail_rows, width = tails[0].shape
    part = LANES
    some = tail_rows - part
    units = 4 * part
    step = total // 2

    def kernel(*refs):
        refs = refs[:11] + refs[11 + len(behind) :]
        part_refs, tail_refs = refs[:2], refs[2:6]
        vec_ref, place_ref, hot_ref, rope_ref, bias_ref = refs[6:11]
        keep_ref, send_ref, qkv_ref, att_ref, act_ref, slope_ref, wout_ref, wdown_ref = refs[11:19]
        table_ref, ffn_ref = refs[19:]
        first = pl.program_id(0) == 0

        @pl.when(first)
        def _():
            for number, ref in enumerate(tail_refs):
                block = block_of(place_ref, number)
                wdown_ref[pl.ds(pl.multiple_of(block * part, part), part), :] = ref[:part, :]
                wout_ref[pl.ds(pl.multiple_of(block * some, some), some), :] = ref[part:, :]
            sums = part_refs[0][...] + part_refs[1][...]
            table_ref[...] = sums[:, : 3 * LANES]
            y, k, c = place_ref[0], place_ref[2], place_ref[4]
            bias_up = jnp.concatenate(
                [
                    vec_ref[0:1, pl.ds(unit_start(width, j, y, k, c, part), part)]
                    for j in range(4)
                ],
                1,
            )
            act, slope = gelu_pair(sums[:, 3 * LANES :] + bias_up)
            act = act.astype(LOW)
            act_ref[...] = act
            slope_ref[...] = slope
            ffn_ref[...] = mm(act, wdown_ref[...])

        for pack in range(step // slots):
            here = slice(pack * slots, (pack + 1) * slots)
            hot_here = hot_ref[here, :]
            rope_here = [rope_ref[j, here, :] for j in range(3)]
            q = turn_by(exact_rows(hot_here, table_ref[:, :LANES]), rope_here, 1.0).astype(LOW)
            k = turn_by(
                exact_rows(hot_here, table_ref[:, LANES : 2 * LANES]), rope_here, 1.0
            ).astype(LOW)
            v = mm(hot_here, table_ref[:, 2 * LANES :].astype(LOW)).astype(LOW)
            qkv_ref[here, :LANES] = q
            qkv_ref[here, LANES : 2 * LANES] = k
            qkv_ref[here, 2 * LANES :] = v
            att_ref[here, :] = attend_pair(q, k, v, bias_ref[here, :])
        out = mm(att_ref[...], wout_ref[...]) + exact_rows(hot_ref[...], ffn_ref[...])

        @pl.when(first)
        def _():
            send_ref[...] = out.astype(LOW)

        @pl.when(jnp.logical_not(first))
        def _():
            keep_ref[...] = out

    def by_rows(columns):
        return pl.BlockSpec((step, columns), lambda s: (1 - s, 0))

    args = (*parts, *tails, vec)
    return pl.pallas_call(
        kernel,
        grid=(2,),
        in_specs=[whole_spec(arg.shape) for arg in args]
        + [
            pl.BlockSpec(memory_space=pltpu.SMEM),
            by_rows(vocab),
            pl.BlockSpec((3, step, LANES), lambda s: (0, 1 - s, 0)),
            by_rows(slots),
        ]
        + [pl.BlockSpec(memory_space=pl.ANY)] * len(behind),
        out_specs=[
            whole_spec((step, width)),
            whole_spec((step, width)),
            by_rows(3 * LANES),
            by_rows(LANES),
            whole_spec((vocab, units)),
            whole_spec((vocab, units)),
            whole_spec((4 * some, width)),
            whole_spec((units, width)),
        ],
        out_shape=[
            jax.ShapeDtypeStruct((step, width), F32),
            jax.ShapeDtypeStruct((step, width), LOW),
            jax.ShapeDtypeStruct((total, 3 * LANES), LOW),
            jax.ShapeDtypeStruct((total, LANES), LOW),
            jax.ShapeDtypeStruct((vocab, units), LOW),
            jax.ShapeDtypeStruct((vocab, units), F32),
            jax.ShapeDtypeStruct((4 * some, width), LOW),
            jax.ShapeDtypeStruct((units, width), LOW),
        ],
        scratch_shapes=[pltpu.VMEM((vocab, 3 * LANES), F32), pltpu.VMEM((vocab, width), F32)],
        compiler_params=params(),
        cost_estimate=cost(9),
        name="first_group_forward",
    )(*args, place, hot, rope, bias, *behind)


def unit_start(width, j, y, k, c, part):
    unit = (j // 2 * 8 + k * 4 + j % 2 * 2 + c) * 2 * part + y * part
    return pl.multiple_of(3 * width + unit, LANES)


def first_finish_rows(pieces, hot, low_tables, vec, behind):
    rows, width = pieces[0].shape
    vocab = hot.shape[1]

    def kernel(p0, p1, p2, p3, hot_ref, low_ref, vec_ref, x_ref, h_ref):
        stay = low_ref[:vocab, :].astype(F32) + vec_ref[0:1, 2 * width : 3 * width]
        x = exact_rows(hot_ref[:rows, :], stay) + p0[...]
        x = x + p1[...].astype(F32) + p2[...].astype(F32) + p3[...].astype(F32)
        x = x.astype(LOW)
        x_ref[...] = x
        h_ref[...] = layer_norm(
            x.astype(F32), vec_ref[1:2, :width], vec_ref[1:2, width : 2 * width]
        )[0].astype(LOW)

    outs = [((rows, width), LOW), ((rows, width), LOW)]
    return simple(kernel, "first_finish", outs, *pieces, hot, low_tables, vec, behind=behind)


def group_forward(pieces, shards, vec, place, rope, bias):
    slots, width = pieces[0].shape
    total = slots * len(pieces)
    step = total // 2
    part = LANES
    units, columns = 4 * part, 7 * LANES
    some = part // 4

    def kernel(*refs):
        piece_refs, shard_refs = refs[:8], refs[8:20]
        vec_ref, place_ref, rope_ref, bias_ref = refs[20:24]
        keep_ref, send_ref, h_ref, qkv_ref, att_ref, act_ref, slope_ref = refs[24:31]
        win_ref, wout_ref, wdown_ref = refs[31:]
        half = 1 - pl.program_id(0)

        @pl.when(half == 1)
        def _():
            for number in range(4):
                three = shard_refs[3 * number : 3 * number + 3]
                block = block_of(place_ref, number)
                for kk in range(2):
                    start = (block // 2 * 4 + kk * 2 + block % 2) * part
                    here = pl.ds(pl.multiple_of(start, part), part)
                    win_ref[here, :] = three[kk][:, :columns]
                here = pl.ds(pl.multiple_of(block * some, some), some)
                for j in range(8):
                    there = slice(j % 4 * some, (j % 4 + 1) * some)
                    wout_ref[here, j * LANES : (j + 1) * LANES] = three[j // 4][there, columns:]
                here = pl.ds(pl.multiple_of(block * part, part), part)
                wdown_ref[here, :] = three[2][...]

        for s in range(2):

            @pl.when(half == s)
            def _():
                for j in range(4):
                    h_ref[j * slots : (j + 1) * slots, :] = piece_refs[4 * s + j][...]

        h = h_ref[...]
        proj = mm(h, win_ref[:, : 3 * LANES])
        spans = [slice(j * LANES, (j + 1) * LANES) for j in range(3)]
        qkv_ref[:, spans[0]] = turn_by(proj[:, spans[0]], rope_ref, 1.0).astype(LOW)
        qkv_ref[:, spans[1]] = turn_by(proj[:, spans[1]], rope_ref, 1.0).astype(LOW)
        qkv_ref[:, spans[2]] = proj[:, spans[2]].astype(LOW)
        for pack in range(step // slots):
            here = slice(pack * slots, (pack + 1) * slots)
            q, k, v = (qkv_ref[here, spans[j]] for j in range(3))
            att_ref[here, :] = attend_pair(q, k, v, bias_ref[here, :])
        y, k, c = place_ref[0], place_ref[2], place_ref[4]
        bias_up = jnp.concatenate(
            [vec_ref[1:2, pl.ds(unit_start(width, j, y, k, c, part), part)] for j in range(4)], 1
        )
        act, slope = gelu_pair(mm(h, win_ref[:, 3 * LANES :]) + bias_up)
        act = act.astype(LOW)
        act_ref[...] = act
        slope_ref[...] = slope
        out = mm(att_ref[...], wout_ref[...]) + mm(act, wdown_ref[...])

        @pl.when(half == 1)
        def _():
            send_ref[...] = out.astype(LOW)

        @pl.when(half == 0)
        def _():
            keep_ref[...] = out

    def by_rows(columns):
        return pl.BlockSpec((step, columns), lambda s: (1 - s, 0))

    args = (*pieces, *shards, vec)
    shapes = [
        ((step, width), F32),
        ((step, width), LOW),
        ((total, width), LOW),
        ((total, 3 * LANES), LOW),
        ((total, LANES), LOW),
        ((total, units), LOW),
        ((total, units), F32),
        ((width, columns), LOW),
        ((LANES, width), LOW),
        ((units, width), LOW),
    ]
    return pl.pallas_call(
        kernel,
        grid=(2,),
        in_specs=[whole_spec(arg.shape) for arg in args]
        + [
            pl.BlockSpec(memory_space=pltpu.SMEM),
            pl.BlockSpec((3, step, LANES), lambda s: (0, 1 - s, 0)),
            by_rows(slots),
        ],
        out_specs=[
            whole_spec(shape) if number < 2 or number > 6 else by_rows(shape[1])
            for number, (shape, _) in enumerate(shapes)
        ],
        out_shape=[jax.ShapeDtypeStruct(shape, kind) for shape, kind in shapes],
        compiler_params=params(),
        cost_estimate=cost(12.5),
        name="group_forward",
    )(*args, place, rope, bias)


def group_backward(pieces, qkv, slope, w_in, w_out, w_down, rope, bias):
    slots, width = pieces[0].shape
    total = slots * len(pieces)
    units = w_down.shape[0]
    step = total // 2

    def kernel(*refs):
        piece_refs = refs[:8]
        win_ref, wout_ref, wdown_ref, qkv_ref, slope_ref, rope_ref, bias_ref = refs[8:15]
        keep_ref, send_ref, d_ref, din_ref, sum_ref = refs[15:]
        half = 1 - pl.program_id(0)
        for s in range(2):

            @pl.when(half == s)
            def _():
                for j in range(4):
                    d_ref[j * slots : (j + 1) * slots, :] = piece_refs[4 * s + j][...]

        d_out = d_ref[...]
        d_att = mm_t(d_out, wout_ref[...]).astype(LOW)
        d_pre = (mm_t(d_out, wdown_ref[...]) * slope_ref[...]).astype(LOW)
        din_ref[:, 3 * LANES :] = d_pre
        sums = jnp.sum(d_pre.astype(F32), 0, keepdims=True)
        spans = [slice(j * LANES, (j + 1) * LANES) for j in range(3)]
        for pack in range(step // slots):
            here = slice(pack * slots, (pack + 1) * slots)
            q, k, v = (qkv_ref[here, spans[j]] for j in range(3))
            dq, dk, dv = attend_pair_back(d_att[here, :], q, k, v, bias_ref[here, :])
            turned = [rope_ref[j, here, :] for j in range(3)]
            din_ref[here, spans[0]] = turn_by(dq, turned, -1.0).astype(LOW)
            din_ref[here, spans[1]] = turn_by(dk, turned, -1.0).astype(LOW)
            din_ref[here, spans[2]] = dv.astype(LOW)
        d_norm = mm_t(din_ref[...], win_ref[...])

        @pl.when(half == 1)
        def _():
            send_ref[...] = d_norm.astype(LOW)
            sum_ref[...] = sums

        @pl.when(half == 0)
        def _():
            keep_ref[...] = d_norm
            sum_ref[...] += sums

    def by_rows(columns):
        return pl.BlockSpec((step, columns), lambda s: (1 - s, 0))

    args = (*pieces, w_in, w_out, w_down)
    return pl.pallas_call(
        kernel,
        grid=(2,),
        in_specs=[whole_spec(arg.shape) for arg in args]
        + [
            by_rows(3 * LANES),
            by_rows(units),
            pl.BlockSpec((3, step, LANES), lambda s: (0, 1 - s, 0)),
            by_rows(slots),
        ],
        out_specs=[
            whole_spec((step, width)),
            whole_spec((step, width)),
            by_rows(width),
            by_rows(3 * LANES + units),
            whole_spec((1, units)),
        ],
        out_shape=[
            jax.ShapeDtypeStruct((step, width), F32),
            jax.ShapeDtypeStruct((step, width), LOW),
            jax.ShapeDtypeStruct((total, width), LOW),
            jax.ShapeDtypeStruct((total, 3 * LANES + units), LOW),
            jax.ShapeDtypeStruct((1, units), F32),
        ],
        compiler_params=params(),
        cost_estimate=cost(13.4),
        name="group_backward",
    )(*args, qkv, slope, rope, bias)


def weight_gradients(hs, d_in, act, att, d_rows, place):
    width = hs.shape[1]
    columns = d_in.shape[1]
    block = LANES
    some = LANES // 4

    def kernel(h_ref, din_ref, act_ref, att_ref, d_ref, place_ref, *refs):
        out_ref = refs[6]
        x = place_ref[3]
        h = pl.program_id(0)

        @pl.when(h == 0)
        def _():
            out_ref[...] = t_mm(att_ref[...], d_ref[...])

        d_in = din_ref[...]
        d_rows = d_ref[...]
        for three, xx in ((refs[:3], x), (refs[3:6], 1 - x)):
            for k in range(2):
                start = pl.multiple_of(((h * 2 + k) * 2 + xx) * block, LANES)
                grad = t_mm(h_ref[:, pl.ds(start, block)], d_in)
                three[k][0, :, :columns] = grad.astype(three[k].dtype)
            start = pl.multiple_of((h * 2 + xx) * some, some)
            grad = out_ref[pl.ds(start, some), :]
            for j in range(8):
                here = slice(j % 4 * some, (j % 4 + 1) * some)
                three[j // 4][0, here, columns:] = grad[:, j * LANES : (j + 1) * LANES].astype(
                    three[j // 4].dtype
                )
            start = pl.multiple_of((h * 2 + xx) * block, LANES)
            three[2][0] = t_mm(act_ref[:, pl.ds(start, block)], d_rows).astype(three[2].dtype)

    args = (hs, d_in, act, att, d_rows)
    shape = (2, block, width)
    return pl.pallas_call(
        kernel,
        grid=(2,),
        in_specs=[whole_spec(arg.shape) for arg in args]
        + [pl.BlockSpec(memory_space=pltpu.SMEM)],
        out_specs=[pl.BlockSpec((1,) + shape[1:], lambda h: (h, 0, 0))] * 6,
        out_shape=[jax.ShapeDtypeStruct(shape, kind) for kind in (F32,) * 3 + (LOW,) * 3],
        scratch_shapes=[pltpu.VMEM((LANES, width), F32)],
        compiler_params=params(),
        cost_estimate=cost(5.0),
        name="weight_gradients",
    )(*args, place)


def add_split(keep_ref, got_ref, place_ref, mine_ref, send_ref):
    b = place_ref[1]
    mine_ref[...] = keep_ref[b] + got_ref[b].astype(F32)
    send_ref[...] = (keep_ref[1 - b] + got_ref[1 - b].astype(F32)).astype(LOW)


def split_two(total):
    high = total.astype(LOW)
    return (high, (total - high.astype(F32)).astype(LOW))


def first_group_backward(pieces, qkv, att, slope, w_out, w_down, hot, rope, bias, mixed, keep, got, place, behind):
    slots, width = pieces[0].shape
    total = slots * len(pieces)
    vocab = hot.shape[1]
    units = w_down.shape[0]
    some = LANES // 4
    columns = 3 * LANES + units + width

    def kernel(*refs):
        piece_refs = refs[:8]
        qkv_ref, att_ref, slope_ref, wout_ref, wdown_ref, hot_ref, rope_ref, bias_ref = refs[8:16]
        mixed_ref, keep_ref, got_ref, place_ref = refs[16:20]
        out_refs, mine_ref, send_ref, sum_ref, grad_ref = refs[20:22], *refs[22:]
        sum_ref[...] = jnp.zeros(sum_ref.shape, F32)
        grad_ref[...] = jnp.zeros(grad_ref.shape, F32)
        spans = [slice(j * LANES, (j + 1) * LANES) for j in range(3)]
        for pack, ref in enumerate(piece_refs):
            here = slice(pack * slots, (pack + 1) * slots)
            d_out = ref[...]
            hot_here = hot_ref[here, :]
            d_att = mm_t(d_out, wout_ref[...]).astype(LOW)
            q, k, v = (qkv_ref[here, spans[j]] for j in range(3))
            dq, dk, dv = attend_pair_back(d_att, q, k, v, bias_ref[here, :])
            turned = [rope_ref[j, here, :] for j in range(3)]
            sum_ref[:, spans[0]] += t_mm(hot_here, turn_by(dq, turned, -1.0).astype(LOW))
            sum_ref[:, spans[1]] += t_mm(hot_here, turn_by(dk, turned, -1.0).astype(LOW))
            sum_ref[:, spans[2]] += t_mm(hot_here, dv.astype(LOW))
            sum_ref[:, 3 * LANES + units :] += t_mm(hot_here, d_out)
            grad_ref[...] += t_mm(att_ref[here, :], d_out)
        high, rest = split_two(sum_ref[:, 3 * LANES + units :])
        down = wdown_ref[...]
        sum_ref[:, 3 * LANES : 3 * LANES + units] = (
            mm_t(high, down) + mm_t(rest, down)
        ) * slope_ref[...]
        for ref, xx in zip(out_refs, (place_ref[3], 1 - place_ref[3])):
            ref[:, :columns] = sum_ref[...].astype(ref.dtype)
            for h in range(2):
                at = columns + h * (width + MIXED)
                start = pl.multiple_of((h * 2 + xx) * some, some)
                ref[:, at : at + width] = grad_ref[pl.ds(start, some), :].astype(ref.dtype)
                for dest in range(8):
                    device = (((dest // 4 * 2 + h) * 2 + dest // 2 % 2) * 2 + xx) * 2 + dest % 2
                    here = slice(dest % 2 * 16, dest % 2 * 16 + 16)
                    start = at + width + dest // 2 * LANES
                    ref[here, start : start + LANES] = mixed_ref[device].astype(ref.dtype)
        add_split(keep_ref, got_ref, place_ref, mine_ref, send_ref)

    wide = columns + 2 * (width + MIXED)
    shape = keep.shape[1:]
    outs = [((vocab, wide), F32), ((vocab, wide), LOW)] + [(shape, F32), (shape, LOW)]
    args = (*pieces, qkv, att, slope, w_out, w_down, hot, rope, bias, mixed, keep, got, place)
    scratch = [pltpu.VMEM((vocab, columns), F32), pltpu.VMEM((LANES, width), F32)]
    return simple(
        kernel,
        "first_group_backward",
        outs,
        *args,
        smem=(19,),
        scratch=scratch,
        us=9.0,
        behind=behind,
    )


def fold(keep, got, down, down_far, place, behind):
    vocab = keep.shape[0]
    by_h = 1024 + MIXED
    columns = keep.shape[1] - 2 * by_h

    def kernel(keep_ref, got_ref, one_ref, two_ref, place_ref, mine_ref, send_ref, down_ref):
        down_ref[...] = (one_ref[...] + two_ref[...].astype(F32)).astype(LOW)
        same = keep_ref[:, :columns] + got_ref[:, :columns].astype(F32)
        mine_ref[:, :columns] = same
        send_ref[:, :columns] = same.astype(LOW)
        for ref, h in ((mine_ref, place_ref[1]), (send_ref, 1 - place_ref[1])):
            here = pl.ds(pl.multiple_of(columns + h * by_h, LANES), by_h)
            ref[:, columns:] = (keep_ref[:, here] + got_ref[:, here].astype(F32)).astype(ref.dtype)

    shape = (vocab, columns + by_h)
    outs = [(shape, F32), (shape, LOW), (down.shape, LOW)]
    args = (keep, got, down, down_far, place)
    return simple(kernel, "fold", outs, *args, smem=(4,), behind=behind)


def add_two(one, two):
    def kernel(one_ref, two_ref, out_ref):
        out_ref[...] = one_ref[...] + two_ref[...]

    return simple(kernel, "add_two", [(one.shape, one.dtype)], one, two)[0]


def token_gradients(parts, h0, weights, act, act_far, place, behind):
    vocab, width = h0.shape
    own_in, shard = weights.shape[1], SHARD
    units = act.shape[1]
    part = units // 4

    def kernel(p0, p1, h_ref, w_ref, act_ref, other_ref, place_ref, in_ref, down_ref, out_ref, dh_ref, rows_ref, mixed_ref, act_out):
        total = p0[...] + p1[...].astype(F32)
        rows = total[:, shard : shard + width]
        rows_ref[...] = rows
        out_ref[...] = total[:, shard + width : shard + 2 * width].astype(LOW)
        for dest in range(8):
            start = shard + 2 * width + dest // 2 * LANES
            here = slice(dest % 2 * 16, dest % 2 * 16 + 16)
            mixed_ref[dest] = total[here, start : start + LANES]
        high, rest = split_two(total[:, :shard])
        h, x = place_ref[1], place_ref[3]
        two = 2 * own_in
        for kk in range(2):
            start = pl.multiple_of(((h * 2 + kk) * 2 + x) * two, LANES)
            mine = h_ref[:, pl.ds(start, two)]
            grad = t_mm(mine, high) + t_mm(mine, rest)
            in_ref[2 * kk : 2 * kk + 2] = grad.astype(LOW).reshape(2, own_in, shard)
            block = w_ref[2 * kk : 2 * kk + 2, :, :shard].reshape(two, shard)
            dh_ref[kk * vocab : (kk + 1) * vocab, :] = mm_t(high, block) + mm_t(rest, block)
        act_out[...] = total[:, 3 * LANES : shard]
        start = pl.multiple_of((h * 2 + x) * part, LANES)
        bias = jnp.sum(act_out[:, pl.ds(start, part)], 0, keepdims=True)
        dh_ref[2 * vocab :, :] = jnp.broadcast_to(bias, (8, LANES))
        high, rest = split_two(rows)
        for j, ref in enumerate((act_ref, other_ref)):
            mine = ref[:, pl.ds(start, part)]
            down_ref[j * part : (j + 1) * part, :] = t_mm(mine, high) + t_mm(mine, rest)

    outs = [
        ((4, own_in, shard), LOW),
        ((2 * part, width), F32),
        ((vocab, width), LOW),
        ((2 * vocab + 8, LANES), F32),
        ((vocab, width), F32),
        ((8, 16, LANES), F32),
    ]
    scratch = [pltpu.VMEM((vocab, units), F32)]
    args = (*parts, h0, weights, act, act_far, place)
    return simple(
        kernel, "token_gradients", outs, *args, smem=(6,), scratch=scratch, behind=behind
    )


def owner_pieces(keeps, gots, down, first_in, first_down, first_out, dh, mixed, scalars, bias_local, place):
    rows, width = keeps[0].shape
    own_in, columns = first_in.shape[1:]
    some = first_out.shape[0]
    vocab = bias_local.shape[1]

    def kernel(k0, k1, g0, g1, upper_ref, in_ref, down_ref, out_ref, dh_ref, mixed_ref, scalar_ref, bias_ref, place_ref, shard_ref, one_ref, two_ref, last_ref, sum_ref):
        y, x = place_ref[0], place_ref[3]
        for j, (keep, got) in enumerate(((k0, g0), (k1, g1))):
            sum_ref[j * rows : (j + 1) * rows, :] = (keep[...] + got[...].astype(F32)).astype(LOW)
        lane = lax.broadcasted_iota(jnp.int32, (vocab, LANES), 1)
        for number in range(8):
            if number < 4:
                shard_ref[number, :, :columns] = in_ref[number]
            else:
                here = slice((number - 4) * own_in, (number - 3) * own_in)
                shard_ref[number, :, :columns] = sum_ref[here, :columns]
            block = dh_ref[number // 4 * vocab : (number // 4 + 1) * vocab, :]
            if number % 4:
                block = pltpu.roll(block, LANES - number % 4 * vocab, 1)
            high = block.astype(LOW).astype(F32)
            rest = pltpu.roll(block - high, vocab, 1)
            both = jnp.where(lane < vocab, high, jnp.where(lane < 2 * vocab, rest, 0.0))
            shard_ref[number, :vocab, columns:] = both.astype(LOW)
            high, rest = split_two(mixed_ref[number])
            shard_ref[number, vocab : vocab + 16, columns:] = high
            shard_ref[number, vocab + 16 :, columns:] = rest
        for j in range(width // LANES):
            here = slice(j * LANES, (j + 1) * LANES)
            upper = sum_ref[j * some : (j + 1) * some, columns:]
            first = out_ref[:, here]
            one_ref[:, here] = jnp.where(x == 0, first, upper)
            two_ref[:, here] = jnp.where(x == 0, upper, first)

        def squares(value):
            value = value.astype(F32)
            return jnp.sum(jnp.sum(value * value, 0, keepdims=True), 1, keepdims=True)

        total = squares(sum_ref[...]) + squares(upper_ref[...]) + squares(out_ref[...])
        total = total + jnp.where(y == 0, squares(down_ref[...]), 0.0)
        for j in range(4):
            total = total + squares(in_ref[j])
        lane = lax.broadcasted_iota(jnp.int32, (1, LANES), 1)
        penalty = jnp.where(y == 0, scalar_ref[0:1, 2:3], 0.0)
        bias = jnp.concatenate([bias_ref[...], jnp.zeros((1, LANES - vocab), F32)], 1)
        row = jnp.where(lane == 0, total, jnp.where(lane == 1, penalty, 0.0))
        last_ref[...] = row + pltpu.roll(bias, vocab, 1)

    outs = [((8, own_in, columns + LANES), LOW)]
    outs = outs + [((some, width), LOW)] * 2
    outs = outs + [((1, LANES), F32)]
    scratch = [pltpu.VMEM((2 * rows, width), LOW)]
    args = (*keeps, *gots, down, first_in, first_down, first_out, dh, mixed, scalars, bias_local, place)
    return simple(kernel, "owner_pieces", outs, *args, smem=(12,), scratch=scratch)


def norm_sums(shards, dh, last, place, behind):
    vocab = 32

    def kernel(shard_ref, dh_ref, last_ref, place_ref, all_ref, mixed_ref, out_ref):
        total = jnp.sum(shard_ref[:, :vocab, SHARD:].astype(F32), 0)
        total = total + pltpu.roll(total, LANES - vocab, 1)
        lane = lax.broadcasted_iota(jnp.int32, (8, LANES), 1)
        packed = total[:8]
        for group in range(1, 4):
            moved = pltpu.roll(total[group * 8 : (group + 1) * 8], group * vocab, 1)
            packed = jnp.where(lane >= group * vocab, moved, packed)
        out_ref[:8, :] = packed
        mixed = jnp.sum(shard_ref[:, vocab : vocab + 16, SHARD:].astype(F32), 0)
        mixed = mixed + jnp.sum(shard_ref[:, vocab + 16 :, SHARD:].astype(F32), 0)
        mixed_ref[...] = mixed
        line = lax.broadcasted_iota(jnp.int32, (16, LANES), 0)
        counted = (line < VECTOR_ROW) | (place_ref[0] == 1)
        squares = jnp.where(counted, mixed * mixed, 0.0)
        squares = jnp.sum(jnp.sum(squares, 0, keepdims=True), 1, keepdims=True)
        first = lax.broadcasted_iota(jnp.int32, (1, LANES), 1) == 0
        row = last_ref[...] + jnp.where(first, squares, 0.0)
        line = lax.broadcasted_iota(jnp.int32, (8, LANES), 0)
        out_ref[8:, :] = jnp.where(line == 0, row, dh_ref[2 * vocab :, :])
        all_ref[...] = jnp.broadcast_to(out_ref[...][None], all_ref.shape)

    outs = [((32, 16, LANES), F32), ((16, LANES), F32)]
    scratch = [pltpu.VMEM((16, LANES), F32)]
    args = (shards, dh, last, place)
    return simple(kernel, "norm_sums", outs, *args, smem=(3,), scratch=scratch, behind=behind)


def update_all(scalars, shards, first_down, down_mine, down_far, out_one, out_two, place, weights, firsts, seconds, rates):
    steps = 4
    own_in = shards.shape[1]
    part, width = down_mine.shape
    some = out_one.shape[0]
    rows = own_in // steps

    def kernel(scalar_ref, shard_ref, first_ref, mine_ref, far_ref, one_ref, two_ref, place_ref, *refs):
        state_refs, out_refs = refs[:12], refs[12:24]
        qkv_ref, up_ref = refs[24:]
        y = place_ref[0]
        early = pl.program_id(0) < steps // 2
        factor = scalar_ref[:, 4:5]
        for number in range(8):
            yy, kk, cc = number >> 2, number >> 1 & 1, number & 1
            start = ((cc * 2 + kk) * 2 + yy) * LANES
            for j in range(3):
                qkv_ref[:, j * width + start : j * width + start + LANES] = shard_ref[
                    number, :, j * LANES : (j + 1) * LANES
                ].astype(F32)
            for j in range(4):
                start = (j // 2 * 8 + kk * 4 + j % 2 * 2 + cc) * 2 * part + yy * part
                up_ref[:, start : start + part] = shard_ref[
                    number, :, (3 + j) * LANES : (4 + j) * LANES
                ].astype(F32)
        upper = jnp.where(early, far_ref[...], mine_ref[...]).astype(F32)
        down = jnp.where(y == 0, first_ref[...], upper)
        out = jnp.where((y == 0) == early, one_ref[...], two_ref[...]).astype(F32)
        for j, (grad, rate) in enumerate(zip((qkv_ref[...], out, up_ref[...], down), rates)):
            new = adam(*(state_refs[part * 4 + j][0] for part in range(3)), grad * factor, rate, DECAY)
            for number, value in enumerate(new):
                out_refs[j * 3 + number][0] = value

    def own(shape):
        return pl.BlockSpec((1, shape[1] // steps, shape[2]), lambda s: (0, s, 0))

    def half(block, which):
        if which is None:
            return pl.BlockSpec(block, lambda s: (s % 2, 0))
        return pl.BlockSpec(block, lambda s: (jnp.clip(s - which, 0, 1), 0))

    shapes = [weight.shape for weight in weights]
    many = 2 * part // steps
    return pl.pallas_call(
        kernel,
        grid=(steps,),
        in_specs=[
            pl.BlockSpec((1, LANES), lambda s: (0, 0)),
            pl.BlockSpec((8, rows, shards.shape[2]), lambda s: (0, s, 0)),
            pl.BlockSpec((many, width), lambda s: (s, 0)),
            half((many, width), steps // 2),
            half((many, width), 0),
            half((2 * some // steps, width), None),
            half((2 * some // steps, width), None),
            pl.BlockSpec(memory_space=pltpu.SMEM),
        ]
        + [own(shape) for shape in shapes] * 3,
        out_specs=[own(shape) for shape in shapes for _ in range(3)],
        out_shape=[jax.ShapeDtypeStruct(shape, F32) for shape in shapes for _ in range(3)],
        scratch_shapes=[pltpu.VMEM((rows, 3 * width), F32), pltpu.VMEM((rows, 4 * width), F32)],
        compiler_params=params(VMEM_MOST),
        cost_estimate=cost(6.0),
        name="update_all",
    )(scalars, shards, first_down, down_mine, down_far, out_one, out_two, place, *weights, *firsts, *seconds)


def fast_input_backward(pieces, x_low, dy, vec, down_sum, bias_up, table_local, ends_local, keeps, gots, later, place):
    rows, width = dy.shape
    part = bias_up.shape[1] // 4
    total = vec.shape[1]
    owners = 32
    vocab = width // owners

    def kernel(p0, p1, p2, p3, x_ref, dy_ref, vec_ref, sum_ref, up_ref, table_ref, ends_ref, k0, k1, g0, g1, later_ref, place_ref, low_ref, mixed_ref, m0, m1, s0, s1, pass_ref, grad_ref):
        add_split(k0, g0, place_ref, m0, s0)
        add_split(k1, g1, place_ref, m1, s1)
        pass_ref[...] = later_ref[...]
        d_norm = p0[...] + p1[...].astype(F32) + p2[...].astype(F32) + p3[...].astype(F32)
        gain = vec_ref[1:2, :width]
        _, normed, inverse = layer_norm(x_ref[...].astype(F32), gain, 0.0)
        low_ref[...] = (dy_ref[...] + norm_back(d_norm, normed, inverse, gain)).astype(LOW)
        grad_ref[:, :width] = jnp.sum(d_norm * normed, 0, keepdims=True)
        grad_ref[:, width : 2 * width] = jnp.sum(d_norm, 0, keepdims=True)
        grad_ref[:, 2 * width : 3 * width] = sum_ref[...]
        grad_ref[:, 3 * width :] = jnp.zeros((1, total - 3 * width), F32)
        y, k, c = place_ref[0], place_ref[2], place_ref[4]
        for j in range(4):
            start = unit_start(width, j, y, k, c, part)
            grad_ref[:, pl.ds(start, part)] = up_ref[:, j * part : (j + 1) * part]
        mixed_ref[:, 8:, :] = jnp.zeros((owners, 8, LANES), F32)
        lane = lax.broadcasted_iota(jnp.int32, (8, LANES), 1)
        for owner in range(owners):
            rows_here = jnp.zeros((8, LANES), F32)
            for group in range(4):
                start = owner * vocab + group * 8
                value = table_ref[start : start + 8, :]
                if group:
                    value = pltpu.roll(value, group * vocab, 1)
                mine = (lane >= group * vocab) & (lane < (group + 1) * vocab)
                rows_here = jnp.where(mine, value, rows_here)
            mixed_ref[owner, :8, :] = rows_here
            block = ends_ref[:, owner // 4 * LANES : (owner // 4 + 1) * LANES]
            if owner % 4:
                block = pltpu.roll(block, LANES - owner % 4 * vocab, 1)
            mine = lax.broadcasted_iota(jnp.int32, (2, LANES), 1) < vocab
            mixed_ref[owner, 8:10, :] = jnp.where(mine, block[:2], 0.0)
        first_half = lax.broadcasted_iota(jnp.int32, (1, LANES), 1) < LANES // 2
        for pair in range(owners // 4):
            at = pair * 7 * LANES
            tiles = [grad_ref[:, at + q * LANES : at + (q + 1) * LANES] for q in range(7)]
            turned = [pltpu.roll(tile, LANES // 2, 1) for tile in tiles[3:]]
            even = tiles[:3] + [jnp.where(first_half, tiles[3], 0.0)]
            odd = [jnp.where(first_half, turned[q], turned[q + 1]) for q in range(3)]
            odd = odd + [jnp.where(first_half, turned[3], 0.0)]
            for side, lines in enumerate((even, odd)):
                for q in range(4):
                    owner = owners // 2 + 2 * pair + side
                    mixed_ref[owner, VECTOR_ROW + q : VECTOR_ROW + q + 1, :] = lines[q]

    outs = [((rows, width), LOW), ((owners, 16, LANES), F32)]
    shape = later.shape[1:]
    outs = outs + [(shape, F32)] * 2 + [(shape, LOW)] * 2 + [(later.shape, LOW)]
    args = (*pieces, x_low, dy, vec, down_sum, bias_up, table_local, ends_local, *keeps, *gots, later, place)
    scratch = [pltpu.VMEM((1, total), F32)]
    return simple(kernel, "input_backward", outs, *args, smem=(16,), scratch=scratch, us=2.0)


def pack_states(vectors, tables, biases, behind):
    features, table_rows = tables[0].shape
    chunk = vectors[0].shape[1]
    many = features + 8

    def kernel(*refs):
        out_ref = refs[9]
        for number in range(3):
            vec_ref, tab_ref, bias_ref = refs[number], refs[3 + number], refs[6 + number]
            start = number * many
            pad = jnp.zeros((features, LANES - table_rows), F32)
            out_ref[start : start + features, :] = jnp.concatenate([tab_ref[...], pad], 1)
            lines = [vec_ref[:, j * LANES : (j + 1) * LANES] for j in range(3)]
            rest = chunk - 3 * LANES
            ends = jnp.concatenate(
                [vec_ref[:, 3 * LANES :], jnp.zeros((1, LANES - rest), F32)], 1
            )
            bias = bias_ref[...]
            bias = jnp.concatenate([bias, jnp.zeros((1, LANES - bias.shape[1]), F32)], 1)
            line = lax.broadcasted_iota(jnp.int32, (8, LANES), 0)
            tail = jnp.zeros((8, LANES), F32)
            for row, value in enumerate(lines + [ends, bias]):
                tail = jnp.where(line == row, value, tail)
            out_ref[start + features : start + many, :] = tail

    args = (*vectors, *tables, *biases)
    return simple(kernel, "pack_states", [((3 * many, LANES), F32)], *args, behind=behind)[0]


def last_sums(dh_all, rows_sum, normed, inverse, vec, mixed, scalars, place, packed, chunk, table_rows):
    vocab, width = rows_sum.shape
    total = vec.shape[1]
    devices = dh_all.shape[0]

    def kernel(*refs):
        dh_all_ref, sum_ref, norm_ref, inv_ref, vec_ref, mixed_ref, known_ref, place_ref = refs[:8]
        packed_ref, scalar_ref, norm_ref_out, parts_ref = refs[8:12]
        vector_outs, table_outs, bias_outs = refs[12:15], refs[15:18], refs[18:21]
        dh_ref, all_ref, emb_ref = refs[21:]
        many = vocab + 8
        table_ins = [packed_ref[j * many : j * many + vocab, :table_rows] for j in range(3)]
        tails = [packed_ref[j * many + vocab : (j + 1) * many, :] for j in range(3)]
        vector_ins = [
            jnp.concatenate([tail[row : row + 1] for row in range(4)], 1)[:, :chunk] for tail in tails
        ]
        bias_ins = [tail[4:5, :vocab] for tail in tails]
        y, me = place_ref[0], place_ref[5]
        scalars = jnp.zeros((1, LANES), F32)
        lane = lax.broadcasted_iota(jnp.int32, (8, LANES), 1)
        for h in range(2):
            for x in range(2):
                for yy in range(2):
                    start = (h * 4 + yy * 2 + x) * LANES
                    tiles = [jnp.zeros((8, LANES), F32)] * 4
                    for spot in range(4):
                        device = ((yy * 2 + h) * 2 + spot // 2) * 4 + x * 2 + spot % 2
                        packed = dh_all_ref[device, :8, :]
                        mine = (lane >= spot * vocab) & (lane < (spot + 1) * vocab)
                        for group in range(4):
                            by = (spot - group) * vocab % LANES
                            moved = pltpu.roll(packed, by, 1) if by else packed
                            tiles[group] = jnp.where(mine, moved, tiles[group])
                        ends = dh_all_ref[device, 8:, :]
                        scalars = scalars + ends[0:1]
                        unit = 3 * width + device % 16 * 2 * LANES + yy * LANES
                        all_ref[:, unit : unit + LANES] = ends[1:2]
                    for group in range(4):
                        dh_ref[group * 8 : (group + 1) * 8, start : start + LANES] = tiles[group]
        dh = dh_ref[...]
        normed = norm_ref[...]
        rows = sum_ref[...]
        embed = rows + norm_back(dh, normed, inv_ref[...], vec_ref[0:1, :width])
        emb_ref[...] = embed
        all_ref[:, :width] = jnp.sum(dh * normed, 0, keepdims=True)
        all_ref[:, width : 2 * width] = jnp.sum(dh, 0, keepdims=True)
        all_ref[:, 2 * width : 3 * width] = jnp.sum(rows, 0, keepdims=True)
        lane = lax.broadcasted_iota(jnp.int32, (1, LANES), 1)
        bias = jnp.where((lane >= vocab) & (lane < 2 * vocab), scalars, 0.0)
        vector = all_ref[...]

        def squares(value):
            return jnp.sum(jnp.sum(value * value, 0, keepdims=True), 1, keepdims=True)

        total_squares = scalars[:, 0:1] + squares(bias) + squares(embed) + squares(vector)
        norm = jnp.sqrt(total_squares)
        factor = jnp.minimum(1.0, CLIP_AT / norm)
        known = known_ref[...]
        row = jnp.where(lane == 0, norm, jnp.where(lane == 1, known[:, 0:1], known[:, 1:2]))
        row = jnp.where(lane == 3, scalars[:, 1:2], row)
        scalar_ref[...] = jnp.where(lane == 4, factor, row)
        norm_ref_out[...] = norm
        parts_ref[...] = row[:, 1:4]

        def update(ins, outs, grad):
            new = adam(*ins, grad * factor, RATE_VEC, 0.0)
            for ref, value in zip(outs, new):
                ref[...] = value

        odd = lax.rem(me, 2)
        start = pl.multiple_of(me * chunk - odd * (LANES // 2), LANES)
        mine = all_ref[:, pl.ds(start, chunk + LANES // 2)]
        mine = jnp.where(odd == 0, mine, pltpu.roll(mine, chunk, 1))
        far = jnp.concatenate(
            [mixed_ref[VECTOR_ROW + q : VECTOR_ROW + q + 1, :] for q in range(4)], 1
        )
        update(vector_ins, vector_outs, jnp.where(y == 0, mine, far)[:, :chunk])
        number = y * (devices // 2) + me
        block = emb_ref[:, pl.ds(pl.multiple_of(number // 4 * LANES, LANES), LANES)]
        block = pltpu.roll(block, lax.rem(LANES - lax.rem(number, 4) * vocab, LANES), 1)
        padded = jnp.concatenate([block, jnp.zeros((LANES - vocab, LANES), F32)], 0).T[:vocab, :]
        wide = lax.broadcasted_iota(jnp.int32, (vocab, LANES), 1)
        head = jnp.concatenate(
            [mixed_ref[:8, :]]
            + [pltpu.roll(mixed_ref[:8, :], LANES - group * vocab, 1) for group in range(1, 4)],
            0,
        )
        ends = jnp.concatenate([mixed_ref[8:16, :], jnp.zeros((LANES - 8, LANES), F32)], 0).T[:vocab]
        grad = jnp.where(wide < vocab, padded, pltpu.roll(head, vocab, 1))
        grad = jnp.where(wide < 2 * vocab, grad, pltpu.roll(ends, 2 * vocab, 1))
        update(table_ins, table_outs, grad[:, :table_rows])
        update(bias_ins, bias_outs, pltpu.roll(bias, LANES - vocab, 1)[:, :vocab])

    args = (dh_all, rows_sum, normed, inverse, vec, mixed, scalars, place, packed)
    outs = [((1, LANES), F32), ((1, 1), F32), ((1, 3), F32)] + [((1, chunk), F32)] * 3 + [((vocab, table_rows), F32)] * 3
    outs = outs + [((1, vocab), F32)] * 3
    scratch = [
        pltpu.VMEM((vocab, width), F32),
        pltpu.VMEM((1, total), F32),
        pltpu.VMEM((vocab, width), F32),
    ]
    return simple(
        kernel, "last_sums", outs, *args, smem=(7,), scratch=scratch
    )


def body_fast(
    tokens,
    lengths,
    counted,
    partners,
    qkv_weight,
    out_weight,
    up_weight,
    down_weight,
    vectors,
    tables,
    head_bias,
    *states,
):
    y, h, k, x, c = (lax.axis_index(a) for a in ALL)
    me = lax.axis_index(PLANE)
    place = scalars_of(y, h, k, x, c, me)
    slots = tokens.shape[1]
    vocab = head_bias.shape[0]
    plane, everyone = 16, 32

    rows, down_keep, down_send, out_one, out_two = cut_first(
        tables.T, vectors, tokens, lengths, down_weight[0], out_weight[0], place
    )
    down_far = flip(down_send, ("y",), (1,))
    routes = [[], []]
    for device in range(everyone):
        yy, hh, kk, xx, cc = (device >> 4, device >> 3 & 1, device >> 2 & 1, device >> 1 & 1, device & 1)
        owner = cc * 8 + kk * 4 + yy * 2 + hh
        for step in range(2):
            routes[step].append(((xx ^ step) * plane + owner, device))
    out_one = lax.ppermute(out_one, ALL, routes[0])
    out_two = lax.ppermute(out_two, ALL, routes[1])
    rows = [rows] + [flip(rows, ("h", "x"), bits) for bits in NEAR]
    tail = first_rows(down_keep, down_far, out_one, out_two, place)
    tails = across(tail)
    shards = cut_weights(qkv_weight[0], up_weight[0], rows, (tail,))
    shards = trade(shards, ("y", "k", "c"))
    table_all = unpack_rows(shards, place)
    low_tables, vec, h0, normed0, inverse0, part = token_products(table_all, shards, place)
    uppers = upper_rows(shards, down_keep, down_far, out_one, out_two, place)
    nears = [flip(piece, ("x",), (1,)) for piece in uppers]
    fars = [flip(piece, ("h",), (1,)) for piece in uppers]
    crosses = [flip(piece, ("x",), (1,)) for piece in fars]
    part = add_two(part, flip(part, ("x",), (1,)))
    parts = [part, flip(part, ("h",), (1,))]
    bias, rope, hot, target_hot, seq_weight, seq_count = slot_tables(
        table_all, counted, place, rope_constant(slots), (part,)
    )

    packed = pack_states(
        (vectors, states[4], states[11]),
        (tables.T, states[5].T, states[12].T),
        (head_bias[None], states[6][None], states[13][None]),
        (seq_count,),
    )

    keep, send, qkv0, att0, act0, slope0, w_out0, w_down0 = first_group_forward(
        parts, tails, vec, place, hot, rope, bias, (fars[0], nears[0], nears[1])
    )
    act_far = flip(act0, ("y",), (1,))
    pieces = group_sums(keep, send, ())
    x_low, h_low = first_finish_rows(pieces, hot, low_tables, vec, (fars[1], crosses[0]))

    uppers = [*uppers, *nears, *fars, *crosses]
    keep, send, hs, qkv, att, act, slope, w_in, w_out, w_down = group_forward(
        group_pieces(h_low), uppers, vec, place, rope, bias
    )
    normed_f, inverse_f, final_low, logp, sums = fast_loss_forward(
        x_low,
        group_sums(keep, send),
        vec,
        low_tables,
        head_bias,
        target_hot,
        seq_weight,
        seq_count,
    )
    sums = spread(sums, ALL).reshape(everyone, LANES)
    dy, dy_low, d_logits, bias_local, down_sum, scalars = fast_loss_backward(
        sums,
        partners,
        place,
        normed_f,
        inverse_f,
        final_low,
        logp,
        low_tables,
        target_hot,
        seq_weight,
        plane,
        seq_count.shape[0],
    )

    table_local, ends_local = loss_tables(d_logits, final_low, normed_f, low_tables)

    keep, send, d_rows, d_in, bias_up = group_backward(
        group_pieces(dy_low), qkv, slope, w_in, w_out, w_down, rope, bias
    )
    keep_1, keep_2, keep_0, send_1, send_2, send_0 = weight_gradients(
        hs, d_in, act, att, d_rows, place
    )
    gots = [flip(piece, ("x",), (1,)) for piece in (send_0, send_1)]
    terms = group_sums(keep, send, (send_0,))
    own_low, mixed, mine_0, mine_1, send_0, send_1, send_2 = fast_input_backward(
        terms,
        x_low,
        dy,
        vec,
        down_sum,
        bias_up,
        table_local,
        ends_local,
        (keep_0, keep_1),
        gots,
        send_2,
        place,
    )

    pieces = group_pieces(own_low)
    got_2 = flip(send_2, ("x",), (1,))
    far_0, far_1 = (flip(piece, ("h",), (1,)) for piece in (send_0, send_1))
    keep, send, mine_2, send_2 = first_group_backward(
        pieces,
        qkv0,
        att0,
        slope0,
        w_out0,
        w_down0,
        hot,
        rope,
        bias,
        mixed,
        keep_2,
        got_2,
        place,
        (far_0,far_1),
    )
    far_2 = flip(send_2, ("h",), (1,))
    part, send, down_mine = fold(keep, flip(send, ("x",), (1,)), mine_0, far_0, place, ())
    down_far = lax.ppermute(down_mine, "y", [(0, 1)])
    parts = [part, flip(send, ("h",), (1,))]
    first_in, first_down, first_out, dh, rows_sum, mixed = token_gradients(
        parts, h0, shards, act0, act_far, place, (far_2,)
    )
    shards, out_one, out_two, last = owner_pieces(
        (mine_1, mine_2),
        (far_1, far_2),
        down_mine,
        first_in,
        first_down,
        first_out,
        dh,
        mixed,
        scalars,
        bias_local,
        place,
    )
    out_one = lax.ppermute(out_one, ALL, [(b, a) for a, b in routes[0]])
    out_two = lax.ppermute(out_two, ALL, [(b, a) for a, b in routes[1]])
    shards = trade(shards, ("y", "k", "c"))
    sums, mixed = norm_sums(shards, dh, last, place, ())
    scalars, norm, parts, *small = last_sums(
        trade(sums, ALL),
        rows_sum,
        normed0,
        inverse0,
        vec,
        mixed,
        scalars,
        place,
        packed,
        vectors.shape[1],
        tables.shape[0],
    )
    results = update_all(
        scalars,
        shards,
        first_down,
        down_mine,
        down_far,
        out_one,
        out_two,
        place,
        (qkv_weight, out_weight, up_weight, down_weight),
        states[:4],
        states[7:11],
        (RATE_MAT, RATE_OUT, RATE_MAT, RATE_MAT),
    )
    results = list(results)
    results.extend(small[:3])
    results.extend(value.T for value in small[3:6])
    results.extend(value[0] for value in small[6:])
    return (norm.reshape(()), parts.reshape(3), *results)


def body(
    tokens,
    lengths,
    counted,
    partners,
    qkv_weight,
    out_weight,
    up_weight,
    down_weight,
    vectors,
    tables,
    head_bias,
    qkv_moment,
    out_moment,
    up_moment,
    down_moment,
    vector_moment,
    table_moment,
    bias_moment,
    qkv_square,
    out_square,
    up_square,
    down_square,
    vector_square,
    table_square,
    bias_square,
):
    sections = lax.axis_size("y")
    spans = lax.axis_size("h")
    plane = lax.axis_size(PLANE)
    everyone = sections * plane
    y, h, k, x, c = (lax.axis_index(a) for a in ALL)
    me = lax.axis_index(PLANE)
    group = Group(sections, spans)
    micro, slots = tokens.shape
    per_pack = lengths.shape[1]
    width = qkv_weight.shape[2] // 3
    hidden = up_weight.shape[2]
    vocab = head_bias.shape[0]
    own_in = qkv_weight.shape[1]
    own_out = out_weight.shape[1]
    own_ff = down_weight.shape[1]
    shares = 4 * sections
    heads = width // HEAD
    shard_heads = heads // shares
    shard_width = width // shares
    shard_ff = hidden // shares
    rows = micro * slots // sections
    block_rows = micro * slots
    group_rows = 4 * block_rows
    group_packs = 4 * micro
    own_packs = max(1, rows // slots)
    own_pack_rows = min(rows, slots)

    low_qkv = qkv_weight[0].astype(LOW)
    low_out = out_weight[0].astype(LOW)
    low_up = up_weight[0].astype(LOW)
    low_down = down_weight[0].astype(LOW)

    table_part = tables.shape[1]
    vector_part = vectors.shape[1]
    small = jnp.concatenate(
        [
            tables.astype(LOW).reshape(-1),
            vectors[0].astype(LOW),
            lengths.astype(LOW).reshape(-1),
        ]
    )
    small_all = spread(small, ALL)
    cut_one = tables.size
    cut_two = cut_one + vector_part
    table_low = (
        small_all[:, :cut_one]
        .reshape(everyone, tables.shape[0], table_part)
        .transpose(1, 0, 2)
        .reshape(tables.shape[0], width)
    )
    vec_low = small_all[:, cut_one:cut_two].reshape(sections, plane * vector_part)
    vec_all = vec_low.astype(F32)
    lengths_all = small_all[:, cut_two:].astype(jnp.int32)
    embed = table_low[:vocab].astype(F32)
    head_low = table_low[vocab : 2 * vocab]
    final_gain = table_low[2 * vocab].astype(F32)
    final_bias = table_low[2 * vocab + 1].astype(F32)
    out_bias = head_bias.astype(LOW).astype(F32)

    segment, position = jax.vmap(lambda row: pack_layout(row, slots))(lengths)
    target = jnp.concatenate([tokens[:, 1:], jnp.zeros((micro, 1), jnp.int32)], 1)
    same = jnp.concatenate([segment[:, 1:] == segment[:, :-1], jnp.zeros((micro, 1), bool)], 1)
    weight = (same & (counted == 1)).astype(F32)
    sequence = segment + per_pack * jnp.arange(micro, dtype=jnp.int32)[:, None]

    def own(array):
        return lax.dynamic_slice_in_dim(array.reshape((block_rows,) + array.shape[2:]), y * rows, rows, 0)

    own_target = own(target)
    own_weight = own(weight)
    own_sequence = own(sequence)
    first_pack = (y * rows) // slots

    def packs_of(array):
        return lax.dynamic_slice_in_dim(array, first_pack, own_packs, 0)

    pack_tokens = packs_of(tokens)
    pack_segment = packs_of(segment)
    pack_position = packs_of(position)
    own_tokens = own(tokens).reshape(own_packs, own_pack_rows)
    own_segment = own(segment).reshape(own_packs, own_pack_rows)
    own_position = own(position).reshape(own_packs, own_pack_rows)
    pack_index = jnp.broadcast_to(jnp.arange(slots, dtype=jnp.int32), (own_packs, slots))
    own_index = (
        jnp.broadcast_to(jnp.arange(own_pack_rows, dtype=jnp.int32), (own_packs, own_pack_rows))
        + (y * rows) % slots
    )
    own_mask = (own_segment[:, :, None] == pack_segment[:, None, :]) & (
        pack_index[:, None, :] <= own_index[:, :, None]
    )
    target_hot = one_hot(own_target, vocab, F32)
    local_seqs = micro * per_pack
    seq_weight = one_hot(own_sequence, local_seqs, F32) * own_weight[:, None]
    seq_count = jnp.sum(
        one_hot(sequence.reshape(-1), local_seqs, F32) * weight.reshape(-1)[:, None], 0
    )
    hot_pack = one_hot(pack_tokens.reshape(-1), vocab, LOW)
    hot_own = one_hot(own_tokens.reshape(-1), vocab, LOW)
    own_bias = jnp.where(own_mask, 0.0, -1e30).reshape(rows, slots)
    own_rope = rope_rows(own_position.reshape(-1))
    pack_rope = own_rope if rows % slots == 0 else rope_rows(pack_position.reshape(-1))

    lengths_plane = lengths_all.reshape(sections, spans, 2, 2, 2, micro * per_pack)[0]
    lengths_group = pick(lengths_plane, h)[:, :, :, :]
    lengths_group = lax.dynamic_index_in_dim(lengths_group, x, 1, keepdims=False)

    parts = []
    for dc in range(2):
        for dk in range(2):
            block_lengths = pick(pick(lengths_group, (k - dk) % 2), (c - dc) % 2)
            parts.append(block_lengths.reshape(micro, per_pack))
    group_lengths = jnp.concatenate(parts, 0)
    group_segment, group_position = jax.vmap(lambda row: pack_layout(row, slots))(group_lengths)
    turn = (y - jnp.arange(sections)) % sections

    def by_offset(array):
        cut = array.reshape((4, sections, rows) + array.shape[2:])
        return jnp.take(cut, turn, axis=1).reshape((4 * sections * rows,) + array.shape[2:])

    if rows % slots == 0:
        group_segment = by_offset(group_segment).reshape(group_packs, slots)
        group_position = by_offset(group_position).reshape(group_packs, slots)
    group_index = jnp.arange(slots, dtype=jnp.int32)
    group_mask = (group_segment[:, :, None] == group_segment[:, None, :]) & (
        group_index[None, :] <= group_index[:, None]
    )
    group_bias = jnp.where(group_mask, 0.0, -1e30).reshape(group_rows, slots)
    group_rope = rope_rows(group_position.reshape(-1))

    def to_group(value):
        got = group.gather(value).reshape((4, sections, rows) + value.shape[1:])
        if rows % slots:
            got = jnp.take(got, turn, axis=1)
        return got.reshape((group_rows,) + value.shape[1:])

    def from_group(keep, send):
        def cut(value):
            value = value.reshape((2, sections, rows) + value.shape[1:])
            if rows % slots:
                value = jnp.take(value, turn, axis=1)
            return value.reshape((2 * sections, rows) + value.shape[3:])

        return group.scatter(cut(keep), cut(send))

    part_ff = own_ff // sections

    def columns_by_shard(qkv_rows, up_rows):
        cut_qkv = qkv_rows.reshape(own_in, 3, 2, 2, sections, shard_width)
        cut_up = up_rows.reshape(own_in, spans, 2, 2, 2, sections, part_ff)
        pieces = []
        for cc in range(2):
            for kk in range(2):
                for yy in range(sections):
                    pieces.append(
                        jnp.concatenate(
                            [cut_qkv[:, j, cc, kk, yy] for j in range(3)]
                            + [
                                cut_up[:, hh, kk, xx, cc, yy]
                                for hh in range(spans)
                                for xx in range(2)
                            ],
                            1,
                        )
                    )
        return jnp.stack(pieces).reshape((2, 2, sections) + pieces[0].shape)

    def columns_back(shards):
        cut = shards[..., : 3 * shard_width].reshape(2, 2, sections, own_in, 3, shard_width)
        qkv_rows = cut.transpose(3, 4, 0, 1, 2, 5).reshape(own_in, 3 * width)
        cut = shards[..., 3 * shard_width :].reshape(
            2, 2, sections, own_in, spans, 2, part_ff
        )
        up_rows = cut.transpose(3, 4, 1, 5, 0, 2, 6).reshape(own_in, hidden)
        return (qkv_rows, up_rows)

    small_out = width // everyone

    def out_routes(layer):
        routes = [[] for _ in range(sections)]
        for yy in range(sections):
            for hh in range(spans):
                for kk in range(2):
                    for xx in range(2):
                        for cc in range(2):
                            share = (cc * 2 + kk) * sections + yy
                            number = share * (2 * spans) + hh * 2 + xx
                            device = yy * plane + ((hh * 2 + kk) * 2 + xx) * 2 + cc
                            owner = layer * plane + number // sections
                            routes[number % sections].append((owner, device))
        return routes

    share_index = (c * 2 + k) * sections + y
    out_part = (share_index * (2 * spans) + h * 2 + x) % sections

    by_shard = columns_by_shard(low_qkv, low_up)
    give = shift(pick(by_shard, 1 - c), "c", 1)
    over_c = ordered(pick(by_shard, c), give, c, 1)
    give = shift(pick(over_c, 1 - k), "k", 1)
    over_k = ordered(pick(over_c, k), give, k, 0)

    gain0, bias0 = vec_all[0, :width], vec_all[0, width : 2 * width]
    bias_down0, bias_up0 = vec_all[0, 2 * width : 3 * width], vec_all[0, 3 * width :]
    h0_full, normed0, inverse0 = layer_norm(embed, gain0, bias0)
    h0 = h0_full.astype(LOW)
    pair_rows = 2 * own_in
    h0_here = jnp.concatenate(
        [
            lax.dynamic_slice_in_dim(h0, ((h * 2 + kk) * 2 + x) * pair_rows, pair_rows, 1)
            for kk in range(2)
        ],
        1,
    )
    both = [
        mm(h0_here, over_k[:, :, yy].reshape(4 * own_in, -1)) for yy in range(sections)
    ]
    spread_over = 2 * spans
    token_rows = vocab // spread_over
    proj_part = jnp.concatenate([part[:, : 3 * shard_width] for part in both], 1)
    proj_part = proj_part.reshape(spread_over, -1, own_ff)
    u_part = jnp.stack(
        [
            jnp.concatenate(
                [
                    part[:, 3 * shard_width + j * part_ff : 3 * shard_width + (j + 1) * part_ff]
                    for part in both
                ],
                1,
            )
            for j in range(spread_over)
        ]
    )
    mixed = jnp.sum(trade(jnp.concatenate([u_part, proj_part], 1), ("h", "x")), 0)
    u_own = mixed[:vocab] + lax.dynamic_slice_in_dim(bias_up0, me * own_ff, own_ff, 0)
    proj_own = mixed[vocab:]
    a0, slope0 = gelu_pair(u_own)
    a0 = a0.astype(LOW)
    ffn_part = jnp.where(y == 0, mm(a0, low_down), 0.0)
    for yy in range(1, sections):
        got = lax.ppermute(proj_own, "y", [(0, yy)])
        proj_own = jnp.where(y == yy, got, proj_own)
    proj_all = spread(proj_own, PLANE)
    ffn_cols = trade(ffn_part.reshape(vocab, everyone, -1).transpose(1, 0, 2), ALL)
    ffn_cols = jnp.sum(ffn_cols, 0)
    proj_table = (
        proj_all.reshape(spans, 2, 2, 2, token_rows, sections, 3, shard_width)
        .transpose(0, 2, 4, 6, 3, 1, 5, 7)
        .reshape(vocab, 3 * width)
    )
    ffn_table = spread(ffn_cols, ALL).transpose(1, 0, 2).reshape(vocab, width)
    query0, keys0, values0, att0 = first_forward(
        proj_table, hot_own, hot_pack, own_rope, pack_rope, own_bias, own_packs
    )

    first_out = low_out
    for yy in range(1, sections):
        got = lax.ppermute(low_out, "y", [(0, yy)])
        first_out = jnp.where(y == yy, got, first_out)
    pieces = jnp.stack([first_out] + [shift(first_out, "h", s) for s in range(1, spans)])
    pieces = jnp.take(pieces, (h - jnp.arange(spans)) % spans, axis=0)
    pieces = after(pieces, h0)
    pieces = ordered(pieces, after(shift(pieces, "k", 1), mixed), k, 1)
    pieces = ordered(pieces, after(shift(pieces, "x", 1), proj_table), x, 2)
    pieces = ordered(pieces, after(shift(pieces, "c", 1), att0), c, 3)
    first_out = pieces.reshape(width, width)

    stay = embed + ffn_table + bias_down0
    x_low, h_low = first_finish(
        att0, first_out, hot_own, stay, vec_all[1, :width], vec_all[1, width : 2 * width]
    )

    shard_weights = []
    for layer in range(1, sections):
        cut_down = low_down.reshape(sections, part_ff, width)
        down_piece = cut_down[layer]
        for yy in range(sections):
            if yy != layer:
                got = lax.ppermute(cut_down[yy], "y", [(layer, yy)])
                down_piece = jnp.where(y == yy, got, down_piece)
        cut_out = low_out.reshape(sections, small_out, width)
        out_piece = jnp.zeros((small_out, width), LOW)
        for p, route in enumerate(out_routes(layer)):
            got = lax.ppermute(cut_out[p], ALL, route)
            out_piece = jnp.where(out_part == p, got, out_piece)
        tail = jnp.concatenate([down_piece, out_piece], 0)
        tail = across_gather(tail, x, h0, ffn_part, att0)
        w_down = tail[:, :, :part_ff].reshape(shard_ff, width)
        w_out = tail[:, :, part_ff:].reshape(shard_width, width)
        mine = over_k[:, :, layer]
        for yy in range(sections):
            if yy != layer:
                got = lax.ppermute(over_k[:, :, yy], "y", [(layer, yy)])
                mine = jnp.where(y == yy, got, mine)
        whole = across_gather(mine, x, mixed, proj_table, h_low)
        w_in = whole.transpose(0, 2, 1, 3, 4, 5).reshape(width, -1)
        if shard_width < LANES:
            pad = LANES - shard_width
            cut = [w_in[:, j * shard_width : (j + 1) * shard_width] for j in range(3)]
            cut = [jnp.pad(piece, ((0, 0), (0, pad))) for piece in cut]
            w_in = jnp.concatenate(cut + [w_in[:, 3 * shard_width :]], 1)
            w_out = jnp.pad(w_out, ((0, pad), (0, 0)))
        shard_weights.append((w_in, w_out, w_down))

    kept = []
    for layer in range(1, sections):
        w_in, w_out, w_down = shard_weights[layer - 1]
        vec = vec_all[layer]
        gain, bias, bias_down = (vec[j * width : (j + 1) * width] for j in range(3))
        cut = vec[3 * width :].reshape(spans, 2, 2, 2, sections, part_ff)
        cut = lax.dynamic_index_in_dim(cut, k, 1, keepdims=False)
        cut = lax.dynamic_index_in_dim(cut, c, 2, keepdims=False)
        bias_up = lax.dynamic_index_in_dim(cut, y, 2, keepdims=False).reshape(shard_ff)
        if layer > 1:
            x_low = xs.astype(LOW)
            h_low = layer_norm(x_low.astype(F32), gain, bias)[0].astype(LOW)
        hs = to_group(h_low)
        keep, send, qkv, att, act, slope = upper_forward(
            hs, w_in, w_out, w_down, bias_up, group_rope, group_bias, slots
        )
        kept.append((x_low, gain, bias, hs, qkv, att, act, slope))
        pieces = from_group(keep, send)
        if layer < sections - 1:
            xs = x_low.astype(F32) + sum(piece.astype(F32) for piece in pieces) + bias_down

    normed_f, inverse_f, final_low, logp, lik_sum = loss_forward(
        x_low, pieces, bias_down, final_gain, final_bias, head_low, out_bias, target_hot, seq_weight
    )
    sums = spread(jnp.concatenate([lik_sum[0], seq_count]), ALL)
    dy, own_low, table_local, bias_local, down_sum, scalars = loss_backward(
        sums,
        partners,
        me[None],
        normed_f,
        inverse_f,
        final_low,
        logp,
        head_low,
        final_gain,
        target_hot,
        seq_weight,
        plane,
    )
    loss_total, count_total = scalars[0, 0], scalars[0, 1]
    penalty_local = jnp.where(y == 0, scalars[0, 2], 0.0)
    bias_local = bias_local[0]

    def finish_shards(layer, out_grad, down_grad, in_grad, first, second, last):
        tail = jnp.concatenate(
            [
                down_grad.reshape(spans, 2, part_ff, width),
                out_grad.reshape(spans, 2, small_out, width),
            ],
            2,
        )
        tail = across_scatter(tail, x, first, second, last).astype(LOW)
        down_piece, out_piece = tail[:part_ff], tail[part_ff:]
        down_rows = jnp.stack(
            [
                down_piece if yy == layer else lax.ppermute(down_piece, "y", [(yy, layer)])
                for yy in range(sections)
            ]
        ).reshape(own_ff, width)
        out_rows = jnp.stack(
            [
                lax.ppermute(out_piece, ALL, [(b, a) for a, b in route])
                for route in out_routes(layer)
            ]
        ).reshape(own_out, width)
        inner = in_grad.reshape(spans, 2, 2, 2, own_in, -1).transpose(0, 2, 1, 3, 4, 5)
        inner = across_scatter(inner, x, first, second, last).astype(LOW)
        keep = pick(inner, k)
        give = shift(pick(inner, 1 - k), "k", 1)
        over_k = ordered(keep, give, k, 1)
        keep = pick(over_k, c)
        give = shift(pick(over_k, 1 - c), "c", 1)
        over_c = ordered(keep, give, c, 0)
        shards = jnp.stack(
            [
                over_c if yy == layer else lax.ppermute(over_c, "y", [(yy, layer)])
                for yy in range(sections)
            ],
            2,
        )
        qkv_rows, up_rows = columns_back(shards)
        return (qkv_rows, out_rows, up_rows, down_rows)

    pending = []
    vector_locals = []
    for layer in range(sections - 1, 0, -1):
        w_in, w_out, w_down = shard_weights[layer - 1]
        x_low, gain, bias, hs, qkv, att, act, slope = kept[layer - 1]
        d_rows = to_group(own_low)
        keep, send, d_in, bias_up_grad = upper_backward(
            d_rows, qkv, slope, w_in, w_out, w_down, group_rope, group_bias, slots
        )
        pieces = from_group(keep, send)
        above = dy
        own_low, vec_sums, dyb_token = input_backward(pieces, x_low, dy, gain, hot_own)
        dy = own_low.astype(F32)
        att, act, hs, d_in, d_rows = lax.optimization_barrier((att, act, hs, d_in, d_rows, keep))[:5]
        out_grad = t_mm(att, d_rows)[:shard_width]
        down_grad = t_mm(act, d_rows)
        in_grad = t_mm(hs, d_in)
        if shard_width < LANES:
            cut = [in_grad[:, j * LANES : j * LANES + shard_width] for j in range(3)]
            in_grad = jnp.concatenate(cut + [in_grad[:, 3 * LANES :]], 1)
        bias_up_grad = bias_up_grad.reshape(spans, 2, part_ff)
        place = (
            (jnp.arange(2) == k)[None, :, None, None, None, None]
            & (jnp.arange(2) == c)[None, None, None, :, None, None]
            & (jnp.arange(sections) == y)[None, None, None, None, :, None]
        )
        bias_up_grad = jnp.where(place, bias_up_grad[:, None, :, None, None, :], 0.0)
        vector_locals.append(
            jnp.concatenate([vec_sums[0], vec_sums[1], down_sum[0], bias_up_grad.reshape(-1)])
        )
        down_sum = vec_sums[2:3]
        pending.append((layer, out_grad, down_grad, in_grad, keep))
    vector_locals = vector_locals[::-1]

    dyb_cols = trade(dyb_token.reshape(vocab, everyone, -1).transpose(1, 0, 2), ALL)
    dq_token, dk_token, dv_token, first_out_grad = first_backward(
        own_low,
        query0,
        keys0,
        values0,
        att0,
        hot_own,
        hot_pack,
        own_rope,
        pack_rope,
        own_bias,
        first_out,
        own_packs,
    )
    dyb_cols = jnp.sum(after(dyb_cols, first_out_grad), 0)
    dyb_sum = spread(dyb_cols, ALL).transpose(1, 0, 2).reshape(vocab, width)
    token_part = jnp.concatenate([dq_token, dk_token, dv_token], 1)
    token_cols = trade(token_part.reshape(vocab, everyone, -1).transpose(1, 0, 2), ALL)
    token_cols = jnp.sum(token_cols, 0).astype(LOW)
    du_own = (mm_exact(dyb_sum, low_down, ((1,), (1,))) * slope0).astype(LOW)
    du_sum = spread(du_own, PLANE).transpose(1, 0, 2).reshape(vocab, hidden)
    dproj_sum = spread(token_cols, ALL).transpose(1, 0, 2).reshape(vocab, 3 * width)
    dh_own = mm_t(dproj_sum, low_qkv) + mm_t(du_sum, low_up)

    shard_grads = [None] * sections
    for layer, out_grad, down_grad, in_grad, keep in pending:
        shard_grads[layer] = finish_shards(
            layer, out_grad, down_grad, in_grad, own_low, first_out_grad, du_own
        )
    vector_cut = jnp.stack([jnp.zeros_like(vector_locals[0])] + vector_locals)
    vector_cut = vector_cut.reshape(everyone, vector_part)
    table_cut = table_local.reshape(-1, everyone, table_part).transpose(1, 0, 2)
    mixed = jnp.concatenate([vector_cut, table_cut.reshape(everyone, -1)], 1)
    mixed = jnp.sum(trade(after(mixed, first_out_grad), ALL), 0)
    h0_own = lax.dynamic_slice_in_dim(h0, me * own_in, own_in, 1)
    down_first = mm_exact(a0, dyb_sum, ((0,), (0,)))
    qkv_first = t_mm(h0_own, dproj_sum)
    up_first = t_mm(h0_own, du_sum)
    part = first_out_grad.reshape(spans, 2, 2, 2, own_out, width)
    part = jnp.moveaxis(part, 3, 0)
    part = pick(part, c) + shift(pick(part, 1 - c).astype(LOW), "c", 1).astype(F32)
    part = jnp.moveaxis(part, 2, 0)
    part = pick(part, x) + shift(pick(part, 1 - x).astype(LOW), "x", 1).astype(F32)
    part = jnp.moveaxis(part, 1, 0)
    part = pick(part, k) + shift(pick(part, 1 - k).astype(LOW), "k", 1).astype(F32)
    total = pick(part, h)
    for s in range(1, spans):
        total = total + shift(pick(part, (h + s) % spans).astype(LOW), "h", s).astype(F32)
    out_first = total
    for yy in range(1, sections):
        out_first = out_first + lax.ppermute(total.astype(LOW), "y", [(yy, 0)]).astype(F32)

    first = (qkv_first, out_first, up_first, down_first)
    grads = []
    for number in range(4):
        grad = first[number]
        for layer in range(1, sections):
            grad = jnp.where(y == layer, shard_grads[layer][number].astype(F32), grad)
        grads.append(grad[None])
    mixed_vector = mixed[:vector_part]
    mixed_table = mixed[vector_part:].reshape(-1, table_part)

    squares = sum((jnp.sum(g * g) for g in grads)) + jnp.sum(mixed_table * mixed_table)
    squares = squares + jnp.where(y == 0, 0.0, jnp.sum(mixed_vector * mixed_vector))
    up_sum = jnp.sum(du_sum.astype(F32), 0)
    down_sum = jnp.sum(dyb_sum, 0)
    squares = squares + jnp.where(
        (y == 0) & (me == 0), jnp.sum(up_sum * up_sum) + jnp.sum(down_sum * down_sum), 0.0
    )
    last = jnp.concatenate([squares[None], penalty_local[None], bias_local])
    last = jnp.pad(last, (0, (-last.shape[0]) % own_in)).reshape(-1, own_in)
    last = spread(jnp.concatenate([dh_own, last], 0), ALL)
    dh = last[:plane, :vocab].transpose(1, 0, 2).reshape(vocab, width)
    last = jnp.sum(last[:, vocab:], 0).reshape(-1)
    embed_grad = dyb_sum + norm_back(dh, normed0, inverse0, gain0)
    gain_grad, shift_grad = jnp.sum(dh * normed0, 0), jnp.sum(dh, 0)
    vector_first = jnp.concatenate([gain_grad, shift_grad, down_sum, up_sum])
    vector_own = lax.dynamic_slice_in_dim(vector_first, me * vector_part, vector_part, 0)
    vector_grad = jnp.where(y == 0, vector_own, mixed_vector)
    number = y * plane + me
    embed_own = lax.dynamic_slice_in_dim(embed_grad, number * table_part, table_part, 1)
    table_grad = jnp.concatenate([embed_own, mixed_table], 0)
    penalty = last[1]
    bias_grad = last[2 : 2 + vocab]
    squares = last[0] + jnp.sum(embed_grad * embed_grad) + jnp.sum(bias_grad * bias_grad)
    squares = squares + jnp.sum(gain_grad * gain_grad) + jnp.sum(shift_grad * shift_grad)
    grad_norm = jnp.sqrt(squares)
    factor = jnp.minimum(1.0, CLIP_AT / grad_norm)
    grads = grads + [vector_grad[None], table_grad, bias_grad]
    masters = (qkv_weight, out_weight, up_weight, down_weight, vectors, tables, head_bias)
    moments = (
        qkv_moment,
        out_moment,
        up_moment,
        down_moment,
        vector_moment,
        table_moment,
        bias_moment,
    )
    squares_in = (
        qkv_square,
        out_square,
        up_square,
        down_square,
        vector_square,
        table_square,
        bias_square,
    )
    rates = (RATE_MAT, RATE_OUT, RATE_MAT, RATE_MAT, RATE_VEC, RATE_VEC, RATE_VEC)
    decays = (DECAY, DECAY, DECAY, DECAY, 0.0, 0.0, 0.0)
    results = []
    for number in range(7):
        results.extend(
            adam(
                masters[number],
                moments[number],
                squares_in[number],
                grads[number] * factor,
                rates[number],
                decays[number],
            )
        )
    loss_parts = jnp.stack([loss_total, count_total, penalty])
    return (grad_norm, loss_parts, *results)


def solution(mesh):
    sections, plane = mesh.shape["section"], mesh.shape["dp"]
    fine = Mesh(mesh.devices.reshape(sections, plane // 8, 2, 2, 2), ALL)
    matrix = P("y", PLANE, None)
    vector = P("y", PLANE)
    table = P(None, ALL)
    states = (matrix, matrix, matrix, matrix, vector, table, P())
    results = []
    for spec in states:
        results.extend([spec] * 3)
    chosen = body_fast if (sections, plane) == (2, 16) else body
    return jax.shard_map(
        chosen,
        mesh=fine,
        in_specs=(P(PLANE, None), P(PLANE, None), P(PLANE, None), P(PLANE))
        + states
        + states
        + states,
        out_specs=(P(), P(), *results),
        check_vma=False,
    )
```
